32 devices in a mesh: expert: 8 (over z, y), wshard: 4 (over x, core).
Axes of the slice: x: 2, y: 2, z: 4, core: 2. Of those that a mesh axis runs over, the one named last changes fastest.
Arguments:
- tokens: bfloat16 [12288, 1536], P(('expert', 'wshard')), may hold values from -6 to 6
- segments: int32 [32, 384], P(('expert', 'wshard')), may hold values from 0 to 3, never falling along the last dimension, each value on 1 to 192 neighbouring positions
- routes: int32 [12288, 4], P(('expert', 'wshard')), may hold values from 0 to 31, all different within a row; in each aligned block of 384 rows (0 to 383, 384 to 767, ...) at most 72 rows name the same one
- attn_gain: float32 [1536], replicated, may hold values from 0.5 to 1.5
- ffn_gain: float32 [1536], replicated, may hold values from 0.5 to 1.5
- w_query: bfloat16 [1536, 1536], P('wshard'), may hold values from -0.15625 to 0.15625
- key_weight: bfloat16 [1536, 256], P('wshard'), may hold values from -0.15625 to 0.15625
- value_weight: bfloat16 [1536, 256], P('wshard'), may hold values from -0.15625 to 0.15625
- w_out: bfloat16 [1536, 1536], P('wshard'), may hold values from -1.25 to 1.25
- w_router: bfloat16 [1536, 32], P('wshard'), may hold values from -0.078125 to 0.078125
- w_gate: bfloat16 [1536, 24576], P(None, 'expert'), may hold values from -0.15625 to 0.15625
- w_up: bfloat16 [1536, 24576], P(None, 'expert'), may hold values from -0.15625 to 0.15625
- w_down: bfloat16 [24576, 1536], P('expert'), may hold values from -0.21875 to 0.21875
- cotangent: bfloat16 [12288, 1536], P(('expert', 'wshard')), may hold values from -6 to 6
Outputs:
- mixed: bfloat16 [12288, 1536], P(('expert', 'wshard'))
- input_grad: float32 [12288, 1536], P(('expert', 'wshard'))
- attn_gain_grad: float32 [1536], P('wshard')
- ffn_gain_grad: float32 [1536], P('wshard')
- w_query_grad: float32 [1536, 1536], P('wshard')
- w_key_grad: float32 [1536, 256], P('wshard')
- w_value_grad: float32 [1536, 256], P('wshard')
- w_out_grad: float32 [1536, 1536], P('wshard')
- w_router_grad: float32 [1536, 32], P('wshard')
- w_gate_grad: float32 [1536, 24576], P('wshard', 'expert')
- w_up_grad: float32 [1536, 24576], P('wshard', 'expert')
- w_down_grad: float32 [24576, 1536], P('expert', 'wshard')
The draws below stay inside these ranges and needn't reach their ends.
Inputs may be any that keep to these rules, and one draw needn't show every extreme that they name: `routes`: in the rows of one device no expert is named by more than 72 rows, a bound that some block reaches of them; a row names 4 different experts. `segments`: along a sequence the document numbers never fall; a document spans at most 192 positions.
All inputs are finite; a program needn't handle non-finite values.
Results may differ from the reference program's by a relative error of at most 0.018.
Values may be sent and summed in bfloat16 or wider, within the bound.
No kernel may reach another device: no remote copies, remote signals or barrier semaphores. Data moves between devices by JAX's collectives and lax.ppermute only.
A program may use at most 256 MiB of HBM per device.

```python
import math
import jax
import jax.numpy as jnp
import numpy as np
from jax import lax

MODEL_DIM = 1536
QUERY_HEADS = 12
KEY_VALUE_HEADS = 2
HEAD_DIM = 128
FF = 768
TOP = 4
EXPERTS = 32
TOKENS_PER_SEQ = 384
SEQUENCE_COUNT = 32
TOKEN_COUNT = 12288
OWN = 1
FF_DEV = 768
CAP = 72


def block_levels(stream_key, extent, split, low, top_value):
    factor_of, own = 1.0, jax.random.fold_in(stream_key, 6)
    for dim, shards_of in split:
        draws = jnp.exp(jax.random.uniform(jax.random.fold_in(own, dim), (shards_of,), jnp.float32, low / len(split), top_value / len(split)))
        factor_of = factor_of * jnp.repeat(draws, extent[dim] // shards_of).reshape([-1 if axis == dim else 1 for axis in range(len(extent))])
    return factor_of


def split_up(amount, total, limit, skew):
    weights = [(1 << 20) // math.isqrt(grade ** skew) + 1 for grade in range(2, amount + 1)]
    surplus, holding = total - limit - (amount - 1), [1] * (amount - 1)
    while surplus > 0:
        movable = [i for i in range(amount - 1) if holding[i] < limit]
        whole, budget = sum([weights[i] for i in movable]), surplus
        for i in movable:
            addition = min(limit - holding[i], max(1, budget * weights[i] // whole), surplus)
            holding[i] = holding[i] + addition
            surplus = surplus - addition
    return np.array([limit] + holding)


def ragged(rng, count, total, bound, lean):
    if count == 2:
        one = jax.random.randint(rng, (), max(1, total - bound), min(bound, total - 1) + 1)
        return jnp.stack([one, total - one])
    sizes = jnp.asarray(split_up(count, total, bound, lean), jnp.int32)
    pairs = (count - 1) // 2
    source_of, taker = sizes[1:1 + 2 * pairs:2], sizes[2:2 + 2 * pairs:2]
    slack = jnp.minimum(source_of - 1, bound - taker)
    passed = jax.random.randint(jax.random.fold_in(rng, 1), (pairs,), 0, 1 << 20) % (slack + 1)
    sizes = sizes.at[1:1 + 2 * pairs:2].set(source_of - passed).at[2:2 + 2 * pairs:2].set(taker + passed)
    return sizes[jax.random.permutation(jax.random.fold_in(rng, 2), count)]


def assign_block(own_key, own, number, rows, number_of, top, limit, lean):
    order = jax.random.permutation(own_key, number_of)
    heavy_load, usual = portions_of(number_of, rows * top, limit, lean, True), portions_of(number_of, rows * top, limit, lean, False)
    places = jnp.arange(number_of)

    def named(lengths, turn):
        used = int((lengths > 0).sum())
        fixed = max(1, used // 4)
        shifted = fixed + (places - fixed + turn * (used - fixed)) % max(1, number_of - fixed)
        return jnp.zeros((number_of,), jnp.int32).at[order[jnp.where(places < fixed, places, shifted)]].set(jnp.asarray(lengths, jnp.int32))

    lengths = jnp.where(number % 4 == 0, named(heavy_load, number // 4), named(usual, number - number // 4 - 1))
    mixed = jax.random.permutation(jax.random.fold_in(own, 3), number_of)
    source_of, taker = mixed[0:number_of // 2 * 2:2], mixed[1:number_of // 2 * 2:2]
    slack = jnp.minimum(lengths[source_of] - 1, limit - lengths[taker]) // 2
    slack = jnp.where((source_of == order[0]) | (taker == order[0]) | (lengths[taker] == 0), 0, jnp.maximum(slack, 0))
    shifted = jax.random.randint(jax.random.fold_in(own, 4), (number_of // 2,), 0, 1 << 20) % (slack + 1)
    lengths = lengths.at[source_of].add(-shifted).at[taker].add(shifted)
    items = jnp.searchsorted(jnp.cumsum(lengths), jnp.arange(rows * top), side="right").astype(jnp.int32)
    table = items.reshape(top, rows).T
    table = table[jax.random.permutation(jax.random.fold_in(own, 1), rows)]
    turn = jax.random.randint(jax.random.fold_in(own, 2), (rows, 1), 0, top)
    return jnp.take_along_axis(table, (jnp.arange(top)[None, :] + turn) % top, axis=1)


def portions_of(amount, total, limit, lean, full):
    weights = [(1 << 20) // math.isqrt(standing ** lean) + 1 for standing in range(1, amount + 1)]
    largest = limit if full else min(limit, max(-(-total // amount), total * weights[0] // sum(weights)))
    least = 1 if total - largest >= amount - 1 else 0
    given, surplus = [largest] + [least] * (amount - 1), total - largest - least * (amount - 1)
    while surplus > 0:
        candidates = [i for i in range(1, amount) if given[i] < largest] or [i for i in range(1, amount) if given[i] < limit]
        whole, remaining = sum([weights[i] for i in candidates]), surplus
        for i in candidates:
            extra = min(limit - given[i], max(1, remaining * weights[i] // whole), surplus)
            given[i] = given[i] + extra
            surplus = surplus - extra
    return np.array(given)


def noise(rng, dims, spread, bound, split=(), kind=jnp.bfloat16):
    array = jax.random.normal(rng, dims, jnp.float32) * spread
    if len(split) > 0:
        array = block_levels(rng, dims, split, -0.22, 0.18) * array
    return jnp.clip(array, min=-bound, max=bound).astype(kind)


def setup_inputs(seed: int = 0) -> dict:
    arg_keys = jax.random.split(jax.random.key(seed), 15)
    tokens = noise(arg_keys[0], (TOKEN_COUNT, MODEL_DIM), 1.0, 6.0, ((0, 32),))
    segments = jax.vmap(lambda own: jnp.searchsorted(jnp.cumsum(ragged(own, 4, TOKENS_PER_SEQ, TOKENS_PER_SEQ // 2, 1)), jnp.arange(TOKENS_PER_SEQ), side="right"))(jax.random.split(arg_keys[1], SEQUENCE_COUNT)).reshape((SEQUENCE_COUNT, TOKENS_PER_SEQ)).astype(jnp.int32)
    routes_keys = jax.random.split(jax.random.fold_in(arg_keys[2], 1), TOKEN_COUNT // TOKENS_PER_SEQ)
    routes_turns = jax.random.permutation(jax.random.fold_in(arg_keys[2], 3), TOKEN_COUNT // TOKENS_PER_SEQ)
    routes = jax.vmap(lambda own, number: assign_block(jax.random.fold_in(arg_keys[2], 2), own, number, TOKENS_PER_SEQ, EXPERTS, TOP, CAP, 2))(routes_keys, routes_turns).reshape((TOKEN_COUNT, TOP))
    attn_gain = jnp.clip(1.0 + 0.1 * jax.random.normal(arg_keys[3], (MODEL_DIM,), jnp.float32), 0.5, 1.5)
    ffn_gain = jnp.clip(1.0 + 0.1 * jax.random.normal(arg_keys[4], (MODEL_DIM,), jnp.float32), 0.5, 1.5)
    w_query = noise(arg_keys[5], (MODEL_DIM, QUERY_HEADS * HEAD_DIM), MODEL_DIM ** -0.5, 0.15625, ((0, 4),))
    key_weight = noise(arg_keys[6], (MODEL_DIM, KEY_VALUE_HEADS * HEAD_DIM), MODEL_DIM ** -0.5, 0.15625, ((0, 4),))
    value_weight = noise(arg_keys[7], (MODEL_DIM, KEY_VALUE_HEADS * HEAD_DIM), MODEL_DIM ** -0.5, 0.15625, ((0, 4),))
    w_out = noise(arg_keys[8], (QUERY_HEADS * HEAD_DIM, MODEL_DIM), (QUERY_HEADS * HEAD_DIM // 64) ** -0.5, 1.25, ((0, 4),))
    w_router = noise(arg_keys[9], (MODEL_DIM, EXPERTS), (4 * MODEL_DIM) ** -0.5, 0.078125, ((0, 4),))
    w_gate = noise(arg_keys[10], (MODEL_DIM, EXPERTS * FF), MODEL_DIM ** -0.5, 0.15625, ((1, 8),))
    w_up = noise(arg_keys[11], (MODEL_DIM, EXPERTS * FF), MODEL_DIM ** -0.5, 0.15625, ((1, 8),))
    w_down = noise(arg_keys[12], (EXPERTS * FF, MODEL_DIM), FF ** -0.5, 0.21875, ((0, 8),))
    cotangent = noise(arg_keys[13], (TOKEN_COUNT, MODEL_DIM), 1.0, 6.0, ((0, 32),))
    return {"tokens": tokens, "segments": segments, "routes": routes, "attn_gain": attn_gain, "ffn_gain": ffn_gain, "w_query": w_query, "key_weight": key_weight, "value_weight": value_weight, "w_out": w_out, "w_router": w_router, "w_gate": w_gate, "w_up": w_up, "w_down": w_down, "cotangent": cotangent}


EPS = 1e-06
ROPE_BASE = 10000.0
NEG = -1e+30
HIGHEST = lax.Precision.HIGHEST

@jax.custom_vjp
def cast_lower(v):
    return lax.optimization_barrier(v.astype(jnp.bfloat16)).astype(jnp.float32)

@jax.custom_vjp
def low_back(v):
    return v

def low_keep(v):
    return (cast_lower(v), None)

def low_pass(kept, grad):
    return (grad,)

def back_keep(v):
    return (v, None)

def back_low(kept, grad):
    return (cast_lower(grad),)
cast_lower.defvjp(low_keep, low_pass)
low_back.defvjp(back_keep, back_low)

def matmul_high(left, right):
    return jnp.dot(left, right, precision=HIGHEST)

def norm_apply(values, gain):
    return values * lax.rsqrt(lax.optimization_barrier(jnp.mean(values * values, axis=-1, keepdims=True)) + EPS) * gain

def rotary_tables(seq_length, head_size):
    half_size = head_size // 2
    frequency = ROPE_BASE ** (-(jnp.arange(half_size, dtype=jnp.float32) * 2.0 / head_size))
    angles = jnp.arange(seq_length, dtype=jnp.float32)[:, None] * frequency[None, :]
    return (jnp.cos(angles), jnp.sin(angles))

def apply_rotation(values, cosine_lookup, sine_lookup):
    half_size = values.shape[-1] // 2
    first_half = values[..., :half_size]
    second_half = values[..., half_size:]
    cos_part = cosine_lookup[:, None, :]
    sin_part = sine_lookup[:, None, :]
    return jnp.concatenate([first_half * cos_part - second_half * sin_part, second_half * cos_part + first_half * sin_part], axis=-1)

def reference(tokens, segments, routes, attn_gain, ffn_gain, w_query, key_weight, value_weight, w_out, w_router, w_gate, w_up, w_down, cotangent):
    pair_count = TOKEN_COUNT * TOP
    flat_routes = routes.reshape(pair_count).astype(jnp.int32)
    one_hot = (flat_routes[:, None] == jnp.arange(EXPERTS, dtype=jnp.int32)[None, :]).astype(jnp.int32)
    slot_rank = lax.optimization_barrier(jnp.sum((jnp.cumsum(one_hot, axis=0).astype(jnp.int32) - 1) * one_hot, axis=1)).astype(jnp.int32)
    rows_most = SEQUENCE_COUNT * CAP
    table = jnp.full((EXPERTS, rows_most), pair_count, jnp.int32).at[flat_routes, slot_rank].set(jnp.arange(pair_count, dtype=jnp.int32))
    cosine_lookup, sine_lookup = rotary_tables(TOKENS_PER_SEQ, HEAD_DIM)
    cosine_full = jnp.tile(cosine_lookup, (SEQUENCE_COUNT, 1))
    sine_full = jnp.tile(sine_lookup, (SEQUENCE_COUNT, 1))
    positions = jnp.arange(TOKENS_PER_SEQ, dtype=jnp.int32)
    offset = positions[:, None] - positions[None, :]
    causal_mask = offset >= 0
    choose = (routes[:, :, None] == jnp.arange(EXPERTS, dtype=jnp.int32)[None, None, :]).astype(jnp.float32)
    score_scale = HEAD_DIM ** (-0.5)

    def single_sequence(items):
        query_sequence, key_seq, value_seq, segment_row = items
        allowed = causal_mask & (segment_row[:, None] == segment_row[None, :])
        grouped_query = query_sequence.reshape(TOKENS_PER_SEQ, KEY_VALUE_HEADS, QUERY_HEADS // KEY_VALUE_HEADS, HEAD_DIM)
        raw_scores = low_back(jnp.einsum('qagd,kad->agqk', grouped_query, key_seq, precision=HIGHEST))
        scores = jnp.where(allowed, raw_scores * score_scale, NEG)
        attn_probs = cast_lower(jax.nn.softmax(scores, axis=-1))
        return jnp.einsum('agqk,kad->qagd', attn_probs, value_seq, precision=HIGHEST).reshape(TOKENS_PER_SEQ, QUERY_HEADS * HEAD_DIM)

    def forward(stream, gain_one, gain_two, query_w, key_w, value_w, out_w, router_w, gate_w, up_w, down_w):
        first_low = cast_lower(norm_apply(stream, gain_one))
        query_pre = low_back(matmul_high(first_low, query_w))
        key_unrotated = low_back(matmul_high(first_low, key_w))
        value_lowered = cast_lower(low_back(matmul_high(first_low, value_w)))
        query_rotated = cast_lower(apply_rotation(query_pre.reshape(TOKEN_COUNT, QUERY_HEADS, HEAD_DIM), cosine_full, sine_full))
        key_rotated = cast_lower(apply_rotation(key_unrotated.reshape(TOKEN_COUNT, KEY_VALUE_HEADS, HEAD_DIM), cosine_full, sine_full))
        attended_output = lax.map(jax.checkpoint(single_sequence), (query_rotated.reshape(SEQUENCE_COUNT, TOKENS_PER_SEQ, QUERY_HEADS, HEAD_DIM), key_rotated.reshape(SEQUENCE_COUNT, TOKENS_PER_SEQ, KEY_VALUE_HEADS, HEAD_DIM), value_lowered.reshape(SEQUENCE_COUNT, TOKENS_PER_SEQ, KEY_VALUE_HEADS, HEAD_DIM), segments))
        attn_low = cast_lower(low_back(attended_output.reshape(TOKEN_COUNT, QUERY_HEADS * HEAD_DIM)))
        resid = stream + low_back(matmul_high(attn_low, out_w))
        second_low = cast_lower(norm_apply(resid, gain_two))
        logits = low_back(matmul_high(second_low, router_w))
        selected = lax.optimization_barrier(jnp.sum(choose * logits[:, None, :], axis=-1))
        gate_probs = jax.nn.softmax(selected, axis=-1)
        gate_ext = jnp.concatenate([gate_probs.reshape(pair_count), jnp.zeros((1,), jnp.float32)])
        second_ext = jnp.concatenate([second_low, jnp.zeros((1, MODEL_DIM), jnp.float32)], axis=0)
        gate_stack = gate_w.reshape(MODEL_DIM, EXPERTS, FF).transpose(1, 0, 2)
        up_stack = up_w.reshape(MODEL_DIM, EXPERTS, FF).transpose(1, 0, 2)
        down_stack = down_w.reshape(EXPERTS, FF, MODEL_DIM)

        def one_expert(accum, items):
            entries, gate_e, up_e, down_e = items
            token_rows = entries // TOP
            expert_rows = second_ext[token_rows]
            rows_split = low_back(jnp.broadcast_to(expert_rows[None], (OWN, expert_rows.shape[0], MODEL_DIM)))
            gate_pre = low_back(jnp.einsum('ord,dof->orf', rows_split, gate_e.reshape(MODEL_DIM, OWN, FF_DEV), precision=HIGHEST))
            up_pre = low_back(jnp.einsum('ord,dof->orf', rows_split, up_e.reshape(MODEL_DIM, OWN, FF_DEV), precision=HIGHEST))
            hidden = cast_lower(jax.nn.silu(gate_pre) * up_pre)
            partial_value = cast_lower(low_back(jnp.einsum('orf,ofd->ord', hidden, down_e.reshape(OWN, FF_DEV, MODEL_DIM), precision=HIGHEST)))
            result = lax.optimization_barrier(jnp.sum(partial_value, axis=0))
            return (accum.at[token_rows].add(gate_ext[entries][:, None] * result), None)
        moe_ext, unused = lax.scan(jax.checkpoint(one_expert), jnp.zeros((TOKEN_COUNT + 1, MODEL_DIM), jnp.float32), (table, gate_stack, up_stack, down_stack))
        return resid + moe_ext[:TOKEN_COUNT]
    inputs = (tokens.astype(jnp.float32), attn_gain.astype(jnp.float32), ffn_gain.astype(jnp.float32), w_query.astype(jnp.float32), key_weight.astype(jnp.float32), value_weight.astype(jnp.float32), w_out.astype(jnp.float32), w_router.astype(jnp.float32), w_gate.astype(jnp.float32), w_up.astype(jnp.float32), w_down.astype(jnp.float32))
    output, pullback = jax.vjp(forward, *inputs)
    grads = pullback(cotangent.astype(jnp.float32))
    return (output.astype(jnp.bfloat16), grads[0], grads[1], grads[2], grads[3], grads[4], grads[5], grads[6], grads[7], grads[8], grads[9], grads[10])
```

```python
import functools

import jax
import jax.numpy as jnp
from jax import lax
from jax.experimental import pallas as pl
from jax.experimental.pallas import tpu as pltpu
from jax.sharding import PartitionSpec as P

QUERY_HEADS = 12
KEY_VALUE_HEADS = 2
HEAD_DIM = 128
EXPERTS = 32


EPS = 1e-06
ROPE_BASE = 10000.0
NEG = -1e30
LOW = jnp.bfloat16
WIDE = jnp.float32
VMEM_MOST = 60 * 1024 * 1024
def norm_forward(values, gain):
    inverse = lax.rsqrt(jnp.mean(values * values, axis=-1) + EPS)
    normed = values * inverse[:, None]
    return (normed * gain, normed, inverse)


def norm_backward(grad, gain, normed, inverse):
    gain_grad = jnp.sum(grad * normed, axis=0)
    scaled = grad * gain
    centred = scaled - normed * jnp.mean(scaled * normed, axis=-1, keepdims=True)
    return (inverse[:, None] * centred, gain_grad)


def rotary_tables(seq_length, head_size):
    half_size = head_size // 2
    frequency = ROPE_BASE ** (-(jnp.arange(half_size, dtype=jnp.float32) * 2.0 / head_size))
    angles = jnp.arange(seq_length, dtype=jnp.float32)[:, None] * frequency[None, :]
    return (jnp.cos(angles), jnp.sin(angles))


def apply_rotation(values, cosine_lookup, sine_lookup):
    half_size = values.shape[-1] // 2
    first_half = values[..., :half_size]
    second_half = values[..., half_size:]
    cos_part = cosine_lookup[:, None, :]
    sin_part = sine_lookup[:, None, :]
    return jnp.concatenate(
        [
            first_half * cos_part - second_half * sin_part,
            second_half * cos_part + first_half * sin_part,
        ],
        axis=-1,
    )


def reverse_rotation(values, cosine_lookup, sine_lookup):
    half_size = values.shape[-1] // 2
    first_half = values[..., :half_size]
    second_half = values[..., half_size:]
    cos_part = cosine_lookup[:, None, :]
    sin_part = sine_lookup[:, None, :]
    return jnp.concatenate(
        [
            first_half * cos_part + second_half * sin_part,
            second_half * cos_part - first_half * sin_part,
        ],
        axis=-1,
    )


def per_device_exchange(
    tokens,
    segments,
    routes,
    attn_gain,
    ffn_gain,
    w_query,
    key_weight,
    value_weight,
    w_out,
    w_router,
    w_gate,
    w_up,
    w_down,
    cotangent,
):
    lower_dtype = jnp.bfloat16
    wide_type = jnp.float32
    sequence_length, model_width = tokens.shape
    top_count = routes.shape[1]
    axis_count = lax.axis_size("expert")
    owners = max(1, axis_count // EXPERTS)
    holds = max(1, EXPERTS // axis_count)
    groups = EXPERTS // holds
    capacity = max(2, 3 * sequence_length * top_count // (2 * EXPERTS))
    hidden_dev = w_gate.shape[1] // holds
    query_group_width = QUERY_HEADS // KEY_VALUE_HEADS
    score_scale = HEAD_DIM ** (-0.5)
    pair_count = sequence_length * top_count
    query_full, key_full, value_full, out_full, router_full = (
        lax.all_gather(w_query, "wshard", axis=0, tiled=True),
        lax.all_gather(key_weight, "wshard", axis=0, tiled=True),
        lax.all_gather(value_weight, "wshard", axis=0, tiled=True),
        lax.all_gather(w_out, "wshard", axis=0, tiled=True),
        lax.all_gather(w_router, "wshard", axis=0, tiled=True),
    )
    stream = tokens.astype(wide_type)
    first_norm, first_normed, first_inverse = norm_forward(stream, attn_gain)
    first_low = first_norm.astype(lower_dtype)
    cosine_lookup, sine_lookup = rotary_tables(sequence_length, HEAD_DIM)
    query_pre = jnp.dot(first_low, query_full, preferred_element_type=wide_type).reshape(
        sequence_length, QUERY_HEADS, HEAD_DIM
    )
    key_unrotated = jnp.dot(first_low, key_full, preferred_element_type=wide_type).reshape(
        sequence_length, KEY_VALUE_HEADS, HEAD_DIM
    )
    query_rotated = (
        apply_rotation(query_pre, cosine_lookup, sine_lookup)
        .astype(lower_dtype)
        .reshape(sequence_length, KEY_VALUE_HEADS, query_group_width, HEAD_DIM)
    )
    key_rotated = apply_rotation(key_unrotated, cosine_lookup, sine_lookup).astype(lower_dtype)
    value_lowered = (
        jnp.dot(first_low, value_full, preferred_element_type=wide_type)
        .astype(lower_dtype)
        .reshape(sequence_length, KEY_VALUE_HEADS, HEAD_DIM)
    )
    positions = jnp.arange(sequence_length)
    offset = positions[:, None] - positions[None, :]
    segment_row = segments[0]
    allowed = (segment_row[:, None] == segment_row[None, :]) & (offset >= 0)
    raw_scores = jnp.einsum(
        "qagd,kad->agqk", query_rotated, key_rotated, preferred_element_type=wide_type
    )
    scores = jnp.where(allowed, raw_scores * score_scale, NEG)
    score_top = jnp.max(scores, axis=-1, keepdims=True)
    expo_terms = jnp.exp(scores - score_top)
    expo_total = jnp.sum(expo_terms, axis=-1, keepdims=True)
    log_total = score_top + jnp.log(expo_total)
    probs_low = (expo_terms / expo_total).astype(lower_dtype)
    attn_low = (
        jnp.einsum("agqk,kad->qagd", probs_low, value_lowered, preferred_element_type=wide_type)
        .astype(lower_dtype)
        .reshape(sequence_length, QUERY_HEADS * HEAD_DIM)
    )
    resid = stream + jnp.dot(attn_low, out_full, preferred_element_type=wide_type)
    second_norm, second_normed, second_inverse = norm_forward(resid, ffn_gain)
    second_low = second_norm.astype(lower_dtype)
    logits = jnp.dot(second_low, router_full, preferred_element_type=wide_type)
    choose = (routes[:, :, None] == jnp.arange(EXPERTS)[None, None, :]).astype(wide_type)
    selected = jnp.sum(choose * logits[:, None, :], axis=-1)
    gate_probs = jax.nn.softmax(selected, axis=-1)
    flat_routes = routes.reshape(pair_count)
    one_hot = (flat_routes[:, None] == jnp.arange(EXPERTS)[None, :]).astype(jnp.int32)
    slot_rank = jnp.sum((jnp.cumsum(one_hot, axis=0) - 1) * one_hot, axis=1)
    slot_index = (flat_routes // holds * capacity + slot_rank) * holds + flat_routes % holds
    slot_pair = (
        jnp.full((EXPERTS * capacity,), pair_count, jnp.int32)
        .at[slot_index]
        .set(jnp.arange(pair_count, dtype=jnp.int32))
    )
    second_ext = jnp.concatenate([second_low, jnp.zeros((1, model_width), lower_dtype)], axis=0)
    send_rows = jnp.repeat(
        second_ext[slot_pair // top_count].reshape(groups, capacity, holds, model_width),
        owners,
        axis=0,
    )
    gate_local = w_gate.reshape(model_width, holds, hidden_dev)
    up_local = w_up.reshape(model_width, holds, hidden_dev)
    down_local = w_down.reshape(holds, hidden_dev, model_width)

    def owner_total(values):
        summed = jnp.sum(
            values.astype(wide_type).reshape(groups, owners, capacity, holds, model_width), axis=1
        )
        return summed.reshape(EXPERTS * capacity, model_width)

    received = lax.all_to_all(send_rows, "expert", split_axis=0, concat_axis=0, tiled=True)
    gate_pre = jnp.einsum("scld,dlf->sclf", received, gate_local, preferred_element_type=wide_type)
    up_pre = jnp.einsum("scld,dlf->sclf", received, up_local, preferred_element_type=wide_type)
    hidden = (jax.nn.silu(gate_pre) * up_pre).astype(lower_dtype)
    partial_value = jnp.einsum(
        "sclf,lfd->scld", hidden, down_local, preferred_element_type=wide_type
    ).astype(lower_dtype)
    returned = lax.all_to_all(partial_value, "expert", split_axis=0, concat_axis=0, tiled=True)
    expert_wide = owner_total(returned)[slot_index].reshape(sequence_length, top_count, model_width)
    mixed = (resid + jnp.sum(gate_probs[:, :, None] * expert_wide, axis=1)).astype(lower_dtype)
    upstream = cotangent.astype(wide_type)
    query_back, key_back, value_back, out_back, router_back = (
        lax.all_gather(w_query, "wshard", axis=0, tiled=True),
        lax.all_gather(key_weight, "wshard", axis=0, tiled=True),
        lax.all_gather(value_weight, "wshard", axis=0, tiled=True),
        lax.all_gather(w_out, "wshard", axis=0, tiled=True),
        lax.all_gather(w_router, "wshard", axis=0, tiled=True),
    )
    gate_grad = jnp.sum(expert_wide * upstream[:, None, :], axis=-1)
    sel_grad = gate_probs * (gate_grad - jnp.sum(gate_probs * gate_grad, axis=-1, keepdims=True))
    logit_grad = jnp.sum(choose * sel_grad[:, :, None], axis=1).astype(lower_dtype)
    pair_grad = (
        (gate_probs[:, :, None] * upstream[:, None, :])
        .astype(lower_dtype)
        .reshape(pair_count, model_width)
    )
    pair_ext = jnp.concatenate([pair_grad, jnp.zeros((1, model_width), lower_dtype)], axis=0)
    grad_send = jnp.repeat(
        pair_ext[slot_pair].reshape(groups, capacity, holds, model_width), owners, axis=0
    )
    grad_recv, rows_recv = (
        lax.all_to_all(grad_send, "expert", split_axis=0, concat_axis=0, tiled=True),
        lax.all_to_all(send_rows, "expert", split_axis=0, concat_axis=0, tiled=True),
    )
    gate_pre = jnp.einsum("scld,dlf->sclf", rows_recv, gate_local, preferred_element_type=wide_type)
    up_pre = jnp.einsum("scld,dlf->sclf", rows_recv, up_local, preferred_element_type=wide_type)
    sigmoid_gate = jax.nn.sigmoid(gate_pre)
    silu_gate = gate_pre * sigmoid_gate
    hidden = (silu_gate * up_pre).astype(lower_dtype)
    hidden_grad = jnp.einsum(
        "scld,lfd->sclf", grad_recv, down_local, preferred_element_type=wide_type
    )
    gate_pre_grad = (
        hidden_grad * up_pre * sigmoid_gate * (1.0 + gate_pre * (1.0 - sigmoid_gate))
    ).astype(lower_dtype)
    up_pre_grad = (hidden_grad * silu_gate).astype(lower_dtype)
    row_grad = (
        jnp.einsum("sclf,dlf->scld", gate_pre_grad, gate_local, preferred_element_type=wide_type)
        + jnp.einsum("sclf,dlf->scld", up_pre_grad, up_local, preferred_element_type=wide_type)
    ).astype(lower_dtype)
    returned_grad = lax.all_to_all(row_grad, "expert", split_axis=0, concat_axis=0, tiled=True)
    gate_wgrad = jnp.einsum(
        "scld,sclf->dlf", rows_recv, gate_pre_grad, preferred_element_type=wide_type
    ).reshape(model_width, holds * hidden_dev)
    up_wgrad = jnp.einsum(
        "scld,sclf->dlf", rows_recv, up_pre_grad, preferred_element_type=wide_type
    ).reshape(model_width, holds * hidden_dev)
    down_wgrad = jnp.einsum(
        "sclf,scld->lfd", hidden, grad_recv, preferred_element_type=wide_type
    ).reshape(holds * hidden_dev, model_width)
    gate_shard, up_shard, down_shard = (
        lax.psum_scatter(
            gate_wgrad.astype(jnp.bfloat16), "wshard", scatter_dimension=0, tiled=True
        ).astype(jnp.float32),
        lax.psum_scatter(
            up_wgrad.astype(jnp.bfloat16), "wshard", scatter_dimension=0, tiled=True
        ).astype(jnp.float32),
        lax.psum_scatter(
            down_wgrad.astype(jnp.bfloat16), "wshard", scatter_dimension=1, tiled=True
        ).astype(jnp.float32),
    )
    token_grad = owner_total(returned_grad)[slot_index].reshape(
        sequence_length, top_count, model_width
    )
    second_grad = jnp.sum(token_grad, axis=1) + jnp.dot(
        logit_grad, router_back.T, preferred_element_type=wide_type
    )
    router_wgrad = jnp.einsum("td,te->de", second_low, logit_grad, preferred_element_type=wide_type)
    resid_part, ffn_gain_grad = norm_backward(second_grad, ffn_gain, second_normed, second_inverse)
    resid_grad = upstream + resid_part
    resid_low = resid_grad.astype(lower_dtype)
    out_wgrad = jnp.einsum("tc,td->cd", attn_low, resid_low, preferred_element_type=wide_type)
    attn_grad = (
        jnp.dot(resid_low, out_back.T, preferred_element_type=wide_type)
        .astype(lower_dtype)
        .reshape(sequence_length, KEY_VALUE_HEADS, query_group_width, HEAD_DIM)
    )
    raw_again = jnp.einsum(
        "qagd,kad->agqk", query_rotated, key_rotated, preferred_element_type=wide_type
    )
    scores_again = jnp.where(allowed, raw_again * score_scale, NEG)
    probs_again = jnp.exp(scores_again - log_total)
    prob_grad = jnp.einsum(
        "qagd,kad->agqk", attn_grad, value_lowered, preferred_element_type=wide_type
    )
    row_delta = jnp.sum(probs_again * prob_grad, axis=-1, keepdims=True)
    score_grad = (probs_again * (prob_grad - row_delta) * score_scale).astype(lower_dtype)
    value_grad = (
        jnp.einsum("agqk,qagd->kad", probs_low, attn_grad, preferred_element_type=wide_type)
        .astype(lower_dtype)
        .reshape(sequence_length, KEY_VALUE_HEADS * HEAD_DIM)
    )
    query_rot_grad = jnp.einsum(
        "agqk,kad->qagd", score_grad, key_rotated, preferred_element_type=wide_type
    ).reshape(sequence_length, QUERY_HEADS, HEAD_DIM)
    key_rotated_gradient = jnp.einsum(
        "agqk,qagd->kad", score_grad, query_rotated, preferred_element_type=wide_type
    )
    query_grad = (
        reverse_rotation(query_rot_grad, cosine_lookup, sine_lookup)
        .astype(lower_dtype)
        .reshape(sequence_length, QUERY_HEADS * HEAD_DIM)
    )
    key_grad = (
        reverse_rotation(key_rotated_gradient, cosine_lookup, sine_lookup)
        .astype(lower_dtype)
        .reshape(sequence_length, KEY_VALUE_HEADS * HEAD_DIM)
    )
    query_wgrad = jnp.einsum("td,tc->dc", first_low, query_grad, preferred_element_type=wide_type)
    key_wgrad = jnp.einsum("td,tc->dc", first_low, key_grad, preferred_element_type=wide_type)
    value_wgrad = jnp.einsum("td,tc->dc", first_low, value_grad, preferred_element_type=wide_type)
    first_grad = (
        jnp.dot(query_grad, query_back.T, preferred_element_type=wide_type)
        + jnp.dot(key_grad, key_back.T, preferred_element_type=wide_type)
        + jnp.dot(value_grad, value_back.T, preferred_element_type=wide_type)
    )
    stream_part, attn_gain_grad = norm_backward(first_grad, attn_gain, first_normed, first_inverse)
    input_grad = resid_grad + stream_part
    query_part, key_part, value_part, out_part, router_part, attn_gain_part, ffn_gain_part = (
        lax.psum_scatter(
            query_wgrad.astype(jnp.bfloat16), "wshard", scatter_dimension=0, tiled=True
        ).astype(jnp.float32),
        lax.psum_scatter(
            key_wgrad.astype(jnp.bfloat16), "wshard", scatter_dimension=0, tiled=True
        ).astype(jnp.float32),
        lax.psum_scatter(
            value_wgrad.astype(jnp.bfloat16), "wshard", scatter_dimension=0, tiled=True
        ).astype(jnp.float32),
        lax.psum_scatter(
            out_wgrad.astype(jnp.bfloat16), "wshard", scatter_dimension=0, tiled=True
        ).astype(jnp.float32),
        lax.psum_scatter(
            router_wgrad.astype(jnp.bfloat16), "wshard", scatter_dimension=0, tiled=True
        ).astype(jnp.float32),
        lax.psum_scatter(
            attn_gain_grad.astype(jnp.bfloat16), "wshard", scatter_dimension=0, tiled=True
        ).astype(jnp.float32),
        lax.psum_scatter(
            ffn_gain_grad.astype(jnp.bfloat16), "wshard", scatter_dimension=0, tiled=True
        ).astype(jnp.float32),
    )
    query_sum, key_sum, value_sum, out_sum, router_sum, attn_gain_sum, ffn_gain_sum = lax.psum(
        (query_part, key_part, value_part, out_part, router_part, attn_gain_part, ffn_gain_part),
        "expert",
    )
    return (
        mixed,
        input_grad,
        attn_gain_sum,
        ffn_gain_sum,
        query_sum,
        key_sum,
        value_sum,
        out_sum,
        router_sum,
        gate_shard,
        up_shard,
        down_shard,
    )


BLOCK_OFFSETS = (-1, 1, -2, 2, -3, 3, 0, 4)


def ring_order(count):
    return [0] + list(range(1, count, 2)) + list(range(count - 2, 0, -2))


def shifted(value, step, count):
    order = ring_order(count)
    return lax.ppermute(value, "expert", [(order[i], order[(i + step) % count]) for i in range(count)])


def ahead(value, count):
    return shifted(value, 1, count)


def behind(value, count):
    return shifted(value, -1, count)


def swap_core(value):
    size = lax.axis_size("wshard")
    return lax.ppermute(value, "wshard", [(i, i ^ 1) for i in range(size)])


def swap_x(value):
    size = lax.axis_size("wshard")
    return lax.ppermute(value, "wshard", [(i, i ^ 2) for i in range(size)])


def add_low(*terms):
    return sum(term.astype(WIDE) for term in terms).astype(LOW)


def after(value, *others):
    return lax.optimization_barrier((value, *others))[0]


def places(rank_row, slots):
    rows = lax.broadcasted_iota(jnp.int32, (slots, rank_row.shape[-1]), 0)
    return rank_row == rows


def dot_t(a, b):
    return lax.dot_general(a, b, (((0,), (0,)), ((), ())), preferred_element_type=WIDE)


def dot_bt(a, b):
    return lax.dot_general(a, b, (((1,), (1,)), ((), ())), preferred_element_type=WIDE)


def dot(a, b):
    return jnp.dot(a, b, preferred_element_type=WIDE)


def expert_kernel(count, slots, aliased, halved, *refs):
    _, rank_ref, routes_ref = refs[:3]
    parts = 2 if halved else 1
    h_refs = refs[3 : 3 + count * parts]
    dz_refs = refs[3 + count * parts : 3 + 2 * count * parts]
    at = 3 + 2 * count * parts
    wg_ref, wu_ref, wd_ref = refs[at : at + 3]
    rest = refs[at + 3 + (5 if aliased else 0) :]
    d_refs = rest[: 2 * count]
    gain_ref, rows_out, dz_out, gg_out, ug_out, hid_out = rest[2 * count : 2 * count + 6]
    place_scr, back_scr, gate_scr = rest[2 * count + 6 : 2 * count + 9]
    e = pl.program_id(0)
    holds, tokens = rank_ref.shape[1:]
    top_count = routes_ref.shape[1]
    here = pl.ds(pl.multiple_of(e * slots, slots), slots)
    if halved:
        whole_scr, dz_scr = rest[2 * count + 9 :]

    @pl.when(e == 0)
    def _():
        if halved:
            half = h_refs[0].shape[0]
            whole_scr[:half] = h_refs[0][...]
            whole_scr[half:] = h_refs[1][...]
            half = dz_refs[0].shape[0]
            dz_scr[:half] = dz_refs[0][...]
            dz_scr[half:] = dz_refs[1][...]
            sources = [(whole_scr, dz_scr)]
        else:
            sources = list(zip(h_refs, dz_refs))
        for b, (h_ref, dz_ref) in enumerate(sources):
            packed = h_ref[tokens : tokens + 16, :tokens].astype(WIDE)
            gates = packed[:top_count] + packed[top_count : 2 * top_count]
            for l in range(holds):
                band = slice(l * slots, (l + 1) * slots)
                spot = places(rank_ref[b, l : l + 1, :], slots).astype(WIDE)
                named = jnp.where(routes_ref[b] == l, gates, 0.0)
                gate_scr[b, band, :] = jnp.broadcast_to(
                    jnp.sum(spot * jnp.sum(named, axis=0, keepdims=True), axis=1, keepdims=True), (slots, 128)
                )
                place_scr[b, band, :] = spot.astype(LOW)
            for source, target in ((h_ref, rows_out), (dz_ref, dz_out)):
                taken = dot(place_scr[b], source[:tokens]).astype(LOW)
                for l in range(holds):
                    target[l, b * slots : (b + 1) * slots, :] = taken[l * slots : (l + 1) * slots]

    gate = jnp.concatenate([gate_scr[b, here, :] for b in range(count)], axis=0)[:, :1]
    rows = rows_out[e]
    gate_pre = dot(rows, wg_ref[...])
    up_pre = dot(rows, wu_ref[...])
    sig = jax.nn.sigmoid(gate_pre)
    silu = gate_pre * sig
    hidden = (silu * up_pre).astype(LOW).astype(WIDE)
    back = dot_bt(dz_out[e], wd_ref[...])
    gains = jnp.sum(back * hidden, axis=1, keepdims=True)
    back = back * gate
    gate_grad = (back * (up_pre * sig * (1.0 + gate_pre * (1.0 - sig)))).astype(LOW)
    up_grad = (back * silu).astype(LOW)
    gg_out[0] = gate_grad
    ug_out[0] = up_grad
    hid_out[0] = (hidden * gate).astype(LOW)
    row_grad = (dot_bt(gate_grad, wg_ref[...]) + dot_bt(up_grad, wu_ref[...])).astype(LOW)
    for b in range(count):
        band = slice(b * slots, (b + 1) * slots)
        back_scr[b, here, :] = row_grad[band]
        spot = place_scr[b, here, :].astype(WIDE)
        gain_ref[b, pl.ds(e, 1), :] = jnp.sum(spot * gains[band], axis=0, keepdims=True)

    @pl.when(e == pl.num_programs(0) - 1)
    def _():
        half = tokens // 2
        for b in range(count):
            total = dot_t(place_scr[b], back_scr[b]).astype(LOW)
            d_refs[2 * b][...] = total[:half]
            d_refs[2 * b + 1][...] = total[half:]


def expert_call(token, first, blocks, dz_blocks, rank, routes_local, w_gate, w_up, w_down, kept, slots):
    count = len(blocks)
    halved = isinstance(blocks[0], tuple)
    if halved:
        (blocks,), (dz_blocks,) = blocks, dz_blocks
    total, holds, tokens = rank.shape
    width = blocks[0].shape[1]
    hidden = w_gate.shape[1] // holds
    whole = lambda *shape: pl.BlockSpec(shape, lambda e: (0,) * len(shape))
    once = lambda *shape: pl.BlockSpec(shape, lambda e: (0,) * len(shape), pipeline_mode=pl.Buffered(buffer_count=1))
    aliased = kept is not None
    in_specs = (
        [pl.BlockSpec(memory_space=pltpu.SMEM), whole(count, holds, tokens), whole(count, *routes_local.shape[1:])]
        + [once(*b.shape) for b in (*blocks, *dz_blocks)]
        + [
            pl.BlockSpec((width, hidden), lambda e: (0, e)),
            pl.BlockSpec((width, hidden), lambda e: (0, e)),
            pl.BlockSpec((hidden, width), lambda e: (e, 0)),
        ]
    )
    aliases = {len(in_specs) + i: 2 * count + 1 + i for i in range(5)} if aliased else {}
    half = shaped(tokens // 2, width)
    out = pl.pallas_call(
        functools.partial(expert_kernel, count, slots, aliased, halved),
        grid=(holds,),
        in_specs=in_specs + ([pl.BlockSpec(memory_space=pl.ANY)] * 5 if aliased else []),
        out_specs=[whole(tokens // 2, width)] * (2 * count)
        + [whole(count, holds, tokens)]
        + [pl.BlockSpec((holds, count * slots, width), lambda e: (0, first // count, 0))] * 2
        + [pl.BlockSpec((1, count * slots, hidden), lambda e: (e, first // count, 0))] * 3,
        out_shape=[half] * (2 * count)
        + [shaped(count, holds, tokens, dtype=WIDE)]
        + [shaped(holds, total * slots, width)] * 2
        + [shaped(holds, total * slots, hidden)] * 3,
        scratch_shapes=[
            pltpu.VMEM((count, holds * slots, tokens), LOW),
            pltpu.VMEM((count, holds * slots, width), LOW),
            pltpu.VMEM((count, holds * slots, 128), WIDE),
        ]
        + ([pltpu.VMEM((tokens + 16, width), LOW), pltpu.VMEM((tokens, width), LOW)] if halved else []),
        input_output_aliases=aliases,
        compiler_params=pltpu.CompilerParams(vmem_limit_bytes=VMEM_MOST),
        cost_estimate=pl.CostEstimate(
            flops=2 * holds * count * slots * width * (5 * hidden + 3 * tokens),
            bytes_accessed=3 * holds * width * hidden * 2
            + count * tokens * width * 6
            + holds * count * slots * (2 * width + 3 * hidden) * 2,
            transcendentals=holds * count * slots * hidden,
        ),
    )(
        token,
        rank[first : first + count],
        routes_local[first : first + count],
        *blocks,
        *dz_blocks,
        w_gate,
        w_up,
        w_down,
        *(kept if aliased else ()),
    )
    pairs = [(out[2 * b], out[2 * b + 1]) for b in range(count)]
    return pairs, out[2 * count], tuple(out[2 * count + 1 :])


def value_kernel(slots, _, rank_ref, hid_ref, wd_ref, *refs):
    total, holds, tokens = rank_ref.shape
    y_refs, (value_scr, place_scr) = refs[: 2 * total], refs[2 * total :]
    e = pl.program_id(0)
    here = pl.ds(pl.multiple_of(e * slots, slots), slots)
    value = dot(hid_ref[0], wd_ref[...]).astype(LOW)
    for b in range(total):
        value_scr[b, here, :] = value[b * slots : (b + 1) * slots]

    @pl.when(e == pl.num_programs(0) - 1)
    def _():
        half = tokens // 2
        for b in range(total):
            for l in range(holds):
                spot = places(rank_ref[b, l : l + 1, :], slots)
                place_scr[l * slots : (l + 1) * slots, :] = spot.astype(WIDE).astype(LOW)
            y = dot_t(place_scr[...], value_scr[b]).astype(LOW)
            y_refs[2 * b][...] = y[:half]
            y_refs[2 * b + 1][...] = y[half:]


def value_call(token, rank, hidden_rows, w_down, slots):
    total, holds, tokens = rank.shape
    width = w_down.shape[1]
    hidden = hidden_rows.shape[2]
    whole = lambda *shape: pl.BlockSpec(shape, lambda e: (0,) * len(shape))
    out = pl.pallas_call(
        functools.partial(value_kernel, slots),
        grid=(holds,),
        in_specs=[
            pl.BlockSpec(memory_space=pltpu.SMEM),
            whole(*rank.shape),
            pl.BlockSpec((1, total * slots, hidden), lambda e: (e, 0, 0)),
            pl.BlockSpec((hidden, width), lambda e: (e, 0)),
        ],
        out_specs=[whole(tokens // 2, width)] * (2 * total),
        out_shape=[shaped(tokens // 2, width)] * (2 * total),
        scratch_shapes=[pltpu.VMEM((total, holds * slots, width), LOW), pltpu.VMEM((holds * slots, tokens), LOW)],
        compiler_params=pltpu.CompilerParams(vmem_limit_bytes=VMEM_MOST),
        cost_estimate=pl.CostEstimate(
            flops=2 * total * holds * slots * width * (hidden + tokens),
            bytes_accessed=2 * (holds * hidden * (width + total * slots) + total * tokens * width),
            transcendentals=0,
        ),
    )(token, rank, hidden_rows, w_down)
    return [(out[2 * b], out[2 * b + 1]) for b in range(total)]


def wgrad_kernel(place_ref, rows_ref, dz_ref, gg_ref, ug_ref, hid_ref, send_gu, keep_gu, send_d, keep_d):
    step = pl.program_id(0)
    shard = send_d.shape[2]
    columns = pl.ds(pl.multiple_of(jnp.bitwise_xor(place_ref[0], step) * shard, 128), shard)
    rows = rows_ref[0, :, columns]
    gate_part = dot_t(rows, gg_ref[0]).astype(LOW)
    up_part = dot_t(rows, ug_ref[0]).astype(LOW)
    down_part = dot_t(hid_ref[0], dz_ref[0, :, columns]).astype(LOW)

    @pl.when(step % 2 == 1)
    def _():
        send_gu[0, 0] = gate_part
        send_gu[0, 1] = up_part
        send_d[0] = down_part

    @pl.when(step % 2 == 0)
    def _():
        keep_gu[0, 0] = gate_part
        keep_gu[0, 1] = up_part
        keep_d[0] = down_part


def wgrad_call(expert, place, kept):
    _, count, width = kept[0].shape
    hidden = kept[2].shape[2]
    shard = width // 4
    row_spec = lambda d: pl.BlockSpec((1, count, d), lambda s: (expert, 0, 0), pipeline_mode=pl.Buffered(buffer_count=1))
    low = lambda *shape: jax.ShapeDtypeStruct(shape, LOW)
    gu_spec = pl.BlockSpec((1, 2, shard, hidden), lambda s: (s // 2, 0, 0, 0))
    d_spec = pl.BlockSpec((1, hidden, shard), lambda s: (s // 2, 0, 0))
    return pl.pallas_call(
        wgrad_kernel,
        grid=(4,),
        in_specs=[pl.BlockSpec(memory_space=pltpu.SMEM), row_spec(width), row_spec(width)] + [row_spec(hidden)] * 3,
        out_specs=[gu_spec, gu_spec, d_spec, d_spec],
        out_shape=[low(2, 2, shard, hidden), low(2, 2, shard, hidden), low(2, hidden, shard), low(2, hidden, shard)],
        compiler_params=pltpu.CompilerParams(vmem_limit_bytes=VMEM_MOST),
        cost_estimate=pl.CostEstimate(
            flops=2 * count * width * 3 * hidden,
            bytes_accessed=2 * (count * (2 * width + 3 * hidden) + 3 * width * hidden),
            transcendentals=0,
        ),
    )(place, *kept)


def finish_kernel(keep_gu, got_gu, across_gu, keep_d, got_d, across_d, *refs):
    gate_ref, up_ref, down_ref = refs[-3:]

    def total(a, b, c):
        return a.astype(WIDE) + b.astype(WIDE) + c.astype(WIDE)

    gate_ref[...] = total(keep_gu[0, 0], got_gu[0, 0], across_gu[0])
    up_ref[...] = total(keep_gu[0, 1], got_gu[0, 1], across_gu[1])
    down_ref[...] = total(keep_d[0], got_d[0], across_d[...])


def finish_call(expert, holds, terms, kept):
    _, _, shard, hidden = terms[0].shape
    gu_spec = pl.BlockSpec((1, 2, shard, hidden), lambda s: (0, 0, 0, 0))
    d_spec = pl.BlockSpec((1, hidden, shard), lambda s: (0, 0, 0))
    column = pl.BlockSpec((shard, hidden), lambda s: (0, expert))
    wide, tall = shaped(shard, holds * hidden, dtype=WIDE), shaped(holds * hidden, shard, dtype=WIDE)
    return pl.pallas_call(
        finish_kernel,
        grid=(1,),
        in_specs=[gu_spec, gu_spec, pl.BlockSpec((2, shard, hidden), lambda s: (0, 0, 0))]
        + [d_spec, d_spec, pl.BlockSpec((hidden, shard), lambda s: (0, 0))]
        + ([pl.BlockSpec(memory_space=pl.ANY)] * 3 if kept else []),
        out_specs=[column, column, pl.BlockSpec((hidden, shard), lambda s: (expert, 0))],
        out_shape=[wide, wide, tall],
        input_output_aliases={6 + i: i for i in range(3)} if kept else {},
        compiler_params=pltpu.CompilerParams(vmem_limit_bytes=VMEM_MOST),
        cost_estimate=pl.CostEstimate(flops=0, bytes_accessed=30 * shard * hidden, transcendentals=0),
    )(*terms, *(kept or ()))


def piece_columns(mine, s, shard):
    return pl.ds(pl.multiple_of(jnp.bitwise_xor(mine, s) * shard, 128), shard)


def turn(values, cos, sin):
    return values * cos + pltpu.roll(values, HEAD_DIM // 2, 1) * sin


def turn_back(values, cos, sin):
    return values * cos - pltpu.roll(values, HEAD_DIM // 2, 1) * sin


def inverse_rms(values):
    return lax.rsqrt(jnp.mean(values * values, axis=-1, keepdims=True) + EPS)


def head_slice(h):
    return slice(h * HEAD_DIM, (h + 1) * HEAD_DIM)


def stacked_heads(ref, band, group, heads):
    return jnp.concatenate([ref[band, head_slice(group * heads + h)] for h in range(heads)], axis=0)


def probabilities(queries, keys, allowed):
    scores = jnp.where(allowed, dot_bt(queries, keys) * HEAD_DIM ** (-0.5), NEG)
    expo = jnp.exp(scores - jnp.max(scores, axis=-1, keepdims=True))
    return expo * (1.0 / jnp.sum(expo, axis=-1, keepdims=True))


def allowed_pairs(seg_col_ref, seg_row_ref, band, reach, heads):
    size = band.stop - band.start
    rows = band.start + lax.broadcasted_iota(jnp.int32, (size, reach), 0)
    cols = lax.broadcasted_iota(jnp.int32, (size, reach), 1)
    ok = (seg_col_ref[band, :] == seg_row_ref[:, :reach]) & (cols <= rows)
    return jnp.concatenate([ok] * heads, axis=0)


def attention_kernel(
    mine_ref, tokens_ref, gain_ref, p0, p1, p2, p3, seg_row_ref, seg_col_ref, cos_ref, sin_ref,
    h_ref, q_ref, k_ref, v_ref, out_ref,
):
    mine = mine_ref[0]
    stream = tokens_ref[...].astype(WIDE)
    h_ref[...] = (stream * inverse_rms(stream) * gain_ref[...]).astype(LOW)
    shard = p0.shape[0]
    width = q_ref.shape[1]
    cos, sin = cos_ref[...], sin_ref[...]

    def projected(columns):
        return sum(dot(h_ref[:, piece_columns(mine, s, shard)], piece[:, columns]) for s, piece in enumerate((p0, p1, p2, p3)))

    heads = QUERY_HEADS // KEY_VALUE_HEADS
    key_width = KEY_VALUE_HEADS * HEAD_DIM
    keys = projected(slice(width, width + key_width))
    for g in range(KEY_VALUE_HEADS):
        k_ref[:, head_slice(g)] = turn(keys[:, head_slice(g)], cos, sin).astype(LOW)
    v_ref[...] = projected(slice(width + key_width, width + 2 * key_width)).astype(LOW)
    group_width = heads * HEAD_DIM
    for g in range(KEY_VALUE_HEADS):
        queries = projected(slice(g * group_width, (g + 1) * group_width))
        for h in range(heads):
            q_ref[:, head_slice(g * heads + h)] = turn(queries[:, head_slice(h)], cos, sin).astype(LOW)
    length = q_ref.shape[0]
    tile = 128
    for start in range(0, length, tile):
        band, reach = slice(start, start + tile), start + tile
        allowed = allowed_pairs(seg_col_ref, seg_row_ref, band, reach, heads)
        for g in range(KEY_VALUE_HEADS):
            probs = probabilities(stacked_heads(q_ref, band, g, heads), k_ref[:reach, head_slice(g)], allowed)
            mixed = dot(probs.astype(LOW), v_ref[:reach, head_slice(g)]).astype(LOW)
            for h in range(heads):
                out_ref[band, head_slice(g * heads + h)] = mixed[h * tile : (h + 1) * tile]


def vmem_call(kernel, out_shape, flops, transcendentals, token, *args):
    moved = sum(a.size * a.dtype.itemsize for a in args) + sum(
        o.size * o.dtype.itemsize for o in jax.tree.leaves(out_shape)
    )
    return pl.pallas_call(
        kernel,
        in_specs=[pl.BlockSpec(memory_space=pltpu.SMEM)] + [pl.BlockSpec(memory_space=pltpu.VMEM)] * len(args),
        out_specs=[pl.BlockSpec(memory_space=pltpu.VMEM)] * len(out_shape),
        out_shape=out_shape,
        compiler_params=pltpu.CompilerParams(vmem_limit_bytes=VMEM_MOST),
        cost_estimate=pl.CostEstimate(flops=flops, bytes_accessed=moved, transcendentals=transcendentals),
    )(token, *args)


def shaped(*shape, dtype=LOW):
    return jax.ShapeDtypeStruct(shape, dtype)


def attention_call(mine, tokens, gain, pieces, seg_row, seg_col, cos, sin):
    length, width = tokens.shape
    key_width = KEY_VALUE_HEADS * HEAD_DIM
    return vmem_call(
        attention_kernel,
        [shaped(length, width), shaped(length, width), shaped(length, key_width), shaped(length, key_width), shaped(length, width)],
        2 * length * width * (width + 2 * key_width) + 3 * length * length * width,
        QUERY_HEADS * length * length,
        mine, tokens, gain, *pieces, seg_row, seg_col, cos, sin,
    )


def project_kernel(
    mine_ref, tokens_ref, attn_ref, p0, p1, p2, p3, r0, r1, r2, r3, gain_ref, routes_ref, resid_ref, h_ref, gates_ref
):
    mine = mine_ref[0]
    shard = p0.shape[0]
    resid = tokens_ref[...].astype(WIDE)
    for s, piece in enumerate((p0, p1, p2, p3)):
        resid = resid + dot(attn_ref[:, piece_columns(mine, s, shard)], piece[...])
    resid_ref[...] = resid
    length, width = resid.shape
    h_ref[:length] = (resid * inverse_rms(resid) * gain_ref[...]).astype(LOW)
    logits = sum(
        dot_bt(piece[...], h_ref[:length, piece_columns(mine, s, shard)]) for s, piece in enumerate((r0, r1, r2, r3))
    )
    experts = lax.broadcasted_iota(jnp.int32, logits.shape, 0)
    picked = [
        jnp.sum(jnp.where(experts == routes_ref[k : k + 1, :], logits, 0.0), axis=0, keepdims=True)
        for k in range(routes_ref.shape[0])
    ]
    top = functools.reduce(jnp.maximum, picked)
    expo = [jnp.exp(p - top) for p in picked]
    total = sum(expo)
    gates = jnp.concatenate([x / total for x in expo], axis=0)
    gates_ref[...] = gates
    high = gates.astype(LOW).astype(WIDE)
    packed = jnp.concatenate([high, gates - high, jnp.zeros((16 - 2 * len(expo), length), WIDE)], axis=0)
    h_ref[length:] = jnp.zeros((16, width), LOW)
    h_ref[length:, :length] = packed.astype(LOW)


def project_call(mine, tokens, attn, pieces, router_pieces, gain, routes_t):
    length, width = tokens.shape
    return vmem_call(
        project_kernel,
        [shaped(length, width, dtype=WIDE), shaped(length + 16, width), shaped(*routes_t.shape, dtype=WIDE)],
        2 * length * width * (width + EXPERTS),
        length * 8,
        mine, tokens, attn, *pieces, *router_pieces, gain, routes_t,
    )


def as_column(row):
    return jnp.transpose(jnp.broadcast_to(row, (8, row.shape[1])))[:, :1]


def norm_back(grad, gain, normed, inverse):
    scaled = grad * gain
    return inverse * (scaled - normed * jnp.mean(scaled * normed, axis=-1, keepdims=True))


def resid_back_kernel(
    mine_ref, resid_ref, gain_ref, dz_ref, t0, t1, t2, b0, b1, b2, gains_ref, gates_ref, routes_ref, h_ref, attn_ref,
    p0, p1, p2, p3, r0, r1, r2, r3, grad_ref, attn_grad_ref, send_ref, keep_ref, second_scr, low_scr,
):
    mine = mine_ref[0]
    shard, width = p0.shape
    length = resid_ref.shape[0]
    routers = (r0, r1, r2, r3)
    gains = gains_ref[...]
    experts = lax.broadcasted_iota(jnp.int32, gains.shape, 0)
    gates = jnp.zeros(gains.shape, WIDE)
    for k in range(routes_ref.shape[0]):
        gates = gates + jnp.where(experts == routes_ref[k : k + 1, :], gates_ref[k : k + 1, :], 0.0)
    logit_grad = (gates * (gains - jnp.sum(gates * gains, axis=0, keepdims=True))).astype(LOW)
    half = t0.shape[0]
    second_scr[:half] = t0[...].astype(WIDE) + t1[...].astype(WIDE) + t2[...].astype(WIDE)
    second_scr[half:] = b0[...].astype(WIDE) + b1[...].astype(WIDE) + b2[...].astype(WIDE)
    for s, piece in enumerate(routers):
        columns = piece_columns(mine, s, shard)
        second_scr[:, columns] = second_scr[:, columns] + dot_t(logit_grad, piece[...])
    resid = resid_ref[...]
    inverse = inverse_rms(resid)
    normed = resid * inverse
    second = second_scr[...]
    gain_grad = jnp.sum(second * normed, axis=0, keepdims=True)
    grad = dz_ref[...].astype(WIDE) + norm_back(second, gain_ref[...], normed, inverse)
    grad_ref[...] = grad
    low_scr[...] = grad.astype(LOW)
    second_scr[:1, :] = gain_grad
    low = low_scr[...]
    for s, piece in enumerate((p0, p1, p2, p3)):
        columns = piece_columns(mine, s, shard)
        attn_grad_ref[:, columns] = dot_bt(low, piece[...]).astype(LOW)
        out_part = dot_t(attn_ref[:, columns], low).astype(LOW)
        router_part = lax.dot_general(
            h_ref[:length, columns], logit_grad, (((0,), (1,)), ((), ())), preferred_element_type=WIDE
        )
        small = jnp.concatenate(
            [router_part, as_column(second_scr[:1, columns]), jnp.zeros((shard, 128 - EXPERTS - 1), WIDE)], axis=1
        ).astype(LOW)
        target = send_ref if s % 2 else keep_ref
        target[s // 2, :, :width] = out_part
        target[s // 2, :, width:] = small


def resid_back_call(mine, resid, gain, dz, terms, gains, gates, routes_t, h, attn, pieces, router_pieces):
    length, width = resid.shape
    shard = pieces[0].shape[0]
    return pl.pallas_call(
        resid_back_kernel,
        in_specs=[pl.BlockSpec(memory_space=pltpu.SMEM)] + [pl.BlockSpec(memory_space=pltpu.VMEM)] * 22,
        out_specs=[pl.BlockSpec(memory_space=pltpu.VMEM)] * 4,
        out_shape=[
            shaped(length, width, dtype=WIDE),
            shaped(length, width),
            shaped(2, shard, width + 128),
            shaped(2, shard, width + 128),
        ],
        scratch_shapes=[pltpu.VMEM((length, width), WIDE), pltpu.VMEM((length, width), LOW)],
        compiler_params=pltpu.CompilerParams(vmem_limit_bytes=VMEM_MOST),
        cost_estimate=pl.CostEstimate(
            flops=4 * length * width * (width + EXPERTS), bytes_accessed=length * width * 40, transcendentals=0
        ),
    )(mine, resid, gain, dz, *terms, gains, gates, routes_t, h, attn, *pieces, *router_pieces)


def attention_back_kernel(
    mine_ref, q_ref, k_ref, v_ref, do_ref, h_ref, tokens_ref, gain_ref, grad_ref, p0, p1, p2, p3,
    seg_row_ref, seg_col_ref, cos_ref, sin_ref, input_ref, send_ref, keep_ref, qkv_scr, dk_scr, dv_scr, dh_scr,
):
    mine = mine_ref[0]
    length, width = q_ref.shape
    shard, qkv_width = p0.shape
    heads = QUERY_HEADS // KEY_VALUE_HEADS
    key_width = KEY_VALUE_HEADS * HEAD_DIM
    tile = 128
    dk_scr[...] = jnp.zeros_like(dk_scr)
    dv_scr[...] = jnp.zeros_like(dv_scr)
    for start in range(0, length, tile):
        band, reach = slice(start, start + tile), start + tile
        allowed = allowed_pairs(seg_col_ref, seg_row_ref, band, reach, heads)
        cos, sin = cos_ref[band, :], sin_ref[band, :]
        for g in range(KEY_VALUE_HEADS):
            queries = stacked_heads(q_ref, band, g, heads)
            grads = stacked_heads(do_ref, band, g, heads)
            keys = k_ref[:reach, head_slice(g)]
            probs = probabilities(queries, keys, allowed)
            prob_grad = dot_bt(grads, v_ref[:reach, head_slice(g)])
            delta = jnp.sum(probs * prob_grad, axis=-1, keepdims=True)
            score_grad = (probs * (prob_grad - delta) * HEAD_DIM ** (-0.5)).astype(LOW)
            dv_scr[:reach, head_slice(g)] += dot_t(probs.astype(LOW), grads)
            dk_scr[:reach, head_slice(g)] += dot_t(score_grad, queries)
            dq = dot(score_grad, keys)
            for h in range(heads):
                qkv_scr[band, head_slice(g * heads + h)] = turn_back(dq[h * tile : (h + 1) * tile], cos, sin).astype(LOW)
    for g in range(KEY_VALUE_HEADS):
        at = width + g * HEAD_DIM
        qkv_scr[:, at : at + HEAD_DIM] = turn_back(dk_scr[:, head_slice(g)], cos_ref[...], sin_ref[...]).astype(LOW)
    qkv_scr[:, width + key_width :] = dv_scr[...].astype(LOW)
    qkv = qkv_scr[...]
    pieces = (p0, p1, p2, p3)
    for s, piece in enumerate(pieces):
        dh_scr[:, piece_columns(mine, s, shard)] = dot_bt(qkv, piece[...])
    stream = tokens_ref[...].astype(WIDE)
    inverse = inverse_rms(stream)
    normed = stream * inverse
    first = dh_scr[...]
    gain_grad = jnp.sum(first * normed, axis=0, keepdims=True)
    input_ref[...] = grad_ref[...] + norm_back(first, gain_ref[...], normed, inverse)
    dh_scr[:1, :] = gain_grad
    for s in range(4):
        columns = piece_columns(mine, s, shard)
        target = send_ref if s % 2 else keep_ref
        target[s // 2, :, :qkv_width] = dot_t(h_ref[:, columns], qkv).astype(LOW)
        small = jnp.concatenate([as_column(dh_scr[:1, columns]), jnp.zeros((shard, 127), WIDE)], axis=1)
        target[s // 2, :, qkv_width:] = small.astype(LOW)


def attention_back_call(mine, q, k, v, do, h, tokens, gain, grad, pieces, seg_row, seg_col, cos, sin):
    length, width = q.shape
    shard, qkv_width = pieces[0].shape
    key_width = KEY_VALUE_HEADS * HEAD_DIM
    return pl.pallas_call(
        attention_back_kernel,
        in_specs=[pl.BlockSpec(memory_space=pltpu.SMEM)] + [pl.BlockSpec(memory_space=pltpu.VMEM)] * 16,
        out_specs=[pl.BlockSpec(memory_space=pltpu.VMEM)] * 3,
        out_shape=[
            shaped(length, width, dtype=WIDE),
            shaped(2, shard, qkv_width + 128),
            shaped(2, shard, qkv_width + 128),
        ],
        scratch_shapes=[
            pltpu.VMEM((length, qkv_width), LOW),
            pltpu.VMEM((length, key_width), WIDE),
            pltpu.VMEM((length, key_width), WIDE),
            pltpu.VMEM((length, width), WIDE),
        ],
        compiler_params=pltpu.CompilerParams(vmem_limit_bytes=VMEM_MOST),
        cost_estimate=pl.CostEstimate(
            flops=4 * length * width * qkv_width + 7 * length * length * width,
            bytes_accessed=length * width * 40,
            transcendentals=QUERY_HEADS * length * length,
        ),
    )(mine, q, k, v, do, h, tokens, gain, grad, *pieces, seg_row, seg_col, cos, sin)


def per_device_ring(
    tokens,
    segments,
    routes,
    attn_gain,
    ffn_gain,
    w_query,
    key_weight,
    value_weight,
    w_out,
    w_router,
    w_gate,
    w_up,
    w_down,
    cotangent,
):
    length, model_width = tokens.shape
    top_count = routes.shape[1]
    count = lax.axis_size("expert")
    holds = EXPERTS // count
    capacity = max(2, 3 * length * top_count // (2 * EXPERTS))
    slots = -(-capacity // 16) * 16
    shard = model_width // 4
    key_width = KEY_VALUE_HEADS * HEAD_DIM
    half = length // 2
    mine = lax.axis_index("wshard").astype(jnp.int32)
    token = mine.reshape(1)
    order = jnp.array(ring_order(count), jnp.int32)
    spot_of = jnp.array([ring_order(count).index(i) for i in range(count)], jnp.int32)
    here = lax.axis_index("expert")
    spot = spot_of[here]

    def gather_pieces(own):
        across = swap_x(own)
        return (own, swap_core(own), across, swap_core(across))

    router_pieces = gather_pieces(w_router.T)
    qkv_pieces = gather_pieces(jnp.concatenate([w_query, key_weight, value_weight], axis=1))

    dz = {0: cotangent}
    for step in (1, 2, 3):
        dz[-step], dz[step] = ahead(dz[1 - step], count), behind(dz[step - 1], count)
    dz[4] = (ahead(dz[-3][:half], count), behind(dz[3][half:], count))

    routes_t = routes.T
    others = {j: shifted(routes_t, -j, count) for j in BLOCK_OFFSETS if j}
    routes_local = jnp.stack([others[j] if j else routes_t for j in BLOCK_OFFSETS]) - here * holds
    local_ids = jnp.arange(holds, dtype=jnp.int32)
    named = jnp.any(routes_local[:, :, None, :] == local_ids[None, None, :, None], axis=1)
    triangle = (jnp.arange(length)[:, None] <= jnp.arange(length)[None, :]).astype(LOW)
    before = dot(named.reshape(count * holds, length).astype(LOW), triangle).reshape(count, holds, length)
    rank = jnp.where(named, before.astype(jnp.int32) - 1, -1)

    cosine, sine = rotary_tables(length, HEAD_DIM)
    cos = jnp.concatenate([cosine, cosine], axis=1)
    sin = jnp.concatenate([-sine, sine], axis=1)
    seg_col = segments.reshape(length, 1)
    gain_one, gain_two = attn_gain[None], ffn_gain[None]

    first_low, query, key, value, attn = attention_call(
        token, tokens, gain_one, qkv_pieces, segments, seg_col, cos, sin
    )
    out_pieces = gather_pieces(after(w_out, qkv_pieces[2]))
    resid, second, gates = project_call(token, tokens, attn, out_pieces, router_pieces, gain_two, routes_t)

    def experts(first, offsets, kept):
        return expert_call(
            token, first, [h[j] for j in offsets], [dz[j] for j in offsets], rank, routes_local, w_gate, w_up, w_down,
            kept, slots,
        )

    h = {0: second}
    h[-1], h[1] = ahead(h[0], count), behind(h[0], count)
    (d_own,), gain_own, kept = experts(6, (0,), None)
    h[-2], h[2] = ahead(h[-1], count), behind(h[1], count)
    (d_l1, d_r1), gain_1, kept = experts(0, (-1, 1), kept)
    h[-3], h[3] = ahead(h[-2], count), behind(h[2], count)
    (d_l2, d_r2), gain_2, kept = experts(2, (-2, 2), kept)
    h[4] = (ahead(h[-3][:half], count), behind(h[3][half:], count))
    (d_l3, d_r3), gain_3, kept = experts(4, (-3, 3), kept)
    (d_far,), gain_far, kept = experts(7, (4,), kept)

    def ring_sum(parts, hooks):
        from_behind, from_ahead = ahead(parts[4][0], count), behind(parts[4][1], count)
        up = (add_low(parts[3][0], from_behind), parts[3][1])
        down = (parts[-3][0], add_low(parts[-3][1], from_ahead))
        hooks[0](up[0], down[1])
        for step in (2, 1):
            from_behind = [ahead(u, count) for u in up]
            from_ahead = [behind(d, count) for d in down]
            up = [add_low(p, f) for p, f in zip(parts[step], from_behind)]
            down = [add_low(p, f) for p, f in zip(parts[-step], from_ahead)]
            hooks[3 - step](*up, *down)
        from_behind = [ahead(u, count) for u in up]
        from_ahead = [behind(d, count) for d in down]
        return [(parts[0][i], from_behind[i], from_ahead[i]) for i in range(2)]

    state = {"finished": None}
    sums, shards = {}, {}

    def weight_grads(expert, *wait_for):
        send_gu, keep_gu, send_d, keep_d = wgrad_call(expert, after(token, *wait_for), kept)
        got_gu, got_d = swap_core(send_gu), swap_core(send_d)
        sums[expert] = (keep_gu, got_gu, keep_d, got_d)

    def weight_sums(expert, *wait_for):
        keep_gu, got_gu, keep_d, got_d = sums[expert]
        half_gu, half_d = add_low(keep_gu[1], got_gu[1]), add_low(keep_d[1], got_d[1])
        if wait_for:
            half_gu, half_d = lax.optimization_barrier((half_gu, half_d, *wait_for))[:2]
        state["finished"] = finish_call(
            expert, holds, (keep_gu, got_gu, swap_x(half_gu), keep_d, got_d, swap_x(half_d)), state["finished"]
        )

    def first_hook(*sums_done):
        weight_grads(1, *sums_done)
        weight_grads(2, *sums_done)

    def second_hook(*sums_done):
        weight_grads(3, *sums_done)

    values = []

    def third_hook(*sums_done):
        values.extend(value_call(after(token, *sums_done), rank, kept[4], w_down, slots))

    weight_grads(0)
    terms = ring_sum(
        {0: d_own, 1: d_r1, -1: d_l1, 2: d_r2, -2: d_l2, 3: d_r3, -3: d_l3, 4: d_far},
        (first_hook, second_hook, third_hook),
    )
    weight_sums(0)
    weight_sums(1)
    weight_sums(2)

    gains = jnp.concatenate([gain_1, gain_2, gain_3, gain_own, gain_far], axis=0)
    block_of = jnp.array([BLOCK_OFFSETS.index(j if j <= count // 2 else j - count) for j in range(count)], jnp.int32)
    gain_send = gains[block_of[(spot_of - spot) % count]]
    gain_dense = lax.all_to_all(gain_send, "expert", split_axis=0, concat_axis=0, tiled=True).reshape(EXPERTS, length)

    grad, attn_grad, out_send, out_keep = resid_back_call(
        token, resid, gain_two, cotangent, (*terms[0], *terms[1]), gain_dense, gates, routes_t, second, attn, out_pieces,
        router_pieces,
    )
    out_got = swap_core(out_send)
    input_grad, qkv_send, qkv_keep = attention_back_call(
        token, query, key, value, attn_grad, first_low, tokens, gain_one, grad, qkv_pieces, segments, seg_col, cos, sin
    )
    qkv_got = swap_core(qkv_send)

    y = dict(zip(BLOCK_OFFSETS, values))
    nothing = lambda *_: None
    y_terms = ring_sum(y, (nothing, nothing, nothing))
    moe = jnp.concatenate([sum(t.astype(WIDE) for t in y_terms[i]) for i in range(2)], axis=0)
    mixed = (resid + moe).astype(LOW)

    def ring_total(values):
        rows, width = values.shape
        chunk = rows // count
        rolled = values.reshape(count, chunk, width)[(spot + jnp.arange(count)) % count]
        up, down = rolled[4], rolled[5]
        for step in (3, 2, 1):
            up = add_low(rolled[step], ahead(up, count))
            if step > 1:
                down = add_low(rolled[count + 1 - step], behind(down, count))
        own = add_low(rolled[0], ahead(up, count), behind(down, count))
        a1, b1 = ahead(own, count), behind(own, count)
        a2, b2 = ahead(a1, count), behind(b1, count)
        a3, b3 = ahead(a2, count), behind(b2, count)
        a4 = ahead(a3, count)
        stacked = jnp.stack([own, b1, b2, b3, a4, a3, a2, a1])
        return stacked[(jnp.arange(count) - spot) % count].reshape(rows, width).astype(WIDE)

    def shard_total(keep, got):
        across = swap_x(add_low(keep[1], got[1]))
        return ring_total(add_low(keep[0], got[0], across)), across

    out_sum, _ = shard_total(out_keep, out_got)
    qkv_sum, qkv_across = shard_total(qkv_keep, qkv_got)
    weight_sums(3, qkv_across)
    gate_shard, up_shard, down_shard = state["finished"]
    qkv_width = model_width + 2 * key_width
    return (
        mixed,
        input_grad,
        qkv_sum[:, qkv_width],
        out_sum[:, model_width + EXPERTS],
        qkv_sum[:, :model_width],
        qkv_sum[:, model_width : model_width + key_width],
        qkv_sum[:, model_width + key_width : qkv_width],
        out_sum[:, :model_width],
        out_sum[:, model_width : model_width + EXPERTS],
        gate_shard,
        up_shard,
        down_shard,
    )


def solution(mesh):
    ring = mesh.shape["expert"] == len(BLOCK_OFFSETS) and mesh.shape["wshard"] == 4
    body = per_device_ring if ring else per_device_exchange
    in_specs = (
        P(("expert", "wshard"), None),
        P(("expert", "wshard"), None),
        P(("expert", "wshard"), None),
        P(),
        P(),
        P("wshard", None),
        P("wshard", None),
        P("wshard", None),
        P("wshard", None),
        P("wshard", None),
        P(None, "expert"),
        P(None, "expert"),
        P("expert", None),
        P(("expert", "wshard"), None),
    )
    out_specs = (
        P(("expert", "wshard"), None),
        P(("expert", "wshard"), None),
        P("wshard"),
        P("wshard"),
        P("wshard", None),
        P("wshard", None),
        P("wshard", None),
        P("wshard", None),
        P("wshard", None),
        P("wshard", "expert"),
        P("wshard", "expert"),
        P("expert", "wshard"),
    )
    return jax.shard_map(
        body, mesh=mesh, in_specs=in_specs, out_specs=out_specs, check_vma=False
    )
```

```python
import functools

import jax
import jax.numpy as jnp
from jax import lax
from jax.experimental import pallas as pl
from jax.experimental.pallas import tpu as pltpu
from jax.sharding import PartitionSpec as P

QUERY_HEADS = 12
KEY_VALUE_HEADS = 2
HEAD_DIM = 128
EXPERTS = 32
TOP = 4


EPS = 1e-06
ROPE_BASE = 10000.0
NEG = -1e30
LOW = jnp.bfloat16
WIDE = jnp.float32
VMEM_MOST = 60 * 1024 * 1024
def norm_forward(values, gain):
    inverse = lax.rsqrt(jnp.mean(values * values, axis=-1) + EPS)
    normed = values * inverse[:, None]
    return (normed * gain, normed, inverse)


def norm_backward(grad, gain, normed, inverse):
    gain_grad = jnp.sum(grad * normed, axis=0)
    scaled = grad * gain
    centred = scaled - normed * jnp.mean(scaled * normed, axis=-1, keepdims=True)
    return (inverse[:, None] * centred, gain_grad)


def rotary_tables(seq_length, head_size):
    half_size = head_size // 2
    frequency = ROPE_BASE ** (-(jnp.arange(half_size, dtype=jnp.float32) * 2.0 / head_size))
    angles = jnp.arange(seq_length, dtype=jnp.float32)[:, None] * frequency[None, :]
    return (jnp.cos(angles), jnp.sin(angles))


def apply_rotation(values, cosine_lookup, sine_lookup):
    half_size = values.shape[-1] // 2
    first_half = values[..., :half_size]
    second_half = values[..., half_size:]
    cos_part = cosine_lookup[:, None, :]
    sin_part = sine_lookup[:, None, :]
    return jnp.concatenate(
        [
            first_half * cos_part - second_half * sin_part,
            second_half * cos_part + first_half * sin_part,
        ],
        axis=-1,
    )


def reverse_rotation(values, cosine_lookup, sine_lookup):
    half_size = values.shape[-1] // 2
    first_half = values[..., :half_size]
    second_half = values[..., half_size:]
    cos_part = cosine_lookup[:, None, :]
    sin_part = sine_lookup[:, None, :]
    return jnp.concatenate(
        [
            first_half * cos_part + second_half * sin_part,
            second_half * cos_part - first_half * sin_part,
        ],
        axis=-1,
    )


def per_device_exchange(
    tokens,
    segments,
    routes,
    attn_gain,
    ffn_gain,
    w_query,
    key_weight,
    value_weight,
    w_out,
    w_router,
    w_gate,
    w_up,
    w_down,
    cotangent,
):
    lower_dtype = jnp.bfloat16
    wide_type = jnp.float32
    sequence_length, model_width = tokens.shape
    top_count = routes.shape[1]
    axis_count = lax.axis_size("expert")
    owners = max(1, axis_count // EXPERTS)
    holds = max(1, EXPERTS // axis_count)
    groups = EXPERTS // holds
    capacity = max(2, 3 * sequence_length * top_count // (2 * EXPERTS))
    hidden_dev = w_gate.shape[1] // holds
    query_group_width = QUERY_HEADS // KEY_VALUE_HEADS
    score_scale = HEAD_DIM ** (-0.5)
    pair_count = sequence_length * top_count
    query_full, key_full, value_full, out_full, router_full = (
        lax.all_gather(w_query, "wshard", axis=0, tiled=True),
        lax.all_gather(key_weight, "wshard", axis=0, tiled=True),
        lax.all_gather(value_weight, "wshard", axis=0, tiled=True),
        lax.all_gather(w_out, "wshard", axis=0, tiled=True),
        lax.all_gather(w_router, "wshard", axis=0, tiled=True),
    )
    stream = tokens.astype(wide_type)
    first_norm, first_normed, first_inverse = norm_forward(stream, attn_gain)
    first_low = first_norm.astype(lower_dtype)
    cosine_lookup, sine_lookup = rotary_tables(sequence_length, HEAD_DIM)
    query_pre = jnp.dot(first_low, query_full, preferred_element_type=wide_type).reshape(
        sequence_length, QUERY_HEADS, HEAD_DIM
    )
    key_unrotated = jnp.dot(first_low, key_full, preferred_element_type=wide_type).reshape(
        sequence_length, KEY_VALUE_HEADS, HEAD_DIM
    )
    query_rotated = (
        apply_rotation(query_pre, cosine_lookup, sine_lookup)
        .astype(lower_dtype)
        .reshape(sequence_length, KEY_VALUE_HEADS, query_group_width, HEAD_DIM)
    )
    key_rotated = apply_rotation(key_unrotated, cosine_lookup, sine_lookup).astype(lower_dtype)
    value_lowered = (
        jnp.dot(first_low, value_full, preferred_element_type=wide_type)
        .astype(lower_dtype)
        .reshape(sequence_length, KEY_VALUE_HEADS, HEAD_DIM)
    )
    positions = jnp.arange(sequence_length)
    offset = positions[:, None] - positions[None, :]
    segment_row = segments[0]
    allowed = (segment_row[:, None] == segment_row[None, :]) & (offset >= 0)
    raw_scores = jnp.einsum(
        "qagd,kad->agqk", query_rotated, key_rotated, preferred_element_type=wide_type
    )
    scores = jnp.where(allowed, raw_scores * score_scale, NEG)
    score_top = jnp.max(scores, axis=-1, keepdims=True)
    expo_terms = jnp.exp(scores - score_top)
    expo_total = jnp.sum(expo_terms, axis=-1, keepdims=True)
    log_total = score_top + jnp.log(expo_total)
    probs_low = (expo_terms / expo_total).astype(lower_dtype)
    attn_low = (
        jnp.einsum("agqk,kad->qagd", probs_low, value_lowered, preferred_element_type=wide_type)
        .astype(lower_dtype)
        .reshape(sequence_length, QUERY_HEADS * HEAD_DIM)
    )
    resid = stream + jnp.dot(attn_low, out_full, preferred_element_type=wide_type)
    second_norm, second_normed, second_inverse = norm_forward(resid, ffn_gain)
    second_low = second_norm.astype(lower_dtype)
    logits = jnp.dot(second_low, router_full, preferred_element_type=wide_type)
    choose = (routes[:, :, None] == jnp.arange(EXPERTS)[None, None, :]).astype(wide_type)
    selected = jnp.sum(choose * logits[:, None, :], axis=-1)
    gate_probs = jax.nn.softmax(selected, axis=-1)
    flat_routes = routes.reshape(pair_count)
    one_hot = (flat_routes[:, None] == jnp.arange(EXPERTS)[None, :]).astype(jnp.int32)
    slot_rank = jnp.sum((jnp.cumsum(one_hot, axis=0) - 1) * one_hot, axis=1)
    slot_index = (flat_routes // holds * capacity + slot_rank) * holds + flat_routes % holds
    slot_pair = (
        jnp.full((EXPERTS * capacity,), pair_count, jnp.int32)
        .at[slot_index]
        .set(jnp.arange(pair_count, dtype=jnp.int32))
    )
    second_ext = jnp.concatenate([second_low, jnp.zeros((1, model_width), lower_dtype)], axis=0)
    send_rows = jnp.repeat(
        second_ext[slot_pair // top_count].reshape(groups, capacity, holds, model_width),
        owners,
        axis=0,
    )
    gate_local = w_gate.reshape(model_width, holds, hidden_dev)
    up_local = w_up.reshape(model_width, holds, hidden_dev)
    down_local = w_down.reshape(holds, hidden_dev, model_width)

    def owner_total(values):
        summed = jnp.sum(
            values.astype(wide_type).reshape(groups, owners, capacity, holds, model_width), axis=1
        )
        return summed.reshape(EXPERTS * capacity, model_width)

    received = lax.all_to_all(send_rows, "expert", split_axis=0, concat_axis=0, tiled=True)
    gate_pre = jnp.einsum("scld,dlf->sclf", received, gate_local, preferred_element_type=wide_type)
    up_pre = jnp.einsum("scld,dlf->sclf", received, up_local, preferred_element_type=wide_type)
    hidden = (jax.nn.silu(gate_pre) * up_pre).astype(lower_dtype)
    partial_value = jnp.einsum(
        "sclf,lfd->scld", hidden, down_local, preferred_element_type=wide_type
    ).astype(lower_dtype)
    returned = lax.all_to_all(partial_value, "expert", split_axis=0, concat_axis=0, tiled=True)
    expert_wide = owner_total(returned)[slot_index].reshape(sequence_length, top_count, model_width)
    mixed = (resid + jnp.sum(gate_probs[:, :, None] * expert_wide, axis=1)).astype(lower_dtype)
    upstream = cotangent.astype(wide_type)
    query_back, key_back, value_back, out_back, router_back = (
        lax.all_gather(w_query, "wshard", axis=0, tiled=True),
        lax.all_gather(key_weight, "wshard", axis=0, tiled=True),
        lax.all_gather(value_weight, "wshard", axis=0, tiled=True),
        lax.all_gather(w_out, "wshard", axis=0, tiled=True),
        lax.all_gather(w_router, "wshard", axis=0, tiled=True),
    )
    gate_grad = jnp.sum(expert_wide * upstream[:, None, :], axis=-1)
    sel_grad = gate_probs * (gate_grad - jnp.sum(gate_probs * gate_grad, axis=-1, keepdims=True))
    logit_grad = jnp.sum(choose * sel_grad[:, :, None], axis=1).astype(lower_dtype)
    pair_grad = (
        (gate_probs[:, :, None] * upstream[:, None, :])
        .astype(lower_dtype)
        .reshape(pair_count, model_width)
    )
    pair_ext = jnp.concatenate([pair_grad, jnp.zeros((1, model_width), lower_dtype)], axis=0)
    grad_send = jnp.repeat(
        pair_ext[slot_pair].reshape(groups, capacity, holds, model_width), owners, axis=0
    )
    grad_recv, rows_recv = (
        lax.all_to_all(grad_send, "expert", split_axis=0, concat_axis=0, tiled=True),
        lax.all_to_all(send_rows, "expert", split_axis=0, concat_axis=0, tiled=True),
    )
    gate_pre = jnp.einsum("scld,dlf->sclf", rows_recv, gate_local, preferred_element_type=wide_type)
    up_pre = jnp.einsum("scld,dlf->sclf", rows_recv, up_local, preferred_element_type=wide_type)
    sigmoid_gate = jax.nn.sigmoid(gate_pre)
    silu_gate = gate_pre * sigmoid_gate
    hidden = (silu_gate * up_pre).astype(lower_dtype)
    hidden_grad = jnp.einsum(
        "scld,lfd->sclf", grad_recv, down_local, preferred_element_type=wide_type
    )
    gate_pre_grad = (
        hidden_grad * up_pre * sigmoid_gate * (1.0 + gate_pre * (1.0 - sigmoid_gate))
    ).astype(lower_dtype)
    up_pre_grad = (hidden_grad * silu_gate).astype(lower_dtype)
    row_grad = (
        jnp.einsum("sclf,dlf->scld", gate_pre_grad, gate_local, preferred_element_type=wide_type)
        + jnp.einsum("sclf,dlf->scld", up_pre_grad, up_local, preferred_element_type=wide_type)
    ).astype(lower_dtype)
    returned_grad = lax.all_to_all(row_grad, "expert", split_axis=0, concat_axis=0, tiled=True)
    gate_wgrad = jnp.einsum(
        "scld,sclf->dlf", rows_recv, gate_pre_grad, preferred_element_type=wide_type
    ).reshape(model_width, holds * hidden_dev)
    up_wgrad = jnp.einsum(
        "scld,sclf->dlf", rows_recv, up_pre_grad, preferred_element_type=wide_type
    ).reshape(model_width, holds * hidden_dev)
    down_wgrad = jnp.einsum(
        "sclf,scld->lfd", hidden, grad_recv, preferred_element_type=wide_type
    ).reshape(holds * hidden_dev, model_width)
    gate_shard, up_shard, down_shard = (
        lax.psum_scatter(
            gate_wgrad.astype(jnp.bfloat16), "wshard", scatter_dimension=0, tiled=True
        ).astype(jnp.float32),
        lax.psum_scatter(
            up_wgrad.astype(jnp.bfloat16), "wshard", scatter_dimension=0, tiled=True
        ).astype(jnp.float32),
        lax.psum_scatter(
            down_wgrad.astype(jnp.bfloat16), "wshard", scatter_dimension=1, tiled=True
        ).astype(jnp.float32),
    )
    token_grad = owner_total(returned_grad)[slot_index].reshape(
        sequence_length, top_count, model_width
    )
    second_grad = jnp.sum(token_grad, axis=1) + jnp.dot(
        logit_grad, router_back.T, preferred_element_type=wide_type
    )
    router_wgrad = jnp.einsum("td,te->de", second_low, logit_grad, preferred_element_type=wide_type)
    resid_part, ffn_gain_grad = norm_backward(second_grad, ffn_gain, second_normed, second_inverse)
    resid_grad = upstream + resid_part
    resid_low = resid_grad.astype(lower_dtype)
    out_wgrad = jnp.einsum("tc,td->cd", attn_low, resid_low, preferred_element_type=wide_type)
    attn_grad = (
        jnp.dot(resid_low, out_back.T, preferred_element_type=wide_type)
        .astype(lower_dtype)
        .reshape(sequence_length, KEY_VALUE_HEADS, query_group_width, HEAD_DIM)
    )
    raw_again = jnp.einsum(
        "qagd,kad->agqk", query_rotated, key_rotated, preferred_element_type=wide_type
    )
    scores_again = jnp.where(allowed, raw_again * score_scale, NEG)
    probs_again = jnp.exp(scores_again - log_total)
    prob_grad = jnp.einsum(
        "qagd,kad->agqk", attn_grad, value_lowered, preferred_element_type=wide_type
    )
    row_delta = jnp.sum(probs_again * prob_grad, axis=-1, keepdims=True)
    score_grad = (probs_again * (prob_grad - row_delta) * score_scale).astype(lower_dtype)
    value_grad = (
        jnp.einsum("agqk,qagd->kad", probs_low, attn_grad, preferred_element_type=wide_type)
        .astype(lower_dtype)
        .reshape(sequence_length, KEY_VALUE_HEADS * HEAD_DIM)
    )
    query_rot_grad = jnp.einsum(
        "agqk,kad->qagd", score_grad, key_rotated, preferred_element_type=wide_type
    ).reshape(sequence_length, QUERY_HEADS, HEAD_DIM)
    key_rotated_gradient = jnp.einsum(
        "agqk,qagd->kad", score_grad, query_rotated, preferred_element_type=wide_type
    )
    query_grad = (
        reverse_rotation(query_rot_grad, cosine_lookup, sine_lookup)
        .astype(lower_dtype)
        .reshape(sequence_length, QUERY_HEADS * HEAD_DIM)
    )
    key_grad = (
        reverse_rotation(key_rotated_gradient, cosine_lookup, sine_lookup)
        .astype(lower_dtype)
        .reshape(sequence_length, KEY_VALUE_HEADS * HEAD_DIM)
    )
    query_wgrad = jnp.einsum("td,tc->dc", first_low, query_grad, preferred_element_type=wide_type)
    key_wgrad = jnp.einsum("td,tc->dc", first_low, key_grad, preferred_element_type=wide_type)
    value_wgrad = jnp.einsum("td,tc->dc", first_low, value_grad, preferred_element_type=wide_type)
    first_grad = (
        jnp.dot(query_grad, query_back.T, preferred_element_type=wide_type)
        + jnp.dot(key_grad, key_back.T, preferred_element_type=wide_type)
        + jnp.dot(value_grad, value_back.T, preferred_element_type=wide_type)
    )
    stream_part, attn_gain_grad = norm_backward(first_grad, attn_gain, first_normed, first_inverse)
    input_grad = resid_grad + stream_part
    query_part, key_part, value_part, out_part, router_part, attn_gain_part, ffn_gain_part = (
        lax.psum_scatter(
            query_wgrad.astype(jnp.bfloat16), "wshard", scatter_dimension=0, tiled=True
        ).astype(jnp.float32),
        lax.psum_scatter(
            key_wgrad.astype(jnp.bfloat16), "wshard", scatter_dimension=0, tiled=True
        ).astype(jnp.float32),
        lax.psum_scatter(
            value_wgrad.astype(jnp.bfloat16), "wshard", scatter_dimension=0, tiled=True
        ).astype(jnp.float32),
        lax.psum_scatter(
            out_wgrad.astype(jnp.bfloat16), "wshard", scatter_dimension=0, tiled=True
        ).astype(jnp.float32),
        lax.psum_scatter(
            router_wgrad.astype(jnp.bfloat16), "wshard", scatter_dimension=0, tiled=True
        ).astype(jnp.float32),
        lax.psum_scatter(
            attn_gain_grad.astype(jnp.bfloat16), "wshard", scatter_dimension=0, tiled=True
        ).astype(jnp.float32),
        lax.psum_scatter(
            ffn_gain_grad.astype(jnp.bfloat16), "wshard", scatter_dimension=0, tiled=True
        ).astype(jnp.float32),
    )
    query_sum, key_sum, value_sum, out_sum, router_sum, attn_gain_sum, ffn_gain_sum = lax.psum(
        (query_part, key_part, value_part, out_part, router_part, attn_gain_part, ffn_gain_part),
        "expert",
    )
    return (
        mixed,
        input_grad,
        attn_gain_sum,
        ffn_gain_sum,
        query_sum,
        key_sum,
        value_sum,
        out_sum,
        router_sum,
        gate_shard,
        up_shard,
        down_shard,
    )


BLOCK_OFFSETS = (-1, 1, -2, 2, -3, 3, 0, 4)


def ring_order(count):
    return [0] + list(range(1, count, 2)) + list(range(count - 2, 0, -2))


def shifted(value, step, count):
    order = ring_order(count)
    return lax.ppermute(value, "expert", [(order[i], order[(i + step) % count]) for i in range(count)])


def ahead(value, count):
    return shifted(value, 1, count)


def behind(value, count):
    return shifted(value, -1, count)


def swap_core(value):
    size = lax.axis_size("wshard")
    return lax.ppermute(value, "wshard", [(i, i ^ 1) for i in range(size)])


def swap_x(value):
    size = lax.axis_size("wshard")
    return lax.ppermute(value, "wshard", [(i, i ^ 2) for i in range(size)])


def work(flops, bytes_accessed, transcendentals):
    scale = 8
    return pl.CostEstimate(
        flops=flops // scale, bytes_accessed=bytes_accessed // scale, transcendentals=transcendentals // scale
    )


def add_low(*terms):
    return sum(term.astype(WIDE) for term in terms).astype(LOW)


def after(value, *others):
    return lax.optimization_barrier((value, *others))[0]


def places(rank_row, slots):
    rows = lax.broadcasted_iota(jnp.int32, (slots, rank_row.shape[-1]), 0)
    return rank_row == rows


def expert_ranks(routes, holds):
    tokens = routes.shape[1]
    names = [jnp.sum((routes == l).astype(WIDE), axis=0, keepdims=True) for l in range(holds)]
    names = jnp.concatenate(names + [jnp.zeros((16 - holds, tokens), WIDE)], axis=0)
    rows = lax.broadcasted_iota(jnp.int32, (tokens, tokens), 0)
    columns = lax.broadcasted_iota(jnp.int32, (tokens, tokens), 1)
    before = dot(names.astype(LOW), (rows <= columns).astype(WIDE).astype(LOW))
    return jnp.where(names > 0.0, before - 1.0, -1.0)[:holds].astype(jnp.int32)


def pack_routing(gates, routes):
    high = gates.astype(LOW).astype(WIDE)
    rows = [high, gates - high, routes.astype(WIDE)]
    spare = 16 - 3 * gates.shape[0]
    return jnp.concatenate(rows + [jnp.zeros((spare, gates.shape[1]), WIDE)], axis=0).astype(LOW)


def unpack_routing(packed):
    top_count = TOP
    packed = packed.astype(WIDE)
    return packed[:top_count] + packed[top_count : 2 * top_count], packed[2 * top_count : 3 * top_count]


def dot_t(a, b):
    return lax.dot_general(a, b, (((0,), (0,)), ((), ())), preferred_element_type=WIDE)


def dot_bt(a, b):
    return lax.dot_general(a, b, (((1,), (1,)), ((), ())), preferred_element_type=WIDE)


def dot(a, b):
    return jnp.dot(a, b, preferred_element_type=WIDE)


def expert_kernel(count, slots, aliased, *refs):
    token_ref = refs[0]
    h_refs, dz_refs = refs[1 : 1 + count], refs[1 + count : 1 + 2 * count]
    wg_ref, wu_ref, wd_ref = refs[1 + 2 * count : 4 + 2 * count]
    rest = refs[4 + 2 * count + (7 if aliased else 0) :]
    d_refs = rest[:count]
    gain_ref, rank_ref, rows_out, dz_out, gg_out, ug_out, hid_out = rest[count : count + 7]
    place_scr, back_scr, gate_scr = rest[count + 7 :]
    e = pl.program_id(0)
    holds, tokens = rank_ref.shape[1:]
    here = pl.ds(pl.multiple_of(e * slots, slots), slots)
    @pl.when(e == 0)
    def _():
        for b, (h_ref, dz_ref) in enumerate(zip(h_refs, dz_refs)):
            gates, routes = unpack_routing(h_ref[tokens : tokens + 16, :tokens])
            routes = routes - (token_ref[1] * holds).astype(WIDE)
            ranks = expert_ranks(routes, holds)
            rank_ref[b] = ranks
            for l in range(holds):
                band = slice(l * slots, (l + 1) * slots)
                spot = places(ranks[l : l + 1], slots).astype(WIDE)
                named = jnp.where(routes == l, gates, 0.0)
                gate_scr[b, band, :] = jnp.broadcast_to(
                    jnp.sum(spot * jnp.sum(named, axis=0, keepdims=True), axis=1, keepdims=True), (slots, 128)
                )
                place_scr[b, band, :] = spot.astype(LOW)
            for source, target in ((h_ref, rows_out), (dz_ref, dz_out)):
                taken = dot(place_scr[b], source[:tokens]).astype(LOW)
                for l in range(holds):
                    target[l, b * slots : (b + 1) * slots, :] = taken[l * slots : (l + 1) * slots]

    gate = jnp.concatenate([gate_scr[b, here, :] for b in range(count)], axis=0)[:, :1]
    rows = rows_out[e]
    gate_pre = dot(rows, wg_ref[...])
    up_pre = dot(rows, wu_ref[...])
    sig = jax.nn.sigmoid(gate_pre)
    silu = gate_pre * sig
    hidden = (silu * up_pre).astype(LOW).astype(WIDE)
    back = dot_bt(dz_out[e], wd_ref[...])
    gains = jnp.sum(back * hidden, axis=1, keepdims=True)
    back = back * gate
    gate_grad = (back * (up_pre * sig * (1.0 + gate_pre * (1.0 - sig)))).astype(LOW)
    up_grad = (back * silu).astype(LOW)
    gg_out[0] = gate_grad
    ug_out[0] = up_grad
    hid_out[0] = (hidden * gate).astype(LOW)
    row_grad = (dot_bt(gate_grad, wg_ref[...]) + dot_bt(up_grad, wu_ref[...])).astype(LOW)
    for b in range(count):
        band = slice(b * slots, (b + 1) * slots)
        back_scr[b, here, :] = row_grad[band]
        spot = place_scr[b, here, :].astype(WIDE)
        gain_ref[b, pl.ds(e, 1), :] = jnp.sum(spot * gains[band], axis=0, keepdims=True)

    @pl.when(e == pl.num_programs(0) - 1)
    def _():
        for b in range(count):
            d_refs[b][...] = dot_t(place_scr[b], back_scr[b]).astype(LOW)


def expert_call(token, first, blocks, dz_blocks, w_gate, w_up, w_down, kept, holds, slots, total):
    count = len(blocks)
    tokens, width = dz_blocks[0].shape
    hidden = w_gate.shape[1] // holds
    whole = lambda *shape: pl.BlockSpec(shape, lambda e: (0,) * len(shape))
    once = lambda *shape: pl.BlockSpec(shape, lambda e: (0,) * len(shape), pipeline_mode=pl.Buffered(buffer_count=1))
    aliased = kept is not None
    in_specs = (
        [pl.BlockSpec(memory_space=pltpu.SMEM)]
        + [once(*b.shape) for b in (*blocks, *dz_blocks)]
        + [
            pl.BlockSpec((width, hidden), lambda e: (0, e)),
            pl.BlockSpec((width, hidden), lambda e: (0, e)),
            pl.BlockSpec((hidden, width), lambda e: (e, 0)),
        ]
    )
    aliases = {len(in_specs) + i: count + i for i in range(7)} if aliased else {}
    out = pl.pallas_call(
        functools.partial(expert_kernel, count, slots, aliased),
        grid=(holds,),
        in_specs=in_specs + ([pl.BlockSpec(memory_space=pl.ANY)] * 7 if aliased else []),
        out_specs=[whole(tokens, width)] * count
        + [pl.BlockSpec((count, holds, tokens), lambda e: (first // count, 0, 0))] * 2
        + [pl.BlockSpec((holds, count * slots, width), lambda e: (0, first // count, 0))] * 2
        + [pl.BlockSpec((1, count * slots, hidden), lambda e: (e, first // count, 0))] * 3,
        out_shape=[shaped(tokens, width)] * count
        + [shaped(total, holds, tokens, dtype=WIDE), shaped(total, holds, tokens, dtype=jnp.int32)]
        + [shaped(holds, total * slots, width)] * 2
        + [shaped(holds, total * slots, hidden)] * 3,
        scratch_shapes=[
            pltpu.VMEM((count, holds * slots, tokens), LOW),
            pltpu.VMEM((count, holds * slots, width), LOW),
            pltpu.VMEM((count, holds * slots, 128), WIDE),
        ],
        input_output_aliases=aliases,
        compiler_params=pltpu.CompilerParams(vmem_limit_bytes=VMEM_MOST),
        cost_estimate=work(
            flops=2 * holds * count * slots * width * (5 * hidden + 3 * tokens),
            bytes_accessed=3 * holds * width * hidden * 2
            + count * tokens * width * 6
            + holds * count * slots * (2 * width + 3 * hidden) * 2,
            transcendentals=holds * count * slots * hidden,
        ),
    )(token, *blocks, *dz_blocks, w_gate, w_up, w_down, *(kept if aliased else ()))
    return out[:count], tuple(out[count:])


def value_kernel(slots, _, rank_ref, hid_ref, wd_ref, *refs):
    total, holds, tokens = rank_ref.shape
    y_refs, (value_scr, place_scr) = refs[:total], refs[total:]
    e = pl.program_id(0)
    here = pl.ds(pl.multiple_of(e * slots, slots), slots)
    value = dot(hid_ref[0], wd_ref[...]).astype(LOW)
    for b in range(total):
        value_scr[b, here, :] = value[b * slots : (b + 1) * slots]

    @pl.when(e == pl.num_programs(0) - 1)
    def _():
        for b in range(total):
            for l in range(holds):
                spot = places(rank_ref[b, l : l + 1, :], slots)
                place_scr[l * slots : (l + 1) * slots, :] = spot.astype(WIDE).astype(LOW)
            y_refs[b][...] = dot_t(place_scr[...], value_scr[b]).astype(LOW)


def value_call(token, rank, hidden_rows, w_down, slots):
    total, holds, tokens = rank.shape
    width = w_down.shape[1]
    hidden = hidden_rows.shape[2]
    whole = lambda *shape: pl.BlockSpec(shape, lambda e: (0,) * len(shape))
    out = pl.pallas_call(
        functools.partial(value_kernel, slots),
        grid=(holds,),
        in_specs=[
            pl.BlockSpec(memory_space=pltpu.SMEM),
            whole(*rank.shape),
            pl.BlockSpec((1, total * slots, hidden), lambda e: (e, 0, 0)),
            pl.BlockSpec((hidden, width), lambda e: (e, 0)),
        ],
        out_specs=[whole(tokens, width)] * total,
        out_shape=[shaped(tokens, width)] * total,
        scratch_shapes=[pltpu.VMEM((total, holds * slots, width), LOW), pltpu.VMEM((holds * slots, tokens), LOW)],
        compiler_params=pltpu.CompilerParams(vmem_limit_bytes=VMEM_MOST),
        cost_estimate=work(
            flops=2 * total * holds * slots * width * (hidden + tokens),
            bytes_accessed=2 * (holds * hidden * (width + total * slots) + total * tokens * width),
            transcendentals=0,
        ),
    )(token, rank, hidden_rows, w_down)
    return out


def wgrad_kernel(apart, place_ref, rows_ref, dz_ref, gg_ref, ug_ref, hid_ref, *outs):
    step = pl.program_id(0)
    shard = outs[0].shape[1]
    columns = pl.ds(pl.multiple_of(jnp.bitwise_xor(place_ref[0], step) * shard, 128), shard)
    rows, grads = rows_ref[0, :, columns], dz_ref[0, :, columns]
    parts = [dot_t(rows, gg_ref[0]), dot_t(rows, ug_ref[0]), dot_t(grads, hid_ref[0])]
    parts = [part.astype(LOW) for part in parts]
    for s in range(4):

        @pl.when(step == s)
        def _():
            for i, part in enumerate(parts):
                if s == 3 and apart:
                    outs[3 + i][...] = part
                else:
                    outs[s][i] = part


def wgrad_call(expert, place, kept, apart=False):
    _, count, width = kept[0].shape
    hidden = kept[2].shape[2]
    shard = width // 4
    row_spec = lambda d: pl.BlockSpec((1, count, d), lambda s: (expert, 0, 0), pipeline_mode=pl.Buffered(buffer_count=1))
    shapes = [(3, shard, hidden)] * 3 + ([(shard, hidden)] * 3 if apart else [(3, shard, hidden)])
    out = pl.pallas_call(
        functools.partial(wgrad_kernel, apart),
        grid=(4,),
        in_specs=[pl.BlockSpec(memory_space=pltpu.SMEM), row_spec(width), row_spec(width)] + [row_spec(hidden)] * 3,
        out_specs=[pl.BlockSpec(shape, lambda s, zeros=(0,) * len(shape): zeros) for shape in shapes],
        out_shape=[shaped(*shape) for shape in shapes],
        compiler_params=pltpu.CompilerParams(vmem_limit_bytes=VMEM_MOST),
        cost_estimate=work(
            flops=2 * count * width * 3 * hidden,
            bytes_accessed=2 * (count * (2 * width + 3 * hidden) + 3 * width * hidden),
            transcendentals=0,
        ),
    )(place, *kept)
    return [*out[:3], out[3:] if apart else out[3]]


def sums_kernel(plan, _, *refs):
    inputs, outputs = list(refs[: sum(map(sum, plan))]), refs[sum(map(sum, plan)) :]
    for sizes, out in zip(plan, outputs):
        lead = 0
        for size in sizes:
            total = sum(inputs.pop(0)[...].astype(WIDE) for _ in range(size)).astype(out.dtype)
            if len(sizes) == 1:
                out[...] = total
            elif total.ndim == 2:
                out[lead] = total
                lead += 1
            else:
                out[lead : lead + total.shape[0]] = total
                lead += total.shape[0]


def sums_call(token, *outputs):
    steps = 4
    in_specs, operands, out_specs, out_shapes, moved = [], [], [], [], 0
    for sums in outputs:
        lead = 0
        for terms in sums:
            for term in terms:
                array, part = term if isinstance(term, tuple) else (term, None)
                rows, width = array.shape[-2:]
                if part is None:
                    head, start = array.shape[:-2], (0,) * (array.ndim - 2)
                elif isinstance(part, range):
                    head, start = (len(part),), (0,)
                else:
                    head, start = (None,), (part,)
                in_specs.append(
                    pl.BlockSpec((*head, rows // steps, width), lambda i, start=start: (*start, i, 0))
                )
                operands.append(array)
            lead += head[0] if head and head[0] else 1
        whole = (lead,) if len(sums) > 1 or (head and head[0]) else ()
        out_specs.append(
            pl.BlockSpec((*whole, rows // steps, width), lambda i, zeros=(0,) * len(whole): (*zeros, i, 0))
        )
        out_shapes.append(shaped(*whole, rows, width))
        moved += 6 * out_shapes[-1].size
    return pl.pallas_call(
        functools.partial(sums_kernel, [[len(terms) for terms in sums] for sums in outputs]),
        grid=(steps,),
        in_specs=[pl.BlockSpec(memory_space=pltpu.SMEM)] + in_specs,
        out_specs=out_specs,
        out_shape=out_shapes,
        compiler_params=pltpu.CompilerParams(vmem_limit_bytes=VMEM_MOST),
        cost_estimate=work(flops=0, bytes_accessed=moved, transcendentals=0),
    )(token, *operands)


def finish_kernel(sizes, *refs):
    outs = refs[-3:]
    at = 0
    for i, out in enumerate(outs):
        total = sum(ref[...].astype(WIDE) for ref in refs[at : at + sizes[i]])
        at += sizes[i]
        out[...] = total if i < 2 else jnp.transpose(total)


def finish_call(expert, holds, terms, kept):
    shard, hidden = terms[0][0][0].shape[1:]
    column, row = (shard, hidden), (hidden, shard)
    out_specs = [pl.BlockSpec(column, lambda s: (0, expert))] * 2 + [pl.BlockSpec(row, lambda s: (expert, 0))]
    wide, tall = shaped(shard, holds * hidden, dtype=WIDE), shaped(holds * hidden, shard, dtype=WIDE)
    flat = [term for group in terms for term in group]
    return pl.pallas_call(
        functools.partial(finish_kernel, [len(group) for group in terms]),
        grid=(1,),
        in_specs=[pl.BlockSpec((None, *column), lambda s, at=at: (at, 0, 0)) for _, at in flat]
        + ([pl.BlockSpec(memory_space=pl.ANY)] * 3 if kept else []),
        out_specs=out_specs,
        out_shape=[wide, wide, tall],
        input_output_aliases={len(flat) + i: i for i in range(3)} if kept else {},
        compiler_params=pltpu.CompilerParams(vmem_limit_bytes=VMEM_MOST),
        cost_estimate=work(flops=0, bytes_accessed=30 * shard * hidden, transcendentals=0),
    )(*[array for array, _ in flat], *(kept or ()))


def piece_columns(mine, s, shard):
    return pl.ds(pl.multiple_of(jnp.bitwise_xor(mine, s) * shard, 128), shard)


def turn(values, cos, sin):
    return values * cos + pltpu.roll(values, HEAD_DIM // 2, 1) * sin


def turn_back(values, cos, sin):
    return values * cos - pltpu.roll(values, HEAD_DIM // 2, 1) * sin


def inverse_rms(values):
    return lax.rsqrt(jnp.mean(values * values, axis=-1, keepdims=True) + EPS)


def head_slice(h):
    return slice(h * HEAD_DIM, (h + 1) * HEAD_DIM)


def stacked_heads(ref, band, group, heads):
    return jnp.concatenate([ref[band, head_slice(group * heads + h)] for h in range(heads)], axis=0)


def probabilities(queries, keys, allowed):
    scores = jnp.where(allowed, dot_bt(queries, keys) * HEAD_DIM ** (-0.5), NEG)
    expo = jnp.exp(scores - jnp.max(scores, axis=-1, keepdims=True))
    return expo * (1.0 / jnp.sum(expo, axis=-1, keepdims=True))


def allowed_pairs(seg_col_ref, seg_row_ref, band, reach, heads):
    size = band.stop - band.start
    rows = band.start + lax.broadcasted_iota(jnp.int32, (size, reach), 0)
    cols = lax.broadcasted_iota(jnp.int32, (size, reach), 1)
    ok = (seg_col_ref[band, :] == seg_row_ref[:, :reach]) & (cols <= rows)
    return jnp.concatenate([ok] * heads, axis=0)


def attention_kernel(
    mine_ref, tokens_ref, gain_ref, p0, p1, p2, p3, s0, s1, s2, s3, seg_row_ref, seg_col_ref, cos_ref, sin_ref,
    h_ref, q_ref, k_ref, v_ref, out_ref,
):
    mine = mine_ref[0]
    stream = tokens_ref[...].astype(WIDE)
    h_ref[...] = (stream * inverse_rms(stream) * gain_ref[...]).astype(LOW)
    shard = p0.shape[0]
    width = q_ref.shape[1]
    cos, sin = cos_ref[...], sin_ref[...]

    def projected(pieces, columns):
        return sum(dot(h_ref[:, piece_columns(mine, s, shard)], piece[:, columns]) for s, piece in enumerate(pieces))

    heads = QUERY_HEADS // KEY_VALUE_HEADS
    key_width = KEY_VALUE_HEADS * HEAD_DIM
    shared = (s0, s1, s2, s3)
    keys = projected(shared, slice(0, key_width))
    for g in range(KEY_VALUE_HEADS):
        k_ref[:, head_slice(g)] = turn(keys[:, head_slice(g)], cos, sin).astype(LOW)
    v_ref[...] = projected(shared, slice(key_width, 2 * key_width)).astype(LOW)
    group_width = heads * HEAD_DIM
    for g in range(KEY_VALUE_HEADS):
        queries = projected((p0, p1, p2, p3), slice(g * group_width, (g + 1) * group_width))
        for h in range(heads):
            q_ref[:, head_slice(g * heads + h)] = turn(queries[:, head_slice(h)], cos, sin).astype(LOW)
    length = q_ref.shape[0]
    tile = 128
    for start in range(0, length, tile):
        band, reach = slice(start, start + tile), start + tile
        allowed = allowed_pairs(seg_col_ref, seg_row_ref, band, reach, heads)
        for g in range(KEY_VALUE_HEADS):
            probs = probabilities(stacked_heads(q_ref, band, g, heads), k_ref[:reach, head_slice(g)], allowed)
            mixed = dot(probs.astype(LOW), v_ref[:reach, head_slice(g)]).astype(LOW)
            for h in range(heads):
                out_ref[band, head_slice(g * heads + h)] = mixed[h * tile : (h + 1) * tile]


def vmem_call(kernel, out_shape, flops, transcendentals, token, *args):
    moved = sum(a.size * a.dtype.itemsize for a in args) + sum(
        o.size * o.dtype.itemsize for o in jax.tree.leaves(out_shape)
    )
    return pl.pallas_call(
        kernel,
        in_specs=[pl.BlockSpec(memory_space=pltpu.SMEM)] + [pl.BlockSpec(memory_space=pltpu.VMEM)] * len(args),
        out_specs=[pl.BlockSpec(memory_space=pltpu.VMEM)] * len(out_shape),
        out_shape=out_shape,
        compiler_params=pltpu.CompilerParams(vmem_limit_bytes=VMEM_MOST),
        cost_estimate=work(flops=flops, bytes_accessed=moved, transcendentals=transcendentals),
    )(token, *args)


def shaped(*shape, dtype=LOW):
    return jax.ShapeDtypeStruct(shape, dtype)


def attention_call(mine, tokens, gain, pieces, shared_pieces, seg_row, seg_col, cos, sin):
    length, width = tokens.shape
    key_width = KEY_VALUE_HEADS * HEAD_DIM
    return vmem_call(
        attention_kernel,
        [shaped(length, width), shaped(length, width), shaped(length, key_width), shaped(length, key_width), shaped(length, width)],
        2 * length * width * (width + 2 * key_width) + 3 * length * length * width,
        QUERY_HEADS * length * length,
        mine, tokens, gain, *pieces, *shared_pieces, seg_row, seg_col, cos, sin,
    )


def project_kernel(
    mine_ref, tokens_ref, attn_ref, p0, p1, p2, p3, r0, r1, r2, r3, gain_ref, routes_ref, resid_ref, h_ref
):
    mine = mine_ref[0]
    shard = p0.shape[0]
    resid = tokens_ref[...].astype(WIDE)
    for s, piece in enumerate((p0, p1, p2, p3)):
        resid = resid + dot(attn_ref[:, piece_columns(mine, s, shard)], piece[...])
    resid_ref[...] = resid
    length, width = resid.shape
    h_ref[:length] = (resid * inverse_rms(resid) * gain_ref[...]).astype(LOW)
    logits = jnp.transpose(
        sum(
            dot(h_ref[:length, piece_columns(mine, s, shard)], piece[:, -128:])
            for s, piece in enumerate((r0, r1, r2, r3))
        )
    )
    experts = lax.broadcasted_iota(jnp.int32, logits.shape, 0)
    picked = [
        jnp.sum(jnp.where(experts == routes_ref[k : k + 1, :], logits, 0.0), axis=0, keepdims=True)
        for k in range(routes_ref.shape[0])
    ]
    top = functools.reduce(jnp.maximum, picked)
    expo = [jnp.exp(p - top) for p in picked]
    total = sum(expo)
    gates = jnp.concatenate([x / total for x in expo], axis=0)
    h_ref[length:] = jnp.zeros((16, width), LOW)
    h_ref[length:, :length] = pack_routing(gates, routes_ref[...])


def project_call(mine, tokens, attn, pieces, shared_pieces, gain, routes_t):
    length, width = tokens.shape
    return vmem_call(
        project_kernel,
        [shaped(length, width, dtype=WIDE), shaped(length + 16, width)],
        2 * length * width * (width + EXPERTS),
        length * 8,
        mine, tokens, attn, *pieces, *shared_pieces, gain, routes_t,
    )


def as_column(row):
    return jnp.transpose(jnp.broadcast_to(row, (8, row.shape[1])))[:, :1]


def norm_back(grad, gain, normed, inverse):
    scaled = grad * gain
    return inverse * (scaled - normed * jnp.mean(scaled * normed, axis=-1, keepdims=True))


def shard_parts(s, shard, targets):
    size = shard // len(targets[s])
    return [(target, slice(i * size, (i + 1) * size)) for i, target in enumerate(targets[s])]


def resid_back_kernel(
    mine_ref, resid_ref, gain_ref, dz_ref, t0, t1, t2, gains_ref, h_ref, attn_ref,
    p0, p1, p2, p3, r0, r1, r2, r3, grad_ref, attn_grad_ref, o0, o1, o2, o3, o4, second_scr, low_scr,
):
    mine = mine_ref[0]
    shard, width = p0.shape
    length = resid_ref.shape[0]
    routers = (r0, r1, r2, r3)
    gains = gains_ref[...]
    experts = lax.broadcasted_iota(jnp.int32, gains.shape, 0)
    gate_rows, routes = unpack_routing(h_ref[length:, :length])
    gates = jnp.zeros(gains.shape, WIDE)
    for k in range(TOP):
        gates = gates + jnp.where(experts.astype(WIDE) == routes[k : k + 1], gate_rows[k : k + 1], 0.0)
    logit_grad = gates * (gains - jnp.sum(gates * gains, axis=0, keepdims=True))
    logit_grad = jnp.concatenate([logit_grad, jnp.zeros((128 - EXPERTS, length), WIDE)], axis=0)
    logit_grad = jnp.transpose(logit_grad).astype(LOW)
    second_scr[...] = t0[...].astype(WIDE) + t1[...].astype(WIDE) + t2[...].astype(WIDE)
    for s, piece in enumerate(routers):
        columns = piece_columns(mine, s, shard)
        second_scr[:, columns] = second_scr[:, columns] + dot_bt(logit_grad, piece[:, -128:])
    resid = resid_ref[...]
    inverse = inverse_rms(resid)
    normed = resid * inverse
    second = second_scr[...]
    gain_grad = jnp.sum(second * normed, axis=0, keepdims=True)
    grad = dz_ref[...].astype(WIDE) + norm_back(second, gain_ref[...], normed, inverse)
    grad_ref[...] = grad
    low_scr[...] = grad.astype(LOW)
    second_scr[:1, :] = gain_grad
    low = low_scr[...]
    for s, piece in enumerate((p0, p1, p2, p3)):
        columns = piece_columns(mine, s, shard)
        attn_grad_ref[:, columns] = dot_bt(low, piece[...]).astype(LOW)
        out_part = dot_t(attn_ref[:, columns], low).astype(LOW)
        router_part = dot_t(h_ref[:length, columns], logit_grad)
        lanes = lax.broadcasted_iota(jnp.int32, router_part.shape, 1)
        small = jnp.where(lanes == EXPERTS, as_column(second_scr[:1, columns]), router_part).astype(LOW)
        for target, rows in shard_parts(s, shard, ((o0,), (o1,), (o2,), (o3, o4))):
            target[:, :width] = out_part[rows]
            target[:, width:] = small[rows]


def resid_back_call(mine, resid, gain, dz, terms, gains, h, attn, pieces, shared_pieces):
    length, width = resid.shape
    shard = pieces[0].shape[0]
    return pl.pallas_call(
        resid_back_kernel,
        in_specs=[pl.BlockSpec(memory_space=pltpu.SMEM)] + [pl.BlockSpec(memory_space=pltpu.VMEM)] * 17,
        out_specs=[pl.BlockSpec(memory_space=pltpu.VMEM)] * 7,
        out_shape=[shaped(length, width, dtype=WIDE), shaped(length, width)]
        + [shaped(shard, width + 128)] * 3
        + [shaped(shard // 2, width + 128)] * 2,
        scratch_shapes=[pltpu.VMEM((length, width), WIDE), pltpu.VMEM((length, width), LOW)],
        compiler_params=pltpu.CompilerParams(vmem_limit_bytes=VMEM_MOST),
        cost_estimate=work(
            flops=4 * length * width * (width + EXPERTS), bytes_accessed=length * width * 40, transcendentals=0
        ),
    )(mine, resid, gain, dz, *terms, gains, h, attn, *pieces, *shared_pieces)


def attention_back_kernel(
    mine_ref, q_ref, k_ref, v_ref, do_ref, h_ref, tokens_ref, gain_ref, grad_ref, p0, p1, p2, p3, s0, s1, s2, s3,
    seg_row_ref, seg_col_ref, cos_ref, sin_ref, input_ref, o0, o1, o2, o3, o4, o5, qkv_scr, dk_scr, dv_scr, dh_scr,
):
    mine = mine_ref[0]
    length, width = q_ref.shape
    shard = p0.shape[0]
    qkv_width = width + 2 * KEY_VALUE_HEADS * HEAD_DIM
    heads = QUERY_HEADS // KEY_VALUE_HEADS
    key_width = KEY_VALUE_HEADS * HEAD_DIM
    tile = 128
    dk_scr[...] = jnp.zeros_like(dk_scr)
    dv_scr[...] = jnp.zeros_like(dv_scr)
    for start in range(0, length, tile):
        band, reach = slice(start, start + tile), start + tile
        allowed = allowed_pairs(seg_col_ref, seg_row_ref, band, reach, heads)
        cos, sin = cos_ref[band, :], sin_ref[band, :]
        for g in range(KEY_VALUE_HEADS):
            queries = stacked_heads(q_ref, band, g, heads)
            grads = stacked_heads(do_ref, band, g, heads)
            keys = k_ref[:reach, head_slice(g)]
            probs = probabilities(queries, keys, allowed)
            prob_grad = dot_bt(grads, v_ref[:reach, head_slice(g)])
            delta = jnp.sum(probs * prob_grad, axis=-1, keepdims=True)
            score_grad = (probs * (prob_grad - delta) * HEAD_DIM ** (-0.5)).astype(LOW)
            dv_scr[:reach, head_slice(g)] += dot_t(probs.astype(LOW), grads)
            dk_scr[:reach, head_slice(g)] += dot_t(score_grad, queries)
            dq = dot(score_grad, keys)
            for h in range(heads):
                qkv_scr[band, head_slice(g * heads + h)] = turn_back(dq[h * tile : (h + 1) * tile], cos, sin).astype(LOW)
    for g in range(KEY_VALUE_HEADS):
        at = width + g * HEAD_DIM
        qkv_scr[:, at : at + HEAD_DIM] = turn_back(dk_scr[:, head_slice(g)], cos_ref[...], sin_ref[...]).astype(LOW)
    qkv_scr[:, width + key_width :] = dv_scr[...].astype(LOW)
    qkv = qkv_scr[...]
    for s, (piece, shared) in enumerate(zip((p0, p1, p2, p3), (s0, s1, s2, s3))):
        dh_scr[:, piece_columns(mine, s, shard)] = dot_bt(qkv[:, :width], piece[...]) + dot_bt(qkv[:, width:], shared[:, : 2 * key_width])
    stream = tokens_ref[...].astype(WIDE)
    inverse = inverse_rms(stream)
    normed = stream * inverse
    first = dh_scr[...]
    gain_grad = jnp.sum(first * normed, axis=0, keepdims=True)
    input_ref[...] = grad_ref[...] + norm_back(first, gain_ref[...], normed, inverse)
    dh_scr[:1, :] = gain_grad
    for s in range(4):
        columns = piece_columns(mine, s, shard)
        part = dot_t(h_ref[:, columns], qkv).astype(LOW)
        small = jnp.concatenate([as_column(dh_scr[:1, columns]), jnp.zeros((shard, 127), WIDE)], axis=1).astype(LOW)
        for target, rows in shard_parts(s, shard, ((o0,), (o1,), (o2, o3), (o4, o5))):
            target[:, :qkv_width] = part[rows]
            target[:, qkv_width:] = small[rows]


def attention_back_call(mine, q, k, v, do, h, tokens, gain, grad, pieces, shared_pieces, seg_row, seg_col, cos, sin):
    length, width = q.shape
    shard = pieces[0].shape[0]
    qkv_width = width + 2 * KEY_VALUE_HEADS * HEAD_DIM
    key_width = KEY_VALUE_HEADS * HEAD_DIM
    return pl.pallas_call(
        attention_back_kernel,
        in_specs=[pl.BlockSpec(memory_space=pltpu.SMEM)] + [pl.BlockSpec(memory_space=pltpu.VMEM)] * 20,
        out_specs=[pl.BlockSpec(memory_space=pltpu.VMEM)] * 7,
        out_shape=[shaped(length, width, dtype=WIDE)]
        + [shaped(shard, qkv_width + 128)] * 2
        + [shaped(shard // 2, qkv_width + 128)] * 4,
        scratch_shapes=[
            pltpu.VMEM((length, qkv_width), LOW),
            pltpu.VMEM((length, key_width), WIDE),
            pltpu.VMEM((length, key_width), WIDE),
            pltpu.VMEM((length, width), WIDE),
        ],
        compiler_params=pltpu.CompilerParams(vmem_limit_bytes=VMEM_MOST),
        cost_estimate=work(
            flops=4 * length * width * qkv_width + 7 * length * length * width,
            bytes_accessed=length * width * 40,
            transcendentals=QUERY_HEADS * length * length,
        ),
    )(mine, q, k, v, do, h, tokens, gain, grad, *pieces, *shared_pieces, seg_row, seg_col, cos, sin)


def spread_kernel(count, halved, token_ref, *refs):
    outs = refs[-count - halved : -halved] if halved else refs[-count:]
    terms = refs[: 3 + halved]
    if halved:
        scratch = refs[-1]
        half = terms[2].shape[0]
        scratch[:half] = terms[2][...]
        scratch[half:] = terms[3][...]
        terms = (*terms[:2], scratch)
    chunk = outs[0].shape[0]
    for j, out in enumerate(outs):
        rows = pl.ds(pl.multiple_of(lax.rem(token_ref[2] + j, count) * chunk, 16), chunk)
        out[...] = sum(term[rows, :].astype(WIDE) for term in terms).astype(LOW)


def spread_call(token, count, *terms):
    rows, width = terms[0].shape
    halved = len(terms) - 3
    whole = lambda shape: pl.BlockSpec(shape, lambda i: (0, 0))
    return pl.pallas_call(
        functools.partial(spread_kernel, count, halved),
        grid=(1,),
        in_specs=[pl.BlockSpec(memory_space=pltpu.SMEM)] + [whole(t.shape) for t in terms],
        out_specs=[whole((rows // count, width))] * count,
        out_shape=[shaped(rows // count, width)] * count,
        scratch_shapes=[pltpu.VMEM((rows, width), LOW)] * halved,
        compiler_params=pltpu.CompilerParams(vmem_limit_bytes=VMEM_MOST),
        cost_estimate=work(flops=0, bytes_accessed=8 * rows * width, transcendentals=0),
    )(token, *terms)


def assemble_kernel(count, widths, token_ref, *refs):
    chunks, outs = refs[:count], refs[count:]
    chunk = chunks[0].shape[0]
    for j, ref in enumerate(chunks):
        rows = pl.ds(pl.multiple_of(lax.rem(token_ref[2] + j, count) * chunk, 16), chunk)
        values = ref[...].astype(WIDE)
        at = 0
        for width, out in zip(widths, outs):
            out[rows, :] = values[:, at : at + width]
            at += width


def assemble_call(token, chunks, widths):
    count, (rows, width) = len(chunks), chunks[0].shape
    whole = lambda *shape: pl.BlockSpec(shape, lambda i: (0, 0))
    return pl.pallas_call(
        functools.partial(assemble_kernel, count, widths),
        grid=(1,),
        in_specs=[pl.BlockSpec(memory_space=pltpu.SMEM)] + [whole(rows, width)] * count,
        out_specs=[whole(count * rows, w) for w in widths],
        out_shape=[shaped(count * rows, w, dtype=WIDE) for w in widths],
        compiler_params=pltpu.CompilerParams(vmem_limit_bytes=VMEM_MOST),
        cost_estimate=work(flops=0, bytes_accessed=6 * count * rows * width, transcendentals=0),
    )(token, *chunks)


def per_device_ring(
    tokens,
    segments,
    routes,
    attn_gain,
    ffn_gain,
    w_query,
    key_weight,
    value_weight,
    w_out,
    w_router,
    w_gate,
    w_up,
    w_down,
    cotangent,
):
    length, model_width = tokens.shape
    top_count = routes.shape[1]
    count = lax.axis_size("expert")
    holds = EXPERTS // count
    capacity = max(2, 3 * length * top_count // (2 * EXPERTS))
    slots = -(-capacity // 16) * 16
    shard = model_width // 4
    key_width = KEY_VALUE_HEADS * HEAD_DIM
    half = length // 2
    mine = lax.axis_index("wshard").astype(jnp.int32)
    order = jnp.array(ring_order(count), jnp.int32)
    spot_of = jnp.array([ring_order(count).index(i) for i in range(count)], jnp.int32)
    here = lax.axis_index("expert").astype(jnp.int32)
    spot = spot_of[here]
    token = jnp.stack([mine, here, spot])
    routes_t = routes.T

    cosine, sine = rotary_tables(length, HEAD_DIM)
    cos = jnp.concatenate([cosine, cosine], axis=1)
    sin = jnp.concatenate([-sine, sine], axis=1)
    seg_col = segments.reshape(length, 1)
    gain_one, gain_two = attn_gain[None], ffn_gain[None]

    def pieces_of(own, across, *ready):
        return (own, swap_core(own), across, swap_core(after(across, *ready)))

    dz = {0: cotangent}
    dz[-1], dz[1] = ahead(dz[0], count), behind(dz[0], count)
    query_across = swap_x(w_query)
    query_pieces = pieces_of(w_query, query_across)
    spare = jnp.zeros((shard, 128 - EXPERTS), LOW)
    shared = jnp.concatenate([key_weight, value_weight, w_router, spare], axis=1)
    shared, token, seg_col, cos, sin, routes_t, gain_one, gain_two = lax.optimization_barrier(
        (shared, token, seg_col, cos, sin, routes_t, gain_one, gain_two)
    )
    shared_across = swap_x(after(shared, query_across, dz[-1], dz[1]))
    dz[-2], dz[2] = ahead(dz[-1], count), behind(dz[1], count)
    shared_pieces = pieces_of(shared, shared_across)
    out_across = swap_x(after(w_out, shared_across))

    first_low, query, key, value, attn = attention_call(
        after(token, dz[-2], dz[2]), tokens, gain_one, query_pieces, shared_pieces, segments, seg_col, cos, sin
    )
    out_pieces = pieces_of(w_out, out_across, attn)
    dz[-3], dz[3] = ahead(dz[-2], count), behind(dz[2], count)
    resid, second = project_call(after(token, dz[-3], dz[3]), tokens, attn, out_pieces, shared_pieces, gain_two, routes_t)

    def experts(ready, first, offsets, kept):
        return expert_call(
            after(token, *ready), first, [h[j] for j in offsets], [dz[j] for j in offsets], w_gate, w_up, w_down, kept,
            holds, slots, count,
        )

    h = {0: second}
    h[-1], h[1] = ahead(h[0], count), behind(h[0], count)
    (d_own,), kept = experts((), 6, (0,), None)
    h[-2], h[2] = ahead(after(h[-1], d_own), count), behind(after(h[1], d_own), count)
    (d_l1, d_r1), kept = experts((), 0, (-1, 1), kept)
    h[-3], h[3] = ahead(after(h[-2], d_l1), count), behind(after(h[2], d_l1), count)
    (d_l2, d_r2), kept = experts((), 2, (-2, 2), kept)
    h[4], dz[4] = ahead(after(h[-3], d_l2), count), behind(after(dz[3], d_l2), count)
    (d_l3, d_r3), kept = experts((), 4, (-3, 3), kept)
    (d_far,), (gains, rank, *kept) = experts((), 7, (4,), kept)

    block_of = jnp.array([BLOCK_OFFSETS.index(j if j <= count // 2 else j - count) for j in range(count)], jnp.int32)
    gain_send = gains[block_of[(spot_of - spot) % count]]

    def weight_grads(expert, *ready):
        return wgrad_call(expert, after(token, *ready), kept)

    def over_cores(grads, *ready):
        return swap_core(after(grads[3], *ready))

    both, last = range(2), 2

    def sum_of(grads, got, part):
        return [(grads[2], part), (got, part)]

    up_sent, down_sent = ahead(d_far, count), behind(d_l3, count)
    grads = [wgrad_call(0, token, kept, True)]
    got = [[swap_core(v) for v in grads[0][3][:2]]]
    grads.append(weight_grads(1, grads[0][0]))
    up, down, half_a = sums_call(
        after(token, grads[1][0]), [[d_r3, up_sent]], [[d_l2, down_sent]],
        [[(grads[0][2], i), got[0][i]] for i in both],
    )

    up_sent, down_sent, across_a = ahead(up, count), behind(down, count), swap_x(half_a)
    got[0].append(swap_core(after(grads[0][3][2], up)))
    got.append(over_cores(grads[1], up))
    gain_dense = lax.all_to_all(after(gain_send, up), "expert", split_axis=0, concat_axis=0, tiled=True)
    gain_dense = gain_dense.reshape(EXPERTS, length)
    grads.append(weight_grads(2, up))
    up, down, half_b, half_c = sums_call(
        after(token, grads[2][0], gain_dense, across_a), [[d_r2, up_sent]], [[d_l1, down_sent]],
        [sum_of(grads[1], got[1], both)], [[(grads[0][2], last), got[0][last]], sum_of(grads[1], got[1], last)],
    )

    up_sent, down_sent, across_b = ahead(up, count), behind(down, count), swap_x(half_b)
    got.append(over_cores(grads[2], up))
    y = dict(zip(BLOCK_OFFSETS, value_call(after(token, up), rank, kept[4], w_down, slots)))
    up, half_d = sums_call(after(token, y[0], across_b, down_sent), [[d_r1, up_sent]], [sum_of(grads[2], got[2], both)])

    up_sent, y_down, across_c = ahead(up, count), behind(after(y[4], up), count), swap_x(after(half_c, up))
    (down,) = sums_call(after(token, up_sent, across_c), [[y[-3], y_down]])
    y_up, y_down, across_d = ahead(after(y[3], down), count), behind(down, count), swap_x(after(half_d, down))
    grad, attn_grad, *out_parts = resid_back_call(
        after(token, down), resid, gain_two, cotangent, (d_own, up_sent, down_sent), gain_dense, second,
        attn, out_pieces, shared_pieces,
    )
    out_first = swap_core(out_parts[3]), swap_core(out_parts[4])
    grads.append(weight_grads(3, grad))
    out_half, up, down = sums_call(
        after(token, grads[3][0], across_d), [[out_parts[2], jnp.concatenate(out_first, axis=0)]], [[y[2], y_up]],
        [[y[-2], y_down]],
    )

    y_up, y_down, out_across = ahead(up, count), behind(down, count), swap_x(out_half)
    got.append(over_cores(grads[3], up))
    out_got = swap_core(after(out_parts[1], up))
    input_grad, *qkv_parts = attention_back_call(
        after(token, up), query, key, value, attn_grad, first_low, tokens, gain_one, grad, query_pieces,
        shared_pieces, segments, seg_col, cos, sin,
    )
    up, down, half_e = sums_call(
        after(token, input_grad, out_across, out_got), [[y[1], y_up]], [[y[-1], y_down]],
        [sum_of(grads[2], got[2], last), sum_of(grads[3], got[3], range(3))],
    )

    y_up, y_down = ahead(up, count), behind(down, count)
    qkv_first = [swap_core(after(v, up)) for v in qkv_parts[4:]]
    qkv_got = swap_core(after(qkv_parts[1], up))
    out_parts = spread_call(after(token, up), count, out_parts[0], out_got, out_across)
    qkv_half = sums_call(after(token, out_parts[0]), *[[[a, b]] for a, b in zip(qkv_parts[2:4], qkv_first)])
    qkv_across = [swap_x(qkv_half[0])]
    qkv_across.append(swap_x(after(qkv_half[1], qkv_across[0])))

    def sum_step(parts, up, down, step):
        up = add_low(parts[step], ahead(up, count))
        down = behind(down, count)
        return up, add_low(parts[count + 1 - step], down) if step > 1 else down

    def copy_step(up, down):
        return up + [ahead(up[-1], count)], down + [behind(down[-1], count)]

    out_up, out_down = after(out_parts[4], qkv_half[0]), after(out_parts[5], qkv_half[0])
    for step in (3, 2, 1):
        if step == 1:
            out_up, out_down = after(out_up, qkv_across[0]), after(out_down, qkv_across[0])
        out_up, out_down = sum_step(out_parts, out_up, out_down, step)
    out_own = add_low(out_parts[0], ahead(out_up, count), out_down)
    late = [swap_core(after(g[1], qkv_across[0])) for g in grads[:2]]
    mixed = (resid + sum(t.astype(WIDE) for t in (after(y[0], out_own), y_up, y_down))).astype(LOW)
    across = [[(across_a, 0), (across_a, 1), (across_c, 0)], [(across_b, 0), (across_b, 1), (across_c, 1)]]

    def finish(ready, expert, kept_out):
        own = after(grads[expert][0], ready)
        terms = [[(own, i), (late[expert], i), across[expert][i]] for i in range(3)]
        return finish_call(expert, holds, terms, kept_out)

    finished = finish(out_own, 1, finish(out_own, 0, None))
    qkv_parts = spread_call(after(token, mixed, finished[0]), count, qkv_parts[0], qkv_got, *qkv_across)
    across_e = swap_x(after(half_e, qkv_parts[0]))
    late += [swap_core(after(g[1], qkv_parts[0])) for g in grads[2:]]
    across += [[(across_d, 0), (across_d, 1), (across_e, 0)], [(across_e, 1), (across_e, 2), (across_e, 3)]]
    out_ups, out_downs = [after(out_own, qkv_parts[0])], [after(out_own, qkv_parts[0])]
    qkv_up, qkv_down = qkv_parts[4], qkv_parts[5]
    for step in (3, 2, 1):
        out_ups, out_downs = copy_step(out_ups, out_downs)
        qkv_up, qkv_down = sum_step(qkv_parts, qkv_up, qkv_down, step)
    out_ups.append(ahead(out_ups[-1], count))
    qkv_own = add_low(qkv_parts[0], ahead(qkv_up, count), qkv_down)
    qkv_ups, qkv_downs = [qkv_own], [qkv_own]
    for step in (3, 2, 1):
        qkv_ups, qkv_downs = copy_step(qkv_ups, qkv_downs)
    out_sum, out_small = assemble_call(after(token, qkv_own), out_downs + out_ups[:0:-1], (model_width, 128))
    qkv_ups.append(ahead(after(qkv_ups[-1], out_sum), count))
    finished = finish(qkv_ups[3], 2, finished)
    query_sum, key_sum, value_sum, qkv_small = assemble_call(
        after(token, finished[0]), qkv_downs + qkv_ups[:0:-1], (model_width, key_width, key_width, 128)
    )
    gate_shard, up_shard, down_shard = finish(query_sum, 3, finished)
    return (
        mixed,
        input_grad,
        qkv_small[:, 0],
        out_small[:, EXPERTS],
        query_sum,
        key_sum,
        value_sum,
        out_sum,
        out_small[:, :EXPERTS],
        gate_shard,
        up_shard,
        down_shard,
    )


def solution(mesh):
    ring = mesh.shape["expert"] == len(BLOCK_OFFSETS) and mesh.shape["wshard"] == 4
    body = per_device_ring if ring else per_device_exchange
    in_specs = (
        P(("expert", "wshard"), None),
        P(("expert", "wshard"), None),
        P(("expert", "wshard"), None),
        P(),
        P(),
        P("wshard", None),
        P("wshard", None),
        P("wshard", None),
        P("wshard", None),
        P("wshard", None),
        P(None, "expert"),
        P(None, "expert"),
        P("expert", None),
        P(("expert", "wshard"), None),
    )
    out_specs = (
        P(("expert", "wshard"), None),
        P(("expert", "wshard"), None),
        P("wshard"),
        P("wshard"),
        P("wshard", None),
        P("wshard", None),
        P("wshard", None),
        P("wshard", None),
        P("wshard", None),
        P("wshard", "expert"),
        P("wshard", "expert"),
        P("expert", "wshard"),
    )
    return jax.shard_map(
        body, mesh=mesh, in_specs=in_specs, out_specs=out_specs, check_vma=False
    )
```

```python
import functools

import jax
import jax.numpy as jnp
from jax import lax
from jax.experimental import pallas as pl
from jax.experimental.pallas import tpu as pltpu
from jax.sharding import PartitionSpec as P

QUERY_HEADS = 12
KEY_VALUE_HEADS = 2
HEAD_DIM = 128
EXPERTS = 32
TOP = 4


EPS = 1e-06
ROPE_BASE = 10000.0
NEG = -1e30
LOW = jnp.bfloat16
WIDE = jnp.float32
VMEM_MOST = 60 * 1024 * 1024
def norm_forward(values, gain):
    inverse = lax.rsqrt(jnp.mean(values * values, axis=-1) + EPS)
    normed = values * inverse[:, None]
    return (normed * gain, normed, inverse)


def norm_backward(grad, gain, normed, inverse):
    gain_grad = jnp.sum(grad * normed, axis=0)
    scaled = grad * gain
    centred = scaled - normed * jnp.mean(scaled * normed, axis=-1, keepdims=True)
    return (inverse[:, None] * centred, gain_grad)


def rotary_tables(seq_length, head_size):
    half_size = head_size // 2
    frequency = ROPE_BASE ** (-(jnp.arange(half_size, dtype=jnp.float32) * 2.0 / head_size))
    angles = jnp.arange(seq_length, dtype=jnp.float32)[:, None] * frequency[None, :]
    return (jnp.cos(angles), jnp.sin(angles))


def apply_rotation(values, cosine_lookup, sine_lookup):
    half_size = values.shape[-1] // 2
    first_half = values[..., :half_size]
    second_half = values[..., half_size:]
    cos_part = cosine_lookup[:, None, :]
    sin_part = sine_lookup[:, None, :]
    return jnp.concatenate(
        [
            first_half * cos_part - second_half * sin_part,
            second_half * cos_part + first_half * sin_part,
        ],
        axis=-1,
    )


def reverse_rotation(values, cosine_lookup, sine_lookup):
    half_size = values.shape[-1] // 2
    first_half = values[..., :half_size]
    second_half = values[..., half_size:]
    cos_part = cosine_lookup[:, None, :]
    sin_part = sine_lookup[:, None, :]
    return jnp.concatenate(
        [
            first_half * cos_part + second_half * sin_part,
            second_half * cos_part - first_half * sin_part,
        ],
        axis=-1,
    )


def per_device_exchange(
    tokens,
    segments,
    routes,
    attn_gain,
    ffn_gain,
    w_query,
    key_weight,
    value_weight,
    w_out,
    w_router,
    w_gate,
    w_up,
    w_down,
    cotangent,
):
    lower_dtype = jnp.bfloat16
    wide_type = jnp.float32
    sequence_length, model_width = tokens.shape
    top_count = routes.shape[1]
    axis_count = lax.axis_size("expert")
    owners = max(1, axis_count // EXPERTS)
    holds = max(1, EXPERTS // axis_count)
    groups = EXPERTS // holds
    capacity = max(2, 3 * sequence_length * top_count // (2 * EXPERTS))
    hidden_dev = w_gate.shape[1] // holds
    query_group_width = QUERY_HEADS // KEY_VALUE_HEADS
    score_scale = HEAD_DIM ** (-0.5)
    pair_count = sequence_length * top_count
    query_full, key_full, value_full, out_full, router_full = (
        lax.all_gather(w_query, "wshard", axis=0, tiled=True),
        lax.all_gather(key_weight, "wshard", axis=0, tiled=True),
        lax.all_gather(value_weight, "wshard", axis=0, tiled=True),
        lax.all_gather(w_out, "wshard", axis=0, tiled=True),
        lax.all_gather(w_router, "wshard", axis=0, tiled=True),
    )
    stream = tokens.astype(wide_type)
    first_norm, first_normed, first_inverse = norm_forward(stream, attn_gain)
    first_low = first_norm.astype(lower_dtype)
    cosine_lookup, sine_lookup = rotary_tables(sequence_length, HEAD_DIM)
    query_pre = jnp.dot(first_low, query_full, preferred_element_type=wide_type).reshape(
        sequence_length, QUERY_HEADS, HEAD_DIM
    )
    key_unrotated = jnp.dot(first_low, key_full, preferred_element_type=wide_type).reshape(
        sequence_length, KEY_VALUE_HEADS, HEAD_DIM
    )
    query_rotated = (
        apply_rotation(query_pre, cosine_lookup, sine_lookup)
        .astype(lower_dtype)
        .reshape(sequence_length, KEY_VALUE_HEADS, query_group_width, HEAD_DIM)
    )
    key_rotated = apply_rotation(key_unrotated, cosine_lookup, sine_lookup).astype(lower_dtype)
    value_lowered = (
        jnp.dot(first_low, value_full, preferred_element_type=wide_type)
        .astype(lower_dtype)
        .reshape(sequence_length, KEY_VALUE_HEADS, HEAD_DIM)
    )
    positions = jnp.arange(sequence_length)
    offset = positions[:, None] - positions[None, :]
    segment_row = segments[0]
    allowed = (segment_row[:, None] == segment_row[None, :]) & (offset >= 0)
    raw_scores = jnp.einsum(
        "qagd,kad->agqk", query_rotated, key_rotated, preferred_element_type=wide_type
    )
    scores = jnp.where(allowed, raw_scores * score_scale, NEG)
    score_top = jnp.max(scores, axis=-1, keepdims=True)
    expo_terms = jnp.exp(scores - score_top)
    expo_total = jnp.sum(expo_terms, axis=-1, keepdims=True)
    log_total = score_top + jnp.log(expo_total)
    probs_low = (expo_terms / expo_total).astype(lower_dtype)
    attn_low = (
        jnp.einsum("agqk,kad->qagd", probs_low, value_lowered, preferred_element_type=wide_type)
        .astype(lower_dtype)
        .reshape(sequence_length, QUERY_HEADS * HEAD_DIM)
    )
    resid = stream + jnp.dot(attn_low, out_full, preferred_element_type=wide_type)
    second_norm, second_normed, second_inverse = norm_forward(resid, ffn_gain)
    second_low = second_norm.astype(lower_dtype)
    logits = jnp.dot(second_low, router_full, preferred_element_type=wide_type)
    choose = (routes[:, :, None] == jnp.arange(EXPERTS)[None, None, :]).astype(wide_type)
    selected = jnp.sum(choose * logits[:, None, :], axis=-1)
    gate_probs = jax.nn.softmax(selected, axis=-1)
    flat_routes = routes.reshape(pair_count)
    one_hot = (flat_routes[:, None] == jnp.arange(EXPERTS)[None, :]).astype(jnp.int32)
    slot_rank = jnp.sum((jnp.cumsum(one_hot, axis=0) - 1) * one_hot, axis=1)
    slot_index = (flat_routes // holds * capacity + slot_rank) * holds + flat_routes % holds
    slot_pair = (
        jnp.full((EXPERTS * capacity,), pair_count, jnp.int32)
        .at[slot_index]
        .set(jnp.arange(pair_count, dtype=jnp.int32))
    )
    second_ext = jnp.concatenate([second_low, jnp.zeros((1, model_width), lower_dtype)], axis=0)
    send_rows = jnp.repeat(
        second_ext[slot_pair // top_count].reshape(groups, capacity, holds, model_width),
        owners,
        axis=0,
    )
    gate_local = w_gate.reshape(model_width, holds, hidden_dev)
    up_local = w_up.reshape(model_width, holds, hidden_dev)
    down_local = w_down.reshape(holds, hidden_dev, model_width)

    def owner_total(values):
        summed = jnp.sum(
            values.astype(wide_type).reshape(groups, owners, capacity, holds, model_width), axis=1
        )
        return summed.reshape(EXPERTS * capacity, model_width)

    received = lax.all_to_all(send_rows, "expert", split_axis=0, concat_axis=0, tiled=True)
    gate_pre = jnp.einsum("scld,dlf->sclf", received, gate_local, preferred_element_type=wide_type)
    up_pre = jnp.einsum("scld,dlf->sclf", received, up_local, preferred_element_type=wide_type)
    hidden = (jax.nn.silu(gate_pre) * up_pre).astype(lower_dtype)
    partial_value = jnp.einsum(
        "sclf,lfd->scld", hidden, down_local, preferred_element_type=wide_type
    ).astype(lower_dtype)
    returned = lax.all_to_all(partial_value, "expert", split_axis=0, concat_axis=0, tiled=True)
    expert_wide = owner_total(returned)[slot_index].reshape(sequence_length, top_count, model_width)
    mixed = (resid + jnp.sum(gate_probs[:, :, None] * expert_wide, axis=1)).astype(lower_dtype)
    upstream = cotangent.astype(wide_type)
    query_back, key_back, value_back, out_back, router_back = (
        lax.all_gather(w_query, "wshard", axis=0, tiled=True),
        lax.all_gather(key_weight, "wshard", axis=0, tiled=True),
        lax.all_gather(value_weight, "wshard", axis=0, tiled=True),
        lax.all_gather(w_out, "wshard", axis=0, tiled=True),
        lax.all_gather(w_router, "wshard", axis=0, tiled=True),
    )
    gate_grad = jnp.sum(expert_wide * upstream[:, None, :], axis=-1)
    sel_grad = gate_probs * (gate_grad - jnp.sum(gate_probs * gate_grad, axis=-1, keepdims=True))
    logit_grad = jnp.sum(choose * sel_grad[:, :, None], axis=1).astype(lower_dtype)
    pair_grad = (
        (gate_probs[:, :, None] * upstream[:, None, :])
        .astype(lower_dtype)
        .reshape(pair_count, model_width)
    )
    pair_ext = jnp.concatenate([pair_grad, jnp.zeros((1, model_width), lower_dtype)], axis=0)
    grad_send = jnp.repeat(
        pair_ext[slot_pair].reshape(groups, capacity, holds, model_width), owners, axis=0
    )
    grad_recv, rows_recv = (
        lax.all_to_all(grad_send, "expert", split_axis=0, concat_axis=0, tiled=True),
        lax.all_to_all(send_rows, "expert", split_axis=0, concat_axis=0, tiled=True),
    )
    gate_pre = jnp.einsum("scld,dlf->sclf", rows_recv, gate_local, preferred_element_type=wide_type)
    up_pre = jnp.einsum("scld,dlf->sclf", rows_recv, up_local, preferred_element_type=wide_type)
    sigmoid_gate = jax.nn.sigmoid(gate_pre)
    silu_gate = gate_pre * sigmoid_gate
    hidden = (silu_gate * up_pre).astype(lower_dtype)
    hidden_grad = jnp.einsum(
        "scld,lfd->sclf", grad_recv, down_local, preferred_element_type=wide_type
    )
    gate_pre_grad = (
        hidden_grad * up_pre * sigmoid_gate * (1.0 + gate_pre * (1.0 - sigmoid_gate))
    ).astype(lower_dtype)
    up_pre_grad = (hidden_grad * silu_gate).astype(lower_dtype)
    row_grad = (
        jnp.einsum("sclf,dlf->scld", gate_pre_grad, gate_local, preferred_element_type=wide_type)
        + jnp.einsum("sclf,dlf->scld", up_pre_grad, up_local, preferred_element_type=wide_type)
    ).astype(lower_dtype)
    returned_grad = lax.all_to_all(row_grad, "expert", split_axis=0, concat_axis=0, tiled=True)
    gate_wgrad = jnp.einsum(
        "scld,sclf->dlf", rows_recv, gate_pre_grad, preferred_element_type=wide_type
    ).reshape(model_width, holds * hidden_dev)
    up_wgrad = jnp.einsum(
        "scld,sclf->dlf", rows_recv, up_pre_grad, preferred_element_type=wide_type
    ).reshape(model_width, holds * hidden_dev)
    down_wgrad = jnp.einsum(
        "sclf,scld->lfd", hidden, grad_recv, preferred_element_type=wide_type
    ).reshape(holds * hidden_dev, model_width)
    gate_shard, up_shard, down_shard = (
        lax.psum_scatter(
            gate_wgrad.astype(jnp.bfloat16), "wshard", scatter_dimension=0, tiled=True
        ).astype(jnp.float32),
        lax.psum_scatter(
            up_wgrad.astype(jnp.bfloat16), "wshard", scatter_dimension=0, tiled=True
        ).astype(jnp.float32),
        lax.psum_scatter(
            down_wgrad.astype(jnp.bfloat16), "wshard", scatter_dimension=1, tiled=True
        ).astype(jnp.float32),
    )
    token_grad = owner_total(returned_grad)[slot_index].reshape(
        sequence_length, top_count, model_width
    )
    second_grad = jnp.sum(token_grad, axis=1) + jnp.dot(
        logit_grad, router_back.T, preferred_element_type=wide_type
    )
    router_wgrad = jnp.einsum("td,te->de", second_low, logit_grad, preferred_element_type=wide_type)
    resid_part, ffn_gain_grad = norm_backward(second_grad, ffn_gain, second_normed, second_inverse)
    resid_grad = upstream + resid_part
    resid_low = resid_grad.astype(lower_dtype)
    out_wgrad = jnp.einsum("tc,td->cd", attn_low, resid_low, preferred_element_type=wide_type)
    attn_grad = (
        jnp.dot(resid_low, out_back.T, preferred_element_type=wide_type)
        .astype(lower_dtype)
        .reshape(sequence_length, KEY_VALUE_HEADS, query_group_width, HEAD_DIM)
    )
    raw_again = jnp.einsum(
        "qagd,kad->agqk", query_rotated, key_rotated, preferred_element_type=wide_type
    )
    scores_again = jnp.where(allowed, raw_again * score_scale, NEG)
    probs_again = jnp.exp(scores_again - log_total)
    prob_grad = jnp.einsum(
        "qagd,kad->agqk", attn_grad, value_lowered, preferred_element_type=wide_type
    )
    row_delta = jnp.sum(probs_again * prob_grad, axis=-1, keepdims=True)
    score_grad = (probs_again * (prob_grad - row_delta) * score_scale).astype(lower_dtype)
    value_grad = (
        jnp.einsum("agqk,qagd->kad", probs_low, attn_grad, preferred_element_type=wide_type)
        .astype(lower_dtype)
        .reshape(sequence_length, KEY_VALUE_HEADS * HEAD_DIM)
    )
    query_rot_grad = jnp.einsum(
        "agqk,kad->qagd", score_grad, key_rotated, preferred_element_type=wide_type
    ).reshape(sequence_length, QUERY_HEADS, HEAD_DIM)
    key_rotated_gradient = jnp.einsum(
        "agqk,qagd->kad", score_grad, query_rotated, preferred_element_type=wide_type
    )
    query_grad = (
        reverse_rotation(query_rot_grad, cosine_lookup, sine_lookup)
        .astype(lower_dtype)
        .reshape(sequence_length, QUERY_HEADS * HEAD_DIM)
    )
    key_grad = (
        reverse_rotation(key_rotated_gradient, cosine_lookup, sine_lookup)
        .astype(lower_dtype)
        .reshape(sequence_length, KEY_VALUE_HEADS * HEAD_DIM)
    )
    query_wgrad = jnp.einsum("td,tc->dc", first_low, query_grad, preferred_element_type=wide_type)
    key_wgrad = jnp.einsum("td,tc->dc", first_low, key_grad, preferred_element_type=wide_type)
    value_wgrad = jnp.einsum("td,tc->dc", first_low, value_grad, preferred_element_type=wide_type)
    first_grad = (
        jnp.dot(query_grad, query_back.T, preferred_element_type=wide_type)
        + jnp.dot(key_grad, key_back.T, preferred_element_type=wide_type)
        + jnp.dot(value_grad, value_back.T, preferred_element_type=wide_type)
    )
    stream_part, attn_gain_grad = norm_backward(first_grad, attn_gain, first_normed, first_inverse)
    input_grad = resid_grad + stream_part
    query_part, key_part, value_part, out_part, router_part, attn_gain_part, ffn_gain_part = (
        lax.psum_scatter(
            query_wgrad.astype(jnp.bfloat16), "wshard", scatter_dimension=0, tiled=True
        ).astype(jnp.float32),
        lax.psum_scatter(
            key_wgrad.astype(jnp.bfloat16), "wshard", scatter_dimension=0, tiled=True
        ).astype(jnp.float32),
        lax.psum_scatter(
            value_wgrad.astype(jnp.bfloat16), "wshard", scatter_dimension=0, tiled=True
        ).astype(jnp.float32),
        lax.psum_scatter(
            out_wgrad.astype(jnp.bfloat16), "wshard", scatter_dimension=0, tiled=True
        ).astype(jnp.float32),
        lax.psum_scatter(
            router_wgrad.astype(jnp.bfloat16), "wshard", scatter_dimension=0, tiled=True
        ).astype(jnp.float32),
        lax.psum_scatter(
            attn_gain_grad.astype(jnp.bfloat16), "wshard", scatter_dimension=0, tiled=True
        ).astype(jnp.float32),
        lax.psum_scatter(
            ffn_gain_grad.astype(jnp.bfloat16), "wshard", scatter_dimension=0, tiled=True
        ).astype(jnp.float32),
    )
    query_sum, key_sum, value_sum, out_sum, router_sum, attn_gain_sum, ffn_gain_sum = lax.psum(
        (query_part, key_part, value_part, out_part, router_part, attn_gain_part, ffn_gain_part),
        "expert",
    )
    return (
        mixed,
        input_grad,
        attn_gain_sum,
        ffn_gain_sum,
        query_sum,
        key_sum,
        value_sum,
        out_sum,
        router_sum,
        gate_shard,
        up_shard,
        down_shard,
    )


BLOCK_OFFSETS = (-1, 1, -2, 2, -3, 3, 0, 4)


def ring_order(count):
    return [0] + list(range(1, count, 2)) + list(range(count - 2, 0, -2))


def shifted(value, step, count):
    order = ring_order(count)
    return lax.ppermute(value, "expert", [(order[i], order[(i + step) % count]) for i in range(count)])


def ahead(value, count):
    return shifted(value, 1, count)


def behind(value, count):
    return shifted(value, -1, count)


def swap_core(value):
    size = lax.axis_size("wshard")
    return lax.ppermute(value, "wshard", [(i, i ^ 1) for i in range(size)])


def swap_x(value):
    size = lax.axis_size("wshard")
    return lax.ppermute(value, "wshard", [(i, i ^ 2) for i in range(size)])


def work(flops, bytes_accessed, transcendentals):
    scale = 8
    return pl.CostEstimate(
        flops=flops // scale, bytes_accessed=bytes_accessed // scale, transcendentals=transcendentals // scale
    )


def add_low(*terms):
    return sum(term.astype(WIDE) for term in terms).astype(LOW)


def after(value, *others):
    return lax.optimization_barrier((value, *others))[0]


def places(rank_row, slots):
    rows = lax.broadcasted_iota(jnp.int32, (slots, rank_row.shape[-1]), 0)
    return rank_row == rows


def expert_ranks(routes, holds):
    tokens = routes.shape[1]
    names = [jnp.sum((routes == l).astype(WIDE), axis=0, keepdims=True) for l in range(holds)]
    names = jnp.concatenate(names + [jnp.zeros((16 - holds, tokens), WIDE)], axis=0)
    rows = lax.broadcasted_iota(jnp.int32, (tokens, tokens), 0)
    columns = lax.broadcasted_iota(jnp.int32, (tokens, tokens), 1)
    before = dot(names.astype(LOW), (rows <= columns).astype(WIDE).astype(LOW))
    return jnp.where(names > 0.0, before - 1.0, -1.0)[:holds].astype(jnp.int32)


def pack_routing(gates, routes):
    high = gates.astype(LOW).astype(WIDE)
    rows = [high, gates - high, routes.astype(WIDE)]
    spare = 16 - 3 * gates.shape[0]
    return jnp.concatenate(rows + [jnp.zeros((spare, gates.shape[1]), WIDE)], axis=0).astype(LOW)


def unpack_routing(packed):
    top_count = TOP
    packed = packed.astype(WIDE)
    return packed[:top_count] + packed[top_count : 2 * top_count], packed[2 * top_count : 3 * top_count]


def dot_t(a, b):
    return lax.dot_general(a, b, (((0,), (0,)), ((), ())), preferred_element_type=WIDE)


def dot_bt(a, b):
    return lax.dot_general(a, b, (((1,), (1,)), ((), ())), preferred_element_type=WIDE)


def dot(a, b):
    return jnp.dot(a, b, preferred_element_type=WIDE)


def expert_kernel(count, slots, aliased, *refs):
    token_ref = refs[0]
    h_refs, dz_refs = refs[1 : 1 + count], refs[1 + count : 1 + 2 * count]
    wg_ref, wu_ref, wd_ref = refs[1 + 2 * count : 4 + 2 * count]
    rest = refs[4 + 2 * count + (7 if aliased else 0) :]
    d_refs = rest[:count]
    gain_ref, rank_ref, rows_out, dz_out, gg_out, ug_out, hid_out = rest[count : count + 7]
    place_scr, back_scr, gate_scr, wg_scr, wu_scr, wd_scr, sems = rest[count + 7 :]
    e = pl.program_id(0)
    holds, tokens = rank_ref.shape[1:]
    hidden_width = wd_scr.shape[1]

    def weights(expert, slot):
        band = pl.ds(pl.multiple_of(expert * hidden_width, hidden_width), hidden_width)
        return [
            pltpu.make_async_copy(source, target.at[slot], sems.at[slot, i])
            for i, (source, target) in enumerate(
                ((wg_ref.at[:, band], wg_scr), (wu_ref.at[:, band], wu_scr), (wd_ref.at[band, :], wd_scr))
            )
        ]

    slot = lax.rem(e, 2)

    @pl.when(e == 0)
    def _():
        for copy in weights(0, 0):
            copy.start()

    @pl.when(e + 1 < holds)
    def _():
        for copy in weights(e + 1, 1 - slot):
            copy.start()

    here = pl.ds(pl.multiple_of(e * slots, slots), slots)
    @pl.when(e == 0)
    def _():
        for b, (h_ref, dz_ref) in enumerate(zip(h_refs, dz_refs)):
            gates, routes = unpack_routing(h_ref[tokens : tokens + 16, :tokens])
            routes = routes - (token_ref[1] * holds).astype(WIDE)
            ranks = expert_ranks(routes, holds)
            rank_ref[b] = ranks
            for l in range(holds):
                band = slice(l * slots, (l + 1) * slots)
                spot = places(ranks[l : l + 1], slots).astype(WIDE)
                named = jnp.where(routes == l, gates, 0.0)
                gate_scr[b, band, :] = jnp.broadcast_to(
                    jnp.sum(spot * jnp.sum(named, axis=0, keepdims=True), axis=1, keepdims=True), (slots, 128)
                )
                place_scr[b, band, :] = spot.astype(LOW)
            for source, target in ((h_ref, rows_out), (dz_ref, dz_out)):
                taken = dot(place_scr[b], source[:tokens]).astype(LOW)
                for l in range(holds):
                    target[l, b * slots : (b + 1) * slots, :] = taken[l * slots : (l + 1) * slots]

    gate = jnp.concatenate([gate_scr[b, here, :] for b in range(count)], axis=0)[:, :1]
    rows = rows_out[e]
    for copy in weights(e, slot):
        copy.wait()
    gate_pre = dot(rows, wg_scr[slot])
    up_pre = dot(rows, wu_scr[slot])
    sig = jax.nn.sigmoid(gate_pre)
    silu = gate_pre * sig
    hidden = (silu * up_pre).astype(LOW).astype(WIDE)
    back = dot_bt(dz_out[e], wd_scr[slot])
    gains = jnp.sum(back * hidden, axis=1, keepdims=True)
    back = back * gate
    gate_grad = (back * (up_pre * sig * (1.0 + gate_pre * (1.0 - sig)))).astype(LOW)
    up_grad = (back * silu).astype(LOW)
    gg_out[0] = gate_grad
    ug_out[0] = up_grad
    hid_out[0] = (hidden * gate).astype(LOW)
    row_grad = (dot_bt(gate_grad, wg_scr[slot]) + dot_bt(up_grad, wu_scr[slot])).astype(LOW)
    for b in range(count):
        band = slice(b * slots, (b + 1) * slots)
        back_scr[b, here, :] = row_grad[band]
        spot = place_scr[b, here, :].astype(WIDE)
        gain_ref[b, pl.ds(e, 1), :] = jnp.sum(spot * gains[band], axis=0, keepdims=True)

    @pl.when(e == pl.num_programs(0) - 1)
    def _():
        for b in range(count):
            d_refs[b][...] = dot_t(place_scr[b], back_scr[b]).astype(LOW)


def expert_call(token, first, blocks, dz_blocks, w_gate, w_up, w_down, kept, holds, slots, total):
    count = len(blocks)
    tokens, width = dz_blocks[0].shape
    hidden = w_gate.shape[1] // holds
    whole = lambda *shape: pl.BlockSpec(shape, lambda e: (0,) * len(shape))
    once = lambda *shape: pl.BlockSpec(shape, lambda e: (0,) * len(shape), pipeline_mode=pl.Buffered(buffer_count=1))
    aliased = kept is not None
    in_specs = (
        [pl.BlockSpec(memory_space=pltpu.SMEM)]
        + [once(*b.shape) for b in (*blocks, *dz_blocks)]
        + [pl.BlockSpec(memory_space=pl.ANY)] * 3
    )
    aliases = {len(in_specs) + i: count + i for i in range(7)} if aliased else {}
    out = pl.pallas_call(
        functools.partial(expert_kernel, count, slots, aliased),
        grid=(holds,),
        in_specs=in_specs + ([pl.BlockSpec(memory_space=pl.ANY)] * 7 if aliased else []),
        out_specs=[whole(tokens, width)] * count
        + [pl.BlockSpec((count, holds, tokens), lambda e: (first // count, 0, 0))] * 2
        + [pl.BlockSpec((holds, count * slots, width), lambda e: (0, first // count, 0))] * 2
        + [pl.BlockSpec((1, count * slots, hidden), lambda e: (e, first // count, 0))] * 3,
        out_shape=[shaped(tokens, width)] * count
        + [shaped(total, holds, tokens, dtype=WIDE), shaped(total, holds, tokens, dtype=jnp.int32)]
        + [shaped(holds, total * slots, width)] * 2
        + [shaped(holds, total * slots, hidden)] * 3,
        scratch_shapes=[
            pltpu.VMEM((count, holds * slots, tokens), LOW),
            pltpu.VMEM((count, holds * slots, width), LOW),
            pltpu.VMEM((count, holds * slots, 128), WIDE),
            pltpu.VMEM((2, width, hidden), LOW),
            pltpu.VMEM((2, width, hidden), LOW),
            pltpu.VMEM((2, hidden, width), LOW),
            pltpu.SemaphoreType.DMA((2, 3)),
        ],
        input_output_aliases=aliases,
        compiler_params=pltpu.CompilerParams(vmem_limit_bytes=VMEM_MOST),
        cost_estimate=work(
            flops=2 * holds * count * slots * width * (5 * hidden + 3 * tokens),
            bytes_accessed=3 * holds * width * hidden * 2
            + count * tokens * width * 6
            + holds * count * slots * (2 * width + 3 * hidden) * 2,
            transcendentals=holds * count * slots * hidden,
        ),
    )(token, *blocks, *dz_blocks, w_gate, w_up, w_down, *(kept if aliased else ()))
    return out[:count], tuple(out[count:])


def value_kernel(slots, _, rank_ref, hid_ref, wd_ref, *refs):
    total, holds, tokens = rank_ref.shape
    y_refs, (value_scr, place_scr) = refs[:total], refs[total:]
    e = pl.program_id(0)
    here = pl.ds(pl.multiple_of(e * slots, slots), slots)
    value = dot(hid_ref[0], wd_ref[...]).astype(LOW)
    for b in range(total):
        value_scr[b, here, :] = value[b * slots : (b + 1) * slots]

    @pl.when(e == pl.num_programs(0) - 1)
    def _():
        for b in range(total):
            for l in range(holds):
                spot = places(rank_ref[b, l : l + 1, :], slots)
                place_scr[l * slots : (l + 1) * slots, :] = spot.astype(WIDE).astype(LOW)
            y_refs[b][...] = dot_t(place_scr[...], value_scr[b]).astype(LOW)


def value_call(token, rank, hidden_rows, w_down, slots):
    total, holds, tokens = rank.shape
    width = w_down.shape[1]
    hidden = hidden_rows.shape[2]
    whole = lambda *shape: pl.BlockSpec(shape, lambda e: (0,) * len(shape))
    out = pl.pallas_call(
        functools.partial(value_kernel, slots),
        grid=(holds,),
        in_specs=[
            pl.BlockSpec(memory_space=pltpu.SMEM),
            whole(*rank.shape),
            pl.BlockSpec((1, total * slots, hidden), lambda e: (e, 0, 0)),
            pl.BlockSpec((hidden, width), lambda e: (e, 0)),
        ],
        out_specs=[whole(tokens, width)] * total,
        out_shape=[shaped(tokens, width)] * total,
        scratch_shapes=[pltpu.VMEM((total, holds * slots, width), LOW), pltpu.VMEM((holds * slots, tokens), LOW)],
        compiler_params=pltpu.CompilerParams(vmem_limit_bytes=VMEM_MOST),
        cost_estimate=work(
            flops=2 * total * holds * slots * width * (hidden + tokens),
            bytes_accessed=2 * (holds * hidden * (width + total * slots) + total * tokens * width),
            transcendentals=0,
        ),
    )(token, rank, hidden_rows, w_down)
    return out


def wgrad_kernel(apart, place_ref, rows_ref, dz_ref, gg_ref, ug_ref, hid_ref, *outs):
    step = pl.program_id(0)
    shard = outs[0].shape[1]
    columns = pl.ds(pl.multiple_of(jnp.bitwise_xor(place_ref[0], step) * shard, 128), shard)
    rows, grads = rows_ref[0, :, columns], dz_ref[0, :, columns]
    parts = [dot_t(rows, gg_ref[0]), dot_t(rows, ug_ref[0]), dot_t(grads, hid_ref[0])]
    parts = [part.astype(LOW) for part in parts]
    for s in range(4):

        @pl.when(step == s)
        def _():
            for i, part in enumerate(parts):
                if s == 3 and apart:
                    outs[3 + i][...] = part
                else:
                    outs[s][i] = part


def wgrad_call(expert, place, kept, apart=False):
    _, count, width = kept[0].shape
    hidden = kept[2].shape[2]
    shard = width // 4
    row_spec = lambda d: pl.BlockSpec((1, count, d), lambda s: (expert, 0, 0), pipeline_mode=pl.Buffered(buffer_count=1))
    shapes = [(3, shard, hidden)] * 3 + ([(shard, hidden)] * 3 if apart else [(3, shard, hidden)])
    out = pl.pallas_call(
        functools.partial(wgrad_kernel, apart),
        grid=(4,),
        in_specs=[pl.BlockSpec(memory_space=pltpu.SMEM), row_spec(width), row_spec(width)] + [row_spec(hidden)] * 3,
        out_specs=[pl.BlockSpec(shape, lambda s, zeros=(0,) * len(shape): zeros) for shape in shapes],
        out_shape=[shaped(*shape) for shape in shapes],
        compiler_params=pltpu.CompilerParams(vmem_limit_bytes=VMEM_MOST),
        cost_estimate=work(
            flops=2 * count * width * 3 * hidden,
            bytes_accessed=2 * (count * (2 * width + 3 * hidden) + 3 * width * hidden),
            transcendentals=0,
        ),
    )(place, *kept)
    return [*out[:3], out[3:] if apart else out[3]]


def sums_call(gates, *sums):
    every = [term[0] if isinstance(term, tuple) else term for terms in sums for term in terms]

    def part_of(term, ready=()):
        array, part = term if isinstance(term, tuple) else (term, None)
        array = after(array, *ready) if ready else array
        return array if part is None else array[: len(part)] if isinstance(part, range) else array[part]

    totals = [add_low(part_of(terms[0], (*gates, *every)), *map(part_of, terms[1:])) for terms in sums]
    return [after(total, *totals) for total in totals] if len(totals) > 1 else totals


def finish_kernel(sizes, *refs):
    outs = refs[-3:]
    at = 0
    for i, out in enumerate(outs):
        total = sum(ref[...].astype(WIDE) for ref in refs[at : at + sizes[i]])
        at += sizes[i]
        out[...] = total if i < 2 else jnp.transpose(total)


def finish_call(expert, holds, terms, kept):
    shard, hidden = terms[0][0][0].shape[1:]
    steps = shard // 128
    wide, tall = shaped(shard, holds * hidden, dtype=WIDE), shaped(holds * hidden, shard, dtype=WIDE)
    flat = [term for group in terms for term in group]
    return pl.pallas_call(
        functools.partial(finish_kernel, [len(group) for group in terms]),
        grid=(steps,),
        in_specs=[
            pl.BlockSpec((128, hidden), lambda s: (s, 0))
            if at is None
            else pl.BlockSpec((None, 128, hidden), lambda s, at=at: (at, s, 0))
            for _, at in flat
        ]
        + ([pl.BlockSpec(memory_space=pl.ANY)] * 3 if kept else []),
        out_specs=[pl.BlockSpec((128, hidden), lambda s: (s, expert))] * 2
        + [pl.BlockSpec((hidden, 128), lambda s: (expert, s))],
        out_shape=[wide, wide, tall],
        input_output_aliases={len(flat) + i: i for i in range(3)} if kept else {},
        compiler_params=pltpu.CompilerParams(vmem_limit_bytes=VMEM_MOST),
        cost_estimate=work(flops=0, bytes_accessed=30 * shard * hidden, transcendentals=0),
    )(*[array for array, _ in flat], *(kept or ()))


def piece_columns(mine, s, shard):
    return pl.ds(pl.multiple_of(jnp.bitwise_xor(mine, s) * shard, 128), shard)


def turn(values, cos, sin):
    return values * cos + pltpu.roll(values, HEAD_DIM // 2, 1) * sin


def turn_back(values, cos, sin):
    return values * cos - pltpu.roll(values, HEAD_DIM // 2, 1) * sin


def inverse_rms(values):
    return lax.rsqrt(jnp.mean(values * values, axis=-1, keepdims=True) + EPS)


def head_slice(h):
    return slice(h * HEAD_DIM, (h + 1) * HEAD_DIM)


def stacked_heads(ref, band, group, heads):
    return jnp.concatenate([ref[band, head_slice(group * heads + h)] for h in range(heads)], axis=0)


def probabilities(queries, keys, allowed):
    scores = jnp.where(allowed, dot_bt(queries, keys) * HEAD_DIM ** (-0.5), NEG)
    expo = jnp.exp(scores - jnp.max(scores, axis=-1, keepdims=True))
    return expo * (1.0 / jnp.sum(expo, axis=-1, keepdims=True))


def allowed_pairs(seg_col_ref, seg_row_ref, band, reach, heads):
    size = band.stop - band.start
    rows = band.start + lax.broadcasted_iota(jnp.int32, (size, reach), 0)
    cols = lax.broadcasted_iota(jnp.int32, (size, reach), 1)
    ok = (seg_col_ref[band, :] == seg_row_ref[:, :reach]) & (cols <= rows)
    return jnp.concatenate([ok] * heads, axis=0)


def attention_kernel(
    mine_ref, tokens_ref, gain_ref, p0, p1, p2, p3, s0, s1, s2, s3, seg_row_ref, seg_col_ref, cos_ref, sin_ref,
    h_ref, q_ref, k_ref, v_ref, out_ref,
):
    mine = mine_ref[0]
    stream = tokens_ref[...].astype(WIDE)
    h_ref[...] = (stream * inverse_rms(stream) * gain_ref[...]).astype(LOW)
    shard = p0.shape[0]
    width = q_ref.shape[1]
    cos, sin = cos_ref[...], sin_ref[...]

    def projected(pieces, columns):
        return sum(dot(h_ref[:, piece_columns(mine, s, shard)], piece[:, columns]) for s, piece in enumerate(pieces))

    heads = QUERY_HEADS // KEY_VALUE_HEADS
    key_width = KEY_VALUE_HEADS * HEAD_DIM
    shared = (s0, s1, s2, s3)
    keys = projected(shared, slice(0, key_width))
    for g in range(KEY_VALUE_HEADS):
        k_ref[:, head_slice(g)] = turn(keys[:, head_slice(g)], cos, sin).astype(LOW)
    v_ref[...] = projected(shared, slice(key_width, 2 * key_width)).astype(LOW)
    group_width = heads * HEAD_DIM
    for g in range(KEY_VALUE_HEADS):
        queries = projected((p0, p1, p2, p3), slice(g * group_width, (g + 1) * group_width))
        for h in range(heads):
            q_ref[:, head_slice(g * heads + h)] = turn(queries[:, head_slice(h)], cos, sin).astype(LOW)
    length = q_ref.shape[0]
    tile = 128
    for start in range(0, length, tile):
        band, reach = slice(start, start + tile), start + tile
        allowed = allowed_pairs(seg_col_ref, seg_row_ref, band, reach, heads)
        for g in range(KEY_VALUE_HEADS):
            probs = probabilities(stacked_heads(q_ref, band, g, heads), k_ref[:reach, head_slice(g)], allowed)
            mixed = dot(probs.astype(LOW), v_ref[:reach, head_slice(g)]).astype(LOW)
            for h in range(heads):
                out_ref[band, head_slice(g * heads + h)] = mixed[h * tile : (h + 1) * tile]


def vmem_call(kernel, out_shape, flops, transcendentals, token, *args):
    moved = sum(a.size * a.dtype.itemsize for a in args) + sum(
        o.size * o.dtype.itemsize for o in jax.tree.leaves(out_shape)
    )
    return pl.pallas_call(
        kernel,
        in_specs=[pl.BlockSpec(memory_space=pltpu.SMEM)] + [pl.BlockSpec(memory_space=pltpu.VMEM)] * len(args),
        out_specs=[pl.BlockSpec(memory_space=pltpu.VMEM)] * len(out_shape),
        out_shape=out_shape,
        compiler_params=pltpu.CompilerParams(vmem_limit_bytes=VMEM_MOST),
        cost_estimate=work(flops=flops, bytes_accessed=moved, transcendentals=transcendentals),
    )(token, *args)


def shaped(*shape, dtype=LOW):
    return jax.ShapeDtypeStruct(shape, dtype)


def attention_call(mine, tokens, gain, pieces, shared_pieces, seg_row, seg_col, cos, sin):
    length, width = tokens.shape
    key_width = KEY_VALUE_HEADS * HEAD_DIM
    return vmem_call(
        attention_kernel,
        [shaped(length, width), shaped(length, width), shaped(length, key_width), shaped(length, key_width), shaped(length, width)],
        2 * length * width * (width + 2 * key_width) + 3 * length * length * width,
        QUERY_HEADS * length * length,
        mine, tokens, gain, *pieces, *shared_pieces, seg_row, seg_col, cos, sin,
    )


def project_kernel(
    mine_ref, tokens_ref, attn_ref, p0, p1, p2, p3, r0, r1, r2, r3, gain_ref, routes_ref, resid_ref, h_ref
):
    mine = mine_ref[0]
    shard = p0.shape[0]
    resid = tokens_ref[...].astype(WIDE)
    for s, piece in enumerate((p0, p1, p2, p3)):
        resid = resid + dot(attn_ref[:, piece_columns(mine, s, shard)], piece[...])
    resid_ref[...] = resid
    length, width = resid.shape
    h_ref[:length] = (resid * inverse_rms(resid) * gain_ref[...]).astype(LOW)
    logits = jnp.transpose(
        sum(
            dot(h_ref[:length, piece_columns(mine, s, shard)], piece[:, -128:])
            for s, piece in enumerate((r0, r1, r2, r3))
        )
    )
    experts = lax.broadcasted_iota(jnp.int32, logits.shape, 0)
    picked = [
        jnp.sum(jnp.where(experts == routes_ref[k : k + 1, :], logits, 0.0), axis=0, keepdims=True)
        for k in range(routes_ref.shape[0])
    ]
    top = functools.reduce(jnp.maximum, picked)
    expo = [jnp.exp(p - top) for p in picked]
    total = sum(expo)
    gates = jnp.concatenate([x / total for x in expo], axis=0)
    h_ref[length:] = jnp.zeros((16, width), LOW)
    h_ref[length:, :length] = pack_routing(gates, routes_ref[...])


def project_call(mine, tokens, attn, pieces, shared_pieces, gain, routes_t):
    length, width = tokens.shape
    return vmem_call(
        project_kernel,
        [shaped(length, width, dtype=WIDE), shaped(length + 16, width)],
        2 * length * width * (width + EXPERTS),
        length * 8,
        mine, tokens, attn, *pieces, *shared_pieces, gain, routes_t,
    )


def as_column(row):
    return jnp.transpose(jnp.broadcast_to(row, (8, row.shape[1])))[:, :1]


def norm_back(grad, gain, normed, inverse):
    scaled = grad * gain
    return inverse * (scaled - normed * jnp.mean(scaled * normed, axis=-1, keepdims=True))


def shard_parts(targets):
    at, parts = 0, []
    for target in targets:
        parts.append((target, slice(at, at + target.shape[0])))
        at += target.shape[0]
    return parts


def resid_back_kernel(
    mine_ref, resid_ref, gain_ref, dz_ref, t0, t1, t2, gains_ref, h_ref, attn_ref,
    p0, p1, p2, p3, r0, r1, r2, r3, grad_ref, attn_grad_ref, o0, o1, o2, o3, o4, o5, second_scr, low_scr,
):
    mine = mine_ref[0]
    shard, width = p0.shape
    length = resid_ref.shape[0]
    routers = (r0, r1, r2, r3)
    gains = gains_ref[...]
    experts = lax.broadcasted_iota(jnp.int32, gains.shape, 0)
    gate_rows, routes = unpack_routing(h_ref[length:, :length])
    gates = jnp.zeros(gains.shape, WIDE)
    for k in range(TOP):
        gates = gates + jnp.where(experts.astype(WIDE) == routes[k : k + 1], gate_rows[k : k + 1], 0.0)
    logit_grad = gates * (gains - jnp.sum(gates * gains, axis=0, keepdims=True))
    logit_grad = jnp.concatenate([logit_grad, jnp.zeros((128 - EXPERTS, length), WIDE)], axis=0)
    logit_grad = jnp.transpose(logit_grad).astype(LOW)
    second_scr[...] = t0[...].astype(WIDE) + t1[...].astype(WIDE) + t2[...].astype(WIDE)
    for s, piece in enumerate(routers):
        columns = piece_columns(mine, s, shard)
        second_scr[:, columns] = second_scr[:, columns] + dot_bt(logit_grad, piece[:, -128:])
    resid = resid_ref[...]
    inverse = inverse_rms(resid)
    normed = resid * inverse
    second = second_scr[...]
    gain_grad = jnp.sum(second * normed, axis=0, keepdims=True)
    grad = dz_ref[...].astype(WIDE) + norm_back(second, gain_ref[...], normed, inverse)
    grad_ref[...] = grad
    low_scr[...] = grad.astype(LOW)
    second_scr[:1, :] = gain_grad
    low = low_scr[...]
    for s, piece in enumerate((p0, p1, p2, p3)):
        columns = piece_columns(mine, s, shard)
        attn_grad_ref[:, columns] = dot_bt(low, piece[...]).astype(LOW)
        out_part = dot_t(attn_ref[:, columns], low).astype(LOW)
        router_part = dot_t(h_ref[:length, columns], logit_grad)
        lanes = lax.broadcasted_iota(jnp.int32, router_part.shape, 1)
        small = jnp.where(lanes == EXPERTS, as_column(second_scr[:1, columns]), router_part).astype(LOW)
        for target, rows in shard_parts(((o0,), (o1,), (o2, o3), (o4, o5))[s]):
            target[:, :width] = out_part[rows]
            target[:, width:] = small[rows]


def resid_back_call(mine, resid, gain, dz, terms, gains, h, attn, pieces, shared_pieces):
    length, width = resid.shape
    shard = pieces[0].shape[0]
    return pl.pallas_call(
        resid_back_kernel,
        in_specs=[pl.BlockSpec(memory_space=pltpu.SMEM)] + [pl.BlockSpec(memory_space=pltpu.VMEM)] * 17,
        out_specs=[pl.BlockSpec(memory_space=pltpu.VMEM)] * 8,
        out_shape=[shaped(length, width, dtype=WIDE), shaped(length, width)]
        + [shaped(shard, width + 128)] * 2
        + [shaped(shard // 2, width + 128)] * 4,
        scratch_shapes=[pltpu.VMEM((length, width), WIDE), pltpu.VMEM((length, width), LOW)],
        compiler_params=pltpu.CompilerParams(vmem_limit_bytes=VMEM_MOST),
        cost_estimate=work(
            flops=4 * length * width * (width + EXPERTS), bytes_accessed=length * width * 40, transcendentals=0
        ),
    )(mine, resid, gain, dz, *terms, gains, h, attn, *pieces, *shared_pieces)


def attention_back_kernel(
    mine_ref, q_ref, k_ref, v_ref, do_ref, h_ref, tokens_ref, gain_ref, grad_ref, p0, p1, p2, p3, s0, s1, s2, s3,
    seg_row_ref, seg_col_ref, cos_ref, sin_ref, input_ref, o0, o1, o2, o3, o4, o5, qkv_scr, dk_scr, dv_scr, dh_scr,
):
    mine = mine_ref[0]
    length, width = q_ref.shape
    shard = p0.shape[0]
    qkv_width = width + 2 * KEY_VALUE_HEADS * HEAD_DIM
    heads = QUERY_HEADS // KEY_VALUE_HEADS
    key_width = KEY_VALUE_HEADS * HEAD_DIM
    tile = 128
    dk_scr[...] = jnp.zeros_like(dk_scr)
    dv_scr[...] = jnp.zeros_like(dv_scr)
    for start in range(0, length, tile):
        band, reach = slice(start, start + tile), start + tile
        allowed = allowed_pairs(seg_col_ref, seg_row_ref, band, reach, heads)
        cos, sin = cos_ref[band, :], sin_ref[band, :]
        for g in range(KEY_VALUE_HEADS):
            queries = stacked_heads(q_ref, band, g, heads)
            grads = stacked_heads(do_ref, band, g, heads)
            keys = k_ref[:reach, head_slice(g)]
            probs = probabilities(queries, keys, allowed)
            prob_grad = dot_bt(grads, v_ref[:reach, head_slice(g)])
            delta = jnp.sum(probs * prob_grad, axis=-1, keepdims=True)
            score_grad = (probs * (prob_grad - delta) * HEAD_DIM ** (-0.5)).astype(LOW)
            dv_scr[:reach, head_slice(g)] += dot_t(probs.astype(LOW), grads)
            dk_scr[:reach, head_slice(g)] += dot_t(score_grad, queries)
            dq = dot(score_grad, keys)
            for h in range(heads):
                qkv_scr[band, head_slice(g * heads + h)] = turn_back(dq[h * tile : (h + 1) * tile], cos, sin).astype(LOW)
    for g in range(KEY_VALUE_HEADS):
        at = width + g * HEAD_DIM
        qkv_scr[:, at : at + HEAD_DIM] = turn_back(dk_scr[:, head_slice(g)], cos_ref[...], sin_ref[...]).astype(LOW)
    qkv_scr[:, width + key_width :] = dv_scr[...].astype(LOW)
    qkv = qkv_scr[...]
    for s, (piece, shared) in enumerate(zip((p0, p1, p2, p3), (s0, s1, s2, s3))):
        dh_scr[:, piece_columns(mine, s, shard)] = dot_bt(qkv[:, :width], piece[...]) + dot_bt(qkv[:, width:], shared[:, : 2 * key_width])
    stream = tokens_ref[...].astype(WIDE)
    inverse = inverse_rms(stream)
    normed = stream * inverse
    first = dh_scr[...]
    gain_grad = jnp.sum(first * normed, axis=0, keepdims=True)
    input_ref[...] = grad_ref[...] + norm_back(first, gain_ref[...], normed, inverse)
    dh_scr[:1, :] = gain_grad
    for s in range(4):
        columns = piece_columns(mine, s, shard)
        part = dot_t(h_ref[:, columns], qkv).astype(LOW)
        small = jnp.concatenate([as_column(dh_scr[:1, columns]), jnp.zeros((shard, 127), WIDE)], axis=1).astype(LOW)
        for target, rows in shard_parts(((o0,), (o1,), (o2, o3), (o4, o5))[s]):
            target[:, :qkv_width] = part[rows]
            target[:, qkv_width:] = small[rows]


def attention_back_call(mine, q, k, v, do, h, tokens, gain, grad, pieces, shared_pieces, seg_row, seg_col, cos, sin):
    length, width = q.shape
    shard = pieces[0].shape[0]
    qkv_width = width + 2 * KEY_VALUE_HEADS * HEAD_DIM
    key_width = KEY_VALUE_HEADS * HEAD_DIM
    return pl.pallas_call(
        attention_back_kernel,
        in_specs=[pl.BlockSpec(memory_space=pltpu.SMEM)] + [pl.BlockSpec(memory_space=pltpu.VMEM)] * 20,
        out_specs=[pl.BlockSpec(memory_space=pltpu.VMEM)] * 7,
        out_shape=[shaped(length, width, dtype=WIDE)]
        + [shaped(shard, qkv_width + 128)] * 2
        + [shaped(shard * 2 // 3, qkv_width + 128), shaped(shard // 3, qkv_width + 128)] * 2,
        scratch_shapes=[
            pltpu.VMEM((length, qkv_width), LOW),
            pltpu.VMEM((length, key_width), WIDE),
            pltpu.VMEM((length, key_width), WIDE),
            pltpu.VMEM((length, width), WIDE),
        ],
        compiler_params=pltpu.CompilerParams(vmem_limit_bytes=VMEM_MOST),
        cost_estimate=work(
            flops=4 * length * width * qkv_width + 7 * length * length * width,
            bytes_accessed=length * width * 40,
            transcendentals=QUERY_HEADS * length * length,
        ),
    )(mine, q, k, v, do, h, tokens, gain, grad, *pieces, *shared_pieces, seg_row, seg_col, cos, sin)


def spread_kernel(count, token_ref, *refs):
    parts, outs, scratch = refs[2 : -count - 1], refs[-count - 1 : -1], refs[-1]
    for part, rows in shard_parts(parts):
        scratch[rows] = part[...]
    chunk = outs[0].shape[0]
    for j, out in enumerate(outs):
        rows = pl.ds(pl.multiple_of(lax.rem(token_ref[2] + j, count) * chunk, 16), chunk)
        out[...] = sum(term[rows, :].astype(WIDE) for term in (*refs[:2], scratch)).astype(LOW)


def spread_call(token, count, *terms):
    rows, width = terms[0].shape
    whole = lambda shape: pl.BlockSpec(shape, lambda i: (0, 0))
    return pl.pallas_call(
        functools.partial(spread_kernel, count),
        grid=(1,),
        in_specs=[pl.BlockSpec(memory_space=pltpu.SMEM)] + [whole(t.shape) for t in terms],
        out_specs=[whole((rows // count, width))] * count,
        out_shape=[shaped(rows // count, width)] * count,
        scratch_shapes=[pltpu.VMEM((rows, width), LOW)],
        compiler_params=pltpu.CompilerParams(vmem_limit_bytes=VMEM_MOST),
        cost_estimate=work(flops=0, bytes_accessed=8 * rows * width, transcendentals=0),
    )(token, *terms)


def assemble_kernel(count, widths, names, token_ref, *refs):
    chunks, outs, scratch = refs[:count], refs[count:-1], refs[-1]
    chunk = chunks[0].shape[0]
    for j, ref in enumerate(chunks):
        rows = pl.ds(pl.multiple_of(lax.rem(token_ref[2] + j, count) * chunk, 16), chunk)
        values = ref[...].astype(WIDE)
        at = 0
        for width, out in zip(widths, outs):
            out[rows, :] = values[:, at : at + width]
            at += width
        scratch[rows, :] = values[:, at : at + 128]
    if names:
        outs[-2][...] = scratch[:, :names]
    outs[-1][...] = jnp.transpose(scratch[...])[names]


def assemble_call(token, chunks, widths, names):
    count, (rows, width) = len(chunks), chunks[0].shape
    whole = lambda shape: pl.BlockSpec(shape, lambda i: (0,) * len(shape))
    shapes = [(count * rows, w) for w in widths] + ([(count * rows, names)] if names else []) + [(count * rows,)]
    return pl.pallas_call(
        functools.partial(assemble_kernel, count, widths, names),
        grid=(1,),
        in_specs=[pl.BlockSpec(memory_space=pltpu.SMEM)] + [whole((rows, width))] * count,
        out_specs=[whole(shape) for shape in shapes],
        out_shape=[shaped(*shape, dtype=WIDE) for shape in shapes],
        scratch_shapes=[pltpu.VMEM((count * rows, 128), WIDE)],
        compiler_params=pltpu.CompilerParams(vmem_limit_bytes=VMEM_MOST),
        cost_estimate=work(flops=0, bytes_accessed=6 * count * rows * width, transcendentals=0),
    )(token, *chunks)


def per_device_ring(
    tokens,
    segments,
    routes,
    attn_gain,
    ffn_gain,
    w_query,
    key_weight,
    value_weight,
    w_out,
    w_router,
    w_gate,
    w_up,
    w_down,
    cotangent,
):
    length, model_width = tokens.shape
    top_count = routes.shape[1]
    count = lax.axis_size("expert")
    holds = EXPERTS // count
    capacity = max(2, 3 * length * top_count // (2 * EXPERTS))
    slots = -(-capacity // 16) * 16
    shard = model_width // 4
    key_width = KEY_VALUE_HEADS * HEAD_DIM
    half = length // 2
    mine = lax.axis_index("wshard").astype(jnp.int32)
    order = jnp.array(ring_order(count), jnp.int32)
    spot_of = jnp.array([ring_order(count).index(i) for i in range(count)], jnp.int32)
    here = lax.axis_index("expert").astype(jnp.int32)
    spot = spot_of[here]
    token = jnp.stack([mine, here, spot])
    routes_t = routes.T

    cosine, sine = rotary_tables(length, HEAD_DIM)
    cos = jnp.concatenate([cosine, cosine], axis=1)
    sin = jnp.concatenate([-sine, sine], axis=1)
    seg_col = segments.reshape(length, 1)
    gain_one, gain_two = attn_gain[None], ffn_gain[None]

    def pieces_of(own, across, *ready):
        return (own, swap_core(own), across, swap_core(after(across, *ready)))

    dz = {0: cotangent}
    dz[-1], dz[1] = ahead(dz[0], count), behind(dz[0], count)
    query_across = swap_x(w_query)
    query_pieces = pieces_of(w_query, query_across)
    spare = jnp.zeros((shard, 128 - EXPERTS), LOW)
    shared = jnp.concatenate([key_weight, value_weight, w_router, spare], axis=1)
    shared, token, seg_col, cos, sin, routes_t, gain_one, gain_two = lax.optimization_barrier(
        (shared, token, seg_col, cos, sin, routes_t, gain_one, gain_two)
    )
    shared_across = swap_x(after(shared, query_across, dz[-1], dz[1]))
    dz[-2], dz[2] = ahead(dz[-1], count), behind(dz[1], count)
    shared_pieces = pieces_of(shared, shared_across)
    out_across = swap_x(after(w_out, shared_across))

    first_low, query, key, value, attn = attention_call(
        after(token, dz[-2], dz[2]), tokens, gain_one, query_pieces, shared_pieces, segments, seg_col, cos, sin
    )
    out_pieces = pieces_of(w_out, out_across, attn)
    dz[-3], dz[3] = ahead(dz[-2], count), behind(dz[2], count)
    resid, second = project_call(after(token, dz[-3], dz[3]), tokens, attn, out_pieces, shared_pieces, gain_two, routes_t)

    def experts(ready, first, offsets, kept):
        return expert_call(
            after(token, *ready), first, [h[j] for j in offsets], [dz[j] for j in offsets], w_gate, w_up, w_down, kept,
            holds, slots, count,
        )

    h = {0: second}
    h[-1], h[1] = ahead(h[0], count), behind(h[0], count)
    (d_own,), kept = experts((), 6, (0,), None)
    h[-2], h[2] = ahead(after(h[-1], d_own), count), behind(after(h[1], d_own), count)
    (d_l1, d_r1), kept = experts((), 0, (-1, 1), kept)
    h[-3], h[3] = ahead(after(h[-2], d_l1), count), behind(after(h[2], d_l1), count)
    (d_l2, d_r2), kept = experts((), 2, (-2, 2), kept)
    h[4], dz[4] = ahead(after(h[-3], d_l2), count), behind(after(dz[3], d_l2), count)
    (d_l3, d_r3), kept = experts((), 4, (-3, 3), kept)
    (d_far,), (gains, rank, *kept) = experts((), 7, (4,), kept)

    block_of = jnp.array([BLOCK_OFFSETS.index(j if j <= count // 2 else j - count) for j in range(count)], jnp.int32)
    gain_send = gains[block_of[(spot_of - spot) % count]]

    def weight_grads(expert, *ready):
        return wgrad_call(expert, after(token, *ready), kept)

    def over_cores(grads, *ready):
        return swap_core(after(grads[3], *ready))

    both, last = range(2), 2

    def sum_of(grads, got, part):
        return (grads[2], part), (got, part)

    up_sent, down_sent = ahead(d_far, count), behind(d_l3, count)
    grads = [wgrad_call(0, token, kept, True)]
    got = [[swap_core(v) for v in grads[0][3]]]
    grads.append(weight_grads(1, grads[0][0]))
    up, down = sums_call((grads[1][0], *got[0],), (d_r3, up_sent), (d_l2, down_sent))

    up_sent, down_sent = ahead(up, count), behind(down, count)
    got.append(over_cores(grads[1], up))
    halves = [sums_call((up,), *[((grads[0][2], i), got[0][i]) for i in range(3)])]
    across = [[(swap_x(v), None) for v in halves[0][:2]]]
    grads.append(weight_grads(2, gain_send, *halves[0]))
    up, down = sums_call((grads[2][0], across[0][0][0], across[0][1][0],), (d_r2, up_sent), (d_l1, down_sent))

    up_sent, down_sent = ahead(up, count), behind(down, count)
    got.append(over_cores(grads[2], up))
    halves.append(sums_call((up,), sum_of(grads[1], got[1], both), sum_of(grads[1], got[1], last)))
    across_b = swap_x(halves[1][0])
    y = dict(zip(BLOCK_OFFSETS, value_call(after(token, *halves[1]), rank, kept[4], w_down, slots)))
    late = [swap_core(after(grads[0][1], up))]
    (up,) = sums_call((y[0], across_b, down_sent, late[0]), (d_r1, up_sent))

    up_sent, y_down = ahead(up, count), behind(after(y[4], up), count)
    across[0].append((swap_x(after(halves[0][2], up)), None))
    across.append([(across_b, 0), (across_b, 1), (swap_x(after(halves[1][1], up)), None)])
    gain_dense = lax.all_to_all(after(gain_send, up), "expert", split_axis=0, concat_axis=0, tiled=True)
    gain_dense = gain_dense.reshape(EXPERTS, length)
    halves.append(sums_call((up,), sum_of(grads[2], got[2], both), sum_of(grads[2], got[2], last)))
    late.append(swap_core(after(grads[1][1], up)))
    grads.append(weight_grads(3, *halves[2]))
    (down,) = sums_call(
        (up_sent, across[0][2][0], across[1][2][0], gain_dense, late[1], grads[3][0]), (y[-3], y_down)
    )

    y_up, y_down, across_d = ahead(after(y[3], down), count), behind(down, count), swap_x(after(halves[2][0], down))
    grad, attn_grad, *out_parts = resid_back_call(
        after(token, down), resid, gain_two, cotangent, (d_own, up_sent, down_sent), gain_dense, second,
        attn, out_pieces, shared_pieces,
    )
    def finish(ready, expert, kept_out):
        own = after(grads[expert][0], *ready)
        terms = [[(own, i), (late[expert], i), across[expert][i]] for i in range(3)]
        return finish_call(expert, holds, terms, kept_out)

    out_first = [swap_core(v) for v in out_parts[4:]]
    finished = finish((grad,), 0, None)
    *out_half, up, down = sums_call(
        (finished[0], across_d), *zip(out_parts[2:4], out_first), (y[2], y_up), (y[-2], y_down)
    )

    y_up, y_down, out_across = ahead(up, count), behind(down, count), [swap_x(v) for v in out_half]
    out_got = swap_core(after(out_parts[1], up))
    input_grad, *qkv_parts = attention_back_call(
        after(token, up), query, key, value, attn_grad, first_low, tokens, gain_one, grad, query_pieces,
        shared_pieces, segments, seg_col, cos, sin,
    )
    up, down = sums_call((input_grad, *out_across, out_got), (y[1], y_up), (y[-1], y_down))

    y_up, y_down = ahead(up, count), behind(down, count)
    qkv_first = [swap_core(after(v, up)) for v in qkv_parts[4:]]
    qkv_half = sums_call((up,), *zip(qkv_parts[2:4], qkv_first))
    qkv_across = [swap_x(qkv_half[0])]
    out_parts = spread_call(after(token, *qkv_half), count, out_parts[0], out_got, *out_across)
    finished = finish(qkv_half, 1, finished)
    qkv_got = swap_core(after(qkv_parts[1], qkv_across[0]))
    got.append(over_cores(grads[3], qkv_across[0]))
    y_own = after(y[0], qkv_across[0], out_parts[0], finished[0])
    mixed = (resid + sum(t.astype(WIDE) for t in (y_own, y_up, y_down))).astype(LOW)
    qkv_across.append(swap_x(after(qkv_half[1], qkv_across[0])))
    (half_e,) = sums_call((mixed,), sum_of(grads[3], got[3], range(3)))

    def sum_step(parts, up, down, step):
        up = add_low(parts[step], ahead(up, count))
        down = behind(down, count)
        return up, add_low(parts[count + 1 - step], down) if step > 1 else down

    def copy_step(up, down):
        return up + [ahead(up[-1], count)], down + [behind(down[-1], count)]

    out_up, out_down = after(out_parts[4], mixed), after(out_parts[5], mixed)
    for step in (3, 2, 1):
        out_up, out_down = sum_step(out_parts, out_up, out_down, step)
        if step == 2:
            out_up = after(out_up, qkv_across[1])
    out_own = add_low(out_parts[0], ahead(out_up, count), out_down)
    qkv_parts = spread_call(after(token, out_own), count, qkv_parts[0], qkv_got, *qkv_across)
    across_e = swap_x(after(halves[2][1], qkv_parts[0])), swap_x(after(half_e, qkv_parts[0]))
    late += [swap_core(after(g[1], qkv_parts[0])) for g in grads[2:]]
    across.append([(across_d, 0), (across_d, 1), (across_e[0], None)])
    across.append([(across_e[1], i) for i in range(3)])
    out_ups, out_downs = [after(out_own, qkv_parts[0])], [after(out_own, qkv_parts[0])]
    qkv_up, qkv_down = qkv_parts[4], qkv_parts[5]
    for step in (3, 2, 1):
        out_ups, out_downs = copy_step(out_ups, out_downs)
        qkv_up, qkv_down = sum_step(qkv_parts, qkv_up, qkv_down, step)
        qkv_up = after(qkv_up, out_ups[-1], out_downs[-1])
    out_ups.append(ahead(out_ups[-1], count))
    qkv_own = add_low(after(qkv_parts[0], out_ups[-1]), ahead(qkv_up, count), qkv_down)
    qkv_ups, qkv_downs = [qkv_own], [qkv_own]
    for step in (3, 2, 1):
        qkv_ups, qkv_downs = copy_step(qkv_ups, qkv_downs)
        if step == 2:
            finished = finish((qkv_ups[-1],), 2, finished)
            qkv_ups[-1] = after(qkv_ups[-1], finished[0])
    out_sum, router_sum, ffn_gain_sum = assemble_call(
        after(token, qkv_ups[2]), out_downs + out_ups[:0:-1], (model_width,), EXPERTS
    )
    qkv_ups.append(ahead(after(qkv_ups[-1], out_sum, across_e[1]), count))
    finished = finish((qkv_ups[3],), 3, finished)
    query_sum, key_sum, value_sum, attn_gain_sum = assemble_call(
        after(token, finished[0]), qkv_downs + qkv_ups[:0:-1], (model_width, key_width, key_width), 0
    )
    gate_shard, up_shard, down_shard = finished
    return (
        mixed,
        input_grad,
        attn_gain_sum,
        ffn_gain_sum,
        query_sum,
        key_sum,
        value_sum,
        out_sum,
        router_sum,
        gate_shard,
        up_shard,
        down_shard,
    )


def solution(mesh):
    ring = mesh.shape["expert"] == len(BLOCK_OFFSETS) and mesh.shape["wshard"] == 4
    body = per_device_ring if ring else per_device_exchange
    in_specs = (
        P(("expert", "wshard"), None),
        P(("expert", "wshard"), None),
        P(("expert", "wshard"), None),
        P(),
        P(),
        P("wshard", None),
        P("wshard", None),
        P("wshard", None),
        P("wshard", None),
        P("wshard", None),
        P(None, "expert"),
        P(None, "expert"),
        P("expert", None),
        P(("expert", "wshard"), None),
    )
    out_specs = (
        P(("expert", "wshard"), None),
        P(("expert", "wshard"), None),
        P("wshard"),
        P("wshard"),
        P("wshard", None),
        P("wshard", None),
        P("wshard", None),
        P("wshard", None),
        P("wshard", None),
        P("wshard", "expert"),
        P("wshard", "expert"),
        P("expert", "wshard"),
    )
    return jax.shard_map(
        body, mesh=mesh, in_specs=in_specs, out_specs=out_specs, check_vma=False
    )
```

```python
import functools

import jax
import jax.numpy as jnp
from jax import lax
from jax.experimental import pallas as pl
from jax.experimental.pallas import tpu as pltpu
from jax.sharding import PartitionSpec as P

QUERY_HEADS = 12
KEY_VALUE_HEADS = 2
HEAD_DIM = 128
EXPERTS = 32
TOP = 4


EPS = 1e-06
ROPE_BASE = 10000.0
NEG = -1e30
LOW = jnp.bfloat16
WIDE = jnp.float32
VMEM_MOST = 60 * 1024 * 1024
def norm_forward(values, gain):
    inverse = lax.rsqrt(jnp.mean(values * values, axis=-1) + EPS)
    normed = values * inverse[:, None]
    return (normed * gain, normed, inverse)


def norm_backward(grad, gain, normed, inverse):
    gain_grad = jnp.sum(grad * normed, axis=0)
    scaled = grad * gain
    centred = scaled - normed * jnp.mean(scaled * normed, axis=-1, keepdims=True)
    return (inverse[:, None] * centred, gain_grad)


def rotary_tables(seq_length, head_size):
    half_size = head_size // 2
    frequency = ROPE_BASE ** (-(jnp.arange(half_size, dtype=jnp.float32) * 2.0 / head_size))
    angles = jnp.arange(seq_length, dtype=jnp.float32)[:, None] * frequency[None, :]
    return (jnp.cos(angles), jnp.sin(angles))


def apply_rotation(values, cosine_lookup, sine_lookup):
    half_size = values.shape[-1] // 2
    first_half = values[..., :half_size]
    second_half = values[..., half_size:]
    cos_part = cosine_lookup[:, None, :]
    sin_part = sine_lookup[:, None, :]
    return jnp.concatenate(
        [
            first_half * cos_part - second_half * sin_part,
            second_half * cos_part + first_half * sin_part,
        ],
        axis=-1,
    )


def reverse_rotation(values, cosine_lookup, sine_lookup):
    half_size = values.shape[-1] // 2
    first_half = values[..., :half_size]
    second_half = values[..., half_size:]
    cos_part = cosine_lookup[:, None, :]
    sin_part = sine_lookup[:, None, :]
    return jnp.concatenate(
        [
            first_half * cos_part + second_half * sin_part,
            second_half * cos_part - first_half * sin_part,
        ],
        axis=-1,
    )


def per_device_exchange(
    tokens,
    segments,
    routes,
    attn_gain,
    ffn_gain,
    w_query,
    key_weight,
    value_weight,
    w_out,
    w_router,
    w_gate,
    w_up,
    w_down,
    cotangent,
):
    lower_dtype = jnp.bfloat16
    wide_type = jnp.float32
    sequence_length, model_width = tokens.shape
    top_count = routes.shape[1]
    axis_count = lax.axis_size("expert")
    owners = max(1, axis_count // EXPERTS)
    holds = max(1, EXPERTS // axis_count)
    groups = EXPERTS // holds
    capacity = max(2, 3 * sequence_length * top_count // (2 * EXPERTS))
    hidden_dev = w_gate.shape[1] // holds
    query_group_width = QUERY_HEADS // KEY_VALUE_HEADS
    score_scale = HEAD_DIM ** (-0.5)
    pair_count = sequence_length * top_count
    query_full, key_full, value_full, out_full, router_full = (
        lax.all_gather(w_query, "wshard", axis=0, tiled=True),
        lax.all_gather(key_weight, "wshard", axis=0, tiled=True),
        lax.all_gather(value_weight, "wshard", axis=0, tiled=True),
        lax.all_gather(w_out, "wshard", axis=0, tiled=True),
        lax.all_gather(w_router, "wshard", axis=0, tiled=True),
    )
    stream = tokens.astype(wide_type)
    first_norm, first_normed, first_inverse = norm_forward(stream, attn_gain)
    first_low = first_norm.astype(lower_dtype)
    cosine_lookup, sine_lookup = rotary_tables(sequence_length, HEAD_DIM)
    query_pre = jnp.dot(first_low, query_full, preferred_element_type=wide_type).reshape(
        sequence_length, QUERY_HEADS, HEAD_DIM
    )
    key_unrotated = jnp.dot(first_low, key_full, preferred_element_type=wide_type).reshape(
        sequence_length, KEY_VALUE_HEADS, HEAD_DIM
    )
    query_rotated = (
        apply_rotation(query_pre, cosine_lookup, sine_lookup)
        .astype(lower_dtype)
        .reshape(sequence_length, KEY_VALUE_HEADS, query_group_width, HEAD_DIM)
    )
    key_rotated = apply_rotation(key_unrotated, cosine_lookup, sine_lookup).astype(lower_dtype)
    value_lowered = (
        jnp.dot(first_low, value_full, preferred_element_type=wide_type)
        .astype(lower_dtype)
        .reshape(sequence_length, KEY_VALUE_HEADS, HEAD_DIM)
    )
    positions = jnp.arange(sequence_length)
    offset = positions[:, None] - positions[None, :]
    segment_row = segments[0]
    allowed = (segment_row[:, None] == segment_row[None, :]) & (offset >= 0)
    raw_scores = jnp.einsum(
        "qagd,kad->agqk", query_rotated, key_rotated, preferred_element_type=wide_type
    )
    scores = jnp.where(allowed, raw_scores * score_scale, NEG)
    score_top = jnp.max(scores, axis=-1, keepdims=True)
    expo_terms = jnp.exp(scores - score_top)
    expo_total = jnp.sum(expo_terms, axis=-1, keepdims=True)
    log_total = score_top + jnp.log(expo_total)
    probs_low = (expo_terms / expo_total).astype(lower_dtype)
    attn_low = (
        jnp.einsum("agqk,kad->qagd", probs_low, value_lowered, preferred_element_type=wide_type)
        .astype(lower_dtype)
        .reshape(sequence_length, QUERY_HEADS * HEAD_DIM)
    )
    resid = stream + jnp.dot(attn_low, out_full, preferred_element_type=wide_type)
    second_norm, second_normed, second_inverse = norm_forward(resid, ffn_gain)
    second_low = second_norm.astype(lower_dtype)
    logits = jnp.dot(second_low, router_full, preferred_element_type=wide_type)
    choose = (routes[:, :, None] == jnp.arange(EXPERTS)[None, None, :]).astype(wide_type)
    selected = jnp.sum(choose * logits[:, None, :], axis=-1)
    gate_probs = jax.nn.softmax(selected, axis=-1)
    flat_routes = routes.reshape(pair_count)
    one_hot = (flat_routes[:, None] == jnp.arange(EXPERTS)[None, :]).astype(jnp.int32)
    slot_rank = jnp.sum((jnp.cumsum(one_hot, axis=0) - 1) * one_hot, axis=1)
    slot_index = (flat_routes // holds * capacity + slot_rank) * holds + flat_routes % holds
    slot_pair = (
        jnp.full((EXPERTS * capacity,), pair_count, jnp.int32)
        .at[slot_index]
        .set(jnp.arange(pair_count, dtype=jnp.int32))
    )
    second_ext = jnp.concatenate([second_low, jnp.zeros((1, model_width), lower_dtype)], axis=0)
    send_rows = jnp.repeat(
        second_ext[slot_pair // top_count].reshape(groups, capacity, holds, model_width),
        owners,
        axis=0,
    )
    gate_local = w_gate.reshape(model_width, holds, hidden_dev)
    up_local = w_up.reshape(model_width, holds, hidden_dev)
    down_local = w_down.reshape(holds, hidden_dev, model_width)

    def owner_total(values):
        summed = jnp.sum(
            values.astype(wide_type).reshape(groups, owners, capacity, holds, model_width), axis=1
        )
        return summed.reshape(EXPERTS * capacity, model_width)

    received = lax.all_to_all(send_rows, "expert", split_axis=0, concat_axis=0, tiled=True)
    gate_pre = jnp.einsum("scld,dlf->sclf", received, gate_local, preferred_element_type=wide_type)
    up_pre = jnp.einsum("scld,dlf->sclf", received, up_local, preferred_element_type=wide_type)
    hidden = (jax.nn.silu(gate_pre) * up_pre).astype(lower_dtype)
    partial_value = jnp.einsum(
        "sclf,lfd->scld", hidden, down_local, preferred_element_type=wide_type
    ).astype(lower_dtype)
    returned = lax.all_to_all(partial_value, "expert", split_axis=0, concat_axis=0, tiled=True)
    expert_wide = owner_total(returned)[slot_index].reshape(sequence_length, top_count, model_width)
    mixed = (resid + jnp.sum(gate_probs[:, :, None] * expert_wide, axis=1)).astype(lower_dtype)
    upstream = cotangent.astype(wide_type)
    query_back, key_back, value_back, out_back, router_back = (
        lax.all_gather(w_query, "wshard", axis=0, tiled=True),
        lax.all_gather(key_weight, "wshard", axis=0, tiled=True),
        lax.all_gather(value_weight, "wshard", axis=0, tiled=True),
        lax.all_gather(w_out, "wshard", axis=0, tiled=True),
        lax.all_gather(w_router, "wshard", axis=0, tiled=True),
    )
    gate_grad = jnp.sum(expert_wide * upstream[:, None, :], axis=-1)
    sel_grad = gate_probs * (gate_grad - jnp.sum(gate_probs * gate_grad, axis=-1, keepdims=True))
    logit_grad = jnp.sum(choose * sel_grad[:, :, None], axis=1).astype(lower_dtype)
    pair_grad = (
        (gate_probs[:, :, None] * upstream[:, None, :])
        .astype(lower_dtype)
        .reshape(pair_count, model_width)
    )
    pair_ext = jnp.concatenate([pair_grad, jnp.zeros((1, model_width), lower_dtype)], axis=0)
    grad_send = jnp.repeat(
        pair_ext[slot_pair].reshape(groups, capacity, holds, model_width), owners, axis=0
    )
    grad_recv, rows_recv = (
        lax.all_to_all(grad_send, "expert", split_axis=0, concat_axis=0, tiled=True),
        lax.all_to_all(send_rows, "expert", split_axis=0, concat_axis=0, tiled=True),
    )
    gate_pre = jnp.einsum("scld,dlf->sclf", rows_recv, gate_local, preferred_element_type=wide_type)
    up_pre = jnp.einsum("scld,dlf->sclf", rows_recv, up_local, preferred_element_type=wide_type)
    sigmoid_gate = jax.nn.sigmoid(gate_pre)
    silu_gate = gate_pre * sigmoid_gate
    hidden = (silu_gate * up_pre).astype(lower_dtype)
    hidden_grad = jnp.einsum(
        "scld,lfd->sclf", grad_recv, down_local, preferred_element_type=wide_type
    )
    gate_pre_grad = (
        hidden_grad * up_pre * sigmoid_gate * (1.0 + gate_pre * (1.0 - sigmoid_gate))
    ).astype(lower_dtype)
    up_pre_grad = (hidden_grad * silu_gate).astype(lower_dtype)
    row_grad = (
        jnp.einsum("sclf,dlf->scld", gate_pre_grad, gate_local, preferred_element_type=wide_type)
        + jnp.einsum("sclf,dlf->scld", up_pre_grad, up_local, preferred_element_type=wide_type)
    ).astype(lower_dtype)
    returned_grad = lax.all_to_all(row_grad, "expert", split_axis=0, concat_axis=0, tiled=True)
    gate_wgrad = jnp.einsum(
        "scld,sclf->dlf", rows_recv, gate_pre_grad, preferred_element_type=wide_type
    ).reshape(model_width, holds * hidden_dev)
    up_wgrad = jnp.einsum(
        "scld,sclf->dlf", rows_recv, up_pre_grad, preferred_element_type=wide_type
    ).reshape(model_width, holds * hidden_dev)
    down_wgrad = jnp.einsum(
        "sclf,scld->lfd", hidden, grad_recv, preferred_element_type=wide_type
    ).reshape(holds * hidden_dev, model_width)
    gate_shard, up_shard, down_shard = (
        lax.psum_scatter(
            gate_wgrad.astype(jnp.bfloat16), "wshard", scatter_dimension=0, tiled=True
        ).astype(jnp.float32),
        lax.psum_scatter(
            up_wgrad.astype(jnp.bfloat16), "wshard", scatter_dimension=0, tiled=True
        ).astype(jnp.float32),
        lax.psum_scatter(
            down_wgrad.astype(jnp.bfloat16), "wshard", scatter_dimension=1, tiled=True
        ).astype(jnp.float32),
    )
    token_grad = owner_total(returned_grad)[slot_index].reshape(
        sequence_length, top_count, model_width
    )
    second_grad = jnp.sum(token_grad, axis=1) + jnp.dot(
        logit_grad, router_back.T, preferred_element_type=wide_type
    )
    router_wgrad = jnp.einsum("td,te->de", second_low, logit_grad, preferred_element_type=wide_type)
    resid_part, ffn_gain_grad = norm_backward(second_grad, ffn_gain, second_normed, second_inverse)
    resid_grad = upstream + resid_part
    resid_low = resid_grad.astype(lower_dtype)
    out_wgrad = jnp.einsum("tc,td->cd", attn_low, resid_low, preferred_element_type=wide_type)
    attn_grad = (
        jnp.dot(resid_low, out_back.T, preferred_element_type=wide_type)
        .astype(lower_dtype)
        .reshape(sequence_length, KEY_VALUE_HEADS, query_group_width, HEAD_DIM)
    )
    raw_again = jnp.einsum(
        "qagd,kad->agqk", query_rotated, key_rotated, preferred_element_type=wide_type
    )
    scores_again = jnp.where(allowed, raw_again * score_scale, NEG)
    probs_again = jnp.exp(scores_again - log_total)
    prob_grad = jnp.einsum(
        "qagd,kad->agqk", attn_grad, value_lowered, preferred_element_type=wide_type
    )
    row_delta = jnp.sum(probs_again * prob_grad, axis=-1, keepdims=True)
    score_grad = (probs_again * (prob_grad - row_delta) * score_scale).astype(lower_dtype)
    value_grad = (
        jnp.einsum("agqk,qagd->kad", probs_low, attn_grad, preferred_element_type=wide_type)
        .astype(lower_dtype)
        .reshape(sequence_length, KEY_VALUE_HEADS * HEAD_DIM)
    )
    query_rot_grad = jnp.einsum(
        "agqk,kad->qagd", score_grad, key_rotated, preferred_element_type=wide_type
    ).reshape(sequence_length, QUERY_HEADS, HEAD_DIM)
    key_rotated_gradient = jnp.einsum(
        "agqk,qagd->kad", score_grad, query_rotated, preferred_element_type=wide_type
    )
    query_grad = (
        reverse_rotation(query_rot_grad, cosine_lookup, sine_lookup)
        .astype(lower_dtype)
        .reshape(sequence_length, QUERY_HEADS * HEAD_DIM)
    )
    key_grad = (
        reverse_rotation(key_rotated_gradient, cosine_lookup, sine_lookup)
        .astype(lower_dtype)
        .reshape(sequence_length, KEY_VALUE_HEADS * HEAD_DIM)
    )
    query_wgrad = jnp.einsum("td,tc->dc", first_low, query_grad, preferred_element_type=wide_type)
    key_wgrad = jnp.einsum("td,tc->dc", first_low, key_grad, preferred_element_type=wide_type)
    value_wgrad = jnp.einsum("td,tc->dc", first_low, value_grad, preferred_element_type=wide_type)
    first_grad = (
        jnp.dot(query_grad, query_back.T, preferred_element_type=wide_type)
        + jnp.dot(key_grad, key_back.T, preferred_element_type=wide_type)
        + jnp.dot(value_grad, value_back.T, preferred_element_type=wide_type)
    )
    stream_part, attn_gain_grad = norm_backward(first_grad, attn_gain, first_normed, first_inverse)
    input_grad = resid_grad + stream_part
    query_part, key_part, value_part, out_part, router_part, attn_gain_part, ffn_gain_part = (
        lax.psum_scatter(
            query_wgrad.astype(jnp.bfloat16), "wshard", scatter_dimension=0, tiled=True
        ).astype(jnp.float32),
        lax.psum_scatter(
            key_wgrad.astype(jnp.bfloat16), "wshard", scatter_dimension=0, tiled=True
        ).astype(jnp.float32),
        lax.psum_scatter(
            value_wgrad.astype(jnp.bfloat16), "wshard", scatter_dimension=0, tiled=True
        ).astype(jnp.float32),
        lax.psum_scatter(
            out_wgrad.astype(jnp.bfloat16), "wshard", scatter_dimension=0, tiled=True
        ).astype(jnp.float32),
        lax.psum_scatter(
            router_wgrad.astype(jnp.bfloat16), "wshard", scatter_dimension=0, tiled=True
        ).astype(jnp.float32),
        lax.psum_scatter(
            attn_gain_grad.astype(jnp.bfloat16), "wshard", scatter_dimension=0, tiled=True
        ).astype(jnp.float32),
        lax.psum_scatter(
            ffn_gain_grad.astype(jnp.bfloat16), "wshard", scatter_dimension=0, tiled=True
        ).astype(jnp.float32),
    )
    query_sum, key_sum, value_sum, out_sum, router_sum, attn_gain_sum, ffn_gain_sum = lax.psum(
        (query_part, key_part, value_part, out_part, router_part, attn_gain_part, ffn_gain_part),
        "expert",
    )
    return (
        mixed,
        input_grad,
        attn_gain_sum,
        ffn_gain_sum,
        query_sum,
        key_sum,
        value_sum,
        out_sum,
        router_sum,
        gate_shard,
        up_shard,
        down_shard,
    )


BLOCK_OFFSETS = (-1, 1, -2, 2, -3, 3, 0, 4)


def ring_order(count):
    return [0] + list(range(1, count, 2)) + list(range(count - 2, 0, -2))


def shifted(value, step, count):
    order = ring_order(count)
    return lax.ppermute(value, "expert", [(order[i], order[(i + step) % count]) for i in range(count)])


def ahead(value, count):
    return shifted(value, 1, count)


def behind(value, count):
    return shifted(value, -1, count)


def swap_core(value):
    size = lax.axis_size("wshard")
    return lax.ppermute(value, "wshard", [(i, i ^ 1) for i in range(size)])


def swap_x(value):
    size = lax.axis_size("wshard")
    return lax.ppermute(value, "wshard", [(i, i ^ 2) for i in range(size)])


def work(flops, bytes_accessed, transcendentals):
    scale = 8
    return pl.CostEstimate(
        flops=flops // scale, bytes_accessed=bytes_accessed // scale, transcendentals=transcendentals // scale
    )


def add_low(*terms):
    return sum(term.astype(WIDE) for term in terms).astype(LOW)


def after(value, *others):
    return lax.optimization_barrier((value, *others))[0]


def places(rank_row, slots):
    rows = lax.broadcasted_iota(jnp.int32, (slots, rank_row.shape[-1]), 0)
    return rank_row == rows


def expert_ranks(routes, holds):
    tokens = routes.shape[1]
    names = [jnp.sum((routes == l).astype(WIDE), axis=0, keepdims=True) for l in range(holds)]
    names = jnp.concatenate(names + [jnp.zeros((16 - holds, tokens), WIDE)], axis=0)
    rows = lax.broadcasted_iota(jnp.int32, (tokens, tokens), 0)
    columns = lax.broadcasted_iota(jnp.int32, (tokens, tokens), 1)
    before = dot(names.astype(LOW), (rows <= columns).astype(WIDE).astype(LOW))
    return jnp.where(names > 0.0, before - 1.0, -1.0)[:holds].astype(jnp.int32)


def pack_routing(gates, routes):
    high = gates.astype(LOW).astype(WIDE)
    rows = [high, gates - high, routes.astype(WIDE)]
    spare = 16 - 3 * gates.shape[0]
    return jnp.concatenate(rows + [jnp.zeros((spare, gates.shape[1]), WIDE)], axis=0).astype(LOW)


def unpack_routing(packed):
    top_count = TOP
    packed = packed.astype(WIDE)
    return packed[:top_count] + packed[top_count : 2 * top_count], packed[2 * top_count : 3 * top_count]


def dot_t(a, b):
    return lax.dot_general(a, b, (((0,), (0,)), ((), ())), preferred_element_type=WIDE)


def dot_bt(a, b):
    return lax.dot_general(a, b, (((1,), (1,)), ((), ())), preferred_element_type=WIDE)


def dot(a, b):
    return jnp.dot(a, b, preferred_element_type=WIDE)


def expert_kernel(count, slots, aliased, *refs):
    token_ref = refs[0]
    h_refs, dz_refs = refs[1 : 1 + count], refs[1 + count : 1 + 2 * count]
    wg_ref, wu_ref, wd_ref = refs[1 + 2 * count : 4 + 2 * count]
    rest = refs[4 + 2 * count + (7 if aliased else 0) :]
    d_refs = rest[:count]
    gain_ref, rank_ref, rows_out, dz_out, gg_out, ug_out, hid_out = rest[count : count + 7]
    place_scr, back_scr, gate_scr, wg_scr, wu_scr, wd_scr, sems = rest[count + 7 :]
    e = pl.program_id(0)
    holds, tokens = rank_ref.shape[1:]
    hidden_width = wd_scr.shape[1]

    def weights(expert, slot):
        band = pl.ds(pl.multiple_of(expert * hidden_width, hidden_width), hidden_width)
        return [
            pltpu.make_async_copy(source, target.at[slot], sems.at[slot, i])
            for i, (source, target) in enumerate(
                ((wg_ref.at[:, band], wg_scr), (wu_ref.at[:, band], wu_scr), (wd_ref.at[band, :], wd_scr))
            )
        ]

    slot = lax.rem(e, 2)

    @pl.when(e == 0)
    def _():
        for copy in weights(0, 0):
            copy.start()

    @pl.when(e + 1 < holds)
    def _():
        for copy in weights(e + 1, 1 - slot):
            copy.start()

    here = pl.ds(pl.multiple_of(e * slots, slots), slots)
    @pl.when(e == 0)
    def _():
        for b, (h_ref, dz_ref) in enumerate(zip(h_refs, dz_refs)):
            gates, routes = unpack_routing(h_ref[tokens : tokens + 16, :tokens])
            routes = routes - (token_ref[1] * holds).astype(WIDE)
            ranks = expert_ranks(routes, holds)
            rank_ref[b] = ranks
            for l in range(holds):
                band = slice(l * slots, (l + 1) * slots)
                spot = places(ranks[l : l + 1], slots).astype(WIDE)
                named = jnp.where(routes == l, gates, 0.0)
                gate_scr[b, band, :] = jnp.broadcast_to(
                    jnp.sum(spot * jnp.sum(named, axis=0, keepdims=True), axis=1, keepdims=True), (slots, 128)
                )
                place_scr[b, band, :] = spot.astype(LOW)
            for source, target in ((h_ref, rows_out), (dz_ref, dz_out)):
                taken = dot(place_scr[b], source[:tokens]).astype(LOW)
                for l in range(holds):
                    target[l, b * slots : (b + 1) * slots, :] = taken[l * slots : (l + 1) * slots]

    gate = jnp.concatenate([gate_scr[b, here, :] for b in range(count)], axis=0)[:, :1]
    rows = rows_out[e]
    for copy in weights(e, slot):
        copy.wait()
    gate_pre = dot(rows, wg_scr[slot])
    up_pre = dot(rows, wu_scr[slot])
    sig = jax.nn.sigmoid(gate_pre)
    silu = gate_pre * sig
    hidden = (silu * up_pre).astype(LOW).astype(WIDE)
    back = dot_bt(dz_out[e], wd_scr[slot])
    gains = jnp.sum(back * hidden, axis=1, keepdims=True)
    back = back * gate
    gate_grad = (back * (up_pre * sig * (1.0 + gate_pre * (1.0 - sig)))).astype(LOW)
    up_grad = (back * silu).astype(LOW)
    gg_out[0] = gate_grad
    ug_out[0] = up_grad
    hid_out[0] = (hidden * gate).astype(LOW)
    row_grad = (dot_bt(gate_grad, wg_scr[slot]) + dot_bt(up_grad, wu_scr[slot])).astype(LOW)
    for b in range(count):
        band = slice(b * slots, (b + 1) * slots)
        back_scr[b, here, :] = row_grad[band]
        spot = place_scr[b, here, :].astype(WIDE)
        gain_ref[b, pl.ds(e, 1), :] = jnp.sum(spot * gains[band], axis=0, keepdims=True)

    @pl.when(e == pl.num_programs(0) - 1)
    def _():
        for b in range(count):
            d_refs[b][...] = dot_t(place_scr[b], back_scr[b]).astype(LOW)


def expert_call(token, first, blocks, dz_blocks, w_gate, w_up, w_down, kept, holds, slots, total):
    count = len(blocks)
    tokens, width = dz_blocks[0].shape
    hidden = w_gate.shape[1] // holds
    whole = lambda *shape: pl.BlockSpec(shape, lambda e: (0,) * len(shape))
    once = lambda *shape: pl.BlockSpec(shape, lambda e: (0,) * len(shape), pipeline_mode=pl.Buffered(buffer_count=1))
    aliased = kept is not None
    in_specs = (
        [pl.BlockSpec(memory_space=pltpu.SMEM)]
        + [once(*b.shape) for b in (*blocks, *dz_blocks)]
        + [pl.BlockSpec(memory_space=pl.ANY)] * 3
    )
    aliases = {len(in_specs) + i: count + i for i in range(7)} if aliased else {}
    out = pl.pallas_call(
        functools.partial(expert_kernel, count, slots, aliased),
        grid=(holds,),
        in_specs=in_specs + ([pl.BlockSpec(memory_space=pl.ANY)] * 7 if aliased else []),
        out_specs=[whole(tokens, width)] * count
        + [pl.BlockSpec((count, holds, tokens), lambda e: (first // count, 0, 0))] * 2
        + [pl.BlockSpec((holds, count * slots, width), lambda e: (0, first // count, 0))] * 2
        + [pl.BlockSpec((1, count * slots, hidden), lambda e: (e, first // count, 0))] * 3,
        out_shape=[shaped(tokens, width)] * count
        + [shaped(total, holds, tokens, dtype=WIDE), shaped(total, holds, tokens, dtype=jnp.int32)]
        + [shaped(holds, total * slots, width)] * 2
        + [shaped(holds, total * slots, hidden)] * 3,
        scratch_shapes=[
            pltpu.VMEM((count, holds * slots, tokens), LOW),
            pltpu.VMEM((count, holds * slots, width), LOW),
            pltpu.VMEM((count, holds * slots, 128), WIDE),
            pltpu.VMEM((2, width, hidden), LOW),
            pltpu.VMEM((2, width, hidden), LOW),
            pltpu.VMEM((2, hidden, width), LOW),
            pltpu.SemaphoreType.DMA((2, 3)),
        ],
        input_output_aliases=aliases,
        compiler_params=pltpu.CompilerParams(vmem_limit_bytes=VMEM_MOST),
        cost_estimate=work(
            flops=2 * holds * count * slots * width * (5 * hidden + 3 * tokens),
            bytes_accessed=3 * holds * width * hidden * 2
            + count * tokens * width * 6
            + holds * count * slots * (2 * width + 3 * hidden) * 2,
            transcendentals=holds * count * slots * hidden,
        ),
    )(token, *blocks, *dz_blocks, w_gate, w_up, w_down, *(kept if aliased else ()))
    return out[:count], tuple(out[count:])


def value_kernel(slots, _, rank_ref, hid_ref, wd_ref, *refs):
    total, holds, tokens = rank_ref.shape
    y_refs, (value_scr, place_scr) = refs[:total], refs[total:]
    e = pl.program_id(0)
    here = pl.ds(pl.multiple_of(e * slots, slots), slots)
    value = dot(hid_ref[0], wd_ref[...]).astype(LOW)
    for b in range(total):
        value_scr[b, here, :] = value[b * slots : (b + 1) * slots]

    @pl.when(e == pl.num_programs(0) - 1)
    def _():
        for b in range(total):
            for l in range(holds):
                spot = places(rank_ref[b, l : l + 1, :], slots)
                place_scr[l * slots : (l + 1) * slots, :] = spot.astype(WIDE).astype(LOW)
            y_refs[b][...] = dot_t(place_scr[...], value_scr[b]).astype(LOW)


def value_call(token, rank, hidden_rows, w_down, slots):
    total, holds, tokens = rank.shape
    width = w_down.shape[1]
    hidden = hidden_rows.shape[2]
    whole = lambda *shape: pl.BlockSpec(shape, lambda e: (0,) * len(shape))
    out = pl.pallas_call(
        functools.partial(value_kernel, slots),
        grid=(holds,),
        in_specs=[
            pl.BlockSpec(memory_space=pltpu.SMEM),
            whole(*rank.shape),
            pl.BlockSpec((1, total * slots, hidden), lambda e: (e, 0, 0)),
            pl.BlockSpec((hidden, width), lambda e: (e, 0)),
        ],
        out_specs=[whole(tokens, width)] * total,
        out_shape=[shaped(tokens, width)] * total,
        scratch_shapes=[pltpu.VMEM((total, holds * slots, width), LOW), pltpu.VMEM((holds * slots, tokens), LOW)],
        compiler_params=pltpu.CompilerParams(vmem_limit_bytes=VMEM_MOST),
        cost_estimate=work(
            flops=2 * total * holds * slots * width * (hidden + tokens),
            bytes_accessed=2 * (holds * hidden * (width + total * slots) + total * tokens * width),
            transcendentals=0,
        ),
    )(token, rank, hidden_rows, w_down)
    return out


def wgrad_kernel(apart, place_ref, rows_ref, dz_ref, gg_ref, ug_ref, hid_ref, *outs):
    step = pl.program_id(0)
    shard = outs[0].shape[1]
    columns = pl.ds(pl.multiple_of(jnp.bitwise_xor(place_ref[0], step) * shard, 128), shard)
    rows, grads = rows_ref[0, :, columns], dz_ref[0, :, columns]
    parts = [dot_t(rows, gg_ref[0]), dot_t(rows, ug_ref[0]), dot_t(grads, hid_ref[0])]
    parts = [part.astype(LOW) for part in parts]
    for s in range(4):

        @pl.when(step == s)
        def _():
            for i, part in enumerate(parts):
                if s == 3 and apart:
                    outs[3 + i][...] = part
                elif s % 2 and not apart:
                    outs[2][3 - 3 * (s // 2) + i] = part
                else:
                    outs[s if apart else s // 2][i] = part


def wgrad_call(expert, place, kept, apart=False):
    _, count, width = kept[0].shape
    hidden = kept[2].shape[2]
    shard = width // 4
    row_spec = lambda d: pl.BlockSpec((1, count, d), lambda s: (expert, 0, 0), pipeline_mode=pl.Buffered(buffer_count=1))
    shapes = [(3, shard, hidden)] * 3 + [(shard, hidden)] * 3 if apart else [(3, shard, hidden)] * 2 + [(6, shard, hidden)]
    out = pl.pallas_call(
        functools.partial(wgrad_kernel, apart),
        grid=(4,),
        in_specs=[pl.BlockSpec(memory_space=pltpu.SMEM), row_spec(width), row_spec(width)] + [row_spec(hidden)] * 3,
        out_specs=[pl.BlockSpec(shape, lambda s, zeros=(0,) * len(shape): zeros) for shape in shapes],
        out_shape=[shaped(*shape) for shape in shapes],
        compiler_params=pltpu.CompilerParams(vmem_limit_bytes=VMEM_MOST),
        cost_estimate=work(
            flops=2 * count * width * 3 * hidden,
            bytes_accessed=2 * (count * (2 * width + 3 * hidden) + 3 * width * hidden),
            transcendentals=0,
        ),
    )(place, *kept)
    return (out[0], out[2], out[3:], out[1]) if apart else out


def sums_call(gates, *sums):
    every = [term[0] if isinstance(term, tuple) else term for terms in sums for term in terms]

    def part_of(term, ready=()):
        array, part = term if isinstance(term, tuple) else (term, None)
        array = after(array, *ready) if ready else array
        return array if part is None else array[: len(part)] if isinstance(part, range) else array[part]

    totals = [add_low(part_of(terms[0], (*gates, *every)), *map(part_of, terms[1:])) for terms in sums]
    return totals


def finish_kernel(sizes, *refs):
    outs = refs[-3:]
    at = 0
    for i, out in enumerate(outs):
        total = sum(ref[...].astype(WIDE) for ref in refs[at : at + sizes[i]])
        at += sizes[i]
        out[...] = total if i < 2 else jnp.transpose(total)


def finish_call(expert, holds, terms, kept):
    shard, hidden = terms[0][0][0].shape[1:]
    steps = shard // 128
    wide, tall = shaped(shard, holds * hidden, dtype=WIDE), shaped(holds * hidden, shard, dtype=WIDE)
    flat = [term for group in terms for term in group]
    return pl.pallas_call(
        functools.partial(finish_kernel, [len(group) for group in terms]),
        grid=(steps,),
        in_specs=[
            pl.BlockSpec((128, hidden), lambda s: (s, 0))
            if at is None
            else pl.BlockSpec((None, 128, hidden), lambda s, at=at: (at, s, 0))
            for _, at in flat
        ]
        + ([pl.BlockSpec(memory_space=pl.ANY)] * 3 if kept else []),
        out_specs=[pl.BlockSpec((128, hidden), lambda s: (s, expert))] * 2
        + [pl.BlockSpec((hidden, 128), lambda s: (expert, s))],
        out_shape=[wide, wide, tall],
        input_output_aliases={len(flat) + i: i for i in range(3)} if kept else {},
        compiler_params=pltpu.CompilerParams(vmem_limit_bytes=VMEM_MOST),
        cost_estimate=work(flops=0, bytes_accessed=30 * shard * hidden, transcendentals=0),
    )(*[array for array, _ in flat], *(kept or ()))


def piece_columns(mine, s, shard):
    return pl.ds(pl.multiple_of(jnp.bitwise_xor(mine, s) * shard, 128), shard)


def turn(values, cos, sin):
    return values * cos + pltpu.roll(values, HEAD_DIM // 2, 1) * sin


def turn_back(values, cos, sin):
    return values * cos - pltpu.roll(values, HEAD_DIM // 2, 1) * sin


def inverse_rms(values):
    return lax.rsqrt(jnp.mean(values * values, axis=-1, keepdims=True) + EPS)


def head_slice(h):
    return slice(h * HEAD_DIM, (h + 1) * HEAD_DIM)


def stacked_heads(ref, band, group, heads):
    return jnp.concatenate([ref[band, head_slice(group * heads + h)] for h in range(heads)], axis=0)


def probabilities(queries, keys, allowed):
    scores = jnp.where(allowed, dot_bt(queries, keys) * HEAD_DIM ** (-0.5), NEG)
    expo = jnp.exp(scores - jnp.max(scores, axis=-1, keepdims=True))
    return expo * (1.0 / jnp.sum(expo, axis=-1, keepdims=True))


def allowed_pairs(seg_col_ref, seg_row_ref, band, reach, heads):
    size = band.stop - band.start
    rows = band.start + lax.broadcasted_iota(jnp.int32, (size, reach), 0)
    cols = lax.broadcasted_iota(jnp.int32, (size, reach), 1)
    ok = (seg_col_ref[band, :] == seg_row_ref[:, :reach]) & (cols <= rows)
    return jnp.concatenate([ok] * heads, axis=0)


def attention_kernel(
    mine_ref, tokens_ref, gain_ref, p0, p1, p2, p3, s0, s1, s2, s3, seg_row_ref, seg_col_ref, cos_ref, sin_ref,
    h_ref, q_ref, k_ref, v_ref, out_ref,
):
    mine = mine_ref[0]
    stream = tokens_ref[...].astype(WIDE)
    h_ref[...] = (stream * inverse_rms(stream) * gain_ref[...]).astype(LOW)
    shard = p0.shape[0]
    width = q_ref.shape[1]
    cos, sin = cos_ref[...], sin_ref[...]

    def projected(pieces, columns):
        return sum(dot(h_ref[:, piece_columns(mine, s, shard)], piece[:, columns]) for s, piece in enumerate(pieces))

    heads = QUERY_HEADS // KEY_VALUE_HEADS
    key_width = KEY_VALUE_HEADS * HEAD_DIM
    shared = (s0, s1, s2, s3)
    keys = projected(shared, slice(0, key_width))
    for g in range(KEY_VALUE_HEADS):
        k_ref[:, head_slice(g)] = turn(keys[:, head_slice(g)], cos, sin).astype(LOW)
    v_ref[...] = projected(shared, slice(key_width, 2 * key_width)).astype(LOW)
    group_width = heads * HEAD_DIM
    for g in range(KEY_VALUE_HEADS):
        queries = projected((p0, p1, p2, p3), slice(g * group_width, (g + 1) * group_width))
        for h in range(heads):
            q_ref[:, head_slice(g * heads + h)] = turn(queries[:, head_slice(h)], cos, sin).astype(LOW)
    length = q_ref.shape[0]
    tile = 128
    for start in range(0, length, tile):
        band, reach = slice(start, start + tile), start + tile
        allowed = allowed_pairs(seg_col_ref, seg_row_ref, band, reach, heads)
        for g in range(KEY_VALUE_HEADS):
            probs = probabilities(stacked_heads(q_ref, band, g, heads), k_ref[:reach, head_slice(g)], allowed)
            mixed = dot(probs.astype(LOW), v_ref[:reach, head_slice(g)]).astype(LOW)
            for h in range(heads):
                out_ref[band, head_slice(g * heads + h)] = mixed[h * tile : (h + 1) * tile]


def vmem_call(kernel, out_shape, flops, transcendentals, token, *args):
    moved = sum(a.size * a.dtype.itemsize for a in args) + sum(
        o.size * o.dtype.itemsize for o in jax.tree.leaves(out_shape)
    )
    return pl.pallas_call(
        kernel,
        in_specs=[pl.BlockSpec(memory_space=pltpu.SMEM)] + [pl.BlockSpec(memory_space=pltpu.VMEM)] * len(args),
        out_specs=[pl.BlockSpec(memory_space=pltpu.VMEM)] * len(out_shape),
        out_shape=out_shape,
        compiler_params=pltpu.CompilerParams(vmem_limit_bytes=VMEM_MOST),
        cost_estimate=work(flops=flops, bytes_accessed=moved, transcendentals=transcendentals),
    )(token, *args)


def shaped(*shape, dtype=LOW):
    return jax.ShapeDtypeStruct(shape, dtype)


def attention_call(mine, tokens, gain, pieces, shared_pieces, seg_row, seg_col, cos, sin):
    length, width = tokens.shape
    key_width = KEY_VALUE_HEADS * HEAD_DIM
    return vmem_call(
        attention_kernel,
        [shaped(length, width), shaped(length, width), shaped(length, key_width), shaped(length, key_width), shaped(length, width)],
        2 * length * width * (width + 2 * key_width) + 3 * length * length * width,
        QUERY_HEADS * length * length,
        mine, tokens, gain, *pieces, *shared_pieces, seg_row, seg_col, cos, sin,
    )


def project_kernel(
    mine_ref, tokens_ref, attn_ref, p0, p1, p2, p3, r0, r1, r2, r3, gain_ref, routes_ref, resid_ref, h_ref
):
    mine = mine_ref[0]
    shard = p0.shape[0]
    resid = tokens_ref[...].astype(WIDE)
    for s, piece in enumerate((p0, p1, p2, p3)):
        resid = resid + dot(attn_ref[:, piece_columns(mine, s, shard)], piece[...])
    resid_ref[...] = resid
    length, width = resid.shape
    h_ref[:length] = (resid * inverse_rms(resid) * gain_ref[...]).astype(LOW)
    logits = jnp.transpose(
        sum(
            dot(h_ref[:length, piece_columns(mine, s, shard)], piece[...])
            for s, piece in enumerate((r0, r1, r2, r3))
        )
    )
    experts = lax.broadcasted_iota(jnp.int32, logits.shape, 0)
    picked = [
        jnp.sum(jnp.where(experts == routes_ref[k : k + 1, :], logits, 0.0), axis=0, keepdims=True)
        for k in range(routes_ref.shape[0])
    ]
    top = functools.reduce(jnp.maximum, picked)
    expo = [jnp.exp(p - top) for p in picked]
    total = sum(expo)
    gates = jnp.concatenate([x / total for x in expo], axis=0)
    h_ref[length:] = jnp.zeros((16, width), LOW)
    h_ref[length:, :length] = pack_routing(gates, routes_ref[...])


def project_call(mine, tokens, attn, pieces, shared_pieces, gain, routes_t):
    length, width = tokens.shape
    whole = lambda shape: pl.BlockSpec(shape, lambda i: (0,) * len(shape))
    shapes = [shaped(length, width, dtype=WIDE), shaped(length + 16, width)]
    return pl.pallas_call(
        project_kernel,
        grid=(1,),
        in_specs=[pl.BlockSpec(memory_space=pltpu.SMEM)]
        + [whole(a.shape) for a in (tokens, attn, *pieces)]
        + router_columns(shared_pieces)
        + [whole(gain.shape), whole(routes_t.shape)],
        out_specs=[whole(s.shape) for s in shapes],
        out_shape=shapes,
        compiler_params=pltpu.CompilerParams(vmem_limit_bytes=VMEM_MOST),
        cost_estimate=work(
            flops=2 * length * width * (width + EXPERTS), bytes_accessed=length * width * 20, transcendentals=length * 8
        ),
    )(mine, tokens, attn, *pieces, *shared_pieces, gain, routes_t)


def as_column(row):
    return jnp.transpose(jnp.broadcast_to(row, (8, row.shape[1])))[:, :1]


def norm_back(grad, gain, normed, inverse):
    scaled = grad * gain
    return inverse * (scaled - normed * jnp.mean(scaled * normed, axis=-1, keepdims=True))


def shard_parts(targets):
    at, parts = 0, []
    for target in targets:
        parts.append((target, slice(at, at + target.shape[0])))
        at += target.shape[0]
    return parts


def resid_back_kernel(
    mine_ref, resid_ref, gain_ref, dz_ref, t0, t1, t2, gains_ref, h_ref, attn_ref,
    p0, p1, p2, p3, r0, r1, r2, r3, grad_ref, attn_grad_ref, small_ref, o0, o1, o2, o3, o4, o5, second_scr, low_scr,
):
    mine = mine_ref[0]
    shard, width = p0.shape
    length = resid_ref.shape[0]
    routers = (r0, r1, r2, r3)
    gains = gains_ref[...]
    experts = lax.broadcasted_iota(jnp.int32, gains.shape, 0)
    gate_rows, routes = unpack_routing(h_ref[length:, :length])
    gates = jnp.zeros(gains.shape, WIDE)
    for k in range(TOP):
        gates = gates + jnp.where(experts.astype(WIDE) == routes[k : k + 1], gate_rows[k : k + 1], 0.0)
    logit_grad = gates * (gains - jnp.sum(gates * gains, axis=0, keepdims=True))
    logit_grad = jnp.concatenate([logit_grad, jnp.zeros((128 - EXPERTS, length), WIDE)], axis=0)
    logit_grad = jnp.transpose(logit_grad).astype(LOW)
    second_scr[...] = t0[...].astype(WIDE) + t1[...].astype(WIDE) + t2[...].astype(WIDE)
    for s, piece in enumerate(routers):
        columns = piece_columns(mine, s, shard)
        second_scr[:, columns] = second_scr[:, columns] + dot_bt(logit_grad, piece[...])
    resid = resid_ref[...]
    inverse = inverse_rms(resid)
    normed = resid * inverse
    second = second_scr[...]
    gain_grad = jnp.sum(second * normed, axis=0, keepdims=True)
    grad = dz_ref[...].astype(WIDE) + norm_back(second, gain_ref[...], normed, inverse)
    grad_ref[...] = grad
    low_scr[...] = grad.astype(LOW)
    second_scr[:1, :] = gain_grad
    low = low_scr[...]
    for s, piece in enumerate((p0, p1, p2, p3)):
        columns = piece_columns(mine, s, shard)
        attn_grad_ref[:, columns] = dot_bt(low, piece[...]).astype(LOW)
        out_part = dot_t(attn_ref[:, columns], low).astype(LOW)
        router_part = dot_t(h_ref[:length, columns], logit_grad)
        lanes = lax.broadcasted_iota(jnp.int32, router_part.shape, 1)
        small_ref[s] = jnp.where(lanes == EXPERTS, as_column(second_scr[:1, columns]), router_part).astype(LOW)
        for target, rows in shard_parts(((o0,), (o1,), (o2, o3), (o4, o5))[s]):
            target[...] = out_part[rows]


def router_columns(pieces):
    return [pl.BlockSpec((p.shape[0], 128), lambda i, at=p.shape[1] // 128 - 1: (0, at)) for p in pieces]


def resid_back_call(mine, resid, gain, dz, terms, gains, h, attn, pieces, shared_pieces):
    length, width = resid.shape
    shard = pieces[0].shape[0]
    whole = lambda shape: pl.BlockSpec(shape, lambda i: (0,) * len(shape))
    arrays = (resid, gain, dz, *terms, gains, h, attn, *pieces)
    shapes = [shaped(length, width, dtype=WIDE), shaped(length, width), shaped(4, shard, 128)]
    shapes += [shaped(shard, width)] * 2 + [shaped(shard // 2, width)] * 4
    return pl.pallas_call(
        resid_back_kernel,
        grid=(1,),
        in_specs=[pl.BlockSpec(memory_space=pltpu.SMEM)]
        + [whole(a.shape) for a in arrays]
        + router_columns(shared_pieces),
        out_specs=[whole(s.shape) for s in shapes],
        out_shape=shapes,
        scratch_shapes=[pltpu.VMEM((length, width), WIDE), pltpu.VMEM((length, width), LOW)],
        compiler_params=pltpu.CompilerParams(vmem_limit_bytes=VMEM_MOST),
        cost_estimate=work(
            flops=4 * length * width * (width + EXPERTS), bytes_accessed=length * width * 40, transcendentals=0
        ),
    )(mine, *arrays, *shared_pieces)


def attention_back_kernel(
    mine_ref, q_ref, k_ref, v_ref, do_ref, h_ref, tokens_ref, gain_ref, grad_ref, small_ref, p0, p1, p2, p3, s0, s1, s2, s3,
    seg_row_ref, seg_col_ref, cos_ref, sin_ref, input_ref, o0, o1, o2, o3, o4, o5, qkv_scr, dk_scr, dv_scr, dh_scr,
):
    mine = mine_ref[0]
    length, width = q_ref.shape
    shard = p0.shape[0]
    qkv_width = width + 2 * KEY_VALUE_HEADS * HEAD_DIM
    heads = QUERY_HEADS // KEY_VALUE_HEADS
    key_width = KEY_VALUE_HEADS * HEAD_DIM
    tile = 128
    dk_scr[...] = jnp.zeros_like(dk_scr)
    dv_scr[...] = jnp.zeros_like(dv_scr)
    for start in range(0, length, tile):
        band, reach = slice(start, start + tile), start + tile
        allowed = allowed_pairs(seg_col_ref, seg_row_ref, band, reach, heads)
        cos, sin = cos_ref[band, :], sin_ref[band, :]
        for g in range(KEY_VALUE_HEADS):
            queries = stacked_heads(q_ref, band, g, heads)
            grads = stacked_heads(do_ref, band, g, heads)
            keys = k_ref[:reach, head_slice(g)]
            probs = probabilities(queries, keys, allowed)
            prob_grad = dot_bt(grads, v_ref[:reach, head_slice(g)])
            delta = jnp.sum(probs * prob_grad, axis=-1, keepdims=True)
            score_grad = (probs * (prob_grad - delta) * HEAD_DIM ** (-0.5)).astype(LOW)
            dv_scr[:reach, head_slice(g)] += dot_t(probs.astype(LOW), grads)
            dk_scr[:reach, head_slice(g)] += dot_t(score_grad, queries)
            dq = dot(score_grad, keys)
            for h in range(heads):
                qkv_scr[band, head_slice(g * heads + h)] = turn_back(dq[h * tile : (h + 1) * tile], cos, sin).astype(LOW)
    for g in range(KEY_VALUE_HEADS):
        at = width + g * HEAD_DIM
        qkv_scr[:, at : at + HEAD_DIM] = turn_back(dk_scr[:, head_slice(g)], cos_ref[...], sin_ref[...]).astype(LOW)
    qkv_scr[:, width + key_width :] = dv_scr[...].astype(LOW)
    qkv = qkv_scr[...]
    for s, (piece, shared) in enumerate(zip((p0, p1, p2, p3), (s0, s1, s2, s3))):
        dh_scr[:, piece_columns(mine, s, shard)] = dot_bt(qkv[:, :width], piece[...]) + dot_bt(qkv[:, width:], shared[:, : 2 * key_width])
    stream = tokens_ref[...].astype(WIDE)
    inverse = inverse_rms(stream)
    normed = stream * inverse
    first = dh_scr[...]
    gain_grad = jnp.sum(first * normed, axis=0, keepdims=True)
    input_ref[...] = grad_ref[...] + norm_back(first, gain_ref[...], normed, inverse)
    dh_scr[:1, :] = gain_grad
    for s in range(4):
        columns = piece_columns(mine, s, shard)
        part = dot_t(h_ref[:, columns], qkv).astype(LOW)
        small = small_ref[s].astype(WIDE)
        lanes = lax.broadcasted_iota(jnp.int32, small.shape, 1)
        small = jnp.where(lanes == EXPERTS + 1, as_column(dh_scr[:1, columns]), small).astype(LOW)
        for target, rows in shard_parts(((o0,), (o1,), (o2, o3), (o4, o5))[s]):
            target[:, :qkv_width] = part[rows]
            target[:, qkv_width:] = small[rows]


def attention_back_call(
    mine, q, k, v, do, h, tokens, gain, grad, small, pieces, shared_pieces, seg_row, seg_col, cos, sin
):
    length, width = q.shape
    shard = pieces[0].shape[0]
    qkv_width = width + 2 * KEY_VALUE_HEADS * HEAD_DIM
    key_width = KEY_VALUE_HEADS * HEAD_DIM
    return pl.pallas_call(
        attention_back_kernel,
        in_specs=[pl.BlockSpec(memory_space=pltpu.SMEM)] + [pl.BlockSpec(memory_space=pltpu.VMEM)] * 21,
        out_specs=[pl.BlockSpec(memory_space=pltpu.VMEM)] * 7,
        out_shape=[shaped(length, width, dtype=WIDE)]
        + [shaped(shard, qkv_width + 128)] * 2
        + [shaped(shard * 2 // 3, qkv_width + 128), shaped(shard // 3, qkv_width + 128)] * 2,
        scratch_shapes=[
            pltpu.VMEM((length, qkv_width), LOW),
            pltpu.VMEM((length, key_width), WIDE),
            pltpu.VMEM((length, key_width), WIDE),
            pltpu.VMEM((length, width), WIDE),
        ],
        compiler_params=pltpu.CompilerParams(vmem_limit_bytes=VMEM_MOST),
        cost_estimate=work(
            flops=4 * length * width * qkv_width + 7 * length * length * width,
            bytes_accessed=length * width * 40,
            transcendentals=QUERY_HEADS * length * length,
        ),
    )(mine, q, k, v, do, h, tokens, gain, grad, small, *pieces, *shared_pieces, seg_row, seg_col, cos, sin)


def spread_kernel(count, token_ref, *refs):
    parts, outs, scratch = refs[2 : -count - 1], refs[-count - 1 : -1], refs[-1]
    for part, rows in shard_parts(parts):
        scratch[rows] = part[...]
    chunk = outs[0].shape[0]
    for j, out in enumerate(outs):
        rows = pl.ds(pl.multiple_of(lax.rem(token_ref[2] + j, count) * chunk, 16), chunk)
        out[...] = sum(term[rows, :].astype(WIDE) for term in (*refs[:2], scratch)).astype(LOW)


def spread_call(token, count, *terms):
    rows, width = terms[0].shape
    whole = lambda shape: pl.BlockSpec(shape, lambda i: (0, 0))
    return pl.pallas_call(
        functools.partial(spread_kernel, count),
        grid=(1,),
        in_specs=[pl.BlockSpec(memory_space=pltpu.SMEM)] + [whole(t.shape) for t in terms],
        out_specs=[whole((rows // count, width))] * count,
        out_shape=[shaped(rows // count, width)] * count,
        scratch_shapes=[pltpu.VMEM((rows, width), LOW)],
        compiler_params=pltpu.CompilerParams(vmem_limit_bytes=VMEM_MOST),
        cost_estimate=work(flops=0, bytes_accessed=8 * rows * width, transcendentals=0),
    )(token, *terms)


def assemble_kernel(count, widths, token_ref, *refs):
    chunks, outs = refs[:count], refs[count:]
    chunk = chunks[0].shape[0]
    for j, ref in enumerate(chunks):
        rows = pl.ds(pl.multiple_of(lax.rem(token_ref[2] + j, count) * chunk, 16), chunk)
        values = ref[...].astype(WIDE)
        at = 0
        for width, out in zip(widths, outs):
            out[rows, :] = values[:, at : at + width]
            at += width
        if len(outs) > len(widths):
            outs[-1][rows, :] = values[:, at : at + 128]
    if len(outs) > len(widths):
        router_ref, ffn_ref, attn_ref, scratch = outs[len(widths) :]
        small = jnp.transpose(scratch[...])
        router_ref[...] = small[:EXPERTS]
        ffn_ref[...] = small[EXPERTS]
        attn_ref[...] = small[EXPERTS + 1]


def assemble_call(token, chunks, widths):
    count, (rows, width) = len(chunks), chunks[0].shape
    whole = lambda shape: pl.BlockSpec(shape, lambda i: (0,) * len(shape))
    small = width > sum(widths)
    shapes = [(count * rows, w) for w in widths]
    shapes += [(EXPERTS, count * rows), (count * rows,), (count * rows,)] if small else []
    return pl.pallas_call(
        functools.partial(assemble_kernel, count, widths),
        grid=(1,),
        in_specs=[pl.BlockSpec(memory_space=pltpu.SMEM)] + [whole((rows, width))] * count,
        out_specs=[whole(shape) for shape in shapes],
        out_shape=[shaped(*shape, dtype=WIDE) for shape in shapes],
        scratch_shapes=[pltpu.VMEM((count * rows, 128), WIDE)] if small else [],
        compiler_params=pltpu.CompilerParams(vmem_limit_bytes=VMEM_MOST),
        cost_estimate=work(flops=0, bytes_accessed=6 * count * rows * width, transcendentals=0),
    )(token, *chunks)


def per_device_ring(
    tokens,
    segments,
    routes,
    attn_gain,
    ffn_gain,
    w_query,
    key_weight,
    value_weight,
    w_out,
    w_router,
    w_gate,
    w_up,
    w_down,
    cotangent,
):
    length, model_width = tokens.shape
    top_count = routes.shape[1]
    count = lax.axis_size("expert")
    holds = EXPERTS // count
    capacity = max(2, 3 * length * top_count // (2 * EXPERTS))
    slots = -(-capacity // 16) * 16
    shard = model_width // 4
    key_width = KEY_VALUE_HEADS * HEAD_DIM
    half = length // 2
    mine = lax.axis_index("wshard").astype(jnp.int32)
    order = jnp.array(ring_order(count), jnp.int32)
    spot_of = jnp.array([ring_order(count).index(i) for i in range(count)], jnp.int32)
    here = lax.axis_index("expert").astype(jnp.int32)
    spot = spot_of[here]
    token = jnp.stack([mine, here, spot])
    routes_t = routes.T

    cosine, sine = rotary_tables(length, HEAD_DIM)
    cos = jnp.concatenate([cosine, cosine], axis=1)
    sin = jnp.concatenate([-sine, sine], axis=1)
    seg_col = segments.reshape(length, 1)
    gain_one, gain_two = attn_gain[None], ffn_gain[None]

    def pieces_of(own, across, *ready):
        return (own, swap_core(own), across, swap_core(after(across, *ready)))

    dz = {0: cotangent}
    dz[-1], dz[1] = ahead(dz[0], count), behind(dz[0], count)
    query_across = swap_x(w_query)
    query_pieces = pieces_of(w_query, query_across)
    spare = jnp.zeros((shard, 128 - EXPERTS), LOW)
    shared = jnp.concatenate([key_weight, value_weight, w_router, spare], axis=1)
    shared, token, seg_col, cos, sin, routes_t, gain_one, gain_two = lax.optimization_barrier(
        (shared, token, seg_col, cos, sin, routes_t, gain_one, gain_two)
    )
    shared_across = swap_x(after(shared, query_across, dz[-1], dz[1]))
    dz[-2], dz[2] = ahead(dz[-1], count), behind(dz[1], count)
    shared_pieces = pieces_of(shared, shared_across)
    out_across = swap_x(after(w_out, shared_across))

    first_low, query, key, value, attn = attention_call(
        after(token, dz[-2], dz[2]), tokens, gain_one, query_pieces, shared_pieces, segments, seg_col, cos, sin
    )
    out_pieces = pieces_of(w_out, out_across, attn)
    dz[-3], dz[3] = ahead(dz[-2], count), behind(dz[2], count)
    resid, second = project_call(after(token, dz[-3], dz[3]), tokens, attn, out_pieces, shared_pieces, gain_two, routes_t)

    def experts(ready, first, offsets, kept):
        return expert_call(
            after(token, *ready), first, [h[j] for j in offsets], [dz[j] for j in offsets], w_gate, w_up, w_down, kept,
            holds, slots, count,
        )

    h = {0: second}
    h[-1], h[1] = ahead(h[0], count), behind(h[0], count)
    (d_own,), kept = experts((), 6, (0,), None)
    h[-2], h[2] = ahead(after(h[-1], d_own), count), behind(after(h[1], d_own), count)
    (d_l1, d_r1), kept = experts((), 0, (-1, 1), kept)
    h[-3], h[3] = ahead(after(h[-2], d_l1), count), behind(after(h[2], d_l1), count)
    (d_l2, d_r2), kept = experts((), 2, (-2, 2), kept)
    h[4], dz[4] = ahead(after(h[-3], d_l2), count), behind(after(dz[3], d_l2), count)
    (d_l3, d_r3), kept = experts((), 4, (-3, 3), kept)
    (d_far,), (gains, rank, *kept) = experts((), 7, (4,), kept)

    block_of = jnp.array([BLOCK_OFFSETS.index(j if j <= count // 2 else j - count) for j in range(count)], jnp.int32)
    gain_send = gains[block_of[(spot_of - spot) % count]]

    def weight_grads(expert, *ready):
        return wgrad_call(expert, after(token, *ready), kept)

    def over_cores(grads, *ready):
        return swap_core(after(grads[2], *ready))

    both, last = range(2), 2

    def sum_of(grads, got, part):
        return (grads[1], part), (got, part)

    up_sent, down_sent = ahead(d_far, count), behind(d_l3, count)
    grads = [wgrad_call(0, token, kept, True)]
    got = [[swap_core(v) for v in grads[0][2]]]
    grads.append(weight_grads(1, grads[0][0]))
    up, down = sums_call((grads[1][0], *got[0],), (d_r3, up_sent), (d_l2, down_sent))

    up_sent, down_sent = ahead(up, count), behind(down, count)
    got.append(over_cores(grads[1], up))
    halves = [sums_call((up,), *[((grads[0][1], i), got[0][i]) for i in range(3)])]
    across = [[(swap_x(v), None) for v in halves[0][:2]]]
    gain_dense = lax.all_to_all(after(gain_send, halves[0][0]), "expert", split_axis=0, concat_axis=0, tiled=True)
    gain_dense = gain_dense.reshape(EXPERTS, length)
    grads.append(weight_grads(2, gain_send, *halves[0]))
    up, down = sums_call((gain_dense, grads[2][0], across[0][0][0], across[0][1][0],), (d_r2, up_sent), (d_l1, down_sent))

    up_sent, down_sent = ahead(up, count), behind(down, count)
    got.append(over_cores(grads[2], up))
    halves.append(sums_call((up,), sum_of(grads[1], got[1], both), sum_of(grads[1], got[1], last)))
    across_b = swap_x(halves[1][0])
    y = dict(zip(BLOCK_OFFSETS, value_call(after(token, *halves[1]), rank, kept[4], w_down, slots)))
    late = swap_core(after(grads[0][3], up))
    (up,) = sums_call((y[0], across_b, down_sent, late), (d_r1, up_sent))

    up_sent, y_down = ahead(up, count), behind(after(y[4], up), count)
    across[0].append((swap_x(after(halves[0][2], up)), None))
    across.append([(across_b, 0), (across_b, 1), (swap_x(after(halves[1][1], up)), None)])
    halves.append(sums_call((up,), sum_of(grads[2], got[2], both), sum_of(grads[2], got[2], last)))
    grads.append(weight_grads(3, *halves[2]))
    (down,) = sums_call(
        (up_sent, across[0][2][0], across[1][2][0], grads[3][0]), (y[-3], y_down)
    )

    y_up, y_down, across_d = ahead(after(y[3], down), count), behind(down, count), swap_x(after(halves[2][0], down))
    grad, attn_grad, small, *out_parts = resid_back_call(
        after(token, down), resid, gain_two, cotangent, (d_own, up_sent, down_sent), gain_dense, second,
        attn, out_pieces, shared_pieces,
    )
    def finish(ready, expert, kept_out):
        own = after(grads[expert][0], *ready)
        others = (late, 0) if expert == 0 else (got[expert], 3)
        terms = [[(own, i), (others[0], others[1] + i), across[expert][i]] for i in range(3)]
        return finish_call(expert, holds, terms, kept_out)

    out_first = [swap_core(v) for v in out_parts[4:]]
    finished = finish((grad,), 0, None)
    *out_half, up, down = sums_call(
        (finished[0], across_d), *zip(out_parts[2:4], out_first), (y[2], y_up), (y[-2], y_down)
    )

    y_up, y_down, out_across = ahead(up, count), behind(down, count), [swap_x(v) for v in out_half]
    out_got = swap_core(after(out_parts[1], up))
    input_grad, *qkv_parts = attention_back_call(
        after(token, up), query, key, value, attn_grad, first_low, tokens, gain_one, grad, small, query_pieces,
        shared_pieces, segments, seg_col, cos, sin,
    )
    up, down = sums_call((input_grad, *out_across, out_got), (y[1], y_up), (y[-1], y_down))

    y_up, y_down = ahead(up, count), behind(down, count)
    qkv_first = [swap_core(after(v, up)) for v in qkv_parts[4:]]
    qkv_half = sums_call((up,), *zip(qkv_parts[2:4], qkv_first))
    qkv_across = [swap_x(qkv_half[0])]
    out_parts = spread_call(after(token, *qkv_half), count, out_parts[0], out_got, *out_across)
    finished = finish(qkv_half, 1, finished)
    qkv_got = swap_core(after(qkv_parts[1], qkv_across[0]))
    got.append(over_cores(grads[3], qkv_half[0]))
    (half_e,) = sums_call((finished[0],), sum_of(grads[3], got[3], range(3)))
    y_own = after(y[0], qkv_across[0], out_parts[0], half_e)
    mixed = (resid + sum(t.astype(WIDE) for t in (y_own, y_up, y_down))).astype(LOW)
    qkv_across.append(swap_x(after(qkv_half[1], qkv_across[0])))

    def sum_step(parts, up, down, step):
        up = add_low(parts[step], ahead(up, count))
        down = behind(down, count)
        return up, add_low(parts[count + 1 - step], down) if step > 1 else down

    def copy_step(up, down):
        return up + [ahead(up[-1], count)], down + [behind(down[-1], count)]

    out_up, out_down = after(out_parts[4], mixed), after(out_parts[5], mixed)
    for step in (3, 2, 1):
        out_up, out_down = sum_step(out_parts, out_up, out_down, step)
        if step == 2:
            out_up = after(out_up, qkv_across[1])
    out_own = add_low(out_parts[0], ahead(out_up, count), out_down)
    across_e = [swap_x(after(halves[2][1], qkv_across[1])), swap_x(after(half_e, qkv_across[1]))]
    qkv_parts = spread_call(after(token, out_own), count, qkv_parts[0], qkv_got, *qkv_across)
    across.append([(across_d, 0), (across_d, 1), (across_e[0], None)])
    across.append([(across_e[1], i) for i in range(3)])
    out_ups, out_downs = [after(out_own, qkv_parts[0])], [after(out_own, qkv_parts[0])]
    qkv_up, qkv_down = qkv_parts[4], qkv_parts[5]
    for step in (3, 2, 1):
        out_ups, out_downs = copy_step(out_ups, out_downs)
        qkv_up, qkv_down = sum_step(qkv_parts, qkv_up, qkv_down, step)
        qkv_up = after(qkv_up, out_ups[-1], out_downs[-1])
    out_ups.append(ahead(out_ups[-1], count))
    qkv_own = add_low(qkv_parts[0], ahead(qkv_up, count), qkv_down)
    qkv_ups, qkv_downs = [qkv_own], [qkv_own]
    for step in (3, 2, 1):
        qkv_ups, qkv_downs = copy_step(qkv_ups, qkv_downs)
        if step == 3:
            qkv_ups[-1] = after(qkv_ups[-1], out_ups[-1])
        if step == 2:
            finished = finish((qkv_ups[-1],), 2, finished)
            qkv_ups[-1] = after(qkv_ups[-1], finished[0])
    (out_sum,) = assemble_call(after(token, qkv_ups[2]), out_downs + out_ups[:0:-1], (model_width,))
    qkv_ups.append(ahead(after(qkv_ups[-1], out_sum, across_e[1]), count))
    finished = finish((qkv_ups[3],), 3, finished)
    query_sum, key_sum, value_sum, router_sum, ffn_gain_sum, attn_gain_sum = assemble_call(
        after(token, finished[0]), qkv_downs + qkv_ups[:0:-1], (model_width, key_width, key_width)
    )
    gate_shard, up_shard, down_shard = finished
    return (
        mixed,
        input_grad,
        attn_gain_sum,
        ffn_gain_sum,
        query_sum,
        key_sum,
        value_sum,
        out_sum,
        router_sum.T,
        gate_shard,
        up_shard,
        down_shard,
    )


def solution(mesh):
    ring = mesh.shape["expert"] == len(BLOCK_OFFSETS) and mesh.shape["wshard"] == 4
    body = per_device_ring if ring else per_device_exchange
    in_specs = (
        P(("expert", "wshard"), None),
        P(("expert", "wshard"), None),
        P(("expert", "wshard"), None),
        P(),
        P(),
        P("wshard", None),
        P("wshard", None),
        P("wshard", None),
        P("wshard", None),
        P("wshard", None),
        P(None, "expert"),
        P(None, "expert"),
        P("expert", None),
        P(("expert", "wshard"), None),
    )
    out_specs = (
        P(("expert", "wshard"), None),
        P(("expert", "wshard"), None),
        P("wshard"),
        P("wshard"),
        P("wshard", None),
        P("wshard", None),
        P("wshard", None),
        P("wshard", None),
        P("wshard", None),
        P("wshard", "expert"),
        P("wshard", "expert"),
        P("expert", "wshard"),
    )
    return jax.shard_map(
        body, mesh=mesh, in_specs=in_specs, out_specs=out_specs, check_vma=False
    )
```

```python
import functools

import jax
import jax.numpy as jnp
from jax import lax
from jax.experimental import pallas as pl
from jax.experimental.pallas import tpu as pltpu
from jax.sharding import PartitionSpec as P

QUERY_HEADS = 12
KEY_VALUE_HEADS = 2
HEAD_DIM = 128
EXPERTS = 32
TOP = 4


EPS = 1e-06
ROPE_BASE = 10000.0
NEG = -1e30
LOW = jnp.bfloat16
WIDE = jnp.float32
MIB = 1024 * 1024
ONCE = pl.Buffered(buffer_count=1)
def norm_forward(values, gain):
    inverse = lax.rsqrt(jnp.mean(values * values, axis=-1) + EPS)
    normed = values * inverse[:, None]
    return (normed * gain, normed, inverse)


def norm_backward(grad, gain, normed, inverse):
    gain_grad = jnp.sum(grad * normed, axis=0)
    scaled = grad * gain
    centred = scaled - normed * jnp.mean(scaled * normed, axis=-1, keepdims=True)
    return (inverse[:, None] * centred, gain_grad)


def rotary_tables(seq_length, head_size):
    half_size = head_size // 2
    frequency = ROPE_BASE ** (-(jnp.arange(half_size, dtype=jnp.float32) * 2.0 / head_size))
    angles = jnp.arange(seq_length, dtype=jnp.float32)[:, None] * frequency[None, :]
    return (jnp.cos(angles), jnp.sin(angles))


def apply_rotation(values, cosine_lookup, sine_lookup):
    half_size = values.shape[-1] // 2
    first_half = values[..., :half_size]
    second_half = values[..., half_size:]
    cos_part = cosine_lookup[:, None, :]
    sin_part = sine_lookup[:, None, :]
    return jnp.concatenate(
        [
            first_half * cos_part - second_half * sin_part,
            second_half * cos_part + first_half * sin_part,
        ],
        axis=-1,
    )


def reverse_rotation(values, cosine_lookup, sine_lookup):
    half_size = values.shape[-1] // 2
    first_half = values[..., :half_size]
    second_half = values[..., half_size:]
    cos_part = cosine_lookup[:, None, :]
    sin_part = sine_lookup[:, None, :]
    return jnp.concatenate(
        [
            first_half * cos_part + second_half * sin_part,
            second_half * cos_part - first_half * sin_part,
        ],
        axis=-1,
    )


def per_device_exchange(
    tokens,
    segments,
    routes,
    attn_gain,
    ffn_gain,
    w_query,
    key_weight,
    value_weight,
    w_out,
    w_router,
    w_gate,
    w_up,
    w_down,
    cotangent,
):
    lower_dtype = jnp.bfloat16
    wide_type = jnp.float32
    sequence_length, model_width = tokens.shape
    top_count = routes.shape[1]
    axis_count = lax.axis_size("expert")
    owners = max(1, axis_count // EXPERTS)
    holds = max(1, EXPERTS // axis_count)
    groups = EXPERTS // holds
    capacity = max(2, 3 * sequence_length * top_count // (2 * EXPERTS))
    hidden_dev = w_gate.shape[1] // holds
    query_group_width = QUERY_HEADS // KEY_VALUE_HEADS
    score_scale = HEAD_DIM ** (-0.5)
    pair_count = sequence_length * top_count
    query_full, key_full, value_full, out_full, router_full = (
        lax.all_gather(w_query, "wshard", axis=0, tiled=True),
        lax.all_gather(key_weight, "wshard", axis=0, tiled=True),
        lax.all_gather(value_weight, "wshard", axis=0, tiled=True),
        lax.all_gather(w_out, "wshard", axis=0, tiled=True),
        lax.all_gather(w_router, "wshard", axis=0, tiled=True),
    )
    stream = tokens.astype(wide_type)
    first_norm, first_normed, first_inverse = norm_forward(stream, attn_gain)
    first_low = first_norm.astype(lower_dtype)
    cosine_lookup, sine_lookup = rotary_tables(sequence_length, HEAD_DIM)
    query_pre = jnp.dot(first_low, query_full, preferred_element_type=wide_type).reshape(
        sequence_length, QUERY_HEADS, HEAD_DIM
    )
    key_unrotated = jnp.dot(first_low, key_full, preferred_element_type=wide_type).reshape(
        sequence_length, KEY_VALUE_HEADS, HEAD_DIM
    )
    query_rotated = (
        apply_rotation(query_pre, cosine_lookup, sine_lookup)
        .astype(lower_dtype)
        .reshape(sequence_length, KEY_VALUE_HEADS, query_group_width, HEAD_DIM)
    )
    key_rotated = apply_rotation(key_unrotated, cosine_lookup, sine_lookup).astype(lower_dtype)
    value_lowered = (
        jnp.dot(first_low, value_full, preferred_element_type=wide_type)
        .astype(lower_dtype)
        .reshape(sequence_length, KEY_VALUE_HEADS, HEAD_DIM)
    )
    positions = jnp.arange(sequence_length)
    offset = positions[:, None] - positions[None, :]
    segment_row = segments[0]
    allowed = (segment_row[:, None] == segment_row[None, :]) & (offset >= 0)
    raw_scores = jnp.einsum(
        "qagd,kad->agqk", query_rotated, key_rotated, preferred_element_type=wide_type
    )
    scores = jnp.where(allowed, raw_scores * score_scale, NEG)
    score_top = jnp.max(scores, axis=-1, keepdims=True)
    expo_terms = jnp.exp(scores - score_top)
    expo_total = jnp.sum(expo_terms, axis=-1, keepdims=True)
    log_total = score_top + jnp.log(expo_total)
    probs_low = (expo_terms / expo_total).astype(lower_dtype)
    attn_low = (
        jnp.einsum("agqk,kad->qagd", probs_low, value_lowered, preferred_element_type=wide_type)
        .astype(lower_dtype)
        .reshape(sequence_length, QUERY_HEADS * HEAD_DIM)
    )
    resid = stream + jnp.dot(attn_low, out_full, preferred_element_type=wide_type)
    second_norm, second_normed, second_inverse = norm_forward(resid, ffn_gain)
    second_low = second_norm.astype(lower_dtype)
    logits = jnp.dot(second_low, router_full, preferred_element_type=wide_type)
    choose = (routes[:, :, None] == jnp.arange(EXPERTS)[None, None, :]).astype(wide_type)
    selected = jnp.sum(choose * logits[:, None, :], axis=-1)
    gate_probs = jax.nn.softmax(selected, axis=-1)
    flat_routes = routes.reshape(pair_count)
    one_hot = (flat_routes[:, None] == jnp.arange(EXPERTS)[None, :]).astype(jnp.int32)
    slot_rank = jnp.sum((jnp.cumsum(one_hot, axis=0) - 1) * one_hot, axis=1)
    slot_index = (flat_routes // holds * capacity + slot_rank) * holds + flat_routes % holds
    slot_pair = (
        jnp.full((EXPERTS * capacity,), pair_count, jnp.int32)
        .at[slot_index]
        .set(jnp.arange(pair_count, dtype=jnp.int32))
    )
    second_ext = jnp.concatenate([second_low, jnp.zeros((1, model_width), lower_dtype)], axis=0)
    send_rows = jnp.repeat(
        second_ext[slot_pair // top_count].reshape(groups, capacity, holds, model_width),
        owners,
        axis=0,
    )
    gate_local = w_gate.reshape(model_width, holds, hidden_dev)
    up_local = w_up.reshape(model_width, holds, hidden_dev)
    down_local = w_down.reshape(holds, hidden_dev, model_width)

    def owner_total(values):
        summed = jnp.sum(
            values.astype(wide_type).reshape(groups, owners, capacity, holds, model_width), axis=1
        )
        return summed.reshape(EXPERTS * capacity, model_width)

    received = lax.all_to_all(send_rows, "expert", split_axis=0, concat_axis=0, tiled=True)
    gate_pre = jnp.einsum("scld,dlf->sclf", received, gate_local, preferred_element_type=wide_type)
    up_pre = jnp.einsum("scld,dlf->sclf", received, up_local, preferred_element_type=wide_type)
    hidden = (jax.nn.silu(gate_pre) * up_pre).astype(lower_dtype)
    partial_value = jnp.einsum(
        "sclf,lfd->scld", hidden, down_local, preferred_element_type=wide_type
    ).astype(lower_dtype)
    returned = lax.all_to_all(partial_value, "expert", split_axis=0, concat_axis=0, tiled=True)
    expert_wide = owner_total(returned)[slot_index].reshape(sequence_length, top_count, model_width)
    mixed = (resid + jnp.sum(gate_probs[:, :, None] * expert_wide, axis=1)).astype(lower_dtype)
    upstream = cotangent.astype(wide_type)
    query_back, key_back, value_back, out_back, router_back = (
        lax.all_gather(w_query, "wshard", axis=0, tiled=True),
        lax.all_gather(key_weight, "wshard", axis=0, tiled=True),
        lax.all_gather(value_weight, "wshard", axis=0, tiled=True),
        lax.all_gather(w_out, "wshard", axis=0, tiled=True),
        lax.all_gather(w_router, "wshard", axis=0, tiled=True),
    )
    gate_grad = jnp.sum(expert_wide * upstream[:, None, :], axis=-1)
    sel_grad = gate_probs * (gate_grad - jnp.sum(gate_probs * gate_grad, axis=-1, keepdims=True))
    logit_grad = jnp.sum(choose * sel_grad[:, :, None], axis=1).astype(lower_dtype)
    pair_grad = (
        (gate_probs[:, :, None] * upstream[:, None, :])
        .astype(lower_dtype)
        .reshape(pair_count, model_width)
    )
    pair_ext = jnp.concatenate([pair_grad, jnp.zeros((1, model_width), lower_dtype)], axis=0)
    grad_send = jnp.repeat(
        pair_ext[slot_pair].reshape(groups, capacity, holds, model_width), owners, axis=0
    )
    grad_recv, rows_recv = (
        lax.all_to_all(grad_send, "expert", split_axis=0, concat_axis=0, tiled=True),
        lax.all_to_all(send_rows, "expert", split_axis=0, concat_axis=0, tiled=True),
    )
    gate_pre = jnp.einsum("scld,dlf->sclf", rows_recv, gate_local, preferred_element_type=wide_type)
    up_pre = jnp.einsum("scld,dlf->sclf", rows_recv, up_local, preferred_element_type=wide_type)
    sigmoid_gate = jax.nn.sigmoid(gate_pre)
    silu_gate = gate_pre * sigmoid_gate
    hidden = (silu_gate * up_pre).astype(lower_dtype)
    hidden_grad = jnp.einsum(
        "scld,lfd->sclf", grad_recv, down_local, preferred_element_type=wide_type
    )
    gate_pre_grad = (
        hidden_grad * up_pre * sigmoid_gate * (1.0 + gate_pre * (1.0 - sigmoid_gate))
    ).astype(lower_dtype)
    up_pre_grad = (hidden_grad * silu_gate).astype(lower_dtype)
    row_grad = (
        jnp.einsum("sclf,dlf->scld", gate_pre_grad, gate_local, preferred_element_type=wide_type)
        + jnp.einsum("sclf,dlf->scld", up_pre_grad, up_local, preferred_element_type=wide_type)
    ).astype(lower_dtype)
    returned_grad = lax.all_to_all(row_grad, "expert", split_axis=0, concat_axis=0, tiled=True)
    gate_wgrad = jnp.einsum(
        "scld,sclf->dlf", rows_recv, gate_pre_grad, preferred_element_type=wide_type
    ).reshape(model_width, holds * hidden_dev)
    up_wgrad = jnp.einsum(
        "scld,sclf->dlf", rows_recv, up_pre_grad, preferred_element_type=wide_type
    ).reshape(model_width, holds * hidden_dev)
    down_wgrad = jnp.einsum(
        "sclf,scld->lfd", hidden, grad_recv, preferred_element_type=wide_type
    ).reshape(holds * hidden_dev, model_width)
    gate_shard, up_shard, down_shard = (
        lax.psum_scatter(
            gate_wgrad.astype(jnp.bfloat16), "wshard", scatter_dimension=0, tiled=True
        ).astype(jnp.float32),
        lax.psum_scatter(
            up_wgrad.astype(jnp.bfloat16), "wshard", scatter_dimension=0, tiled=True
        ).astype(jnp.float32),
        lax.psum_scatter(
            down_wgrad.astype(jnp.bfloat16), "wshard", scatter_dimension=1, tiled=True
        ).astype(jnp.float32),
    )
    token_grad = owner_total(returned_grad)[slot_index].reshape(
        sequence_length, top_count, model_width
    )
    second_grad = jnp.sum(token_grad, axis=1) + jnp.dot(
        logit_grad, router_back.T, preferred_element_type=wide_type
    )
    router_wgrad = jnp.einsum("td,te->de", second_low, logit_grad, preferred_element_type=wide_type)
    resid_part, ffn_gain_grad = norm_backward(second_grad, ffn_gain, second_normed, second_inverse)
    resid_grad = upstream + resid_part
    resid_low = resid_grad.astype(lower_dtype)
    out_wgrad = jnp.einsum("tc,td->cd", attn_low, resid_low, preferred_element_type=wide_type)
    attn_grad = (
        jnp.dot(resid_low, out_back.T, preferred_element_type=wide_type)
        .astype(lower_dtype)
        .reshape(sequence_length, KEY_VALUE_HEADS, query_group_width, HEAD_DIM)
    )
    raw_again = jnp.einsum(
        "qagd,kad->agqk", query_rotated, key_rotated, preferred_element_type=wide_type
    )
    scores_again = jnp.where(allowed, raw_again * score_scale, NEG)
    probs_again = jnp.exp(scores_again - log_total)
    prob_grad = jnp.einsum(
        "qagd,kad->agqk", attn_grad, value_lowered, preferred_element_type=wide_type
    )
    row_delta = jnp.sum(probs_again * prob_grad, axis=-1, keepdims=True)
    score_grad = (probs_again * (prob_grad - row_delta) * score_scale).astype(lower_dtype)
    value_grad = (
        jnp.einsum("agqk,qagd->kad", probs_low, attn_grad, preferred_element_type=wide_type)
        .astype(lower_dtype)
        .reshape(sequence_length, KEY_VALUE_HEADS * HEAD_DIM)
    )
    query_rot_grad = jnp.einsum(
        "agqk,kad->qagd", score_grad, key_rotated, preferred_element_type=wide_type
    ).reshape(sequence_length, QUERY_HEADS, HEAD_DIM)
    key_rotated_gradient = jnp.einsum(
        "agqk,qagd->kad", score_grad, query_rotated, preferred_element_type=wide_type
    )
    query_grad = (
        reverse_rotation(query_rot_grad, cosine_lookup, sine_lookup)
        .astype(lower_dtype)
        .reshape(sequence_length, QUERY_HEADS * HEAD_DIM)
    )
    key_grad = (
        reverse_rotation(key_rotated_gradient, cosine_lookup, sine_lookup)
        .astype(lower_dtype)
        .reshape(sequence_length, KEY_VALUE_HEADS * HEAD_DIM)
    )
    query_wgrad = jnp.einsum("td,tc->dc", first_low, query_grad, preferred_element_type=wide_type)
    key_wgrad = jnp.einsum("td,tc->dc", first_low, key_grad, preferred_element_type=wide_type)
    value_wgrad = jnp.einsum("td,tc->dc", first_low, value_grad, preferred_element_type=wide_type)
    first_grad = (
        jnp.dot(query_grad, query_back.T, preferred_element_type=wide_type)
        + jnp.dot(key_grad, key_back.T, preferred_element_type=wide_type)
        + jnp.dot(value_grad, value_back.T, preferred_element_type=wide_type)
    )
    stream_part, attn_gain_grad = norm_backward(first_grad, attn_gain, first_normed, first_inverse)
    input_grad = resid_grad + stream_part
    query_part, key_part, value_part, out_part, router_part, attn_gain_part, ffn_gain_part = (
        lax.psum_scatter(
            query_wgrad.astype(jnp.bfloat16), "wshard", scatter_dimension=0, tiled=True
        ).astype(jnp.float32),
        lax.psum_scatter(
            key_wgrad.astype(jnp.bfloat16), "wshard", scatter_dimension=0, tiled=True
        ).astype(jnp.float32),
        lax.psum_scatter(
            value_wgrad.astype(jnp.bfloat16), "wshard", scatter_dimension=0, tiled=True
        ).astype(jnp.float32),
        lax.psum_scatter(
            out_wgrad.astype(jnp.bfloat16), "wshard", scatter_dimension=0, tiled=True
        ).astype(jnp.float32),
        lax.psum_scatter(
            router_wgrad.astype(jnp.bfloat16), "wshard", scatter_dimension=0, tiled=True
        ).astype(jnp.float32),
        lax.psum_scatter(
            attn_gain_grad.astype(jnp.bfloat16), "wshard", scatter_dimension=0, tiled=True
        ).astype(jnp.float32),
        lax.psum_scatter(
            ffn_gain_grad.astype(jnp.bfloat16), "wshard", scatter_dimension=0, tiled=True
        ).astype(jnp.float32),
    )
    query_sum, key_sum, value_sum, out_sum, router_sum, attn_gain_sum, ffn_gain_sum = lax.psum(
        (query_part, key_part, value_part, out_part, router_part, attn_gain_part, ffn_gain_part),
        "expert",
    )
    return (
        mixed,
        input_grad,
        attn_gain_sum,
        ffn_gain_sum,
        query_sum,
        key_sum,
        value_sum,
        out_sum,
        router_sum,
        gate_shard,
        up_shard,
        down_shard,
    )


BLOCK_OFFSETS = (-1, 1, -2, 2, -3, 3, 0, 4)


def ring_order(count):
    return [0] + list(range(1, count, 2)) + list(range(count - 2, 0, -2))


def shifted(value, step, count):
    order = ring_order(count)
    return lax.ppermute(value, "expert", [(order[i], order[(i + step) % count]) for i in range(count)])


def ahead(value, count):
    return shifted(value, 1, count)


def behind(value, count):
    return shifted(value, -1, count)


def swap_core(value):
    size = lax.axis_size("wshard")
    return lax.ppermute(value, "wshard", [(i, i ^ 1) for i in range(size)])


def swap_x(value):
    size = lax.axis_size("wshard")
    return lax.ppermute(value, "wshard", [(i, i ^ 2) for i in range(size)])


def work(flops, bytes_accessed, transcendentals):
    scale = 8
    return pl.CostEstimate(
        flops=flops // scale, bytes_accessed=bytes_accessed // scale, transcendentals=transcendentals // scale
    )


def add_low(*terms):
    return sum(term.astype(WIDE) for term in terms).astype(LOW)


def after(value, *others):
    return lax.optimization_barrier((value, *others))[0]


def places(rank_row, slots):
    rows = lax.broadcasted_iota(jnp.int32, (slots, rank_row.shape[-1]), 0)
    return rank_row == rows


def expert_ranks(routes, holds):
    tokens = routes.shape[1]
    names = [jnp.sum((routes == l).astype(WIDE), axis=0, keepdims=True) for l in range(holds)]
    names = jnp.concatenate(names + [jnp.zeros((16 - holds, tokens), WIDE)], axis=0)
    rows = lax.broadcasted_iota(jnp.int32, (tokens, tokens), 0)
    columns = lax.broadcasted_iota(jnp.int32, (tokens, tokens), 1)
    before = dot(names.astype(LOW), (rows <= columns).astype(WIDE).astype(LOW))
    return jnp.where(names > 0.0, before - 1.0, -1.0)[:holds].astype(jnp.int32)


def pack_routing(gates, routes):
    high = gates.astype(LOW).astype(WIDE)
    rows = [high, gates - high, routes.astype(WIDE)]
    spare = 16 - 3 * gates.shape[0]
    return jnp.concatenate(rows + [jnp.zeros((spare, gates.shape[1]), WIDE)], axis=0).astype(LOW)


def unpack_routing(packed):
    top_count = TOP
    packed = packed.astype(WIDE)
    return packed[:top_count] + packed[top_count : 2 * top_count], packed[2 * top_count : 3 * top_count]


def dot_t(a, b):
    return lax.dot_general(a, b, (((0,), (0,)), ((), ())), preferred_element_type=WIDE)


def dot_bt(a, b):
    return lax.dot_general(a, b, (((1,), (1,)), ((), ())), preferred_element_type=WIDE)


def dot(a, b):
    return jnp.dot(a, b, preferred_element_type=WIDE)


def expert_kernel(count, slots, aliased, *refs):
    token_ref = refs[0]
    h_refs, dz_refs = refs[1 : 1 + count], refs[1 + count : 1 + 2 * count]
    wg_ref, wu_ref, wd_ref = refs[1 + 2 * count : 4 + 2 * count]
    rest = refs[4 + 2 * count + (7 if aliased else 0) :]
    d_refs = rest[:count]
    gain_ref, rank_ref, rows_out, dz_out, gg_out, ug_out, hid_out = rest[count : count + 7]
    place_scr, back_scr, gate_scr, wg_scr, wu_scr, wd_scr, sems = rest[count + 7 :]
    e = pl.program_id(0)
    holds, tokens = rank_ref.shape[1:]
    hidden_width = wd_scr.shape[1]

    def weights(expert, slot):
        band = pl.ds(pl.multiple_of(expert * hidden_width, hidden_width), hidden_width)
        return [
            pltpu.make_async_copy(source, target.at[slot], sems.at[slot, i])
            for i, (source, target) in enumerate(
                ((wg_ref.at[:, band], wg_scr), (wu_ref.at[:, band], wu_scr), (wd_ref.at[band, :], wd_scr))
            )
        ]

    slot = lax.rem(e, 2)

    @pl.when(e == 0)
    def _():
        for copy in weights(0, 0):
            copy.start()

    @pl.when(e + 1 < holds)
    def _():
        for copy in weights(e + 1, 1 - slot):
            copy.start()

    here = pl.ds(pl.multiple_of(e * slots, slots), slots)
    @pl.when(e == 0)
    def _():
        for b, (h_ref, dz_ref) in enumerate(zip(h_refs, dz_refs)):
            gates, routes = unpack_routing(h_ref[tokens : tokens + 16, :tokens])
            routes = routes - (token_ref[1] * holds).astype(WIDE)
            ranks = expert_ranks(routes, holds)
            rank_ref[b] = ranks
            for l in range(holds):
                band = slice(l * slots, (l + 1) * slots)
                spot = places(ranks[l : l + 1], slots).astype(WIDE)
                named = jnp.where(routes == l, gates, 0.0)
                gate_scr[b, band, :] = jnp.broadcast_to(
                    jnp.sum(spot * jnp.sum(named, axis=0, keepdims=True), axis=1, keepdims=True), (slots, 128)
                )
                place_scr[b, band, :] = spot.astype(LOW)
            for source, target in ((h_ref, rows_out), (dz_ref, dz_out)):
                taken = dot(place_scr[b], source[:tokens]).astype(LOW)
                for l in range(holds):
                    target[l, b * slots : (b + 1) * slots, :] = taken[l * slots : (l + 1) * slots]

    gate = jnp.concatenate([gate_scr[b, here, :] for b in range(count)], axis=0)[:, :1]
    rows = rows_out[e]
    for copy in weights(e, slot):
        copy.wait()
    gate_pre = dot(rows, wg_scr[slot])
    up_pre = dot(rows, wu_scr[slot])
    sig = jax.nn.sigmoid(gate_pre)
    silu = gate_pre * sig
    hidden = (silu * up_pre).astype(LOW).astype(WIDE)
    back = dot_bt(dz_out[e], wd_scr[slot])
    gains = jnp.sum(back * hidden, axis=1, keepdims=True)
    back = back * gate
    gate_grad = (back * (up_pre * sig * (1.0 + gate_pre * (1.0 - sig)))).astype(LOW)
    up_grad = (back * silu).astype(LOW)
    gg_out[0] = gate_grad
    ug_out[0] = up_grad
    hid_out[0] = (hidden * gate).astype(LOW)
    row_grad = (dot_bt(gate_grad, wg_scr[slot]) + dot_bt(up_grad, wu_scr[slot])).astype(LOW)
    for b in range(count):
        band = slice(b * slots, (b + 1) * slots)
        back_scr[b, here, :] = row_grad[band]
        spot = place_scr[b, here, :].astype(WIDE)
        gain_ref[b, pl.ds(e, 1), :] = jnp.sum(spot * gains[band], axis=0, keepdims=True)

    @pl.when(e == pl.num_programs(0) - 1)
    def _():
        for b in range(count):
            d_refs[b][...] = dot_t(place_scr[b], back_scr[b]).astype(LOW)


def expert_call(token, first, blocks, dz_blocks, w_gate, w_up, w_down, kept, holds, slots, total):
    count = len(blocks)
    tokens, width = dz_blocks[0].shape
    hidden = w_gate.shape[1] // holds
    whole = lambda *shape: pl.BlockSpec(shape, lambda e: (0,) * len(shape))
    once = lambda *shape: pl.BlockSpec(shape, lambda e: (0,) * len(shape), pipeline_mode=pl.Buffered(buffer_count=1))
    aliased = kept is not None
    in_specs = (
        [pl.BlockSpec(memory_space=pltpu.SMEM)]
        + [once(*b.shape) for b in (*blocks, *dz_blocks)]
        + [pl.BlockSpec(memory_space=pl.ANY)] * 3
    )
    aliases = {len(in_specs) + i: count + i for i in range(7)} if aliased else {}
    out = pl.pallas_call(
        functools.partial(expert_kernel, count, slots, aliased),
        grid=(holds,),
        in_specs=in_specs + ([pl.BlockSpec(memory_space=pl.ANY)] * 7 if aliased else []),
        out_specs=[whole(tokens, width)] * count
        + [pl.BlockSpec((count, holds, tokens), lambda e: (first // count, 0, 0))] * 2
        + [pl.BlockSpec((holds, count * slots, width), lambda e: (0, first // count, 0))] * 2
        + [pl.BlockSpec((1, count * slots, hidden), lambda e: (e, first // count, 0))] * 3,
        out_shape=[shaped(tokens, width)] * count
        + [shaped(total, holds, tokens, dtype=WIDE), shaped(total, holds, tokens, dtype=jnp.int32)]
        + [shaped(holds, total * slots, width)] * 2
        + [shaped(holds, total * slots, hidden)] * 3,
        scratch_shapes=[
            pltpu.VMEM((count, holds * slots, tokens), LOW),
            pltpu.VMEM((count, holds * slots, width), LOW),
            pltpu.VMEM((count, holds * slots, 128), WIDE),
            pltpu.VMEM((2, width, hidden), LOW),
            pltpu.VMEM((2, width, hidden), LOW),
            pltpu.VMEM((2, hidden, width), LOW),
            pltpu.SemaphoreType.DMA((2, 3)),
        ],
        input_output_aliases=aliases,
        compiler_params=pltpu.CompilerParams(vmem_limit_bytes=52 * MIB),
        cost_estimate=work(
            flops=2 * holds * count * slots * width * (5 * hidden + 3 * tokens),
            bytes_accessed=3 * holds * width * hidden * 2
            + count * tokens * width * 6
            + holds * count * slots * (2 * width + 3 * hidden) * 2,
            transcendentals=holds * count * slots * hidden,
        ),
    )(token, *blocks, *dz_blocks, w_gate, w_up, w_down, *(kept if aliased else ()))
    return out[:count], tuple(out[count:])


def value_kernel(slots, _, rank_ref, hid_ref, wd_ref, *refs):
    total, holds, tokens = rank_ref.shape
    y_refs, (value_scr, place_scr) = refs[:total], refs[total:]
    e = pl.program_id(0)
    here = pl.ds(pl.multiple_of(e * slots, slots), slots)
    value = dot(hid_ref[0], wd_ref[...]).astype(LOW)
    for b in range(total):
        value_scr[b, here, :] = value[b * slots : (b + 1) * slots]

    @pl.when(e == pl.num_programs(0) - 1)
    def _():
        for b in range(total):
            for l in range(holds):
                spot = places(rank_ref[b, l : l + 1, :], slots)
                place_scr[l * slots : (l + 1) * slots, :] = spot.astype(WIDE).astype(LOW)
            y_refs[b][...] = dot_t(place_scr[...], value_scr[b]).astype(LOW)


def value_call(token, rank, hidden_rows, w_down, slots):
    total, holds, tokens = rank.shape
    width = w_down.shape[1]
    hidden = hidden_rows.shape[2]
    whole = lambda *shape: pl.BlockSpec(shape, lambda e: (0,) * len(shape))
    out = pl.pallas_call(
        functools.partial(value_kernel, slots),
        grid=(holds,),
        in_specs=[
            pl.BlockSpec(memory_space=pltpu.SMEM),
            whole(*rank.shape),
            pl.BlockSpec((1, total * slots, hidden), lambda e: (e, 0, 0)),
            pl.BlockSpec((hidden, width), lambda e: (e, 0)),
        ],
        out_specs=[whole(tokens, width)] * total,
        out_shape=[shaped(tokens, width)] * total,
        scratch_shapes=[pltpu.VMEM((total, holds * slots, width), LOW), pltpu.VMEM((holds * slots, tokens), LOW)],
        compiler_params=pltpu.CompilerParams(vmem_limit_bytes=44 * MIB),
        cost_estimate=work(
            flops=2 * total * holds * slots * width * (hidden + tokens),
            bytes_accessed=2 * (holds * hidden * (width + total * slots) + total * tokens * width),
            transcendentals=0,
        ),
    )(token, rank, hidden_rows, w_down)
    return out


def wgrad_kernel(apart, place_ref, rows_ref, dz_ref, gg_ref, ug_ref, hid_ref, *outs):
    step = pl.program_id(0)
    shard = outs[0].shape[1]
    columns = pl.ds(pl.multiple_of(jnp.bitwise_xor(place_ref[0], step) * shard, 128), shard)
    rows, grads = rows_ref[0, :, columns], dz_ref[0, :, columns]
    parts = [dot_t(rows, gg_ref[0]), dot_t(rows, ug_ref[0]), dot_t(grads, hid_ref[0])]
    parts = [part.astype(LOW) for part in parts]
    for s in range(4):

        @pl.when(step == s)
        def _():
            for i, part in enumerate(parts):
                if s == 3 and apart:
                    outs[3 + i][...] = part
                elif s % 2 and not apart:
                    outs[2][3 - 3 * (s // 2) + i] = part
                else:
                    outs[s if apart else s // 2][i] = part


def wgrad_call(expert, place, kept, apart=False):
    _, count, width = kept[0].shape
    hidden = kept[2].shape[2]
    shard = width // 4
    row_spec = lambda d: pl.BlockSpec((1, count, d), lambda s: (expert, 0, 0), pipeline_mode=pl.Buffered(buffer_count=1))
    shapes = [(3, shard, hidden)] * 3 + [(shard, hidden)] * 3 if apart else [(3, shard, hidden)] * 2 + [(6, shard, hidden)]
    out = pl.pallas_call(
        functools.partial(wgrad_kernel, apart),
        grid=(4,),
        in_specs=[pl.BlockSpec(memory_space=pltpu.SMEM), row_spec(width), row_spec(width)] + [row_spec(hidden)] * 3,
        out_specs=[pl.BlockSpec(shape, lambda s, zeros=(0,) * len(shape): zeros) for shape in shapes],
        out_shape=[shaped(*shape) for shape in shapes],
        compiler_params=pltpu.CompilerParams(vmem_limit_bytes=28 * MIB),
        cost_estimate=work(
            flops=2 * count * width * 3 * hidden,
            bytes_accessed=2 * (count * (2 * width + 3 * hidden) + 3 * width * hidden),
            transcendentals=0,
        ),
    )(place, *kept)
    return (out[0], out[2], out[3:], out[1]) if apart else out


def sums_call(gates, *sums):
    every = [term[0] if isinstance(term, tuple) else term for terms in sums for term in terms]

    def part_of(term, ready=()):
        array, part = term if isinstance(term, tuple) else (term, None)
        array = after(array, *ready) if ready else array
        return array if part is None else array[: len(part)] if isinstance(part, range) else array[part]

    totals = [add_low(part_of(terms[0], (*gates, *every)), *map(part_of, terms[1:])) for terms in sums]
    return totals


def finish_kernel(sizes, turned, *refs):
    outs = refs[-len(sizes) :]
    at = 0
    for counts, turn, out in zip(sizes, turned, outs):
        for i, size in enumerate(counts):
            total = sum(ref[...].astype(WIDE) for ref in refs[at : at + size])
            at += size
            if turn:
                height = out.shape[0] // len(counts)
                out[i * height : (i + 1) * height, :] = jnp.transpose(total)
            else:
                out[...] = total


def finish_call(holds, pieces, kept):
    shard, hidden = pieces[0][2][0][0][0].shape[-2:]
    steps = shard // 128
    wide, tall = shaped(shard, holds * hidden, dtype=WIDE), shaped(holds * hidden, shard, dtype=WIDE)
    flat = [term for _, _, experts in pieces for terms in experts for term in terms]
    out_specs, out_shapes = [], []
    for which, expert, experts in pieces:
        number = len(experts)
        if which < 2:
            out_specs.append(pl.BlockSpec((128, hidden), lambda s, expert=expert: (s, expert)))
        else:
            block = (number * hidden, 128)
            out_specs.append(pl.BlockSpec(block, lambda s, at=expert // number: (at, s)))
        out_shapes.append(wide if which < 2 else tall)
    kept_in = [kept[which] for which, _, _ in pieces] if kept else []
    out = pl.pallas_call(
        functools.partial(
            finish_kernel, [[len(terms) for terms in experts] for _, _, experts in pieces], [p[0] == 2 for p in pieces]
        ),
        grid=(steps,),
        in_specs=[
            pl.BlockSpec((128, hidden), lambda s: (s, 0))
            if at is None
            else pl.BlockSpec((None, 128, hidden), lambda s, at=at: (at, s, 0))
            for _, at in flat
        ]
        + [pl.BlockSpec(memory_space=pl.ANY)] * len(kept_in),
        out_specs=out_specs,
        out_shape=out_shapes,
        input_output_aliases={len(flat) + i: i for i in range(len(kept_in))},
        compiler_params=pltpu.CompilerParams(vmem_limit_bytes=20 * MIB),
        cost_estimate=work(flops=0, bytes_accessed=30 * shard * hidden, transcendentals=0),
    )(*[array for array, _ in flat], *kept_in)
    result = list(kept) if kept else [None] * 3
    for (which, _, _), value in zip(pieces, out):
        result[which] = value
    return result


def piece_columns(mine, s, shard):
    return pl.ds(pl.multiple_of(jnp.bitwise_xor(mine, s) * shard, 128), shard)


def turn(values, cos, sin):
    return values * cos + pltpu.roll(values, HEAD_DIM // 2, 1) * sin


def turn_back(values, cos, sin):
    return values * cos - pltpu.roll(values, HEAD_DIM // 2, 1) * sin


def inverse_rms(values):
    return lax.rsqrt(jnp.mean(values * values, axis=-1, keepdims=True) + EPS)


def head_slice(h):
    return slice(h * HEAD_DIM, (h + 1) * HEAD_DIM)


def stacked_heads(ref, band, group, heads):
    return jnp.concatenate([ref[band, head_slice(group * heads + h)] for h in range(heads)], axis=0)


def probabilities(queries, keys, allowed):
    scores = jnp.where(allowed, dot_bt(queries, keys) * HEAD_DIM ** (-0.5), NEG)
    expo = jnp.exp(scores - jnp.max(scores, axis=-1, keepdims=True))
    return expo * (1.0 / jnp.sum(expo, axis=-1, keepdims=True))


def allowed_pairs(seg_col_ref, seg_row_ref, band, reach, heads):
    size = band.stop - band.start
    rows = band.start + lax.broadcasted_iota(jnp.int32, (size, reach), 0)
    cols = lax.broadcasted_iota(jnp.int32, (size, reach), 1)
    ok = (seg_col_ref[band, :] == seg_row_ref[:, :reach]) & (cols <= rows)
    return jnp.concatenate([ok] * heads, axis=0)


def attention_kernel(
    mine_ref, tokens_ref, gain_ref, p0, p1, p2, p3, s0, s1, s2, s3, seg_row_ref, seg_col_ref, cos_ref, sin_ref,
    h_ref, q_ref, k_ref, v_ref, out_ref,
):
    mine = mine_ref[0]
    stream = tokens_ref[...].astype(WIDE)
    h_ref[...] = (stream * inverse_rms(stream) * gain_ref[...]).astype(LOW)
    shard = p0.shape[0]
    width = q_ref.shape[1]
    cos, sin = cos_ref[...], sin_ref[...]

    def projected(pieces, columns):
        return sum(dot(h_ref[:, piece_columns(mine, s, shard)], piece[:, columns]) for s, piece in enumerate(pieces))

    heads = QUERY_HEADS // KEY_VALUE_HEADS
    key_width = KEY_VALUE_HEADS * HEAD_DIM
    shared = (s0, s1, s2, s3)
    keys = projected(shared, slice(0, key_width))
    for g in range(KEY_VALUE_HEADS):
        k_ref[:, head_slice(g)] = turn(keys[:, head_slice(g)], cos, sin).astype(LOW)
    v_ref[...] = projected(shared, slice(key_width, 2 * key_width)).astype(LOW)
    group_width = heads * HEAD_DIM
    for g in range(KEY_VALUE_HEADS):
        queries = projected((p0, p1, p2, p3), slice(g * group_width, (g + 1) * group_width))
        for h in range(heads):
            q_ref[:, head_slice(g * heads + h)] = turn(queries[:, head_slice(h)], cos, sin).astype(LOW)
    length = q_ref.shape[0]
    tile = 128
    for start in range(0, length, tile):
        band, reach = slice(start, start + tile), start + tile
        allowed = allowed_pairs(seg_col_ref, seg_row_ref, band, reach, heads)
        for g in range(KEY_VALUE_HEADS):
            probs = probabilities(stacked_heads(q_ref, band, g, heads), k_ref[:reach, head_slice(g)], allowed)
            mixed = dot(probs.astype(LOW), v_ref[:reach, head_slice(g)]).astype(LOW)
            for h in range(heads):
                out_ref[band, head_slice(g * heads + h)] = mixed[h * tile : (h + 1) * tile]


def vmem_call(kernel, out_shape, flops, transcendentals, token, *args):
    moved = sum(a.size * a.dtype.itemsize for a in args) + sum(
        o.size * o.dtype.itemsize for o in jax.tree.leaves(out_shape)
    )
    return pl.pallas_call(
        kernel,
        in_specs=[pl.BlockSpec(memory_space=pltpu.SMEM)] + [pl.BlockSpec(memory_space=pltpu.VMEM)] * len(args),
        out_specs=[pl.BlockSpec(memory_space=pltpu.VMEM)] * len(out_shape),
        out_shape=out_shape,
        compiler_params=pltpu.CompilerParams(vmem_limit_bytes=32 * MIB),
        cost_estimate=work(flops=flops, bytes_accessed=moved, transcendentals=transcendentals),
    )(token, *args)


def shaped(*shape, dtype=LOW):
    return jax.ShapeDtypeStruct(shape, dtype)


def attention_call(mine, tokens, gain, pieces, shared_pieces, seg_row, seg_col, cos, sin):
    length, width = tokens.shape
    key_width = KEY_VALUE_HEADS * HEAD_DIM
    return vmem_call(
        attention_kernel,
        [shaped(length, width), shaped(length, width), shaped(length, key_width), shaped(length, key_width), shaped(length, width)],
        2 * length * width * (width + 2 * key_width) + 3 * length * length * width,
        QUERY_HEADS * length * length,
        mine, tokens, gain, *pieces, *shared_pieces, seg_row, seg_col, cos, sin,
    )


def project_kernel(
    mine_ref, tokens_ref, attn_ref, p0, p1, p2, p3, r0, r1, r2, r3, gain_ref, routes_ref, resid_ref, h_ref
):
    mine = mine_ref[0]
    shard = p0.shape[0]
    resid = tokens_ref[...].astype(WIDE)
    for s, piece in enumerate((p0, p1, p2, p3)):
        resid = resid + dot(attn_ref[:, piece_columns(mine, s, shard)], piece[...])
    resid_ref[...] = resid
    length, width = resid.shape
    h_ref[:length] = (resid * inverse_rms(resid) * gain_ref[...]).astype(LOW)
    logits = jnp.transpose(
        sum(
            dot(h_ref[:length, piece_columns(mine, s, shard)], piece[...])
            for s, piece in enumerate((r0, r1, r2, r3))
        )
    )
    experts = lax.broadcasted_iota(jnp.int32, logits.shape, 0)
    picked = [
        jnp.sum(jnp.where(experts == routes_ref[k : k + 1, :], logits, 0.0), axis=0, keepdims=True)
        for k in range(routes_ref.shape[0])
    ]
    top = functools.reduce(jnp.maximum, picked)
    expo = [jnp.exp(p - top) for p in picked]
    total = sum(expo)
    gates = jnp.concatenate([x / total for x in expo], axis=0)
    h_ref[length:] = jnp.zeros((16, width), LOW)
    h_ref[length:, :length] = pack_routing(gates, routes_ref[...])


def project_call(mine, tokens, attn, pieces, shared_pieces, gain, routes_t):
    length, width = tokens.shape
    whole = lambda shape: pl.BlockSpec(shape, lambda i: (0,) * len(shape), pipeline_mode=ONCE)
    shapes = [shaped(length, width, dtype=WIDE), shaped(length + 16, width)]
    return pl.pallas_call(
        project_kernel,
        grid=(1,),
        in_specs=[pl.BlockSpec(memory_space=pltpu.SMEM)]
        + [whole(a.shape) for a in (tokens, attn, *pieces)]
        + router_columns(shared_pieces)
        + [whole(gain.shape), whole(routes_t.shape)],
        out_specs=[whole(s.shape) for s in shapes],
        out_shape=shapes,
        compiler_params=pltpu.CompilerParams(vmem_limit_bytes=30 * MIB),
        cost_estimate=work(
            flops=2 * length * width * (width + EXPERTS), bytes_accessed=length * width * 20, transcendentals=length * 8
        ),
    )(mine, tokens, attn, *pieces, *shared_pieces, gain, routes_t)


def as_column(row):
    return jnp.transpose(jnp.broadcast_to(row, (8, row.shape[1])))[:, :1]


def norm_back(grad, gain, normed, inverse):
    scaled = grad * gain
    return inverse * (scaled - normed * jnp.mean(scaled * normed, axis=-1, keepdims=True))


def shard_parts(targets):
    at, parts = 0, []
    for target in targets:
        parts.append((target, slice(at, at + target.shape[0])))
        at += target.shape[0]
    return parts


def resid_back_kernel(
    mine_ref, resid_ref, gain_ref, dz_ref, t0, t1, t2, gains_ref, h_ref, attn_ref,
    p0, p1, p2, p3, r0, r1, r2, r3, grad_ref, attn_grad_ref, small_ref, o0, o1, o2, o3, o4, o5, second_scr, low_scr,
):
    mine = mine_ref[0]
    shard, width = p0.shape
    length = resid_ref.shape[0]
    routers = (r0, r1, r2, r3)
    gains = gains_ref[...]
    experts = lax.broadcasted_iota(jnp.int32, gains.shape, 0)
    gate_rows, routes = unpack_routing(h_ref[length:, :length])
    gates = jnp.zeros(gains.shape, WIDE)
    for k in range(TOP):
        gates = gates + jnp.where(experts.astype(WIDE) == routes[k : k + 1], gate_rows[k : k + 1], 0.0)
    logit_grad = gates * (gains - jnp.sum(gates * gains, axis=0, keepdims=True))
    logit_grad = jnp.concatenate([logit_grad, jnp.zeros((128 - EXPERTS, length), WIDE)], axis=0)
    logit_grad = jnp.transpose(logit_grad).astype(LOW)
    second_scr[...] = t0[...].astype(WIDE) + t1[...].astype(WIDE) + t2[...].astype(WIDE)
    for s, piece in enumerate(routers):
        columns = piece_columns(mine, s, shard)
        second_scr[:, columns] = second_scr[:, columns] + dot_bt(logit_grad, piece[...])
    resid = resid_ref[...]
    inverse = inverse_rms(resid)
    normed = resid * inverse
    second = second_scr[...]
    gain_grad = jnp.sum(second * normed, axis=0, keepdims=True)
    grad = dz_ref[...].astype(WIDE) + norm_back(second, gain_ref[...], normed, inverse)
    grad_ref[...] = grad
    low_scr[...] = grad.astype(LOW)
    second_scr[:1, :] = gain_grad
    low = low_scr[...]
    for s, piece in enumerate((p0, p1, p2, p3)):
        columns = piece_columns(mine, s, shard)
        attn_grad_ref[:, columns] = dot_bt(low, piece[...]).astype(LOW)
        out_part = dot_t(attn_ref[:, columns], low).astype(LOW)
        router_part = dot_t(h_ref[:length, columns], logit_grad)
        lanes = lax.broadcasted_iota(jnp.int32, router_part.shape, 1)
        small_ref[s] = jnp.where(lanes == EXPERTS, as_column(second_scr[:1, columns]), router_part).astype(LOW)
        for target, rows in shard_parts(((o0,), (o1,), (o2, o3), (o4, o5))[s]):
            target[...] = out_part[rows]


def router_columns(pieces):
    return [
        pl.BlockSpec((p.shape[0], 128), lambda i, at=p.shape[1] // 128 - 1: (0, at), pipeline_mode=ONCE) for p in pieces
    ]


def resid_back_call(mine, resid, gain, dz, terms, gains, h, attn, pieces, shared_pieces):
    length, width = resid.shape
    shard = pieces[0].shape[0]
    whole = lambda shape: pl.BlockSpec(shape, lambda i: (0,) * len(shape), pipeline_mode=ONCE)
    arrays = (resid, gain, dz, *terms, gains, h, attn, *pieces)
    shapes = [shaped(length, width, dtype=WIDE), shaped(length, width), shaped(4, shard, 128)]
    shapes += [shaped(shard, width)] * 2 + [shaped(shard // 2, width)] * 4
    return pl.pallas_call(
        resid_back_kernel,
        grid=(1,),
        in_specs=[pl.BlockSpec(memory_space=pltpu.SMEM)]
        + [whole(a.shape) for a in arrays]
        + router_columns(shared_pieces),
        out_specs=[whole(s.shape) for s in shapes],
        out_shape=shapes,
        scratch_shapes=[pltpu.VMEM((length, width), WIDE), pltpu.VMEM((length, width), LOW)],
        compiler_params=pltpu.CompilerParams(vmem_limit_bytes=34 * MIB),
        cost_estimate=work(
            flops=4 * length * width * (width + EXPERTS), bytes_accessed=length * width * 40, transcendentals=0
        ),
    )(mine, *arrays, *shared_pieces)


def attention_back_kernel(
    mine_ref, q_ref, k_ref, v_ref, do_ref, h_ref, tokens_ref, gain_ref, grad_ref, small_ref, p0, p1, p2, p3, s0, s1, s2, s3,
    seg_row_ref, seg_col_ref, cos_ref, sin_ref, input_ref, o0, o1, o2, o3, o4, o5, qkv_scr, dk_scr, dv_scr, dh_scr,
):
    mine = mine_ref[0]
    length, width = q_ref.shape
    shard = p0.shape[0]
    qkv_width = width + 2 * KEY_VALUE_HEADS * HEAD_DIM
    heads = QUERY_HEADS // KEY_VALUE_HEADS
    key_width = KEY_VALUE_HEADS * HEAD_DIM
    tile = 128
    dk_scr[...] = jnp.zeros_like(dk_scr)
    dv_scr[...] = jnp.zeros_like(dv_scr)
    for start in range(0, length, tile):
        band, reach = slice(start, start + tile), start + tile
        allowed = allowed_pairs(seg_col_ref, seg_row_ref, band, reach, heads)
        cos, sin = cos_ref[band, :], sin_ref[band, :]
        for g in range(KEY_VALUE_HEADS):
            queries = stacked_heads(q_ref, band, g, heads)
            grads = stacked_heads(do_ref, band, g, heads)
            keys = k_ref[:reach, head_slice(g)]
            probs = probabilities(queries, keys, allowed)
            prob_grad = dot_bt(grads, v_ref[:reach, head_slice(g)])
            delta = jnp.sum(probs * prob_grad, axis=-1, keepdims=True)
            score_grad = (probs * (prob_grad - delta) * HEAD_DIM ** (-0.5)).astype(LOW)
            dv_scr[:reach, head_slice(g)] += dot_t(probs.astype(LOW), grads)
            dk_scr[:reach, head_slice(g)] += dot_t(score_grad, queries)
            dq = dot(score_grad, keys)
            for h in range(heads):
                qkv_scr[band, head_slice(g * heads + h)] = turn_back(dq[h * tile : (h + 1) * tile], cos, sin).astype(LOW)
    for g in range(KEY_VALUE_HEADS):
        at = width + g * HEAD_DIM
        qkv_scr[:, at : at + HEAD_DIM] = turn_back(dk_scr[:, head_slice(g)], cos_ref[...], sin_ref[...]).astype(LOW)
    qkv_scr[:, width + key_width :] = dv_scr[...].astype(LOW)
    qkv = qkv_scr[...]
    for s, (piece, shared) in enumerate(zip((p0, p1, p2, p3), (s0, s1, s2, s3))):
        dh_scr[:, piece_columns(mine, s, shard)] = dot_bt(qkv[:, :width], piece[...]) + dot_bt(qkv[:, width:], shared[:, : 2 * key_width])
    stream = tokens_ref[...].astype(WIDE)
    inverse = inverse_rms(stream)
    normed = stream * inverse
    first = dh_scr[...]
    gain_grad = jnp.sum(first * normed, axis=0, keepdims=True)
    input_ref[...] = grad_ref[...] + norm_back(first, gain_ref[...], normed, inverse)
    dh_scr[:1, :] = gain_grad
    for s in range(4):
        columns = piece_columns(mine, s, shard)
        part = dot_t(h_ref[:, columns], qkv).astype(LOW)
        small = small_ref[s].astype(WIDE)
        lanes = lax.broadcasted_iota(jnp.int32, small.shape, 1)
        small = jnp.where(lanes == EXPERTS + 1, as_column(dh_scr[:1, columns]), small).astype(LOW)
        for target, rows in shard_parts(((o0,), (o1,), (o2, o3), (o4, o5))[s]):
            target[:, :qkv_width] = part[rows]
            target[:, qkv_width:] = small[rows]


def attention_back_call(
    mine, q, k, v, do, h, tokens, gain, grad, small, pieces, shared_pieces, seg_row, seg_col, cos, sin
):
    length, width = q.shape
    shard = pieces[0].shape[0]
    qkv_width = width + 2 * KEY_VALUE_HEADS * HEAD_DIM
    key_width = KEY_VALUE_HEADS * HEAD_DIM
    return pl.pallas_call(
        attention_back_kernel,
        in_specs=[pl.BlockSpec(memory_space=pltpu.SMEM)] + [pl.BlockSpec(memory_space=pltpu.VMEM)] * 21,
        out_specs=[pl.BlockSpec(memory_space=pltpu.VMEM)] * 7,
        out_shape=[shaped(length, width, dtype=WIDE)]
        + [shaped(shard, qkv_width + 128)] * 2
        + [shaped(shard * 2 // 3, qkv_width + 128), shaped(shard // 3, qkv_width + 128)] * 2,
        scratch_shapes=[
            pltpu.VMEM((length, qkv_width), LOW),
            pltpu.VMEM((length, key_width), WIDE),
            pltpu.VMEM((length, key_width), WIDE),
            pltpu.VMEM((length, width), WIDE),
        ],
        compiler_params=pltpu.CompilerParams(vmem_limit_bytes=46 * MIB),
        cost_estimate=work(
            flops=4 * length * width * qkv_width + 7 * length * length * width,
            bytes_accessed=length * width * 40,
            transcendentals=QUERY_HEADS * length * length,
        ),
    )(mine, q, k, v, do, h, tokens, gain, grad, small, *pieces, *shared_pieces, seg_row, seg_col, cos, sin)


def spread_kernel(count, token_ref, *refs):
    parts, outs, scratch = refs[2 : -count - 1], refs[-count - 1 : -1], refs[-1]
    for part, rows in shard_parts(parts):
        scratch[rows] = part[...]
    chunk = outs[0].shape[0]
    for j, out in enumerate(outs):
        rows = pl.ds(pl.multiple_of(lax.rem(token_ref[2] + j, count) * chunk, 16), chunk)
        out[...] = sum(term[rows, :].astype(WIDE) for term in (*refs[:2], scratch)).astype(LOW)


def spread_call(token, count, *terms):
    rows, width = terms[0].shape
    whole = lambda shape: pl.BlockSpec(shape, lambda i: (0, 0), pipeline_mode=ONCE)
    return pl.pallas_call(
        functools.partial(spread_kernel, count),
        grid=(1,),
        in_specs=[pl.BlockSpec(memory_space=pltpu.SMEM)] + [whole(t.shape) for t in terms],
        out_specs=[whole((rows // count, width))] * count,
        out_shape=[shaped(rows // count, width)] * count,
        scratch_shapes=[pltpu.VMEM((rows, width), LOW)],
        compiler_params=pltpu.CompilerParams(vmem_limit_bytes=16 * MIB),
        cost_estimate=work(flops=0, bytes_accessed=8 * rows * width, transcendentals=0),
    )(token, *terms)


def assemble_kernel(count, widths, token_ref, *refs):
    chunks, outs = refs[:count], refs[count:]
    chunk = chunks[0].shape[0]
    for j, ref in enumerate(chunks):
        rows = pl.ds(pl.multiple_of(lax.rem(token_ref[2] + j, count) * chunk, 16), chunk)
        values = ref[...].astype(WIDE)
        at = 0
        for width, out in zip(widths, outs):
            out[rows, :] = values[:, at : at + width]
            at += width
        if len(outs) > len(widths):
            outs[-1][rows, :] = values[:, at : at + 128]
    if len(outs) > len(widths):
        router_ref, ffn_ref, attn_ref, scratch = outs[len(widths) :]
        small = jnp.transpose(scratch[...])
        router_ref[...] = small[:EXPERTS]
        ffn_ref[...] = small[EXPERTS]
        attn_ref[...] = small[EXPERTS + 1]


def assemble_call(token, chunks, widths):
    count, (rows, width) = len(chunks), chunks[0].shape
    whole = lambda shape: pl.BlockSpec(shape, lambda i: (0,) * len(shape), pipeline_mode=ONCE)
    small = width > sum(widths)
    shapes = [(count * rows, w) for w in widths]
    shapes += [(EXPERTS, count * rows), (count * rows,), (count * rows,)] if small else []
    return pl.pallas_call(
        functools.partial(assemble_kernel, count, widths),
        grid=(1,),
        in_specs=[pl.BlockSpec(memory_space=pltpu.SMEM)] + [whole((rows, width))] * count,
        out_specs=[whole(shape) for shape in shapes],
        out_shape=[shaped(*shape, dtype=WIDE) for shape in shapes],
        scratch_shapes=[pltpu.VMEM((count * rows, 128), WIDE)] if small else [],
        compiler_params=pltpu.CompilerParams(vmem_limit_bytes=16 * MIB),
        cost_estimate=work(flops=0, bytes_accessed=6 * count * rows * width, transcendentals=0),
    )(token, *chunks)


def per_device_ring(
    tokens,
    segments,
    routes,
    attn_gain,
    ffn_gain,
    w_query,
    key_weight,
    value_weight,
    w_out,
    w_router,
    w_gate,
    w_up,
    w_down,
    cotangent,
):
    length, model_width = tokens.shape
    top_count = routes.shape[1]
    count = lax.axis_size("expert")
    holds = EXPERTS // count
    capacity = max(2, 3 * length * top_count // (2 * EXPERTS))
    slots = -(-capacity // 16) * 16
    shard = model_width // 4
    key_width = KEY_VALUE_HEADS * HEAD_DIM
    half = length // 2
    mine = lax.axis_index("wshard").astype(jnp.int32)
    order = jnp.array(ring_order(count), jnp.int32)
    spot_of = jnp.array([ring_order(count).index(i) for i in range(count)], jnp.int32)
    here = lax.axis_index("expert").astype(jnp.int32)
    spot = spot_of[here]
    token = jnp.stack([mine, here, spot])
    routes_t = routes.T

    cosine, sine = rotary_tables(length, HEAD_DIM)
    cos = jnp.concatenate([cosine, cosine], axis=1)
    sin = jnp.concatenate([-sine, sine], axis=1)
    seg_col = segments.reshape(length, 1)
    gain_one, gain_two = attn_gain[None], ffn_gain[None]

    def pieces_of(own, across, *ready):
        return (own, swap_core(own), across, swap_core(after(across, *ready)))

    dz = {0: cotangent}
    dz[-1], dz[1] = ahead(dz[0], count), behind(dz[0], count)
    query_across = swap_x(w_query)
    query_pieces = pieces_of(w_query, query_across)
    spare = jnp.zeros((shard, 128 - EXPERTS), LOW)
    shared = jnp.concatenate([key_weight, value_weight, w_router, spare], axis=1)
    shared, token, seg_col, cos, sin, routes_t, gain_one, gain_two = lax.optimization_barrier(
        (shared, token, seg_col, cos, sin, routes_t, gain_one, gain_two)
    )
    shared_across = swap_x(after(shared, query_across, dz[-1], dz[1]))
    dz[-2], dz[2] = ahead(dz[-1], count), behind(dz[1], count)
    shared_pieces = pieces_of(shared, shared_across)
    out_across = swap_x(after(w_out, shared_across))

    first_low, query, key, value, attn = attention_call(
        after(token, dz[-2], dz[2]), tokens, gain_one, query_pieces, shared_pieces, segments, seg_col, cos, sin
    )
    out_pieces = pieces_of(w_out, out_across, attn)
    dz[-3], dz[3] = ahead(dz[-2], count), behind(dz[2], count)
    resid, second = project_call(after(token, dz[-3], dz[3]), tokens, attn, out_pieces, shared_pieces, gain_two, routes_t)

    def experts(ready, first, offsets, kept):
        return expert_call(
            after(token, *ready), first, [h[j] for j in offsets], [dz[j] for j in offsets], w_gate, w_up, w_down, kept,
            holds, slots, count,
        )

    h = {0: second}
    h[-1], h[1] = ahead(h[0], count), behind(h[0], count)
    (d_own,), kept = experts((), 6, (0,), None)
    h[-2], h[2] = ahead(after(h[-1], d_own), count), behind(after(h[1], d_own), count)
    (d_l1, d_r1), kept = experts((), 0, (-1, 1), kept)
    h[-3], h[3] = ahead(after(h[-2], d_l1), count), behind(after(h[2], d_l1), count)
    (d_l2, d_r2), kept = experts((), 2, (-2, 2), kept)
    h[4], dz[4] = ahead(after(h[-3], d_l2), count), behind(after(dz[3], d_l2), count)
    (d_l3, d_r3), kept = experts((), 4, (-3, 3), kept)
    (d_far,), (gains, rank, *kept) = experts((), 7, (4,), kept)

    block_of = jnp.array([BLOCK_OFFSETS.index(j if j <= count // 2 else j - count) for j in range(count)], jnp.int32)
    gain_send = gains[block_of[(spot_of - spot) % count]]

    def weight_grads(expert, *ready):
        return wgrad_call(expert, after(token, *ready), kept)

    def over_cores(grads, *ready):
        return swap_core(after(grads[2], *ready))

    both, last = range(2), 2

    def sum_of(grads, got, part):
        return (grads[1], part), (got, part)

    up_sent, down_sent = ahead(d_far, count), behind(d_l3, count)
    grads = [wgrad_call(0, token, kept, True)]
    got = [[swap_core(v) for v in grads[0][2]]]
    grads.append(weight_grads(1, grads[0][0]))
    up, down = sums_call((grads[1][0], *got[0],), (d_r3, up_sent), (d_l2, down_sent))

    up_sent, down_sent = ahead(up, count), behind(down, count)
    got.append(over_cores(grads[1], up))
    halves = [sums_call((up,), *[((grads[0][1], i), got[0][i]) for i in range(3)])]
    across = [[(swap_x(v), None) for v in halves[0][:2]]]
    gain_dense = lax.all_to_all(after(gain_send, halves[0][0]), "expert", split_axis=0, concat_axis=0, tiled=True)
    gain_dense = gain_dense.reshape(EXPERTS, length)
    grads.append(weight_grads(2, gain_send, *halves[0]))
    up, down = sums_call((gain_dense, grads[2][0], across[0][0][0], across[0][1][0],), (d_r2, up_sent), (d_l1, down_sent))

    up_sent, down_sent = ahead(up, count), behind(down, count)
    got.append(over_cores(grads[2], up))
    halves.append(sums_call((up,), sum_of(grads[1], got[1], both), sum_of(grads[1], got[1], last)))
    across_b = swap_x(halves[1][0])
    y = dict(zip(BLOCK_OFFSETS, value_call(after(token, *halves[1]), rank, kept[4], w_down, slots)))
    late = swap_core(after(grads[0][3], up))
    (up,) = sums_call((y[0], across_b, down_sent, late), (d_r1, up_sent))

    up_sent, y_down = ahead(up, count), behind(after(y[4], up), count)
    across[0].append((swap_x(after(halves[0][2], up)), None))
    across.append([(across_b, 0), (across_b, 1), (swap_x(after(halves[1][1], up)), None)])
    halves.append(sums_call((up,), sum_of(grads[2], got[2], both), sum_of(grads[2], got[2], last)))
    grads.append(weight_grads(3, *halves[2]))
    (down,) = sums_call(
        (up_sent, across[0][2][0], across[1][2][0], grads[3][0]), (y[-3], y_down)
    )

    y_up, y_down, across_d = ahead(after(y[3], down), count), behind(down, count), swap_x(after(halves[2][0], down))
    grad, attn_grad, small, *out_parts = resid_back_call(
        after(token, down), resid, gain_two, cotangent, (d_own, up_sent, down_sent), gain_dense, second,
        attn, out_pieces, shared_pieces,
    )
    def terms_of(expert, i, *ready):
        other = (late, i) if expert == 0 else (got[expert], 3 + i)
        return [(after(grads[expert][0], *ready) if ready else grads[expert][0], i), other, across[expert][i]]

    def finish(ready, expert, kept_out, parts=range(3)):
        return finish_call(holds, [(i, expert, [terms_of(expert, i, *ready)]) for i in parts], kept_out)

    out_first = [swap_core(v) for v in out_parts[4:]]
    finished = finish((grad,), 0, None)
    *out_half, up, down = sums_call(
        (finished[0], across_d), *zip(out_parts[2:4], out_first), (y[2], y_up), (y[-2], y_down)
    )

    y_up, y_down, out_across = ahead(up, count), behind(down, count), [swap_x(v) for v in out_half]
    out_got = swap_core(after(out_parts[1], up))
    input_grad, *qkv_parts = attention_back_call(
        after(token, up), query, key, value, attn_grad, first_low, tokens, gain_one, grad, small, query_pieces,
        shared_pieces, segments, seg_col, cos, sin,
    )
    up, down = sums_call((input_grad, *out_across, out_got), (y[1], y_up), (y[-1], y_down))

    y_up, y_down = ahead(up, count), behind(down, count)
    qkv_first = [swap_core(after(v, up)) for v in qkv_parts[4:]]
    qkv_half = sums_call((up,), *zip(qkv_parts[2:4], qkv_first))
    qkv_across = [swap_x(qkv_half[0])]
    out_parts = spread_call(after(token, *qkv_half), count, out_parts[0], out_got, *out_across)
    finished = finish(qkv_half, 1, finished)
    qkv_got = swap_core(after(qkv_parts[1], qkv_across[0]))
    got.append(over_cores(grads[3], qkv_half[0]))
    (half_e,) = sums_call((finished[0],), sum_of(grads[3], got[3], range(3)))
    across.append([(across_d, 0), (across_d, 1)])
    finished = finish((half_e,), 2, finished, both)
    y_own = after(y[0], qkv_across[0], out_parts[0], finished[0])
    mixed = (resid + sum(t.astype(WIDE) for t in (y_own, y_up, y_down))).astype(LOW)
    qkv_across.append(swap_x(after(qkv_half[1], qkv_across[0])))

    def sum_step(parts, up, down, step):
        up = add_low(parts[step], ahead(up, count))
        down = behind(down, count)
        return up, add_low(parts[count + 1 - step], down) if step > 1 else down

    def copy_step(up, down):
        return up + [ahead(up[-1], count)], down + [behind(down[-1], count)]

    out_up, out_down = after(out_parts[4], mixed), after(out_parts[5], mixed)
    for step in (3, 2, 1):
        out_up, out_down = sum_step(out_parts, out_up, out_down, step)
        if step == 2:
            out_up = after(out_up, qkv_across[1])
    out_own = add_low(out_parts[0], ahead(out_up, count), out_down)
    across_e = [swap_x(after(halves[2][1], qkv_across[1])), swap_x(after(half_e, qkv_across[1]))]
    qkv_parts = spread_call(after(token, out_own), count, qkv_parts[0], qkv_got, *qkv_across)
    across[2].append((across_e[0], None))
    across.append([(across_e[1], i) for i in range(3)])
    out_ups, out_downs = [after(out_own, qkv_parts[0])], [after(out_own, qkv_parts[0])]
    qkv_up, qkv_down = qkv_parts[4], qkv_parts[5]
    for step in (3, 2, 1):
        out_ups, out_downs = copy_step(out_ups, out_downs)
        qkv_up, qkv_down = sum_step(qkv_parts, qkv_up, qkv_down, step)
        qkv_up = after(qkv_up, out_ups[-1], out_downs[-1])
    out_ups.append(ahead(out_ups[-1], count))
    qkv_own = add_low(qkv_parts[0], ahead(qkv_up, count), qkv_down)
    qkv_ups, qkv_downs = [qkv_own], [qkv_own]
    for step in (3, 2, 1):
        qkv_ups, qkv_downs = copy_step(qkv_ups, qkv_downs)
        if step == 3:
            qkv_ups[-1] = after(qkv_ups[-1], out_ups[-1])
    (out_sum,) = assemble_call(after(token, qkv_ups[2]), out_downs + out_ups[:0:-1], (model_width,))
    qkv_ups.append(ahead(after(qkv_ups[-1], out_sum, across_e[1]), count))
    last_rows = [terms_of(2, 2, qkv_ups[3]), terms_of(3, 2)]
    finished = finish_call(
        holds, [(0, 3, [terms_of(3, 0, qkv_ups[3])]), (1, 3, [terms_of(3, 1)]), (2, 2, last_rows)], finished
    )
    query_sum, key_sum, value_sum, router_sum, ffn_gain_sum, attn_gain_sum = assemble_call(
        after(token, finished[0]), qkv_downs + qkv_ups[:0:-1], (model_width, key_width, key_width)
    )
    gate_shard, up_shard, down_shard = finished
    return (
        mixed,
        input_grad,
        attn_gain_sum,
        ffn_gain_sum,
        query_sum,
        key_sum,
        value_sum,
        out_sum,
        router_sum.T,
        gate_shard,
        up_shard,
        down_shard,
    )


def solution(mesh):
    ring = mesh.shape["expert"] == len(BLOCK_OFFSETS) and mesh.shape["wshard"] == 4
    body = per_device_ring if ring else per_device_exchange
    in_specs = (
        P(("expert", "wshard"), None),
        P(("expert", "wshard"), None),
        P(("expert", "wshard"), None),
        P(),
        P(),
        P("wshard", None),
        P("wshard", None),
        P("wshard", None),
        P("wshard", None),
        P("wshard", None),
        P(None, "expert"),
        P(None, "expert"),
        P("expert", None),
        P(("expert", "wshard"), None),
    )
    out_specs = (
        P(("expert", "wshard"), None),
        P(("expert", "wshard"), None),
        P("wshard"),
        P("wshard"),
        P("wshard", None),
        P("wshard", None),
        P("wshard", None),
        P("wshard", None),
        P("wshard", None),
        P("wshard", "expert"),
        P("wshard", "expert"),
        P("expert", "wshard"),
    )
    return jax.shard_map(
        body, mesh=mesh, in_specs=in_specs, out_specs=out_specs, check_vma=False
    )
```

```python
import functools

import jax
import jax.numpy as jnp
from jax import lax
from jax.experimental import pallas as pl
from jax.experimental.pallas import tpu as pltpu
from jax.sharding import PartitionSpec as P

QUERY_HEADS = 12
KEY_VALUE_HEADS = 2
HEAD_DIM = 128
EXPERTS = 32
TOP = 4


EPS = 1e-06
ROPE_BASE = 10000.0
NEG = -1e30
LOW = jnp.bfloat16
WIDE = jnp.float32
MIB = 1024 * 1024
ONCE = pl.Buffered(buffer_count=1)
def norm_forward(values, gain):
    inverse = lax.rsqrt(jnp.mean(values * values, axis=-1) + EPS)
    normed = values * inverse[:, None]
    return (normed * gain, normed, inverse)


def norm_backward(grad, gain, normed, inverse):
    gain_grad = jnp.sum(grad * normed, axis=0)
    scaled = grad * gain
    centred = scaled - normed * jnp.mean(scaled * normed, axis=-1, keepdims=True)
    return (inverse[:, None] * centred, gain_grad)


def rotary_tables(seq_length, head_size):
    half_size = head_size // 2
    frequency = ROPE_BASE ** (-(jnp.arange(half_size, dtype=jnp.float32) * 2.0 / head_size))
    angles = jnp.arange(seq_length, dtype=jnp.float32)[:, None] * frequency[None, :]
    return (jnp.cos(angles), jnp.sin(angles))


def apply_rotation(values, cosine_lookup, sine_lookup):
    half_size = values.shape[-1] // 2
    first_half = values[..., :half_size]
    second_half = values[..., half_size:]
    cos_part = cosine_lookup[:, None, :]
    sin_part = sine_lookup[:, None, :]
    return jnp.concatenate(
        [
            first_half * cos_part - second_half * sin_part,
            second_half * cos_part + first_half * sin_part,
        ],
        axis=-1,
    )


def reverse_rotation(values, cosine_lookup, sine_lookup):
    half_size = values.shape[-1] // 2
    first_half = values[..., :half_size]
    second_half = values[..., half_size:]
    cos_part = cosine_lookup[:, None, :]
    sin_part = sine_lookup[:, None, :]
    return jnp.concatenate(
        [
            first_half * cos_part + second_half * sin_part,
            second_half * cos_part - first_half * sin_part,
        ],
        axis=-1,
    )


def per_device_exchange(
    tokens,
    segments,
    routes,
    attn_gain,
    ffn_gain,
    w_query,
    key_weight,
    value_weight,
    w_out,
    w_router,
    w_gate,
    w_up,
    w_down,
    cotangent,
):
    lower_dtype = jnp.bfloat16
    wide_type = jnp.float32
    sequence_length, model_width = tokens.shape
    top_count = routes.shape[1]
    axis_count = lax.axis_size("expert")
    owners = max(1, axis_count // EXPERTS)
    holds = max(1, EXPERTS // axis_count)
    groups = EXPERTS // holds
    capacity = max(2, 3 * sequence_length * top_count // (2 * EXPERTS))
    hidden_dev = w_gate.shape[1] // holds
    query_group_width = QUERY_HEADS // KEY_VALUE_HEADS
    score_scale = HEAD_DIM ** (-0.5)
    pair_count = sequence_length * top_count
    query_full, key_full, value_full, out_full, router_full = (
        lax.all_gather(w_query, "wshard", axis=0, tiled=True),
        lax.all_gather(key_weight, "wshard", axis=0, tiled=True),
        lax.all_gather(value_weight, "wshard", axis=0, tiled=True),
        lax.all_gather(w_out, "wshard", axis=0, tiled=True),
        lax.all_gather(w_router, "wshard", axis=0, tiled=True),
    )
    stream = tokens.astype(wide_type)
    first_norm, first_normed, first_inverse = norm_forward(stream, attn_gain)
    first_low = first_norm.astype(lower_dtype)
    cosine_lookup, sine_lookup = rotary_tables(sequence_length, HEAD_DIM)
    query_pre = jnp.dot(first_low, query_full, preferred_element_type=wide_type).reshape(
        sequence_length, QUERY_HEADS, HEAD_DIM
    )
    key_unrotated = jnp.dot(first_low, key_full, preferred_element_type=wide_type).reshape(
        sequence_length, KEY_VALUE_HEADS, HEAD_DIM
    )
    query_rotated = (
        apply_rotation(query_pre, cosine_lookup, sine_lookup)
        .astype(lower_dtype)
        .reshape(sequence_length, KEY_VALUE_HEADS, query_group_width, HEAD_DIM)
    )
    key_rotated = apply_rotation(key_unrotated, cosine_lookup, sine_lookup).astype(lower_dtype)
    value_lowered = (
        jnp.dot(first_low, value_full, preferred_element_type=wide_type)
        .astype(lower_dtype)
        .reshape(sequence_length, KEY_VALUE_HEADS, HEAD_DIM)
    )
    positions = jnp.arange(sequence_length)
    offset = positions[:, None] - positions[None, :]
    segment_row = segments[0]
    allowed = (segment_row[:, None] == segment_row[None, :]) & (offset >= 0)
    raw_scores = jnp.einsum(
        "qagd,kad->agqk", query_rotated, key_rotated, preferred_element_type=wide_type
    )
    scores = jnp.where(allowed, raw_scores * score_scale, NEG)
    score_top = jnp.max(scores, axis=-1, keepdims=True)
    expo_terms = jnp.exp(scores - score_top)
    expo_total = jnp.sum(expo_terms, axis=-1, keepdims=True)
    log_total = score_top + jnp.log(expo_total)
    probs_low = (expo_terms / expo_total).astype(lower_dtype)
    attn_low = (
        jnp.einsum("agqk,kad->qagd", probs_low, value_lowered, preferred_element_type=wide_type)
        .astype(lower_dtype)
        .reshape(sequence_length, QUERY_HEADS * HEAD_DIM)
    )
    resid = stream + jnp.dot(attn_low, out_full, preferred_element_type=wide_type)
    second_norm, second_normed, second_inverse = norm_forward(resid, ffn_gain)
    second_low = second_norm.astype(lower_dtype)
    logits = jnp.dot(second_low, router_full, preferred_element_type=wide_type)
    choose = (routes[:, :, None] == jnp.arange(EXPERTS)[None, None, :]).astype(wide_type)
    selected = jnp.sum(choose * logits[:, None, :], axis=-1)
    gate_probs = jax.nn.softmax(selected, axis=-1)
    flat_routes = routes.reshape(pair_count)
    one_hot = (flat_routes[:, None] == jnp.arange(EXPERTS)[None, :]).astype(jnp.int32)
    slot_rank = jnp.sum((jnp.cumsum(one_hot, axis=0) - 1) * one_hot, axis=1)
    slot_index = (flat_routes // holds * capacity + slot_rank) * holds + flat_routes % holds
    slot_pair = (
        jnp.full((EXPERTS * capacity,), pair_count, jnp.int32)
        .at[slot_index]
        .set(jnp.arange(pair_count, dtype=jnp.int32))
    )
    second_ext = jnp.concatenate([second_low, jnp.zeros((1, model_width), lower_dtype)], axis=0)
    send_rows = jnp.repeat(
        second_ext[slot_pair // top_count].reshape(groups, capacity, holds, model_width),
        owners,
        axis=0,
    )
    gate_local = w_gate.reshape(model_width, holds, hidden_dev)
    up_local = w_up.reshape(model_width, holds, hidden_dev)
    down_local = w_down.reshape(holds, hidden_dev, model_width)

    def owner_total(values):
        summed = jnp.sum(
            values.astype(wide_type).reshape(groups, owners, capacity, holds, model_width), axis=1
        )
        return summed.reshape(EXPERTS * capacity, model_width)

    received = lax.all_to_all(send_rows, "expert", split_axis=0, concat_axis=0, tiled=True)
    gate_pre = jnp.einsum("scld,dlf->sclf", received, gate_local, preferred_element_type=wide_type)
    up_pre = jnp.einsum("scld,dlf->sclf", received, up_local, preferred_element_type=wide_type)
    hidden = (jax.nn.silu(gate_pre) * up_pre).astype(lower_dtype)
    partial_value = jnp.einsum(
        "sclf,lfd->scld", hidden, down_local, preferred_element_type=wide_type
    ).astype(lower_dtype)
    returned = lax.all_to_all(partial_value, "expert", split_axis=0, concat_axis=0, tiled=True)
    expert_wide = owner_total(returned)[slot_index].reshape(sequence_length, top_count, model_width)
    mixed = (resid + jnp.sum(gate_probs[:, :, None] * expert_wide, axis=1)).astype(lower_dtype)
    upstream = cotangent.astype(wide_type)
    query_back, key_back, value_back, out_back, router_back = (
        lax.all_gather(w_query, "wshard", axis=0, tiled=True),
        lax.all_gather(key_weight, "wshard", axis=0, tiled=True),
        lax.all_gather(value_weight, "wshard", axis=0, tiled=True),
        lax.all_gather(w_out, "wshard", axis=0, tiled=True),
        lax.all_gather(w_router, "wshard", axis=0, tiled=True),
    )
    gate_grad = jnp.sum(expert_wide * upstream[:, None, :], axis=-1)
    sel_grad = gate_probs * (gate_grad - jnp.sum(gate_probs * gate_grad, axis=-1, keepdims=True))
    logit_grad = jnp.sum(choose * sel_grad[:, :, None], axis=1).astype(lower_dtype)
    pair_grad = (
        (gate_probs[:, :, None] * upstream[:, None, :])
        .astype(lower_dtype)
        .reshape(pair_count, model_width)
    )
    pair_ext = jnp.concatenate([pair_grad, jnp.zeros((1, model_width), lower_dtype)], axis=0)
    grad_send = jnp.repeat(
        pair_ext[slot_pair].reshape(groups, capacity, holds, model_width), owners, axis=0
    )
    grad_recv, rows_recv = (
        lax.all_to_all(grad_send, "expert", split_axis=0, concat_axis=0, tiled=True),
        lax.all_to_all(send_rows, "expert", split_axis=0, concat_axis=0, tiled=True),
    )
    gate_pre = jnp.einsum("scld,dlf->sclf", rows_recv, gate_local, preferred_element_type=wide_type)
    up_pre = jnp.einsum("scld,dlf->sclf", rows_recv, up_local, preferred_element_type=wide_type)
    sigmoid_gate = jax.nn.sigmoid(gate_pre)
    silu_gate = gate_pre * sigmoid_gate
    hidden = (silu_gate * up_pre).astype(lower_dtype)
    hidden_grad = jnp.einsum(
        "scld,lfd->sclf", grad_recv, down_local, preferred_element_type=wide_type
    )
    gate_pre_grad = (
        hidden_grad * up_pre * sigmoid_gate * (1.0 + gate_pre * (1.0 - sigmoid_gate))
    ).astype(lower_dtype)
    up_pre_grad = (hidden_grad * silu_gate).astype(lower_dtype)
    row_grad = (
        jnp.einsum("sclf,dlf->scld", gate_pre_grad, gate_local, preferred_element_type=wide_type)
        + jnp.einsum("sclf,dlf->scld", up_pre_grad, up_local, preferred_element_type=wide_type)
    ).astype(lower_dtype)
    returned_grad = lax.all_to_all(row_grad, "expert", split_axis=0, concat_axis=0, tiled=True)
    gate_wgrad = jnp.einsum(
        "scld,sclf->dlf", rows_recv, gate_pre_grad, preferred_element_type=wide_type
    ).reshape(model_width, holds * hidden_dev)
    up_wgrad = jnp.einsum(
        "scld,sclf->dlf", rows_recv, up_pre_grad, preferred_element_type=wide_type
    ).reshape(model_width, holds * hidden_dev)
    down_wgrad = jnp.einsum(
        "sclf,scld->lfd", hidden, grad_recv, preferred_element_type=wide_type
    ).reshape(holds * hidden_dev, model_width)
    gate_shard, up_shard, down_shard = (
        lax.psum_scatter(
            gate_wgrad.astype(jnp.bfloat16), "wshard", scatter_dimension=0, tiled=True
        ).astype(jnp.float32),
        lax.psum_scatter(
            up_wgrad.astype(jnp.bfloat16), "wshard", scatter_dimension=0, tiled=True
        ).astype(jnp.float32),
        lax.psum_scatter(
            down_wgrad.astype(jnp.bfloat16), "wshard", scatter_dimension=1, tiled=True
        ).astype(jnp.float32),
    )
    token_grad = owner_total(returned_grad)[slot_index].reshape(
        sequence_length, top_count, model_width
    )
    second_grad = jnp.sum(token_grad, axis=1) + jnp.dot(
        logit_grad, router_back.T, preferred_element_type=wide_type
    )
    router_wgrad = jnp.einsum("td,te->de", second_low, logit_grad, preferred_element_type=wide_type)
    resid_part, ffn_gain_grad = norm_backward(second_grad, ffn_gain, second_normed, second_inverse)
    resid_grad = upstream + resid_part
    resid_low = resid_grad.astype(lower_dtype)
    out_wgrad = jnp.einsum("tc,td->cd", attn_low, resid_low, preferred_element_type=wide_type)
    attn_grad = (
        jnp.dot(resid_low, out_back.T, preferred_element_type=wide_type)
        .astype(lower_dtype)
        .reshape(sequence_length, KEY_VALUE_HEADS, query_group_width, HEAD_DIM)
    )
    raw_again = jnp.einsum(
        "qagd,kad->agqk", query_rotated, key_rotated, preferred_element_type=wide_type
    )
    scores_again = jnp.where(allowed, raw_again * score_scale, NEG)
    probs_again = jnp.exp(scores_again - log_total)
    prob_grad = jnp.einsum(
        "qagd,kad->agqk", attn_grad, value_lowered, preferred_element_type=wide_type
    )
    row_delta = jnp.sum(probs_again * prob_grad, axis=-1, keepdims=True)
    score_grad = (probs_again * (prob_grad - row_delta) * score_scale).astype(lower_dtype)
    value_grad = (
        jnp.einsum("agqk,qagd->kad", probs_low, attn_grad, preferred_element_type=wide_type)
        .astype(lower_dtype)
        .reshape(sequence_length, KEY_VALUE_HEADS * HEAD_DIM)
    )
    query_rot_grad = jnp.einsum(
        "agqk,kad->qagd", score_grad, key_rotated, preferred_element_type=wide_type
    ).reshape(sequence_length, QUERY_HEADS, HEAD_DIM)
    key_rotated_gradient = jnp.einsum(
        "agqk,qagd->kad", score_grad, query_rotated, preferred_element_type=wide_type
    )
    query_grad = (
        reverse_rotation(query_rot_grad, cosine_lookup, sine_lookup)
        .astype(lower_dtype)
        .reshape(sequence_length, QUERY_HEADS * HEAD_DIM)
    )
    key_grad = (
        reverse_rotation(key_rotated_gradient, cosine_lookup, sine_lookup)
        .astype(lower_dtype)
        .reshape(sequence_length, KEY_VALUE_HEADS * HEAD_DIM)
    )
    query_wgrad = jnp.einsum("td,tc->dc", first_low, query_grad, preferred_element_type=wide_type)
    key_wgrad = jnp.einsum("td,tc->dc", first_low, key_grad, preferred_element_type=wide_type)
    value_wgrad = jnp.einsum("td,tc->dc", first_low, value_grad, preferred_element_type=wide_type)
    first_grad = (
        jnp.dot(query_grad, query_back.T, preferred_element_type=wide_type)
        + jnp.dot(key_grad, key_back.T, preferred_element_type=wide_type)
        + jnp.dot(value_grad, value_back.T, preferred_element_type=wide_type)
    )
    stream_part, attn_gain_grad = norm_backward(first_grad, attn_gain, first_normed, first_inverse)
    input_grad = resid_grad + stream_part
    query_part, key_part, value_part, out_part, router_part, attn_gain_part, ffn_gain_part = (
        lax.psum_scatter(
            query_wgrad.astype(jnp.bfloat16), "wshard", scatter_dimension=0, tiled=True
        ).astype(jnp.float32),
        lax.psum_scatter(
            key_wgrad.astype(jnp.bfloat16), "wshard", scatter_dimension=0, tiled=True
        ).astype(jnp.float32),
        lax.psum_scatter(
            value_wgrad.astype(jnp.bfloat16), "wshard", scatter_dimension=0, tiled=True
        ).astype(jnp.float32),
        lax.psum_scatter(
            out_wgrad.astype(jnp.bfloat16), "wshard", scatter_dimension=0, tiled=True
        ).astype(jnp.float32),
        lax.psum_scatter(
            router_wgrad.astype(jnp.bfloat16), "wshard", scatter_dimension=0, tiled=True
        ).astype(jnp.float32),
        lax.psum_scatter(
            attn_gain_grad.astype(jnp.bfloat16), "wshard", scatter_dimension=0, tiled=True
        ).astype(jnp.float32),
        lax.psum_scatter(
            ffn_gain_grad.astype(jnp.bfloat16), "wshard", scatter_dimension=0, tiled=True
        ).astype(jnp.float32),
    )
    query_sum, key_sum, value_sum, out_sum, router_sum, attn_gain_sum, ffn_gain_sum = lax.psum(
        (query_part, key_part, value_part, out_part, router_part, attn_gain_part, ffn_gain_part),
        "expert",
    )
    return (
        mixed,
        input_grad,
        attn_gain_sum,
        ffn_gain_sum,
        query_sum,
        key_sum,
        value_sum,
        out_sum,
        router_sum,
        gate_shard,
        up_shard,
        down_shard,
    )


BLOCK_OFFSETS = (-1, 1, -2, 2, -3, 3, 0, 4)


def ring_order(count):
    return [0] + list(range(1, count, 2)) + list(range(count - 2, 0, -2))


def shifted(value, step, count):
    order = ring_order(count)
    return lax.ppermute(value, "expert", [(order[i], order[(i + step) % count]) for i in range(count)])


def ahead(value, count):
    return shifted(value, 1, count)


def behind(value, count):
    return shifted(value, -1, count)


def swap_core(value):
    size = lax.axis_size("wshard")
    return lax.ppermute(value, "wshard", [(i, i ^ 1) for i in range(size)])


def swap_x(value):
    size = lax.axis_size("wshard")
    return lax.ppermute(value, "wshard", [(i, i ^ 2) for i in range(size)])


def work(flops, bytes_accessed, transcendentals):
    scale = 8
    return pl.CostEstimate(
        flops=flops // scale, bytes_accessed=bytes_accessed // scale, transcendentals=transcendentals // scale
    )


def add_low(*terms):
    return sum(term.astype(WIDE) for term in terms).astype(LOW)


def after(value, *others):
    return lax.optimization_barrier((value, *others))[0]


def places(rank_row, slots):
    rows = lax.broadcasted_iota(jnp.int32, (slots, rank_row.shape[-1]), 0)
    return rank_row == rows


def expert_ranks(routes, holds):
    tokens = routes.shape[1]
    names = [jnp.sum((routes == l).astype(WIDE), axis=0, keepdims=True) for l in range(holds)]
    names = jnp.concatenate(names + [jnp.zeros((16 - holds, tokens), WIDE)], axis=0)
    rows = lax.broadcasted_iota(jnp.int32, (tokens, tokens), 0)
    columns = lax.broadcasted_iota(jnp.int32, (tokens, tokens), 1)
    before = dot(names.astype(LOW), (rows <= columns).astype(WIDE).astype(LOW))
    return jnp.where(names > 0.0, before - 1.0, -1.0)[:holds].astype(jnp.int32)


def pack_routing(gates, routes):
    high = gates.astype(LOW).astype(WIDE)
    rows = [high, gates - high, routes.astype(WIDE)]
    spare = 16 - 3 * gates.shape[0]
    return jnp.concatenate(rows + [jnp.zeros((spare, gates.shape[1]), WIDE)], axis=0).astype(LOW)


def unpack_routing(packed):
    top_count = TOP
    packed = packed.astype(WIDE)
    return packed[:top_count] + packed[top_count : 2 * top_count], packed[2 * top_count : 3 * top_count]


def dot_t(a, b):
    return lax.dot_general(a, b, (((0,), (0,)), ((), ())), preferred_element_type=WIDE)


def dot_bt(a, b):
    return lax.dot_general(a, b, (((1,), (1,)), ((), ())), preferred_element_type=WIDE)


def dot(a, b):
    return jnp.dot(a, b, preferred_element_type=WIDE)


def expert_kernel(count, slots, aliased, *refs):
    token_ref = refs[0]
    h_refs, dz_refs = refs[1 : 1 + count], refs[1 + count : 1 + 2 * count]
    wg_ref, wu_ref, wd_ref = refs[1 + 2 * count : 4 + 2 * count]
    rest = refs[4 + 2 * count + (7 if aliased else 0) :]
    d_refs = rest[:count]
    gain_ref, rank_ref, rows_out, dz_out, gg_out, ug_out, hid_out = rest[count : count + 7]
    place_scr, back_scr, gate_scr, wg_scr, wu_scr, wd_scr, sems = rest[count + 7 :]
    e = pl.program_id(0)
    holds, tokens = rank_ref.shape[1:]
    hidden_width = wd_scr.shape[1]

    def weights(expert, slot):
        band = pl.ds(pl.multiple_of(expert * hidden_width, hidden_width), hidden_width)
        return [
            pltpu.make_async_copy(source, target.at[slot], sems.at[slot, i])
            for i, (source, target) in enumerate(
                ((wg_ref.at[:, band], wg_scr), (wu_ref.at[:, band], wu_scr), (wd_ref.at[band, :], wd_scr))
            )
        ]

    slot = lax.rem(e, 2)

    @pl.when(e == 0)
    def _():
        for copy in weights(0, 0):
            copy.start()

    @pl.when(e + 1 < holds)
    def _():
        for copy in weights(e + 1, 1 - slot):
            copy.start()

    here = pl.ds(pl.multiple_of(e * slots, slots), slots)
    @pl.when(e == 0)
    def _():
        for b, (h_ref, dz_ref) in enumerate(zip(h_refs, dz_refs)):
            gates, routes = unpack_routing(h_ref[tokens : tokens + 16, :tokens])
            routes = routes - (token_ref[1] * holds).astype(WIDE)
            ranks = expert_ranks(routes, holds)
            rank_ref[b] = ranks
            for l in range(holds):
                band = slice(l * slots, (l + 1) * slots)
                spot = places(ranks[l : l + 1], slots).astype(WIDE)
                named = jnp.where(routes == l, gates, 0.0)
                gate_scr[b, band, :] = jnp.broadcast_to(
                    jnp.sum(spot * jnp.sum(named, axis=0, keepdims=True), axis=1, keepdims=True), (slots, 128)
                )
                place_scr[b, band, :] = spot.astype(LOW)
            for source, target in ((h_ref, rows_out), (dz_ref, dz_out)):
                taken = dot(place_scr[b], source[:tokens]).astype(LOW)
                for l in range(holds):
                    target[l, b * slots : (b + 1) * slots, :] = taken[l * slots : (l + 1) * slots]

    gate = jnp.concatenate([gate_scr[b, here, :] for b in range(count)], axis=0)[:, :1]
    rows = rows_out[e]
    for copy in weights(e, slot):
        copy.wait()
    gate_pre = dot(rows, wg_scr[slot])
    up_pre = dot(rows, wu_scr[slot])
    sig = jax.nn.sigmoid(gate_pre)
    silu = gate_pre * sig
    hidden = (silu * up_pre).astype(LOW).astype(WIDE)
    back = dot_bt(dz_out[e], wd_scr[slot])
    gains = jnp.sum(back * hidden, axis=1, keepdims=True)
    back = back * gate
    gate_grad = (back * (up_pre * sig * (1.0 + gate_pre * (1.0 - sig)))).astype(LOW)
    up_grad = (back * silu).astype(LOW)
    gg_out[0] = gate_grad
    ug_out[0] = up_grad
    hid_out[0] = (hidden * gate).astype(LOW)
    row_grad = (dot_bt(gate_grad, wg_scr[slot]) + dot_bt(up_grad, wu_scr[slot])).astype(LOW)
    for b in range(count):
        band = slice(b * slots, (b + 1) * slots)
        back_scr[b, here, :] = row_grad[band]
        spot = place_scr[b, here, :].astype(WIDE)
        gain_ref[b, pl.ds(e, 1), :] = jnp.sum(spot * gains[band], axis=0, keepdims=True)

    @pl.when(e == pl.num_programs(0) - 1)
    def _():
        for b in range(count):
            d_refs[b][...] = dot_t(place_scr[b], back_scr[b]).astype(LOW)


def expert_call(token, first, blocks, dz_blocks, w_gate, w_up, w_down, kept, holds, slots, total):
    count = len(blocks)
    tokens, width = dz_blocks[0].shape
    hidden = w_gate.shape[1] // holds
    whole = lambda *shape: pl.BlockSpec(shape, lambda e: (0,) * len(shape))
    once = lambda *shape: pl.BlockSpec(shape, lambda e: (0,) * len(shape), pipeline_mode=pl.Buffered(buffer_count=1))
    aliased = kept is not None
    in_specs = (
        [pl.BlockSpec(memory_space=pltpu.SMEM)]
        + [once(*b.shape) for b in (*blocks, *dz_blocks)]
        + [pl.BlockSpec(memory_space=pl.ANY)] * 3
    )
    aliases = {len(in_specs) + i: count + i for i in range(7)} if aliased else {}
    out = pl.pallas_call(
        functools.partial(expert_kernel, count, slots, aliased),
        grid=(holds,),
        in_specs=in_specs + ([pl.BlockSpec(memory_space=pl.ANY)] * 7 if aliased else []),
        out_specs=[whole(tokens, width)] * count
        + [pl.BlockSpec((count, holds, tokens), lambda e: (first // count, 0, 0))] * 2
        + [pl.BlockSpec((holds, count * slots, width), lambda e: (0, first // count, 0))] * 2
        + [pl.BlockSpec((1, count * slots, hidden), lambda e: (e, first // count, 0))] * 3,
        out_shape=[shaped(tokens, width)] * count
        + [shaped(total, holds, tokens, dtype=WIDE), shaped(total, holds, tokens, dtype=jnp.int32)]
        + [shaped(holds, total * slots, width)] * 2
        + [shaped(holds, total * slots, hidden)] * 3,
        scratch_shapes=[
            pltpu.VMEM((count, holds * slots, tokens), LOW),
            pltpu.VMEM((count, holds * slots, width), LOW),
            pltpu.VMEM((count, holds * slots, 128), WIDE),
            pltpu.VMEM((2, width, hidden), LOW),
            pltpu.VMEM((2, width, hidden), LOW),
            pltpu.VMEM((2, hidden, width), LOW),
            pltpu.SemaphoreType.DMA((2, 3)),
        ],
        input_output_aliases=aliases,
        compiler_params=pltpu.CompilerParams(vmem_limit_bytes=60 * MIB),
        cost_estimate=work(
            flops=2 * holds * count * slots * width * (5 * hidden + 3 * tokens),
            bytes_accessed=3 * holds * width * hidden * 2
            + count * tokens * width * 6
            + holds * count * slots * (2 * width + 3 * hidden) * 2,
            transcendentals=holds * count * slots * hidden,
        ),
    )(token, *blocks, *dz_blocks, w_gate, w_up, w_down, *(kept if aliased else ()))
    return out[:count], tuple(out[count:])


def value_kernel(slots, _, rank_ref, hid_ref, wd_ref, *refs):
    total, holds, tokens = rank_ref.shape
    y_refs, (value_scr, place_scr) = refs[:total], refs[total:]
    e = pl.program_id(0)
    here = pl.ds(pl.multiple_of(e * slots, slots), slots)
    value = dot(hid_ref[0], wd_ref[...]).astype(LOW)
    for b in range(total):
        value_scr[b, here, :] = value[b * slots : (b + 1) * slots]

    @pl.when(e == pl.num_programs(0) - 1)
    def _():
        for b in range(total):
            for l in range(holds):
                spot = places(rank_ref[b, l : l + 1, :], slots)
                place_scr[l * slots : (l + 1) * slots, :] = spot.astype(WIDE).astype(LOW)
            y_refs[b][...] = dot_t(place_scr[...], value_scr[b]).astype(LOW)


def value_call(token, rank, hidden_rows, w_down, slots):
    total, holds, tokens = rank.shape
    width = w_down.shape[1]
    hidden = hidden_rows.shape[2]
    whole = lambda *shape: pl.BlockSpec(shape, lambda e: (0,) * len(shape))
    out = pl.pallas_call(
        functools.partial(value_kernel, slots),
        grid=(holds,),
        in_specs=[
            pl.BlockSpec(memory_space=pltpu.SMEM),
            whole(*rank.shape),
            pl.BlockSpec((1, total * slots, hidden), lambda e: (e, 0, 0)),
            pl.BlockSpec((hidden, width), lambda e: (e, 0)),
        ],
        out_specs=[whole(tokens, width)] * total,
        out_shape=[shaped(tokens, width)] * total,
        scratch_shapes=[pltpu.VMEM((total, holds * slots, width), LOW), pltpu.VMEM((holds * slots, tokens), LOW)],
        compiler_params=pltpu.CompilerParams(vmem_limit_bytes=60 * MIB),
        cost_estimate=work(
            flops=2 * total * holds * slots * width * (hidden + tokens),
            bytes_accessed=2 * (holds * hidden * (width + total * slots) + total * tokens * width),
            transcendentals=0,
        ),
    )(token, rank, hidden_rows, w_down)
    return out


def wgrad_kernel(apart, place_ref, rows_ref, dz_ref, gg_ref, ug_ref, hid_ref, *outs):
    step = pl.program_id(0)
    shard = outs[0].shape[1]
    columns = pl.ds(pl.multiple_of(jnp.bitwise_xor(place_ref[0], step) * shard, 128), shard)
    rows, grads = rows_ref[0, :, columns], dz_ref[0, :, columns]
    parts = [dot_t(rows, gg_ref[0]), dot_t(rows, ug_ref[0]), dot_t(grads, hid_ref[0])]
    parts = [part.astype(LOW) for part in parts]
    for s in range(4):

        @pl.when(step == s)
        def _():
            for i, part in enumerate(parts):
                if s == 3 and apart:
                    outs[3 + i][...] = part
                elif s % 2 and not apart:
                    outs[2][3 - 3 * (s // 2) + i] = part
                else:
                    outs[s if apart else s // 2][i] = part


def wgrad_call(expert, place, kept, apart=False):
    _, count, width = kept[0].shape
    hidden = kept[2].shape[2]
    shard = width // 4
    row_spec = lambda d: pl.BlockSpec((1, count, d), lambda s: (expert, 0, 0), pipeline_mode=pl.Buffered(buffer_count=1))
    shapes = [(3, shard, hidden)] * 3 + [(shard, hidden)] * 3 if apart else [(3, shard, hidden)] * 2 + [(6, shard, hidden)]
    out = pl.pallas_call(
        functools.partial(wgrad_kernel, apart),
        grid=(4,),
        in_specs=[pl.BlockSpec(memory_space=pltpu.SMEM), row_spec(width), row_spec(width)] + [row_spec(hidden)] * 3,
        out_specs=[pl.BlockSpec(shape, lambda s, zeros=(0,) * len(shape): zeros) for shape in shapes],
        out_shape=[shaped(*shape) for shape in shapes],
        compiler_params=pltpu.CompilerParams(vmem_limit_bytes=60 * MIB),
        cost_estimate=work(
            flops=2 * count * width * 3 * hidden,
            bytes_accessed=2 * (count * (2 * width + 3 * hidden) + 3 * width * hidden),
            transcendentals=0,
        ),
    )(place, *kept)
    return (out[0], out[2], out[3:], out[1]) if apart else out


def sums_call(gates, *sums):
    every = [term[0] if isinstance(term, tuple) else term for terms in sums for term in terms]

    def part_of(term, ready=()):
        array, part = term if isinstance(term, tuple) else (term, None)
        array = after(array, *ready) if ready else array
        return array if part is None else array[: len(part)] if isinstance(part, range) else array[part]

    totals = [add_low(part_of(terms[0], (*gates, *every)), *map(part_of, terms[1:])) for terms in sums]
    return totals


def finish_kernel(sizes, turned, *refs):
    outs = refs[-len(sizes) :]
    at = 0
    for counts, turn, out in zip(sizes, turned, outs):
        for i, size in enumerate(counts):
            total = sum(ref[...].astype(WIDE) for ref in refs[at : at + size])
            at += size
            if turn:
                height = out.shape[0] // len(counts)
                out[i * height : (i + 1) * height, :] = jnp.transpose(total)
            else:
                out[...] = total


def finish_call(holds, pieces, kept):
    shard, hidden = pieces[0][2][0][0][0].shape[-2:]
    steps = shard // 128
    wide, tall = shaped(shard, holds * hidden, dtype=WIDE), shaped(holds * hidden, shard, dtype=WIDE)
    flat = [term for _, _, experts in pieces for terms in experts for term in terms]
    out_specs, out_shapes = [], []
    for which, expert, experts in pieces:
        number = len(experts)
        if which < 2:
            out_specs.append(pl.BlockSpec((128, hidden), lambda s, expert=expert: (s, expert)))
        else:
            block = (number * hidden, 128)
            out_specs.append(pl.BlockSpec(block, lambda s, at=expert // number: (at, s)))
        out_shapes.append(wide if which < 2 else tall)
    kept_in = [kept[which] for which, _, _ in pieces] if kept else []
    out = pl.pallas_call(
        functools.partial(
            finish_kernel, [[len(terms) for terms in experts] for _, _, experts in pieces], [p[0] == 2 for p in pieces]
        ),
        grid=(steps,),
        in_specs=[
            pl.BlockSpec((128, hidden), lambda s: (s, 0))
            if at is None
            else pl.BlockSpec((None, 128, hidden), lambda s, at=at: (at, s, 0))
            for _, at in flat
        ]
        + [pl.BlockSpec(memory_space=pl.ANY)] * len(kept_in),
        out_specs=out_specs,
        out_shape=out_shapes,
        input_output_aliases={len(flat) + i: i for i in range(len(kept_in))},
        compiler_params=pltpu.CompilerParams(vmem_limit_bytes=20 * MIB),
        cost_estimate=work(flops=0, bytes_accessed=30 * shard * hidden, transcendentals=0),
    )(*[array for array, _ in flat], *kept_in)
    result = list(kept) if kept else [None] * 3
    for (which, _, _), value in zip(pieces, out):
        result[which] = value
    return result


def piece_columns(mine, s, shard):
    return pl.ds(pl.multiple_of(jnp.bitwise_xor(mine, s) * shard, 128), shard)


def turn(values, cos, sin):
    return values * cos + pltpu.roll(values, HEAD_DIM // 2, 1) * sin


def turn_back(values, cos, sin):
    return values * cos - pltpu.roll(values, HEAD_DIM // 2, 1) * sin


def inverse_rms(values):
    return lax.rsqrt(jnp.mean(values * values, axis=-1, keepdims=True) + EPS)


def head_slice(h):
    return slice(h * HEAD_DIM, (h + 1) * HEAD_DIM)


def stacked_heads(ref, band, group, heads):
    return jnp.concatenate([ref[band, head_slice(group * heads + h)] for h in range(heads)], axis=0)


def probabilities(queries, keys, allowed):
    scores = jnp.where(allowed, dot_bt(queries, keys) * HEAD_DIM ** (-0.5), NEG)
    expo = jnp.exp(scores - jnp.max(scores, axis=-1, keepdims=True))
    return expo * (1.0 / jnp.sum(expo, axis=-1, keepdims=True))


def allowed_pairs(seg_col_ref, seg_row_ref, band, reach, heads):
    size = band.stop - band.start
    rows = band.start + lax.broadcasted_iota(jnp.int32, (size, reach), 0)
    cols = lax.broadcasted_iota(jnp.int32, (size, reach), 1)
    ok = (seg_col_ref[band, :] == seg_row_ref[:, :reach]) & (cols <= rows)
    return jnp.concatenate([ok] * heads, axis=0)


def attention_kernel(
    mine_ref, tokens_ref, gain_ref, p0, p1, p2, p3, s0, s1, s2, s3, seg_row_ref, seg_col_ref, cos_ref, sin_ref,
    h_ref, q_ref, k_ref, v_ref, out_ref,
):
    mine = mine_ref[0]
    stream = tokens_ref[...].astype(WIDE)
    h_ref[...] = (stream * inverse_rms(stream) * gain_ref[...]).astype(LOW)
    shard = p0.shape[0]
    width = q_ref.shape[1]
    cos, sin = cos_ref[...], sin_ref[...]

    def projected(pieces, columns):
        return sum(dot(h_ref[:, piece_columns(mine, s, shard)], piece[:, columns]) for s, piece in enumerate(pieces))

    heads = QUERY_HEADS // KEY_VALUE_HEADS
    key_width = KEY_VALUE_HEADS * HEAD_DIM
    shared = (s0, s1, s2, s3)
    keys = projected(shared, slice(0, key_width))
    for g in range(KEY_VALUE_HEADS):
        k_ref[:, head_slice(g)] = turn(keys[:, head_slice(g)], cos, sin).astype(LOW)
    v_ref[...] = projected(shared, slice(key_width, 2 * key_width)).astype(LOW)
    group_width = heads * HEAD_DIM
    for g in range(KEY_VALUE_HEADS):
        queries = projected((p0, p1, p2, p3), slice(g * group_width, (g + 1) * group_width))
        for h in range(heads):
            q_ref[:, head_slice(g * heads + h)] = turn(queries[:, head_slice(h)], cos, sin).astype(LOW)
    length = q_ref.shape[0]
    tile = 128
    for start in range(0, length, tile):
        band, reach = slice(start, start + tile), start + tile
        allowed = allowed_pairs(seg_col_ref, seg_row_ref, band, reach, heads)
        for g in range(KEY_VALUE_HEADS):
            probs = probabilities(stacked_heads(q_ref, band, g, heads), k_ref[:reach, head_slice(g)], allowed)
            mixed = dot(probs.astype(LOW), v_ref[:reach, head_slice(g)]).astype(LOW)
            for h in range(heads):
                out_ref[band, head_slice(g * heads + h)] = mixed[h * tile : (h + 1) * tile]


def vmem_call(kernel, out_shape, flops, transcendentals, token, *args):
    moved = sum(a.size * a.dtype.itemsize for a in args) + sum(
        o.size * o.dtype.itemsize for o in jax.tree.leaves(out_shape)
    )
    return pl.pallas_call(
        kernel,
        in_specs=[pl.BlockSpec(memory_space=pltpu.SMEM)] + [pl.BlockSpec(memory_space=pltpu.VMEM)] * len(args),
        out_specs=[pl.BlockSpec(memory_space=pltpu.VMEM)] * len(out_shape),
        out_shape=out_shape,
        compiler_params=pltpu.CompilerParams(vmem_limit_bytes=32 * MIB),
        cost_estimate=work(flops=flops, bytes_accessed=moved, transcendentals=transcendentals),
    )(token, *args)


def shaped(*shape, dtype=LOW):
    return jax.ShapeDtypeStruct(shape, dtype)


def attention_call(mine, tokens, gain, pieces, shared_pieces, seg_row, seg_col, cos, sin):
    length, width = tokens.shape
    key_width = KEY_VALUE_HEADS * HEAD_DIM
    return vmem_call(
        attention_kernel,
        [shaped(length, width), shaped(length, width), shaped(length, key_width), shaped(length, key_width), shaped(length, width)],
        2 * length * width * (width + 2 * key_width) + 3 * length * length * width,
        QUERY_HEADS * length * length,
        mine, tokens, gain, *pieces, *shared_pieces, seg_row, seg_col, cos, sin,
    )


def project_kernel(
    mine_ref, tokens_ref, attn_ref, p0, p1, p2, p3, r0, r1, r2, r3, gain_ref, routes_ref, resid_ref, h_ref
):
    mine = mine_ref[0]
    shard = p0.shape[0]
    resid = tokens_ref[...].astype(WIDE)
    for s, piece in enumerate((p0, p1, p2, p3)):
        resid = resid + dot(attn_ref[:, piece_columns(mine, s, shard)], piece[...])
    resid_ref[...] = resid
    length, width = resid.shape
    h_ref[:length] = (resid * inverse_rms(resid) * gain_ref[...]).astype(LOW)
    logits = jnp.transpose(
        sum(
            dot(h_ref[:length, piece_columns(mine, s, shard)], piece[...])
            for s, piece in enumerate((r0, r1, r2, r3))
        )
    )
    experts = lax.broadcasted_iota(jnp.int32, logits.shape, 0)
    picked = [
        jnp.sum(jnp.where(experts == routes_ref[k : k + 1, :], logits, 0.0), axis=0, keepdims=True)
        for k in range(routes_ref.shape[0])
    ]
    top = functools.reduce(jnp.maximum, picked)
    expo = [jnp.exp(p - top) for p in picked]
    total = sum(expo)
    gates = jnp.concatenate([x / total for x in expo], axis=0)
    h_ref[length:] = jnp.zeros((16, width), LOW)
    h_ref[length:, :length] = pack_routing(gates, routes_ref[...])


def project_call(mine, tokens, attn, pieces, shared_pieces, gain, routes_t):
    length, width = tokens.shape
    whole = lambda shape: pl.BlockSpec(shape, lambda i: (0,) * len(shape), pipeline_mode=ONCE)
    shapes = [shaped(length, width, dtype=WIDE), shaped(length + 16, width)]
    return pl.pallas_call(
        project_kernel,
        grid=(1,),
        in_specs=[pl.BlockSpec(memory_space=pltpu.SMEM)]
        + [whole(a.shape) for a in (tokens, attn, *pieces)]
        + router_columns(shared_pieces)
        + [whole(gain.shape), whole(routes_t.shape)],
        out_specs=[whole(s.shape) for s in shapes],
        out_shape=shapes,
        compiler_params=pltpu.CompilerParams(vmem_limit_bytes=30 * MIB),
        cost_estimate=work(
            flops=2 * length * width * (width + EXPERTS), bytes_accessed=length * width * 20, transcendentals=length * 8
        ),
    )(mine, tokens, attn, *pieces, *shared_pieces, gain, routes_t)


def as_column(row):
    return jnp.transpose(jnp.broadcast_to(row, (8, row.shape[1])))[:, :1]


def norm_back(grad, gain, normed, inverse):
    scaled = grad * gain
    return inverse * (scaled - normed * jnp.mean(scaled * normed, axis=-1, keepdims=True))


def shard_parts(targets):
    at, parts = 0, []
    for target in targets:
        parts.append((target, slice(at, at + target.shape[0])))
        at += target.shape[0]
    return parts


def resid_back_kernel(
    mine_ref, resid_ref, gain_ref, dz_ref, t0, t1, t2, gains_ref, h_ref, attn_ref,
    p0, p1, p2, p3, r0, r1, r2, r3, grad_ref, attn_grad_ref, small_ref, o0, o1, o2, o3, o4, o5, second_scr, low_scr,
):
    mine = mine_ref[0]
    shard, width = p0.shape
    length = resid_ref.shape[0]
    routers = (r0, r1, r2, r3)
    gains = gains_ref[...]
    experts = lax.broadcasted_iota(jnp.int32, gains.shape, 0)
    gate_rows, routes = unpack_routing(h_ref[length:, :length])
    gates = jnp.zeros(gains.shape, WIDE)
    for k in range(TOP):
        gates = gates + jnp.where(experts.astype(WIDE) == routes[k : k + 1], gate_rows[k : k + 1], 0.0)
    logit_grad = gates * (gains - jnp.sum(gates * gains, axis=0, keepdims=True))
    logit_grad = jnp.concatenate([logit_grad, jnp.zeros((128 - EXPERTS, length), WIDE)], axis=0)
    logit_grad = jnp.transpose(logit_grad).astype(LOW)
    second_scr[...] = t0[...].astype(WIDE) + t1[...].astype(WIDE) + t2[...].astype(WIDE)
    for s, piece in enumerate(routers):
        columns = piece_columns(mine, s, shard)
        second_scr[:, columns] = second_scr[:, columns] + dot_bt(logit_grad, piece[...])
    resid = resid_ref[...]
    inverse = inverse_rms(resid)
    normed = resid * inverse
    second = second_scr[...]
    gain_grad = jnp.sum(second * normed, axis=0, keepdims=True)
    grad = dz_ref[...].astype(WIDE) + norm_back(second, gain_ref[...], normed, inverse)
    grad_ref[...] = grad
    low_scr[...] = grad.astype(LOW)
    second_scr[:1, :] = gain_grad
    low = low_scr[...]
    for s, piece in enumerate((p0, p1, p2, p3)):
        columns = piece_columns(mine, s, shard)
        attn_grad_ref[:, columns] = dot_bt(low, piece[...]).astype(LOW)
        out_part = dot_t(attn_ref[:, columns], low).astype(LOW)
        router_part = dot_t(h_ref[:length, columns], logit_grad)
        lanes = lax.broadcasted_iota(jnp.int32, router_part.shape, 1)
        small_ref[s] = jnp.where(lanes == EXPERTS, as_column(second_scr[:1, columns]), router_part).astype(LOW)
        for target, rows in shard_parts(((o0,), (o1,), (o2, o3), (o4, o5))[s]):
            target[...] = out_part[rows]


def router_columns(pieces):
    return [
        pl.BlockSpec((p.shape[0], 128), lambda i, at=p.shape[1] // 128 - 1: (0, at), pipeline_mode=ONCE) for p in pieces
    ]


def resid_back_call(mine, resid, gain, dz, terms, gains, h, attn, pieces, shared_pieces):
    length, width = resid.shape
    shard = pieces[0].shape[0]
    whole = lambda shape: pl.BlockSpec(shape, lambda i: (0,) * len(shape), pipeline_mode=ONCE)
    arrays = (resid, gain, dz, *terms, gains, h, attn, *pieces)
    shapes = [shaped(length, width, dtype=WIDE), shaped(length, width), shaped(4, shard, 128)]
    shapes += [shaped(shard, width)] * 2 + [shaped(shard // 2, width)] * 4
    return pl.pallas_call(
        resid_back_kernel,
        grid=(1,),
        in_specs=[pl.BlockSpec(memory_space=pltpu.SMEM)]
        + [whole(a.shape) for a in arrays]
        + router_columns(shared_pieces),
        out_specs=[whole(s.shape) for s in shapes],
        out_shape=shapes,
        scratch_shapes=[pltpu.VMEM((length, width), WIDE), pltpu.VMEM((length, width), LOW)],
        compiler_params=pltpu.CompilerParams(vmem_limit_bytes=34 * MIB),
        cost_estimate=work(
            flops=4 * length * width * (width + EXPERTS), bytes_accessed=length * width * 40, transcendentals=0
        ),
    )(mine, *arrays, *shared_pieces)


def attention_back_kernel(
    mine_ref, q_ref, k_ref, v_ref, do_ref, h_ref, tokens_ref, gain_ref, grad_ref, small_ref, p0, p1, p2, p3, s0, s1, s2, s3,
    seg_row_ref, seg_col_ref, cos_ref, sin_ref, input_ref, o0, o1, o2, o3, o4, o5, qkv_scr, dk_scr, dv_scr, dh_scr,
):
    mine = mine_ref[0]
    length, width = q_ref.shape
    shard = p0.shape[0]
    qkv_width = width + 2 * KEY_VALUE_HEADS * HEAD_DIM
    heads = QUERY_HEADS // KEY_VALUE_HEADS
    key_width = KEY_VALUE_HEADS * HEAD_DIM
    tile = 128
    dk_scr[...] = jnp.zeros_like(dk_scr)
    dv_scr[...] = jnp.zeros_like(dv_scr)
    for start in range(0, length, tile):
        band, reach = slice(start, start + tile), start + tile
        allowed = allowed_pairs(seg_col_ref, seg_row_ref, band, reach, heads)
        cos, sin = cos_ref[band, :], sin_ref[band, :]
        for g in range(KEY_VALUE_HEADS):
            queries = stacked_heads(q_ref, band, g, heads)
            grads = stacked_heads(do_ref, band, g, heads)
            keys = k_ref[:reach, head_slice(g)]
            probs = probabilities(queries, keys, allowed)
            prob_grad = dot_bt(grads, v_ref[:reach, head_slice(g)])
            delta = jnp.sum(probs * prob_grad, axis=-1, keepdims=True)
            score_grad = (probs * (prob_grad - delta) * HEAD_DIM ** (-0.5)).astype(LOW)
            dv_scr[:reach, head_slice(g)] += dot_t(probs.astype(LOW), grads)
            dk_scr[:reach, head_slice(g)] += dot_t(score_grad, queries)
            dq = dot(score_grad, keys)
            for h in range(heads):
                qkv_scr[band, head_slice(g * heads + h)] = turn_back(dq[h * tile : (h + 1) * tile], cos, sin).astype(LOW)
    for g in range(KEY_VALUE_HEADS):
        at = width + g * HEAD_DIM
        qkv_scr[:, at : at + HEAD_DIM] = turn_back(dk_scr[:, head_slice(g)], cos_ref[...], sin_ref[...]).astype(LOW)
    qkv_scr[:, width + key_width :] = dv_scr[...].astype(LOW)
    qkv = qkv_scr[...]
    for s, (piece, shared) in enumerate(zip((p0, p1, p2, p3), (s0, s1, s2, s3))):
        dh_scr[:, piece_columns(mine, s, shard)] = dot_bt(qkv[:, :width], piece[...]) + dot_bt(qkv[:, width:], shared[:, : 2 * key_width])
    stream = tokens_ref[...].astype(WIDE)
    inverse = inverse_rms(stream)
    normed = stream * inverse
    first = dh_scr[...]
    gain_grad = jnp.sum(first * normed, axis=0, keepdims=True)
    input_ref[...] = grad_ref[...] + norm_back(first, gain_ref[...], normed, inverse)
    dh_scr[:1, :] = gain_grad
    for s in range(4):
        columns = piece_columns(mine, s, shard)
        part = dot_t(h_ref[:, columns], qkv).astype(LOW)
        small = small_ref[s].astype(WIDE)
        lanes = lax.broadcasted_iota(jnp.int32, small.shape, 1)
        small = jnp.where(lanes == EXPERTS + 1, as_column(dh_scr[:1, columns]), small).astype(LOW)
        for target, rows in shard_parts(((o0,), (o1,), (o2, o3), (o4, o5))[s]):
            target[:, :qkv_width] = part[rows]
            target[:, qkv_width:] = small[rows]


def attention_back_call(
    mine, q, k, v, do, h, tokens, gain, grad, small, pieces, shared_pieces, seg_row, seg_col, cos, sin
):
    length, width = q.shape
    shard = pieces[0].shape[0]
    qkv_width = width + 2 * KEY_VALUE_HEADS * HEAD_DIM
    key_width = KEY_VALUE_HEADS * HEAD_DIM
    return pl.pallas_call(
        attention_back_kernel,
        in_specs=[pl.BlockSpec(memory_space=pltpu.SMEM)] + [pl.BlockSpec(memory_space=pltpu.VMEM)] * 21,
        out_specs=[pl.BlockSpec(memory_space=pltpu.VMEM)] * 7,
        out_shape=[shaped(length, width, dtype=WIDE)]
        + [shaped(shard, qkv_width + 128)] * 2
        + [shaped(shard * 2 // 3, qkv_width + 128), shaped(shard // 3, qkv_width + 128)] * 2,
        scratch_shapes=[
            pltpu.VMEM((length, qkv_width), LOW),
            pltpu.VMEM((length, key_width), WIDE),
            pltpu.VMEM((length, key_width), WIDE),
            pltpu.VMEM((length, width), WIDE),
        ],
        compiler_params=pltpu.CompilerParams(vmem_limit_bytes=46 * MIB),
        cost_estimate=work(
            flops=4 * length * width * qkv_width + 7 * length * length * width,
            bytes_accessed=length * width * 40,
            transcendentals=QUERY_HEADS * length * length,
        ),
    )(mine, q, k, v, do, h, tokens, gain, grad, small, *pieces, *shared_pieces, seg_row, seg_col, cos, sin)


def spread_kernel(count, token_ref, *refs):
    parts, outs, scratch = refs[2 : -count - 1], refs[-count - 1 : -1], refs[-1]
    for part, rows in shard_parts(parts):
        scratch[rows] = part[...]
    chunk = outs[0].shape[0]
    for j, out in enumerate(outs):
        rows = pl.ds(pl.multiple_of(lax.rem(token_ref[2] + j, count) * chunk, 16), chunk)
        out[...] = sum(term[rows, :].astype(WIDE) for term in (*refs[:2], scratch)).astype(LOW)


def spread_call(token, count, *terms):
    rows, width = terms[0].shape
    whole = lambda shape: pl.BlockSpec(shape, lambda i: (0, 0), pipeline_mode=ONCE)
    return pl.pallas_call(
        functools.partial(spread_kernel, count),
        grid=(1,),
        in_specs=[pl.BlockSpec(memory_space=pltpu.SMEM)] + [whole(t.shape) for t in terms],
        out_specs=[whole((rows // count, width))] * count,
        out_shape=[shaped(rows // count, width)] * count,
        scratch_shapes=[pltpu.VMEM((rows, width), LOW)],
        compiler_params=pltpu.CompilerParams(vmem_limit_bytes=16 * MIB),
        cost_estimate=work(flops=0, bytes_accessed=8 * rows * width, transcendentals=0),
    )(token, *terms)


def assemble_kernel(count, widths, token_ref, *refs):
    chunks, outs = refs[:count], refs[count:]
    chunk = chunks[0].shape[0]
    for j, ref in enumerate(chunks):
        rows = pl.ds(pl.multiple_of(lax.rem(token_ref[2] + j, count) * chunk, 16), chunk)
        values = ref[...].astype(WIDE)
        at = 0
        for width, out in zip(widths, outs):
            out[rows, :] = values[:, at : at + width]
            at += width
        if len(outs) > len(widths):
            outs[-1][rows, :] = values[:, at : at + 128]
    if len(outs) > len(widths):
        router_ref, ffn_ref, attn_ref, scratch = outs[len(widths) :]
        small = jnp.transpose(scratch[...])
        router_ref[...] = small[:EXPERTS]
        ffn_ref[...] = small[EXPERTS]
        attn_ref[...] = small[EXPERTS + 1]


def assemble_call(token, chunks, widths):
    count, (rows, width) = len(chunks), chunks[0].shape
    whole = lambda shape: pl.BlockSpec(shape, lambda i: (0,) * len(shape), pipeline_mode=ONCE)
    small = width > sum(widths)
    shapes = [(count * rows, w) for w in widths]
    shapes += [(EXPERTS, count * rows), (count * rows,), (count * rows,)] if small else []
    return pl.pallas_call(
        functools.partial(assemble_kernel, count, widths),
        grid=(1,),
        in_specs=[pl.BlockSpec(memory_space=pltpu.SMEM)] + [whole((rows, width))] * count,
        out_specs=[whole(shape) for shape in shapes],
        out_shape=[shaped(*shape, dtype=WIDE) for shape in shapes],
        scratch_shapes=[pltpu.VMEM((count * rows, 128), WIDE)] if small else [],
        compiler_params=pltpu.CompilerParams(vmem_limit_bytes=16 * MIB),
        cost_estimate=work(flops=0, bytes_accessed=6 * count * rows * width, transcendentals=0),
    )(token, *chunks)


def per_device_ring(
    tokens,
    segments,
    routes,
    attn_gain,
    ffn_gain,
    w_query,
    key_weight,
    value_weight,
    w_out,
    w_router,
    w_gate,
    w_up,
    w_down,
    cotangent,
):
    length, model_width = tokens.shape
    top_count = routes.shape[1]
    count = lax.axis_size("expert")
    holds = EXPERTS // count
    capacity = max(2, 3 * length * top_count // (2 * EXPERTS))
    slots = -(-capacity // 16) * 16
    shard = model_width // 4
    key_width = KEY_VALUE_HEADS * HEAD_DIM
    half = length // 2
    mine = lax.axis_index("wshard").astype(jnp.int32)
    order = jnp.array(ring_order(count), jnp.int32)
    spot_of = jnp.array([ring_order(count).index(i) for i in range(count)], jnp.int32)
    here = lax.axis_index("expert").astype(jnp.int32)
    spot = spot_of[here]
    token = jnp.stack([mine, here, spot])
    routes_t = routes.T

    cosine, sine = rotary_tables(length, HEAD_DIM)
    cos = jnp.concatenate([cosine, cosine], axis=1)
    sin = jnp.concatenate([-sine, sine], axis=1)
    seg_col = segments.reshape(length, 1)
    gain_one, gain_two = attn_gain[None], ffn_gain[None]

    def pieces_of(own, across, *ready):
        return (own, swap_core(own), across, swap_core(after(across, *ready)))

    dz = {0: cotangent}
    dz[-1], dz[1] = ahead(dz[0], count), behind(dz[0], count)
    query_across = swap_x(w_query)
    query_pieces = pieces_of(w_query, query_across)
    spare = jnp.zeros((shard, 128 - EXPERTS), LOW)
    shared = jnp.concatenate([key_weight, value_weight, w_router, spare], axis=1)
    shared, token, seg_col, cos, sin, routes_t, gain_one, gain_two = lax.optimization_barrier(
        (shared, token, seg_col, cos, sin, routes_t, gain_one, gain_two)
    )
    shared_across = swap_x(after(shared, query_across, dz[-1], dz[1]))
    dz[-2], dz[2] = ahead(dz[-1], count), behind(dz[1], count)
    shared_pieces = pieces_of(shared, shared_across)
    out_across = swap_x(after(w_out, shared_across))

    first_low, query, key, value, attn = attention_call(
        after(token, dz[-2], dz[2]), tokens, gain_one, query_pieces, shared_pieces, segments, seg_col, cos, sin
    )
    out_pieces = pieces_of(w_out, out_across, attn)
    dz[-3], dz[3] = ahead(dz[-2], count), behind(dz[2], count)
    resid, second = project_call(after(token, dz[-3], dz[3]), tokens, attn, out_pieces, shared_pieces, gain_two, routes_t)

    def experts(ready, first, offsets, kept):
        return expert_call(
            after(token, *ready), first, [h[j] for j in offsets], [dz[j] for j in offsets], w_gate, w_up, w_down, kept,
            holds, slots, count,
        )

    h = {0: second}
    h[-1], h[1] = ahead(h[0], count), behind(h[0], count)
    (d_own,), kept = experts((), 6, (0,), None)
    h[-2], h[2] = ahead(after(h[-1], d_own), count), behind(after(h[1], d_own), count)
    (d_l1, d_r1), kept = experts((), 0, (-1, 1), kept)
    h[-3], h[3] = ahead(after(h[-2], d_l1), count), behind(after(h[2], d_l1), count)
    (d_l2, d_r2), kept = experts((), 2, (-2, 2), kept)
    h[4], dz[4] = ahead(after(h[-3], d_l2), count), behind(after(dz[3], d_l2), count)
    (d_l3, d_r3), kept = experts((), 4, (-3, 3), kept)
    (d_far,), (gains, rank, *kept) = experts((), 7, (4,), kept)

    block_of = jnp.array([BLOCK_OFFSETS.index(j if j <= count // 2 else j - count) for j in range(count)], jnp.int32)
    gain_send = gains[block_of[(spot_of - spot) % count]]

    def weight_grads(expert, *ready):
        return wgrad_call(expert, after(token, *ready), kept)

    def over_cores(grads, *ready):
        return swap_core(after(grads[2], *ready))

    both, last = range(2), 2

    def sum_of(grads, got, part):
        return (grads[1], part), (got, part)

    up_sent, down_sent = ahead(d_far, count), behind(d_l3, count)
    grads = [wgrad_call(0, token, kept, True)]
    got = [[swap_core(v) for v in grads[0][2]]]
    grads.append(weight_grads(1, grads[0][0]))
    up, down = sums_call((grads[1][0], *got[0],), (d_r3, up_sent), (d_l2, down_sent))

    up_sent, down_sent = ahead(up, count), behind(down, count)
    got.append(over_cores(grads[1], up))
    halves = [sums_call((up,), *[((grads[0][1], i), got[0][i]) for i in range(3)])]
    across = [[(swap_x(v), None) for v in halves[0][:2]]]
    gain_dense = lax.all_to_all(after(gain_send, halves[0][0]), "expert", split_axis=0, concat_axis=0, tiled=True)
    gain_dense = gain_dense.reshape(EXPERTS, length)
    grads.append(weight_grads(2, gain_send, *halves[0]))
    up, down = sums_call((gain_dense, grads[2][0], across[0][0][0], across[0][1][0],), (d_r2, up_sent), (d_l1, down_sent))

    up_sent, down_sent = ahead(up, count), behind(down, count)
    got.append(over_cores(grads[2], up))
    halves.append(sums_call((up,), sum_of(grads[1], got[1], both), sum_of(grads[1], got[1], last)))
    across_b = swap_x(halves[1][0])
    y = dict(zip(BLOCK_OFFSETS, value_call(after(token, *halves[1]), rank, kept[4], w_down, slots)))
    late = swap_core(after(grads[0][3], up))
    (up,) = sums_call((y[0], across_b, down_sent, late), (d_r1, up_sent))

    up_sent, y_down = ahead(up, count), behind(after(y[4], up), count)
    across[0].append((swap_x(after(halves[0][2], up)), None))
    across.append([(across_b, 0), (across_b, 1), (swap_x(after(halves[1][1], up)), None)])
    halves.append(sums_call((up,), sum_of(grads[2], got[2], both), sum_of(grads[2], got[2], last)))
    grads.append(weight_grads(3, *halves[2]))
    (down,) = sums_call(
        (up_sent, across[0][2][0], across[1][2][0], grads[3][0]), (y[-3], y_down)
    )

    y_up, y_down, across_d = ahead(after(y[3], down), count), behind(down, count), swap_x(after(halves[2][0], down))
    grad, attn_grad, small, *out_parts = resid_back_call(
        after(token, down), resid, gain_two, cotangent, (d_own, up_sent, down_sent), gain_dense, second,
        attn, out_pieces, shared_pieces,
    )
    def terms_of(expert, i, *ready):
        other = (late, i) if expert == 0 else (got[expert], 3 + i)
        return [(after(grads[expert][0], *ready) if ready else grads[expert][0], i), other, across[expert][i]]

    def finish(ready, expert, kept_out, parts=range(3)):
        return finish_call(holds, [(i, expert, [terms_of(expert, i, *ready)]) for i in parts], kept_out)

    out_first = [swap_core(v) for v in out_parts[4:]]
    finished = finish((grad,), 0, None)
    *out_half, up, down = sums_call(
        (finished[0], across_d), *zip(out_parts[2:4], out_first), (y[2], y_up), (y[-2], y_down)
    )

    y_up, y_down, out_across = ahead(up, count), behind(down, count), [swap_x(v) for v in out_half]
    out_got = swap_core(after(out_parts[1], up))
    input_grad, *qkv_parts = attention_back_call(
        after(token, up), query, key, value, attn_grad, first_low, tokens, gain_one, grad, small, query_pieces,
        shared_pieces, segments, seg_col, cos, sin,
    )
    up, down = sums_call((input_grad, *out_across, out_got), (y[1], y_up), (y[-1], y_down))

    y_up, y_down = ahead(up, count), behind(down, count)
    qkv_first = [swap_core(after(v, up)) for v in qkv_parts[4:]]
    qkv_half = sums_call((up,), *zip(qkv_parts[2:4], qkv_first))
    qkv_across = [swap_x(qkv_half[0])]
    out_parts = spread_call(after(token, *qkv_half), count, out_parts[0], out_got, *out_across)
    finished = finish(qkv_half, 1, finished)
    qkv_got = swap_core(after(qkv_parts[1], qkv_across[0]))
    got.append(over_cores(grads[3], qkv_half[0]))
    (half_e,) = sums_call((finished[0],), sum_of(grads[3], got[3], range(3)))
    across.append([(across_d, 0), (across_d, 1)])
    finished = finish((half_e,), 2, finished, both)
    y_own = after(y[0], qkv_across[0], out_parts[0], finished[0])
    mixed = (resid + sum(t.astype(WIDE) for t in (y_own, y_up, y_down))).astype(LOW)
    qkv_across.append(swap_x(after(qkv_half[1], qkv_across[0])))

    def sum_step(parts, up, down, step):
        up = add_low(parts[step], ahead(up, count))
        down = behind(down, count)
        return up, add_low(parts[count + 1 - step], down) if step > 1 else down

    def copy_step(up, down):
        return up + [ahead(up[-1], count)], down + [behind(down[-1], count)]

    out_up, out_down = after(out_parts[4], mixed), after(out_parts[5], mixed)
    for step in (3, 2, 1):
        out_up, out_down = sum_step(out_parts, out_up, out_down, step)
        if step == 2:
            out_up = after(out_up, qkv_across[1])
    out_own = add_low(out_parts[0], ahead(out_up, count), out_down)
    across_e = [swap_x(after(halves[2][1], qkv_across[1])), swap_x(after(half_e, qkv_across[1]))]
    qkv_parts = spread_call(after(token, out_own), count, qkv_parts[0], qkv_got, *qkv_across)
    across[2].append((across_e[0], None))
    across.append([(across_e[1], i) for i in range(3)])
    out_ups, out_downs = [after(out_own, qkv_parts[0])], [after(out_own, qkv_parts[0])]
    qkv_up, qkv_down = qkv_parts[4], qkv_parts[5]
    for step in (3, 2, 1):
        out_ups, out_downs = copy_step(out_ups, out_downs)
        qkv_up, qkv_down = sum_step(qkv_parts, qkv_up, qkv_down, step)
        qkv_up = after(qkv_up, out_ups[-1], out_downs[-1])
    out_ups.append(ahead(out_ups[-1], count))
    qkv_own = add_low(qkv_parts[0], ahead(qkv_up, count), qkv_down)
    qkv_ups, qkv_downs = [qkv_own], [qkv_own]
    for step in (3, 2, 1):
        qkv_ups, qkv_downs = copy_step(qkv_ups, qkv_downs)
        if step == 3:
            qkv_ups[-1] = after(qkv_ups[-1], out_ups[-1])
    (out_sum,) = assemble_call(after(token, qkv_ups[2]), out_downs + out_ups[:0:-1], (model_width,))
    qkv_ups.append(ahead(after(qkv_ups[-1], out_sum, across_e[1]), count))
    last_rows = [terms_of(2, 2, qkv_ups[3]), terms_of(3, 2)]
    finished = finish_call(
        holds, [(0, 3, [terms_of(3, 0, qkv_ups[3])]), (1, 3, [terms_of(3, 1)]), (2, 2, last_rows)], finished
    )
    query_sum, key_sum, value_sum, router_sum, ffn_gain_sum, attn_gain_sum = assemble_call(
        after(token, finished[0]), qkv_downs + qkv_ups[:0:-1], (model_width, key_width, key_width)
    )
    gate_shard, up_shard, down_shard = finished
    return (
        mixed,
        input_grad,
        attn_gain_sum,
        ffn_gain_sum,
        query_sum,
        key_sum,
        value_sum,
        out_sum,
        router_sum.T,
        gate_shard,
        up_shard,
        down_shard,
    )


def solution(mesh):
    ring = mesh.shape["expert"] == len(BLOCK_OFFSETS) and mesh.shape["wshard"] == 4
    body = per_device_ring if ring else per_device_exchange
    in_specs = (
        P(("expert", "wshard"), None),
        P(("expert", "wshard"), None),
        P(("expert", "wshard"), None),
        P(),
        P(),
        P("wshard", None),
        P("wshard", None),
        P("wshard", None),
        P("wshard", None),
        P("wshard", None),
        P(None, "expert"),
        P(None, "expert"),
        P("expert", None),
        P(("expert", "wshard"), None),
    )
    out_specs = (
        P(("expert", "wshard"), None),
        P(("expert", "wshard"), None),
        P("wshard"),
        P("wshard"),
        P("wshard", None),
        P("wshard", None),
        P("wshard", None),
        P("wshard", None),
        P("wshard", None),
        P("wshard", "expert"),
        P("wshard", "expert"),
        P("expert", "wshard"),
    )
    return jax.shard_map(
        body, mesh=mesh, in_specs=in_specs, out_specs=out_specs, check_vma=False
    )
```

```python
import functools

import jax
import jax.numpy as jnp
from jax import lax
from jax.experimental import pallas as pl
from jax.experimental.pallas import tpu as pltpu
from jax.sharding import PartitionSpec as P

QUERY_HEADS = 12
KEY_VALUE_HEADS = 2
HEAD_DIM = 128
EXPERTS = 32
TOP = 4


EPS = 1e-06
ROPE_BASE = 10000.0
NEG = -1e30
LOW = jnp.bfloat16
WIDE = jnp.float32
MIB = 1024 * 1024
ONCE = pl.Buffered(buffer_count=1)
def norm_forward(values, gain):
    inverse = lax.rsqrt(jnp.mean(values * values, axis=-1) + EPS)
    normed = values * inverse[:, None]
    return (normed * gain, normed, inverse)


def norm_backward(grad, gain, normed, inverse):
    gain_grad = jnp.sum(grad * normed, axis=0)
    scaled = grad * gain
    centred = scaled - normed * jnp.mean(scaled * normed, axis=-1, keepdims=True)
    return (inverse[:, None] * centred, gain_grad)


def rotary_tables(seq_length, head_size):
    half_size = head_size // 2
    frequency = ROPE_BASE ** (-(jnp.arange(half_size, dtype=jnp.float32) * 2.0 / head_size))
    angles = jnp.arange(seq_length, dtype=jnp.float32)[:, None] * frequency[None, :]
    return (jnp.cos(angles), jnp.sin(angles))


def apply_rotation(values, cosine_lookup, sine_lookup):
    half_size = values.shape[-1] // 2
    first_half = values[..., :half_size]
    second_half = values[..., half_size:]
    cos_part = cosine_lookup[:, None, :]
    sin_part = sine_lookup[:, None, :]
    return jnp.concatenate(
        [
            first_half * cos_part - second_half * sin_part,
            second_half * cos_part + first_half * sin_part,
        ],
        axis=-1,
    )


def reverse_rotation(values, cosine_lookup, sine_lookup):
    half_size = values.shape[-1] // 2
    first_half = values[..., :half_size]
    second_half = values[..., half_size:]
    cos_part = cosine_lookup[:, None, :]
    sin_part = sine_lookup[:, None, :]
    return jnp.concatenate(
        [
            first_half * cos_part + second_half * sin_part,
            second_half * cos_part - first_half * sin_part,
        ],
        axis=-1,
    )


def per_device_exchange(
    tokens,
    segments,
    routes,
    attn_gain,
    ffn_gain,
    w_query,
    key_weight,
    value_weight,
    w_out,
    w_router,
    w_gate,
    w_up,
    w_down,
    cotangent,
):
    lower_dtype = jnp.bfloat16
    wide_type = jnp.float32
    sequence_length, model_width = tokens.shape
    top_count = routes.shape[1]
    axis_count = lax.axis_size("expert")
    owners = max(1, axis_count // EXPERTS)
    holds = max(1, EXPERTS // axis_count)
    groups = EXPERTS // holds
    capacity = max(2, 3 * sequence_length * top_count // (2 * EXPERTS))
    hidden_dev = w_gate.shape[1] // holds
    query_group_width = QUERY_HEADS // KEY_VALUE_HEADS
    score_scale = HEAD_DIM ** (-0.5)
    pair_count = sequence_length * top_count
    query_full, key_full, value_full, out_full, router_full = (
        lax.all_gather(w_query, "wshard", axis=0, tiled=True),
        lax.all_gather(key_weight, "wshard", axis=0, tiled=True),
        lax.all_gather(value_weight, "wshard", axis=0, tiled=True),
        lax.all_gather(w_out, "wshard", axis=0, tiled=True),
        lax.all_gather(w_router, "wshard", axis=0, tiled=True),
    )
    stream = tokens.astype(wide_type)
    first_norm, first_normed, first_inverse = norm_forward(stream, attn_gain)
    first_low = first_norm.astype(lower_dtype)
    cosine_lookup, sine_lookup = rotary_tables(sequence_length, HEAD_DIM)
    query_pre = jnp.dot(first_low, query_full, preferred_element_type=wide_type).reshape(
        sequence_length, QUERY_HEADS, HEAD_DIM
    )
    key_unrotated = jnp.dot(first_low, key_full, preferred_element_type=wide_type).reshape(
        sequence_length, KEY_VALUE_HEADS, HEAD_DIM
    )
    query_rotated = (
        apply_rotation(query_pre, cosine_lookup, sine_lookup)
        .astype(lower_dtype)
        .reshape(sequence_length, KEY_VALUE_HEADS, query_group_width, HEAD_DIM)
    )
    key_rotated = apply_rotation(key_unrotated, cosine_lookup, sine_lookup).astype(lower_dtype)
    value_lowered = (
        jnp.dot(first_low, value_full, preferred_element_type=wide_type)
        .astype(lower_dtype)
        .reshape(sequence_length, KEY_VALUE_HEADS, HEAD_DIM)
    )
    positions = jnp.arange(sequence_length)
    offset = positions[:, None] - positions[None, :]
    segment_row = segments[0]
    allowed = (segment_row[:, None] == segment_row[None, :]) & (offset >= 0)
    raw_scores = jnp.einsum(
        "qagd,kad->agqk", query_rotated, key_rotated, preferred_element_type=wide_type
    )
    scores = jnp.where(allowed, raw_scores * score_scale, NEG)
    score_top = jnp.max(scores, axis=-1, keepdims=True)
    expo_terms = jnp.exp(scores - score_top)
    expo_total = jnp.sum(expo_terms, axis=-1, keepdims=True)
    log_total = score_top + jnp.log(expo_total)
    probs_low = (expo_terms / expo_total).astype(lower_dtype)
    attn_low = (
        jnp.einsum("agqk,kad->qagd", probs_low, value_lowered, preferred_element_type=wide_type)
        .astype(lower_dtype)
        .reshape(sequence_length, QUERY_HEADS * HEAD_DIM)
    )
    resid = stream + jnp.dot(attn_low, out_full, preferred_element_type=wide_type)
    second_norm, second_normed, second_inverse = norm_forward(resid, ffn_gain)
    second_low = second_norm.astype(lower_dtype)
    logits = jnp.dot(second_low, router_full, preferred_element_type=wide_type)
    choose = (routes[:, :, None] == jnp.arange(EXPERTS)[None, None, :]).astype(wide_type)
    selected = jnp.sum(choose * logits[:, None, :], axis=-1)
    gate_probs = jax.nn.softmax(selected, axis=-1)
    flat_routes = routes.reshape(pair_count)
    one_hot = (flat_routes[:, None] == jnp.arange(EXPERTS)[None, :]).astype(jnp.int32)
    slot_rank = jnp.sum((jnp.cumsum(one_hot, axis=0) - 1) * one_hot, axis=1)
    slot_index = (flat_routes // holds * capacity + slot_rank) * holds + flat_routes % holds
    slot_pair = (
        jnp.full((EXPERTS * capacity,), pair_count, jnp.int32)
        .at[slot_index]
        .set(jnp.arange(pair_count, dtype=jnp.int32))
    )
    second_ext = jnp.concatenate([second_low, jnp.zeros((1, model_width), lower_dtype)], axis=0)
    send_rows = jnp.repeat(
        second_ext[slot_pair // top_count].reshape(groups, capacity, holds, model_width),
        owners,
        axis=0,
    )
    gate_local = w_gate.reshape(model_width, holds, hidden_dev)
    up_local = w_up.reshape(model_width, holds, hidden_dev)
    down_local = w_down.reshape(holds, hidden_dev, model_width)

    def owner_total(values):
        summed = jnp.sum(
            values.astype(wide_type).reshape(groups, owners, capacity, holds, model_width), axis=1
        )
        return summed.reshape(EXPERTS * capacity, model_width)

    received = lax.all_to_all(send_rows, "expert", split_axis=0, concat_axis=0, tiled=True)
    gate_pre = jnp.einsum("scld,dlf->sclf", received, gate_local, preferred_element_type=wide_type)
    up_pre = jnp.einsum("scld,dlf->sclf", received, up_local, preferred_element_type=wide_type)
    hidden = (jax.nn.silu(gate_pre) * up_pre).astype(lower_dtype)
    partial_value = jnp.einsum(
        "sclf,lfd->scld", hidden, down_local, preferred_element_type=wide_type
    ).astype(lower_dtype)
    returned = lax.all_to_all(partial_value, "expert", split_axis=0, concat_axis=0, tiled=True)
    expert_wide = owner_total(returned)[slot_index].reshape(sequence_length, top_count, model_width)
    mixed = (resid + jnp.sum(gate_probs[:, :, None] * expert_wide, axis=1)).astype(lower_dtype)
    upstream = cotangent.astype(wide_type)
    query_back, key_back, value_back, out_back, router_back = (
        lax.all_gather(w_query, "wshard", axis=0, tiled=True),
        lax.all_gather(key_weight, "wshard", axis=0, tiled=True),
        lax.all_gather(value_weight, "wshard", axis=0, tiled=True),
        lax.all_gather(w_out, "wshard", axis=0, tiled=True),
        lax.all_gather(w_router, "wshard", axis=0, tiled=True),
    )
    gate_grad = jnp.sum(expert_wide * upstream[:, None, :], axis=-1)
    sel_grad = gate_probs * (gate_grad - jnp.sum(gate_probs * gate_grad, axis=-1, keepdims=True))
    logit_grad = jnp.sum(choose * sel_grad[:, :, None], axis=1).astype(lower_dtype)
    pair_grad = (
        (gate_probs[:, :, None] * upstream[:, None, :])
        .astype(lower_dtype)
        .reshape(pair_count, model_width)
    )
    pair_ext = jnp.concatenate([pair_grad, jnp.zeros((1, model_width), lower_dtype)], axis=0)
    grad_send = jnp.repeat(
        pair_ext[slot_pair].reshape(groups, capacity, holds, model_width), owners, axis=0
    )
    grad_recv, rows_recv = (
        lax.all_to_all(grad_send, "expert", split_axis=0, concat_axis=0, tiled=True),
        lax.all_to_all(send_rows, "expert", split_axis=0, concat_axis=0, tiled=True),
    )
    gate_pre = jnp.einsum("scld,dlf->sclf", rows_recv, gate_local, preferred_element_type=wide_type)
    up_pre = jnp.einsum("scld,dlf->sclf", rows_recv, up_local, preferred_element_type=wide_type)
    sigmoid_gate = jax.nn.sigmoid(gate_pre)
    silu_gate = gate_pre * sigmoid_gate
    hidden = (silu_gate * up_pre).astype(lower_dtype)
    hidden_grad = jnp.einsum(
        "scld,lfd->sclf", grad_recv, down_local, preferred_element_type=wide_type
    )
    gate_pre_grad = (
        hidden_grad * up_pre * sigmoid_gate * (1.0 + gate_pre * (1.0 - sigmoid_gate))
    ).astype(lower_dtype)
    up_pre_grad = (hidden_grad * silu_gate).astype(lower_dtype)
    row_grad = (
        jnp.einsum("sclf,dlf->scld", gate_pre_grad, gate_local, preferred_element_type=wide_type)
        + jnp.einsum("sclf,dlf->scld", up_pre_grad, up_local, preferred_element_type=wide_type)
    ).astype(lower_dtype)
    returned_grad = lax.all_to_all(row_grad, "expert", split_axis=0, concat_axis=0, tiled=True)
    gate_wgrad = jnp.einsum(
        "scld,sclf->dlf", rows_recv, gate_pre_grad, preferred_element_type=wide_type
    ).reshape(model_width, holds * hidden_dev)
    up_wgrad = jnp.einsum(
        "scld,sclf->dlf", rows_recv, up_pre_grad, preferred_element_type=wide_type
    ).reshape(model_width, holds * hidden_dev)
    down_wgrad = jnp.einsum(
        "sclf,scld->lfd", hidden, grad_recv, preferred_element_type=wide_type
    ).reshape(holds * hidden_dev, model_width)
    gate_shard, up_shard, down_shard = (
        lax.psum_scatter(
            gate_wgrad.astype(jnp.bfloat16), "wshard", scatter_dimension=0, tiled=True
        ).astype(jnp.float32),
        lax.psum_scatter(
            up_wgrad.astype(jnp.bfloat16), "wshard", scatter_dimension=0, tiled=True
        ).astype(jnp.float32),
        lax.psum_scatter(
            down_wgrad.astype(jnp.bfloat16), "wshard", scatter_dimension=1, tiled=True
        ).astype(jnp.float32),
    )
    token_grad = owner_total(returned_grad)[slot_index].reshape(
        sequence_length, top_count, model_width
    )
    second_grad = jnp.sum(token_grad, axis=1) + jnp.dot(
        logit_grad, router_back.T, preferred_element_type=wide_type
    )
    router_wgrad = jnp.einsum("td,te->de", second_low, logit_grad, preferred_element_type=wide_type)
    resid_part, ffn_gain_grad = norm_backward(second_grad, ffn_gain, second_normed, second_inverse)
    resid_grad = upstream + resid_part
    resid_low = resid_grad.astype(lower_dtype)
    out_wgrad = jnp.einsum("tc,td->cd", attn_low, resid_low, preferred_element_type=wide_type)
    attn_grad = (
        jnp.dot(resid_low, out_back.T, preferred_element_type=wide_type)
        .astype(lower_dtype)
        .reshape(sequence_length, KEY_VALUE_HEADS, query_group_width, HEAD_DIM)
    )
    raw_again = jnp.einsum(
        "qagd,kad->agqk", query_rotated, key_rotated, preferred_element_type=wide_type
    )
    scores_again = jnp.where(allowed, raw_again * score_scale, NEG)
    probs_again = jnp.exp(scores_again - log_total)
    prob_grad = jnp.einsum(
        "qagd,kad->agqk", attn_grad, value_lowered, preferred_element_type=wide_type
    )
    row_delta = jnp.sum(probs_again * prob_grad, axis=-1, keepdims=True)
    score_grad = (probs_again * (prob_grad - row_delta) * score_scale).astype(lower_dtype)
    value_grad = (
        jnp.einsum("agqk,qagd->kad", probs_low, attn_grad, preferred_element_type=wide_type)
        .astype(lower_dtype)
        .reshape(sequence_length, KEY_VALUE_HEADS * HEAD_DIM)
    )
    query_rot_grad = jnp.einsum(
        "agqk,kad->qagd", score_grad, key_rotated, preferred_element_type=wide_type
    ).reshape(sequence_length, QUERY_HEADS, HEAD_DIM)
    key_rotated_gradient = jnp.einsum(
        "agqk,qagd->kad", score_grad, query_rotated, preferred_element_type=wide_type
    )
    query_grad = (
        reverse_rotation(query_rot_grad, cosine_lookup, sine_lookup)
        .astype(lower_dtype)
        .reshape(sequence_length, QUERY_HEADS * HEAD_DIM)
    )
    key_grad = (
        reverse_rotation(key_rotated_gradient, cosine_lookup, sine_lookup)
        .astype(lower_dtype)
        .reshape(sequence_length, KEY_VALUE_HEADS * HEAD_DIM)
    )
    query_wgrad = jnp.einsum("td,tc->dc", first_low, query_grad, preferred_element_type=wide_type)
    key_wgrad = jnp.einsum("td,tc->dc", first_low, key_grad, preferred_element_type=wide_type)
    value_wgrad = jnp.einsum("td,tc->dc", first_low, value_grad, preferred_element_type=wide_type)
    first_grad = (
        jnp.dot(query_grad, query_back.T, preferred_element_type=wide_type)
        + jnp.dot(key_grad, key_back.T, preferred_element_type=wide_type)
        + jnp.dot(value_grad, value_back.T, preferred_element_type=wide_type)
    )
    stream_part, attn_gain_grad = norm_backward(first_grad, attn_gain, first_normed, first_inverse)
    input_grad = resid_grad + stream_part
    query_part, key_part, value_part, out_part, router_part, attn_gain_part, ffn_gain_part = (
        lax.psum_scatter(
            query_wgrad.astype(jnp.bfloat16), "wshard", scatter_dimension=0, tiled=True
        ).astype(jnp.float32),
        lax.psum_scatter(
            key_wgrad.astype(jnp.bfloat16), "wshard", scatter_dimension=0, tiled=True
        ).astype(jnp.float32),
        lax.psum_scatter(
            value_wgrad.astype(jnp.bfloat16), "wshard", scatter_dimension=0, tiled=True
        ).astype(jnp.float32),
        lax.psum_scatter(
            out_wgrad.astype(jnp.bfloat16), "wshard", scatter_dimension=0, tiled=True
        ).astype(jnp.float32),
        lax.psum_scatter(
            router_wgrad.astype(jnp.bfloat16), "wshard", scatter_dimension=0, tiled=True
        ).astype(jnp.float32),
        lax.psum_scatter(
            attn_gain_grad.astype(jnp.bfloat16), "wshard", scatter_dimension=0, tiled=True
        ).astype(jnp.float32),
        lax.psum_scatter(
            ffn_gain_grad.astype(jnp.bfloat16), "wshard", scatter_dimension=0, tiled=True
        ).astype(jnp.float32),
    )
    query_sum, key_sum, value_sum, out_sum, router_sum, attn_gain_sum, ffn_gain_sum = lax.psum(
        (query_part, key_part, value_part, out_part, router_part, attn_gain_part, ffn_gain_part),
        "expert",
    )
    return (
        mixed,
        input_grad,
        attn_gain_sum,
        ffn_gain_sum,
        query_sum,
        key_sum,
        value_sum,
        out_sum,
        router_sum,
        gate_shard,
        up_shard,
        down_shard,
    )


BLOCK_OFFSETS = (-1, 1, -2, 2, -3, 3, 0, 4)


def ring_order(count):
    return [0] + list(range(1, count, 2)) + list(range(count - 2, 0, -2))


def shifted(value, step, count):
    order = ring_order(count)
    return lax.ppermute(value, "expert", [(order[i], order[(i + step) % count]) for i in range(count)])


def ahead(value, count):
    return shifted(value, 1, count)


def behind(value, count):
    return shifted(value, -1, count)


def swap_core(value):
    size = lax.axis_size("wshard")
    return lax.ppermute(value, "wshard", [(i, i ^ 1) for i in range(size)])


def swap_x(value):
    size = lax.axis_size("wshard")
    return lax.ppermute(value, "wshard", [(i, i ^ 2) for i in range(size)])


def work(flops, bytes_accessed, transcendentals):
    scale = 8
    return pl.CostEstimate(
        flops=flops // scale, bytes_accessed=bytes_accessed // scale, transcendentals=transcendentals // scale
    )


def add_low(*terms):
    return sum(term.astype(WIDE) for term in terms).astype(LOW)


def after(value, *others):
    return lax.optimization_barrier((value, *others))[0]


def places(rank_row, slots):
    rows = lax.broadcasted_iota(jnp.int32, (slots, rank_row.shape[-1]), 0)
    return rank_row == rows


def expert_ranks(routes, holds):
    tokens = routes.shape[1]
    names = [jnp.sum((routes == l).astype(WIDE), axis=0, keepdims=True) for l in range(holds)]
    names = jnp.concatenate(names + [jnp.zeros((16 - holds, tokens), WIDE)], axis=0)
    rows = lax.broadcasted_iota(jnp.int32, (tokens, tokens), 0)
    columns = lax.broadcasted_iota(jnp.int32, (tokens, tokens), 1)
    before = dot(names.astype(LOW), (rows <= columns).astype(WIDE).astype(LOW))
    return jnp.where(names > 0.0, before - 1.0, -1.0)[:holds].astype(jnp.int32)


def pack_routing(gates, routes):
    high = gates.astype(LOW).astype(WIDE)
    rows = [high, gates - high, routes.astype(WIDE)]
    spare = 16 - 3 * gates.shape[0]
    return jnp.concatenate(rows + [jnp.zeros((spare, gates.shape[1]), WIDE)], axis=0).astype(LOW)


def unpack_routing(packed):
    top_count = TOP
    packed = packed.astype(WIDE)
    return packed[:top_count] + packed[top_count : 2 * top_count], packed[2 * top_count : 3 * top_count]


def dot_t(a, b):
    return lax.dot_general(a, b, (((0,), (0,)), ((), ())), preferred_element_type=WIDE)


def dot_bt(a, b):
    return lax.dot_general(a, b, (((1,), (1,)), ((), ())), preferred_element_type=WIDE)


def dot(a, b):
    return jnp.dot(a, b, preferred_element_type=WIDE)


def expert_kernel(count, slots, aliased, *refs):
    token_ref = refs[0]
    h_refs, dz_refs = refs[1 : 1 + count], refs[1 + count : 1 + 2 * count]
    wg_ref, wu_ref, wd_ref = refs[1 + 2 * count : 4 + 2 * count]
    rest = refs[4 + 2 * count + (4 if aliased else 0) :]
    d_refs = rest[:count]
    gain_ref, rank_ref, rows_out, grads_out = rest[count : count + 4]
    place_scr, back_scr, gate_scr, wg_scr, wu_scr, wd_scr, sems = rest[count + 4 :]
    e = pl.program_id(0)
    holds, tokens = rank_ref.shape[1:]
    hidden_width, width = wd_scr.shape[1:]

    def weights(expert, slot):
        band = pl.ds(pl.multiple_of(expert * hidden_width, hidden_width), hidden_width)
        return [
            pltpu.make_async_copy(source, target.at[slot], sems.at[slot, i])
            for i, (source, target) in enumerate(
                ((wg_ref.at[:, band], wg_scr), (wu_ref.at[:, band], wu_scr), (wd_ref.at[band, :], wd_scr))
            )
        ]

    slot = lax.rem(e, 2)

    @pl.when(e == 0)
    def _():
        for copy in weights(0, 0):
            copy.start()

    @pl.when(e + 1 < holds)
    def _():
        for copy in weights(e + 1, 1 - slot):
            copy.start()

    here = pl.ds(pl.multiple_of(e * slots, slots), slots)
    @pl.when(e == 0)
    def _():
        for b, (h_ref, dz_ref) in enumerate(zip(h_refs, dz_refs)):
            gates, routes = unpack_routing(h_ref[tokens : tokens + 16, :tokens])
            routes = routes - (token_ref[1] * holds).astype(WIDE)
            ranks = expert_ranks(routes, holds)
            rank_ref[b] = ranks
            for l in range(holds):
                band = slice(l * slots, (l + 1) * slots)
                spot = places(ranks[l : l + 1], slots).astype(WIDE)
                named = jnp.where(routes == l, gates, 0.0)
                gate_scr[b, band, :] = jnp.broadcast_to(
                    jnp.sum(spot * jnp.sum(named, axis=0, keepdims=True), axis=1, keepdims=True), (slots, 128)
                )
                place_scr[b, band, :] = spot.astype(LOW)
            for i, source in enumerate((h_ref, dz_ref)):
                taken = dot(place_scr[b], source[:tokens]).astype(LOW)
                for l in range(holds):
                    band = slice(b * slots, (b + 1) * slots)
                    rows_out[l, band, i * width : (i + 1) * width] = taken[l * slots : (l + 1) * slots]

    gate = jnp.concatenate([gate_scr[b, here, :] for b in range(count)], axis=0)[:, :1]
    rows = rows_out[e, :, :width]
    for copy in weights(e, slot):
        copy.wait()
    gate_pre = dot(rows, wg_scr[slot])
    up_pre = dot(rows, wu_scr[slot])
    sig = jax.nn.sigmoid(gate_pre)
    silu = gate_pre * sig
    hidden = (silu * up_pre).astype(LOW).astype(WIDE)
    back = dot_bt(rows_out[e, :, width:], wd_scr[slot])
    gains = jnp.sum(back * hidden, axis=1, keepdims=True)
    back = back * gate
    gate_grad = (back * (up_pre * sig * (1.0 + gate_pre * (1.0 - sig)))).astype(LOW)
    up_grad = (back * silu).astype(LOW)
    for i, part in enumerate((gate_grad, up_grad, (hidden * gate).astype(LOW))):
        grads_out[0, :, i * hidden_width : (i + 1) * hidden_width] = part
    row_grad = (dot_bt(gate_grad, wg_scr[slot]) + dot_bt(up_grad, wu_scr[slot])).astype(LOW)
    for b in range(count):
        band = slice(b * slots, (b + 1) * slots)
        back_scr[b, here, :] = row_grad[band]
        spot = place_scr[b, here, :].astype(WIDE)
        gain_ref[b, pl.ds(e, 1), :] = jnp.sum(spot * gains[band], axis=0, keepdims=True)

    @pl.when(e == pl.num_programs(0) - 1)
    def _():
        for b in range(count):
            d_refs[b][...] = dot_t(place_scr[b], back_scr[b]).astype(LOW)


def expert_call(token, first, blocks, dz_blocks, w_gate, w_up, w_down, kept, holds, slots, total):
    count = len(blocks)
    tokens, width = dz_blocks[0].shape
    hidden = w_gate.shape[1] // holds
    whole = lambda *shape: pl.BlockSpec(shape, lambda e: (0,) * len(shape))
    once = lambda *shape: pl.BlockSpec(shape, lambda e: (0,) * len(shape), pipeline_mode=pl.Buffered(buffer_count=1))
    aliased = kept is not None
    in_specs = (
        [pl.BlockSpec(memory_space=pltpu.SMEM)]
        + [once(*b.shape) for b in (*blocks, *dz_blocks)]
        + [pl.BlockSpec(memory_space=pl.ANY)] * 3
    )
    aliases = {len(in_specs) + i: count + i for i in range(4)} if aliased else {}
    out = pl.pallas_call(
        functools.partial(expert_kernel, count, slots, aliased),
        grid=(holds,),
        in_specs=in_specs + ([pl.BlockSpec(memory_space=pl.ANY)] * 4 if aliased else []),
        out_specs=[whole(tokens, width)] * count
        + [pl.BlockSpec((count, holds, tokens), lambda e: (first // count, 0, 0))] * 2
        + [
            pl.BlockSpec((holds, count * slots, 2 * width), lambda e: (0, first // count, 0)),
            pl.BlockSpec((1, count * slots, 3 * hidden), lambda e: (e, first // count, 0)),
        ],
        out_shape=[shaped(tokens, width)] * count
        + [shaped(total, holds, tokens, dtype=WIDE), shaped(total, holds, tokens, dtype=jnp.int32)]
        + [shaped(holds, total * slots, 2 * width), shaped(holds, total * slots, 3 * hidden)],
        scratch_shapes=[
            pltpu.VMEM((count, holds * slots, tokens), LOW),
            pltpu.VMEM((count, holds * slots, width), LOW),
            pltpu.VMEM((count, holds * slots, 128), WIDE),
            pltpu.VMEM((2, width, hidden), LOW),
            pltpu.VMEM((2, width, hidden), LOW),
            pltpu.VMEM((2, hidden, width), LOW),
            pltpu.SemaphoreType.DMA((2, 3)),
        ],
        input_output_aliases=aliases,
        compiler_params=pltpu.CompilerParams(vmem_limit_bytes=60 * MIB),
        cost_estimate=work(
            flops=2 * holds * count * slots * width * (5 * hidden + 3 * tokens),
            bytes_accessed=3 * holds * width * hidden * 2
            + count * tokens * width * 6
            + holds * count * slots * (2 * width + 3 * hidden) * 2,
            transcendentals=holds * count * slots * hidden,
        ),
    )(token, *blocks, *dz_blocks, w_gate, w_up, w_down, *(kept if aliased else ()))
    return out[:count], tuple(out[count:])


def value_kernel(slots, _, rank_ref, hid_ref, wd_ref, *refs):
    total, holds, tokens = rank_ref.shape
    y_refs, (value_scr, place_scr) = refs[:total], refs[total:]
    e = pl.program_id(0)
    here = pl.ds(pl.multiple_of(e * slots, slots), slots)
    value = dot(hid_ref[0], wd_ref[...]).astype(LOW)
    for b in range(total):
        value_scr[b, here, :] = value[b * slots : (b + 1) * slots]

    @pl.when(e == pl.num_programs(0) - 1)
    def _():
        for b in range(total):
            for l in range(holds):
                spot = places(rank_ref[b, l : l + 1, :], slots)
                place_scr[l * slots : (l + 1) * slots, :] = spot.astype(WIDE).astype(LOW)
            y_refs[b][...] = dot_t(place_scr[...], value_scr[b]).astype(LOW)


def value_call(token, rank, kept_grads, w_down, slots):
    total, holds, tokens = rank.shape
    width = w_down.shape[1]
    hidden = kept_grads.shape[2] // 3
    whole = lambda *shape: pl.BlockSpec(shape, lambda e: (0,) * len(shape))
    out = pl.pallas_call(
        functools.partial(value_kernel, slots),
        grid=(holds,),
        in_specs=[
            pl.BlockSpec(memory_space=pltpu.SMEM),
            whole(*rank.shape),
            pl.BlockSpec((1, total * slots, hidden), lambda e: (e, 0, 2)),
            pl.BlockSpec((hidden, width), lambda e: (e, 0)),
        ],
        out_specs=[whole(tokens, width)] * total,
        out_shape=[shaped(tokens, width)] * total,
        scratch_shapes=[pltpu.VMEM((total, holds * slots, width), LOW), pltpu.VMEM((holds * slots, tokens), LOW)],
        compiler_params=pltpu.CompilerParams(vmem_limit_bytes=56 * MIB),
        cost_estimate=work(
            flops=2 * total * holds * slots * width * (hidden + tokens),
            bytes_accessed=2 * (holds * hidden * (width + total * slots) + total * tokens * width),
            transcendentals=0,
        ),
    )(token, rank, kept_grads, w_down)
    return out


def wgrad_kernel(apart, place_ref, rows_ref, dz_ref, gg_ref, ug_ref, hid_ref, *outs):
    step = pl.program_id(0)
    shard = outs[0].shape[1]
    columns = pl.ds(pl.multiple_of(jnp.bitwise_xor(place_ref[0], step) * shard, 128), shard)
    rows, grads = rows_ref[0, :, columns], dz_ref[0, :, columns]
    parts = [dot_t(rows, gg_ref[0]), dot_t(rows, ug_ref[0]), dot_t(grads, hid_ref[0])]
    parts = [part.astype(LOW) for part in parts]
    for s in range(4):

        @pl.when(step == s)
        def _():
            for i, part in enumerate(parts):
                if s == 3 and apart:
                    outs[3 + i][...] = part
                elif s % 2 and not apart:
                    outs[2][3 - 3 * (s // 2) + i] = part
                else:
                    outs[s if apart else s // 2][i] = part


def wgrad_call(expert, place, kept, apart=False):
    _, count, width = kept[0].shape
    width, hidden = width // 2, kept[1].shape[2] // 3
    shard = width // 4
    row_spec = lambda d, at: pl.BlockSpec((1, count, d), lambda s: (expert, 0, at), pipeline_mode=ONCE)
    shapes = [(3, shard, hidden)] * 3 + [(shard, hidden)] * 3 if apart else [(3, shard, hidden)] * 2 + [(6, shard, hidden)]
    out = pl.pallas_call(
        functools.partial(wgrad_kernel, apart),
        grid=(4,),
        in_specs=[pl.BlockSpec(memory_space=pltpu.SMEM)]
        + [row_spec(width, i) for i in range(2)]
        + [row_spec(hidden, i) for i in range(3)],
        out_specs=[pl.BlockSpec(shape, lambda s, zeros=(0,) * len(shape): zeros) for shape in shapes],
        out_shape=[shaped(*shape) for shape in shapes],
        compiler_params=pltpu.CompilerParams(vmem_limit_bytes=50 * MIB),
        cost_estimate=work(
            flops=2 * count * width * 3 * hidden,
            bytes_accessed=2 * (count * (2 * width + 3 * hidden) + 3 * width * hidden),
            transcendentals=0,
        ),
    )(place, *[kept[0]] * 2, *[kept[1]] * 3)
    return (out[0], out[2], out[3:], out[1]) if apart else out


def sums_call(gates, *sums):
    every = [term[0] if isinstance(term, tuple) else term for terms in sums for term in terms]

    def part_of(term, ready=()):
        array, part = term if isinstance(term, tuple) else (term, None)
        array = after(array, *ready) if ready else array
        return array if part is None else array[: len(part)] if isinstance(part, range) else array[part]

    totals = [add_low(part_of(terms[0], (*gates, *every)), *map(part_of, terms[1:])) for terms in sums]
    return totals


def finish_kernel(sizes, turned, *refs):
    outs = refs[-len(sizes) :]
    at = 0
    for counts, turn, out in zip(sizes, turned, outs):
        for i, size in enumerate(counts):
            total = sum(ref[...].astype(WIDE) for ref in refs[at : at + size])
            at += size
            if turn:
                height = out.shape[0] // len(counts)
                out[i * height : (i + 1) * height, :] = jnp.transpose(total)
            else:
                out[...] = total


def finish_call(holds, pieces, kept):
    shard, hidden = pieces[0][2][0][0][0].shape[-2:]
    steps = shard // 128
    wide, tall = shaped(shard, holds * hidden, dtype=WIDE), shaped(holds * hidden, shard, dtype=WIDE)
    flat = [term for _, _, experts in pieces for terms in experts for term in terms]
    out_specs, out_shapes = [], []
    for which, expert, experts in pieces:
        number = len(experts)
        if which < 2:
            out_specs.append(pl.BlockSpec((128, hidden), lambda s, expert=expert: (s, expert)))
        else:
            block = (number * hidden, 128)
            out_specs.append(pl.BlockSpec(block, lambda s, at=expert // number: (at, s)))
        out_shapes.append(wide if which < 2 else tall)
    kept_in = [kept[which] for which, _, _ in pieces] if kept else []
    out = pl.pallas_call(
        functools.partial(
            finish_kernel, [[len(terms) for terms in experts] for _, _, experts in pieces], [p[0] == 2 for p in pieces]
        ),
        grid=(steps,),
        in_specs=[
            pl.BlockSpec((128, hidden), lambda s: (s, 0))
            if at is None
            else pl.BlockSpec((None, 128, hidden), lambda s, at=at: (at, s, 0))
            for _, at in flat
        ]
        + [pl.BlockSpec(memory_space=pl.ANY)] * len(kept_in),
        out_specs=out_specs,
        out_shape=out_shapes,
        input_output_aliases={len(flat) + i: i for i in range(len(kept_in))},
        compiler_params=pltpu.CompilerParams(vmem_limit_bytes=20 * MIB),
        cost_estimate=work(flops=0, bytes_accessed=30 * shard * hidden, transcendentals=0),
    )(*[array for array, _ in flat], *kept_in)
    result = list(kept) if kept else [None] * 3
    for (which, _, _), value in zip(pieces, out):
        result[which] = value
    return result


def piece_columns(mine, s, shard):
    return pl.ds(pl.multiple_of(jnp.bitwise_xor(mine, s) * shard, 128), shard)


def turn(values, cos, sin):
    return values * cos + pltpu.roll(values, HEAD_DIM // 2, 1) * sin


def turn_back(values, cos, sin):
    return values * cos - pltpu.roll(values, HEAD_DIM // 2, 1) * sin


def inverse_rms(values):
    return lax.rsqrt(jnp.mean(values * values, axis=-1, keepdims=True) + EPS)


def head_slice(h):
    return slice(h * HEAD_DIM, (h + 1) * HEAD_DIM)


def stacked_heads(ref, band, group, heads):
    return jnp.concatenate([ref[band, head_slice(group * heads + h)] for h in range(heads)], axis=0)


def probabilities(queries, keys, allowed):
    scores = jnp.where(allowed, dot_bt(queries, keys) * HEAD_DIM ** (-0.5), NEG)
    expo = jnp.exp(scores - jnp.max(scores, axis=-1, keepdims=True))
    return expo * (1.0 / jnp.sum(expo, axis=-1, keepdims=True))


def allowed_pairs(seg_col_ref, seg_row_ref, band, reach, heads):
    size = band.stop - band.start
    rows = band.start + lax.broadcasted_iota(jnp.int32, (size, reach), 0)
    cols = lax.broadcasted_iota(jnp.int32, (size, reach), 1)
    ok = (seg_col_ref[band, :] == seg_row_ref[:, :reach]) & (cols <= rows)
    return jnp.concatenate([ok] * heads, axis=0)


def attention_kernel(
    mine_ref, tokens_ref, gain_ref, p0, p1, p2, p3, s0, s1, s2, s3, seg_row_ref, seg_col_ref, cos_ref, sin_ref,
    h_ref, q_ref, k_ref, v_ref, out_ref,
):
    mine = mine_ref[0]
    stream = tokens_ref[...].astype(WIDE)
    h_ref[...] = (stream * inverse_rms(stream) * gain_ref[...]).astype(LOW)
    shard = p0.shape[0]
    width = q_ref.shape[1]
    cos, sin = cos_ref[...], sin_ref[...]

    def projected(pieces, columns):
        return sum(dot(h_ref[:, piece_columns(mine, s, shard)], piece[:, columns]) for s, piece in enumerate(pieces))

    heads = QUERY_HEADS // KEY_VALUE_HEADS
    key_width = KEY_VALUE_HEADS * HEAD_DIM
    shared = (s0, s1, s2, s3)
    keys = projected(shared, slice(0, key_width))
    for g in range(KEY_VALUE_HEADS):
        k_ref[:, head_slice(g)] = turn(keys[:, head_slice(g)], cos, sin).astype(LOW)
    v_ref[...] = projected(shared, slice(key_width, 2 * key_width)).astype(LOW)
    group_width = heads * HEAD_DIM
    for g in range(KEY_VALUE_HEADS):
        queries = projected((p0, p1, p2, p3), slice(g * group_width, (g + 1) * group_width))
        for h in range(heads):
            q_ref[:, head_slice(g * heads + h)] = turn(queries[:, head_slice(h)], cos, sin).astype(LOW)
    length = q_ref.shape[0]
    tile = 128
    for start in range(0, length, tile):
        band, reach = slice(start, start + tile), start + tile
        allowed = allowed_pairs(seg_col_ref, seg_row_ref, band, reach, heads)
        for g in range(KEY_VALUE_HEADS):
            probs = probabilities(stacked_heads(q_ref, band, g, heads), k_ref[:reach, head_slice(g)], allowed)
            mixed = dot(probs.astype(LOW), v_ref[:reach, head_slice(g)]).astype(LOW)
            for h in range(heads):
                out_ref[band, head_slice(g * heads + h)] = mixed[h * tile : (h + 1) * tile]


def vmem_call(kernel, out_shape, flops, transcendentals, token, *args):
    moved = sum(a.size * a.dtype.itemsize for a in args) + sum(
        o.size * o.dtype.itemsize for o in jax.tree.leaves(out_shape)
    )
    return pl.pallas_call(
        kernel,
        in_specs=[pl.BlockSpec(memory_space=pltpu.SMEM)] + [pl.BlockSpec(memory_space=pltpu.VMEM)] * len(args),
        out_specs=[pl.BlockSpec(memory_space=pltpu.VMEM)] * len(out_shape),
        out_shape=out_shape,
        compiler_params=pltpu.CompilerParams(vmem_limit_bytes=32 * MIB),
        cost_estimate=work(flops=flops, bytes_accessed=moved, transcendentals=transcendentals),
    )(token, *args)


def shaped(*shape, dtype=LOW):
    return jax.ShapeDtypeStruct(shape, dtype)


def attention_call(mine, tokens, gain, pieces, shared_pieces, seg_row, seg_col, cos, sin):
    length, width = tokens.shape
    key_width = KEY_VALUE_HEADS * HEAD_DIM
    return vmem_call(
        attention_kernel,
        [shaped(length, width), shaped(length, width), shaped(length, key_width), shaped(length, key_width), shaped(length, width)],
        2 * length * width * (width + 2 * key_width) + 3 * length * length * width,
        QUERY_HEADS * length * length,
        mine, tokens, gain, *pieces, *shared_pieces, seg_row, seg_col, cos, sin,
    )


def project_kernel(
    mine_ref, tokens_ref, attn_ref, p0, p1, p2, p3, r0, r1, r2, r3, gain_ref, routes_ref, resid_ref, h_ref
):
    mine = mine_ref[0]
    shard = p0.shape[0]
    resid = tokens_ref[...].astype(WIDE)
    for s, piece in enumerate((p0, p1, p2, p3)):
        resid = resid + dot(attn_ref[:, piece_columns(mine, s, shard)], piece[...])
    resid_ref[...] = resid
    length, width = resid.shape
    h_ref[:length] = (resid * inverse_rms(resid) * gain_ref[...]).astype(LOW)
    logits = jnp.transpose(
        sum(
            dot(h_ref[:length, piece_columns(mine, s, shard)], piece[...])
            for s, piece in enumerate((r0, r1, r2, r3))
        )
    )
    experts = lax.broadcasted_iota(jnp.int32, logits.shape, 0)
    picked = [
        jnp.sum(jnp.where(experts == routes_ref[k : k + 1, :], logits, 0.0), axis=0, keepdims=True)
        for k in range(routes_ref.shape[0])
    ]
    top = functools.reduce(jnp.maximum, picked)
    expo = [jnp.exp(p - top) for p in picked]
    total = sum(expo)
    gates = jnp.concatenate([x / total for x in expo], axis=0)
    h_ref[length:] = jnp.zeros((16, width), LOW)
    h_ref[length:, :length] = pack_routing(gates, routes_ref[...])


def project_call(mine, tokens, attn, pieces, shared_pieces, gain, routes_t):
    length, width = tokens.shape
    whole = lambda shape: pl.BlockSpec(shape, lambda i: (0,) * len(shape), pipeline_mode=ONCE)
    shapes = [shaped(length, width, dtype=WIDE), shaped(length + 16, width)]
    return pl.pallas_call(
        project_kernel,
        grid=(1,),
        in_specs=[pl.BlockSpec(memory_space=pltpu.SMEM)]
        + [whole(a.shape) for a in (tokens, attn, *pieces)]
        + router_columns(shared_pieces)
        + [whole(gain.shape), whole(routes_t.shape)],
        out_specs=[whole(s.shape) for s in shapes],
        out_shape=shapes,
        compiler_params=pltpu.CompilerParams(vmem_limit_bytes=30 * MIB),
        cost_estimate=work(
            flops=2 * length * width * (width + EXPERTS), bytes_accessed=length * width * 20, transcendentals=length * 8
        ),
    )(mine, tokens, attn, *pieces, *shared_pieces, gain, routes_t)


def as_column(row):
    return jnp.transpose(jnp.broadcast_to(row, (8, row.shape[1])))[:, :1]


def norm_back(grad, gain, normed, inverse):
    scaled = grad * gain
    return inverse * (scaled - normed * jnp.mean(scaled * normed, axis=-1, keepdims=True))


def shard_parts(targets):
    at, parts = 0, []
    for target in targets:
        parts.append((target, slice(at, at + target.shape[0])))
        at += target.shape[0]
    return parts


def resid_back_kernel(
    mine_ref, resid_ref, gain_ref, dz_ref, t0, t1, t2, gains_ref, h_ref, attn_ref,
    p0, p1, p2, p3, r0, r1, r2, r3, grad_ref, attn_grad_ref, small_ref, o0, o1, o2, o3, o4, o5, second_scr, low_scr,
):
    mine = mine_ref[0]
    shard, width = p0.shape
    length = resid_ref.shape[0]
    routers = (r0, r1, r2, r3)
    gains = gains_ref[...]
    experts = lax.broadcasted_iota(jnp.int32, gains.shape, 0)
    gate_rows, routes = unpack_routing(h_ref[length:, :length])
    gates = jnp.zeros(gains.shape, WIDE)
    for k in range(TOP):
        gates = gates + jnp.where(experts.astype(WIDE) == routes[k : k + 1], gate_rows[k : k + 1], 0.0)
    logit_grad = gates * (gains - jnp.sum(gates * gains, axis=0, keepdims=True))
    logit_grad = jnp.concatenate([logit_grad, jnp.zeros((128 - EXPERTS, length), WIDE)], axis=0)
    logit_grad = jnp.transpose(logit_grad).astype(LOW)
    second_scr[...] = t0[...].astype(WIDE) + t1[...].astype(WIDE) + t2[...].astype(WIDE)
    for s, piece in enumerate(routers):
        columns = piece_columns(mine, s, shard)
        second_scr[:, columns] = second_scr[:, columns] + dot_bt(logit_grad, piece[...])
    resid = resid_ref[...]
    inverse = inverse_rms(resid)
    normed = resid * inverse
    second = second_scr[...]
    gain_grad = jnp.sum(second * normed, axis=0, keepdims=True)
    grad = dz_ref[...].astype(WIDE) + norm_back(second, gain_ref[...], normed, inverse)
    grad_ref[...] = grad
    low_scr[...] = grad.astype(LOW)
    second_scr[:1, :] = gain_grad
    low = low_scr[...]
    for s, piece in enumerate((p0, p1, p2, p3)):
        columns = piece_columns(mine, s, shard)
        attn_grad_ref[:, columns] = dot_bt(low, piece[...]).astype(LOW)
        out_part = dot_t(attn_ref[:, columns], low).astype(LOW)
        router_part = dot_t(h_ref[:length, columns], logit_grad)
        lanes = lax.broadcasted_iota(jnp.int32, router_part.shape, 1)
        small_ref[s] = jnp.where(lanes == EXPERTS, as_column(second_scr[:1, columns]), router_part).astype(LOW)
        for target, rows in shard_parts(((o0,), (o1,), (o2, o3), (o4, o5))[s]):
            target[...] = out_part[rows]


def router_columns(pieces):
    return [
        pl.BlockSpec((p.shape[0], 128), lambda i, at=p.shape[1] // 128 - 1: (0, at), pipeline_mode=ONCE) for p in pieces
    ]


def resid_back_call(mine, resid, gain, dz, terms, gains, h, attn, pieces, shared_pieces):
    length, width = resid.shape
    shard = pieces[0].shape[0]
    whole = lambda shape: pl.BlockSpec(shape, lambda i: (0,) * len(shape), pipeline_mode=ONCE)
    arrays = (resid, gain, dz, *terms, gains, h, attn, *pieces)
    shapes = [shaped(length, width, dtype=WIDE), shaped(length, width), shaped(4, shard, 128)]
    shapes += [shaped(shard, width)] * 2 + [shaped(shard // 2, width)] * 4
    return pl.pallas_call(
        resid_back_kernel,
        grid=(1,),
        in_specs=[pl.BlockSpec(memory_space=pltpu.SMEM)]
        + [whole(a.shape) for a in arrays]
        + router_columns(shared_pieces),
        out_specs=[whole(s.shape) for s in shapes],
        out_shape=shapes,
        scratch_shapes=[pltpu.VMEM((length, width), WIDE), pltpu.VMEM((length, width), LOW)],
        compiler_params=pltpu.CompilerParams(vmem_limit_bytes=34 * MIB),
        cost_estimate=work(
            flops=4 * length * width * (width + EXPERTS), bytes_accessed=length * width * 40, transcendentals=0
        ),
    )(mine, *arrays, *shared_pieces)


def attention_back_kernel(
    mine_ref, q_ref, k_ref, v_ref, do_ref, h_ref, tokens_ref, gain_ref, grad_ref, small_ref, p0, p1, p2, p3, s0, s1, s2, s3,
    seg_row_ref, seg_col_ref, cos_ref, sin_ref, input_ref, o0, o1, o2, o3, o4, o5, qkv_scr, dk_scr, dv_scr, dh_scr,
):
    mine = mine_ref[0]
    length, width = q_ref.shape
    shard = p0.shape[0]
    qkv_width = width + 2 * KEY_VALUE_HEADS * HEAD_DIM
    heads = QUERY_HEADS // KEY_VALUE_HEADS
    key_width = KEY_VALUE_HEADS * HEAD_DIM
    tile = 128
    dk_scr[...] = jnp.zeros_like(dk_scr)
    dv_scr[...] = jnp.zeros_like(dv_scr)
    for start in range(0, length, tile):
        band, reach = slice(start, start + tile), start + tile
        allowed = allowed_pairs(seg_col_ref, seg_row_ref, band, reach, heads)
        cos, sin = cos_ref[band, :], sin_ref[band, :]
        for g in range(KEY_VALUE_HEADS):
            queries = stacked_heads(q_ref, band, g, heads)
            grads = stacked_heads(do_ref, band, g, heads)
            keys = k_ref[:reach, head_slice(g)]
            probs = probabilities(queries, keys, allowed)
            prob_grad = dot_bt(grads, v_ref[:reach, head_slice(g)])
            delta = jnp.sum(probs * prob_grad, axis=-1, keepdims=True)
            score_grad = (probs * (prob_grad - delta) * HEAD_DIM ** (-0.5)).astype(LOW)
            dv_scr[:reach, head_slice(g)] += dot_t(probs.astype(LOW), grads)
            dk_scr[:reach, head_slice(g)] += dot_t(score_grad, queries)
            dq = dot(score_grad, keys)
            for h in range(heads):
                qkv_scr[band, head_slice(g * heads + h)] = turn_back(dq[h * tile : (h + 1) * tile], cos, sin).astype(LOW)
    for g in range(KEY_VALUE_HEADS):
        at = width + g * HEAD_DIM
        qkv_scr[:, at : at + HEAD_DIM] = turn_back(dk_scr[:, head_slice(g)], cos_ref[...], sin_ref[...]).astype(LOW)
    qkv_scr[:, width + key_width :] = dv_scr[...].astype(LOW)
    qkv = qkv_scr[...]
    for s, (piece, shared) in enumerate(zip((p0, p1, p2, p3), (s0, s1, s2, s3))):
        dh_scr[:, piece_columns(mine, s, shard)] = dot_bt(qkv[:, :width], piece[...]) + dot_bt(qkv[:, width:], shared[:, : 2 * key_width])
    stream = tokens_ref[...].astype(WIDE)
    inverse = inverse_rms(stream)
    normed = stream * inverse
    first = dh_scr[...]
    gain_grad = jnp.sum(first * normed, axis=0, keepdims=True)
    input_ref[...] = grad_ref[...] + norm_back(first, gain_ref[...], normed, inverse)
    dh_scr[:1, :] = gain_grad
    for s in range(4):
        columns = piece_columns(mine, s, shard)
        part = dot_t(h_ref[:, columns], qkv).astype(LOW)
        small = small_ref[s].astype(WIDE)
        lanes = lax.broadcasted_iota(jnp.int32, small.shape, 1)
        small = jnp.where(lanes == EXPERTS + 1, as_column(dh_scr[:1, columns]), small).astype(LOW)
        for target, rows in shard_parts(((o0,), (o1,), (o2, o3), (o4, o5))[s]):
            target[:, :qkv_width] = part[rows]
            target[:, qkv_width:] = small[rows]


def attention_back_call(
    mine, q, k, v, do, h, tokens, gain, grad, small, pieces, shared_pieces, seg_row, seg_col, cos, sin
):
    length, width = q.shape
    shard = pieces[0].shape[0]
    qkv_width = width + 2 * KEY_VALUE_HEADS * HEAD_DIM
    key_width = KEY_VALUE_HEADS * HEAD_DIM
    return pl.pallas_call(
        attention_back_kernel,
        in_specs=[pl.BlockSpec(memory_space=pltpu.SMEM)] + [pl.BlockSpec(memory_space=pltpu.VMEM)] * 21,
        out_specs=[pl.BlockSpec(memory_space=pltpu.VMEM)] * 7,
        out_shape=[shaped(length, width, dtype=WIDE)]
        + [shaped(shard, qkv_width + 128)] * 2
        + [shaped(shard * 2 // 3, qkv_width + 128), shaped(shard // 3, qkv_width + 128)] * 2,
        scratch_shapes=[
            pltpu.VMEM((length, qkv_width), LOW),
            pltpu.VMEM((length, key_width), WIDE),
            pltpu.VMEM((length, key_width), WIDE),
            pltpu.VMEM((length, width), WIDE),
        ],
        compiler_params=pltpu.CompilerParams(vmem_limit_bytes=46 * MIB),
        cost_estimate=work(
            flops=4 * length * width * qkv_width + 7 * length * length * width,
            bytes_accessed=length * width * 40,
            transcendentals=QUERY_HEADS * length * length,
        ),
    )(mine, q, k, v, do, h, tokens, gain, grad, small, *pieces, *shared_pieces, seg_row, seg_col, cos, sin)


def spread_kernel(count, token_ref, *refs):
    parts, outs, scratch = refs[2 : -count - 1], refs[-count - 1 : -1], refs[-1]
    for part, rows in shard_parts(parts):
        scratch[rows] = part[...]
    chunk = outs[0].shape[0]
    for j, out in enumerate(outs):
        rows = pl.ds(pl.multiple_of(lax.rem(token_ref[2] + j, count) * chunk, 16), chunk)
        out[...] = sum(term[rows, :].astype(WIDE) for term in (*refs[:2], scratch)).astype(LOW)


def spread_call(token, count, *terms):
    rows, width = terms[0].shape
    whole = lambda shape: pl.BlockSpec(shape, lambda i: (0, 0), pipeline_mode=ONCE)
    return pl.pallas_call(
        functools.partial(spread_kernel, count),
        grid=(1,),
        in_specs=[pl.BlockSpec(memory_space=pltpu.SMEM)] + [whole(t.shape) for t in terms],
        out_specs=[whole((rows // count, width))] * count,
        out_shape=[shaped(rows // count, width)] * count,
        scratch_shapes=[pltpu.VMEM((rows, width), LOW)],
        compiler_params=pltpu.CompilerParams(vmem_limit_bytes=16 * MIB),
        cost_estimate=work(flops=0, bytes_accessed=8 * rows * width, transcendentals=0),
    )(token, *terms)


def assemble_kernel(count, widths, token_ref, *refs):
    chunks, outs = refs[:count], refs[count:]
    chunk = chunks[0].shape[0]
    for j, ref in enumerate(chunks):
        rows = pl.ds(pl.multiple_of(lax.rem(token_ref[2] + j, count) * chunk, 16), chunk)
        values = ref[...].astype(WIDE)
        at = 0
        for width, out in zip(widths, outs):
            out[rows, :] = values[:, at : at + width]
            at += width
        if len(outs) > len(widths):
            outs[-1][rows, :] = values[:, at : at + 128]
    if len(outs) > len(widths):
        router_ref, ffn_ref, attn_ref, scratch = outs[len(widths) :]
        small = jnp.transpose(scratch[...])
        router_ref[...] = small[:EXPERTS]
        ffn_ref[...] = small[EXPERTS]
        attn_ref[...] = small[EXPERTS + 1]


def assemble_call(token, chunks, widths):
    count, (rows, width) = len(chunks), chunks[0].shape
    whole = lambda shape: pl.BlockSpec(shape, lambda i: (0,) * len(shape), pipeline_mode=ONCE)
    small = width > sum(widths)
    shapes = [(count * rows, w) for w in widths]
    shapes += [(EXPERTS, count * rows), (count * rows,), (count * rows,)] if small else []
    return pl.pallas_call(
        functools.partial(assemble_kernel, count, widths),
        grid=(1,),
        in_specs=[pl.BlockSpec(memory_space=pltpu.SMEM)] + [whole((rows, width))] * count,
        out_specs=[whole(shape) for shape in shapes],
        out_shape=[shaped(*shape, dtype=WIDE) for shape in shapes],
        scratch_shapes=[pltpu.VMEM((count * rows, 128), WIDE)] if small else [],
        compiler_params=pltpu.CompilerParams(vmem_limit_bytes=16 * MIB),
        cost_estimate=work(flops=0, bytes_accessed=6 * count * rows * width, transcendentals=0),
    )(token, *chunks)


def per_device_ring(
    tokens,
    segments,
    routes,
    attn_gain,
    ffn_gain,
    w_query,
    key_weight,
    value_weight,
    w_out,
    w_router,
    w_gate,
    w_up,
    w_down,
    cotangent,
):
    length, model_width = tokens.shape
    top_count = routes.shape[1]
    count = lax.axis_size("expert")
    holds = EXPERTS // count
    capacity = max(2, 3 * length * top_count // (2 * EXPERTS))
    slots = -(-capacity // 16) * 16
    shard = model_width // 4
    key_width = KEY_VALUE_HEADS * HEAD_DIM
    half = length // 2
    mine = lax.axis_index("wshard").astype(jnp.int32)
    order = jnp.array(ring_order(count), jnp.int32)
    spot_of = jnp.array([ring_order(count).index(i) for i in range(count)], jnp.int32)
    here = lax.axis_index("expert").astype(jnp.int32)
    spot = spot_of[here]
    token = jnp.stack([mine, here, spot])
    routes_t = routes.T

    cosine, sine = rotary_tables(length, HEAD_DIM)
    cos = jnp.concatenate([cosine, cosine], axis=1)
    sin = jnp.concatenate([-sine, sine], axis=1)
    seg_col = segments.reshape(length, 1)
    gain_one, gain_two = attn_gain[None], ffn_gain[None]

    def pieces_of(own, across, *ready):
        return (own, swap_core(own), across, swap_core(after(across, *ready)))

    dz = {0: cotangent}
    dz[-1], dz[1] = ahead(dz[0], count), behind(dz[0], count)
    query_across = swap_x(w_query)
    query_pieces = pieces_of(w_query, query_across)
    spare = jnp.zeros((shard, 128 - EXPERTS), LOW)
    shared = jnp.concatenate([key_weight, value_weight, w_router, spare], axis=1)
    shared, token, seg_col, cos, sin, routes_t, gain_one, gain_two = lax.optimization_barrier(
        (shared, token, seg_col, cos, sin, routes_t, gain_one, gain_two)
    )
    shared_across = swap_x(after(shared, query_across, dz[-1], dz[1]))
    dz[-2], dz[2] = ahead(dz[-1], count), behind(dz[1], count)
    shared_pieces = pieces_of(shared, shared_across)
    out_across = swap_x(after(w_out, shared_across))

    first_low, query, key, value, attn = attention_call(
        after(token, dz[-2], dz[2]), tokens, gain_one, query_pieces, shared_pieces, segments, seg_col, cos, sin
    )
    out_pieces = pieces_of(w_out, out_across, attn)
    dz[-3], dz[3] = ahead(dz[-2], count), behind(dz[2], count)
    resid, second = project_call(after(token, dz[-3], dz[3]), tokens, attn, out_pieces, shared_pieces, gain_two, routes_t)

    def experts(ready, first, offsets, kept):
        return expert_call(
            after(token, *ready), first, [h[j] for j in offsets], [dz[j] for j in offsets], w_gate, w_up, w_down, kept,
            holds, slots, count,
        )

    h = {0: second}
    h[-1], h[1] = ahead(h[0], count), behind(h[0], count)
    (d_own,), kept = experts((), 6, (0,), None)
    h[-2], h[2] = ahead(after(h[-1], d_own), count), behind(after(h[1], d_own), count)
    (d_l1, d_r1), kept = experts((), 0, (-1, 1), kept)
    h[-3], h[3] = ahead(after(h[-2], d_l1), count), behind(after(h[2], d_l1), count)
    (d_l2, d_r2), kept = experts((), 2, (-2, 2), kept)
    h[4], dz[4] = ahead(after(h[-3], d_l2), count), behind(after(dz[3], d_l2), count)
    (d_l3, d_r3), kept = experts((), 4, (-3, 3), kept)
    (d_far,), (gains, rank, *kept) = experts((), 7, (4,), kept)

    block_of = jnp.array([BLOCK_OFFSETS.index(j if j <= count // 2 else j - count) for j in range(count)], jnp.int32)
    gain_send = gains[block_of[(spot_of - spot) % count]]

    def weight_grads(expert, *ready):
        return wgrad_call(expert, after(token, *ready), kept)

    def over_cores(grads, *ready):
        return swap_core(after(grads[2], *ready))

    both, last = range(2), 2

    def sum_of(grads, got, part):
        return (grads[1], part), (got, part)

    up_sent, down_sent = ahead(d_far, count), behind(d_l3, count)
    grads = [wgrad_call(0, token, kept, True)]
    got = [[swap_core(v) for v in grads[0][2]]]
    grads.append(weight_grads(1, grads[0][0]))
    up, down = sums_call((grads[1][0], *got[0],), (d_r3, up_sent), (d_l2, down_sent))

    up_sent, down_sent = ahead(up, count), behind(down, count)
    got.append(over_cores(grads[1], up))
    halves = [sums_call((up,), *[((grads[0][1], i), got[0][i]) for i in range(3)])]
    across = [[(swap_x(v), None) for v in halves[0][:2]]]
    gain_dense = lax.all_to_all(after(gain_send, halves[0][0]), "expert", split_axis=0, concat_axis=0, tiled=True)
    gain_dense = gain_dense.reshape(EXPERTS, length)
    grads.append(weight_grads(2, gain_send, *halves[0]))
    up, down = sums_call((gain_dense, grads[2][0], across[0][0][0], across[0][1][0],), (d_r2, up_sent), (d_l1, down_sent))

    up_sent, down_sent = ahead(up, count), behind(down, count)
    got.append(over_cores(grads[2], up))
    halves.append(sums_call((up,), sum_of(grads[1], got[1], both), sum_of(grads[1], got[1], last)))
    across_b = swap_x(halves[1][0])
    y = dict(zip(BLOCK_OFFSETS, value_call(after(token, *halves[1]), rank, kept[1], w_down, slots)))
    late = swap_core(after(grads[0][3], up))
    (up,) = sums_call((y[0], across_b, down_sent, late), (d_r1, up_sent))

    up_sent, y_down = ahead(up, count), behind(after(y[4], up), count)
    across[0].append((swap_x(after(halves[0][2], up)), None))
    across.append([(across_b, 0), (across_b, 1), (swap_x(after(halves[1][1], up)), None)])
    halves.append(sums_call((up,), sum_of(grads[2], got[2], both), sum_of(grads[2], got[2], last)))
    grads.append(weight_grads(3, *halves[2]))
    (down,) = sums_call(
        (up_sent, across[0][2][0], across[1][2][0], grads[3][0]), (y[-3], y_down)
    )

    y_up, y_down, across_d = ahead(after(y[3], down), count), behind(down, count), swap_x(after(halves[2][0], down))
    grad, attn_grad, small, *out_parts = resid_back_call(
        after(token, down), resid, gain_two, cotangent, (d_own, up_sent, down_sent), gain_dense, second,
        attn, out_pieces, shared_pieces,
    )
    def terms_of(expert, i, *ready):
        other = (late, i) if expert == 0 else (got[expert], 3 + i)
        return [(after(grads[expert][0], *ready) if ready else grads[expert][0], i), other, across[expert][i]]

    def finish(ready, expert, kept_out, parts=range(3)):
        return finish_call(holds, [(i, expert, [terms_of(expert, i, *ready)]) for i in parts], kept_out)

    out_first = [swap_core(v) for v in out_parts[4:]]
    finished = finish((grad,), 0, None)
    *out_half, up, down = sums_call(
        (finished[0], across_d), *zip(out_parts[2:4], out_first), (y[2], y_up), (y[-2], y_down)
    )

    y_up, y_down, out_across = ahead(up, count), behind(down, count), [swap_x(v) for v in out_half]
    out_got = swap_core(after(out_parts[1], up))
    input_grad, *qkv_parts = attention_back_call(
        after(token, up), query, key, value, attn_grad, first_low, tokens, gain_one, grad, small, query_pieces,
        shared_pieces, segments, seg_col, cos, sin,
    )
    up, down = sums_call((input_grad, *out_across, out_got), (y[1], y_up), (y[-1], y_down))

    y_up, y_down = ahead(up, count), behind(down, count)
    qkv_first = [swap_core(after(v, up)) for v in qkv_parts[4:]]
    qkv_half = sums_call((up,), *zip(qkv_parts[2:4], qkv_first))
    qkv_across = [swap_x(qkv_half[0])]
    out_parts = spread_call(after(token, *qkv_half), count, out_parts[0], out_got, *out_across)
    finished = finish(qkv_half, 1, finished)
    qkv_got = swap_core(after(qkv_parts[1], qkv_across[0]))
    got.append(over_cores(grads[3], qkv_half[0]))
    (half_e,) = sums_call((finished[0],), sum_of(grads[3], got[3], range(3)))
    across.append([(across_d, 0), (across_d, 1)])
    finished = finish((half_e,), 2, finished, both)
    y_own = after(y[0], qkv_across[0], out_parts[0], finished[0])
    mixed = (resid + sum(t.astype(WIDE) for t in (y_own, y_up, y_down))).astype(LOW)
    qkv_across.append(swap_x(after(qkv_half[1], qkv_across[0])))

    def sum_step(parts, up, down, step):
        up = add_low(parts[step], ahead(up, count))
        down = behind(down, count)
        return up, add_low(parts[count + 1 - step], down) if step > 1 else down

    def copy_step(up, down):
        return up + [ahead(up[-1], count)], down + [behind(down[-1], count)]

    out_up, out_down = after(out_parts[4], mixed), after(out_parts[5], mixed)
    for step in (3, 2, 1):
        out_up, out_down = sum_step(out_parts, out_up, out_down, step)
        if step == 2:
            out_up = after(out_up, qkv_across[1])
    out_own = add_low(out_parts[0], ahead(out_up, count), out_down)
    across_e = [swap_x(after(halves[2][1], qkv_across[1])), swap_x(after(half_e, qkv_across[1]))]
    qkv_parts = spread_call(after(token, out_own), count, qkv_parts[0], qkv_got, *qkv_across)
    across[2].append((across_e[0], None))
    across.append([(across_e[1], i) for i in range(3)])
    out_ups, out_downs = [after(out_own, qkv_parts[0])], [after(out_own, qkv_parts[0])]
    qkv_up, qkv_down = qkv_parts[4], qkv_parts[5]
    for step in (3, 2, 1):
        out_ups, out_downs = copy_step(out_ups, out_downs)
        qkv_up, qkv_down = sum_step(qkv_parts, qkv_up, qkv_down, step)
        qkv_up = after(qkv_up, out_ups[-1], out_downs[-1])
    out_ups.append(ahead(out_ups[-1], count))
    qkv_own = add_low(qkv_parts[0], ahead(qkv_up, count), qkv_down)
    qkv_ups, qkv_downs = [qkv_own], [qkv_own]
    for step in (3, 2, 1):
        qkv_ups, qkv_downs = copy_step(qkv_ups, qkv_downs)
        if step == 3:
            qkv_ups[-1] = after(qkv_ups[-1], out_ups[-1])
    (out_sum,) = assemble_call(after(token, qkv_ups[2]), out_downs + out_ups[:0:-1], (model_width,))
    qkv_ups.append(ahead(after(qkv_ups[-1], out_sum, across_e[1]), count))
    last_rows = [terms_of(2, 2, qkv_ups[3]), terms_of(3, 2)]
    finished = finish_call(
        holds, [(0, 3, [terms_of(3, 0, qkv_ups[3])]), (1, 3, [terms_of(3, 1)]), (2, 2, last_rows)], finished
    )
    query_sum, key_sum, value_sum, router_sum, ffn_gain_sum, attn_gain_sum = assemble_call(
        after(token, finished[0]), qkv_downs + qkv_ups[:0:-1], (model_width, key_width, key_width)
    )
    gate_shard, up_shard, down_shard = finished
    return (
        mixed,
        input_grad,
        attn_gain_sum,
        ffn_gain_sum,
        query_sum,
        key_sum,
        value_sum,
        out_sum,
        router_sum.T,
        gate_shard,
        up_shard,
        down_shard,
    )


def solution(mesh):
    ring = mesh.shape["expert"] == len(BLOCK_OFFSETS) and mesh.shape["wshard"] == 4
    body = per_device_ring if ring else per_device_exchange
    in_specs = (
        P(("expert", "wshard"), None),
        P(("expert", "wshard"), None),
        P(("expert", "wshard"), None),
        P(),
        P(),
        P("wshard", None),
        P("wshard", None),
        P("wshard", None),
        P("wshard", None),
        P("wshard", None),
        P(None, "expert"),
        P(None, "expert"),
        P("expert", None),
        P(("expert", "wshard"), None),
    )
    out_specs = (
        P(("expert", "wshard"), None),
        P(("expert", "wshard"), None),
        P("wshard"),
        P("wshard"),
        P("wshard", None),
        P("wshard", None),
        P("wshard", None),
        P("wshard", None),
        P("wshard", None),
        P("wshard", "expert"),
        P("wshard", "expert"),
        P("expert", "wshard"),
    )
    return jax.shard_map(
        body, mesh=mesh, in_specs=in_specs, out_specs=out_specs, check_vma=False
    )
```

```python
import functools

import jax
import jax.numpy as jnp
from jax import lax
from jax.experimental import pallas as pl
from jax.experimental.pallas import tpu as pltpu
from jax.sharding import PartitionSpec as P

QUERY_HEADS = 12
KEY_VALUE_HEADS = 2
HEAD_DIM = 128
EXPERTS = 32
TOP = 4


EPS = 1e-06
ROPE_BASE = 10000.0
NEG = -1e30
LOW = jnp.bfloat16
WIDE = jnp.float32
MIB = 1024 * 1024
ONCE = pl.Buffered(buffer_count=1)
def norm_forward(values, gain):
    inverse = lax.rsqrt(jnp.mean(values * values, axis=-1) + EPS)
    normed = values * inverse[:, None]
    return (normed * gain, normed, inverse)


def norm_backward(grad, gain, normed, inverse):
    gain_grad = jnp.sum(grad * normed, axis=0)
    scaled = grad * gain
    centred = scaled - normed * jnp.mean(scaled * normed, axis=-1, keepdims=True)
    return (inverse[:, None] * centred, gain_grad)


def rotary_tables(seq_length, head_size):
    half_size = head_size // 2
    frequency = ROPE_BASE ** (-(jnp.arange(half_size, dtype=jnp.float32) * 2.0 / head_size))
    angles = jnp.arange(seq_length, dtype=jnp.float32)[:, None] * frequency[None, :]
    return (jnp.cos(angles), jnp.sin(angles))


def apply_rotation(values, cosine_lookup, sine_lookup):
    half_size = values.shape[-1] // 2
    first_half = values[..., :half_size]
    second_half = values[..., half_size:]
    cos_part = cosine_lookup[:, None, :]
    sin_part = sine_lookup[:, None, :]
    return jnp.concatenate(
        [
            first_half * cos_part - second_half * sin_part,
            second_half * cos_part + first_half * sin_part,
        ],
        axis=-1,
    )


def reverse_rotation(values, cosine_lookup, sine_lookup):
    half_size = values.shape[-1] // 2
    first_half = values[..., :half_size]
    second_half = values[..., half_size:]
    cos_part = cosine_lookup[:, None, :]
    sin_part = sine_lookup[:, None, :]
    return jnp.concatenate(
        [
            first_half * cos_part + second_half * sin_part,
            second_half * cos_part - first_half * sin_part,
        ],
        axis=-1,
    )


def per_device_exchange(
    tokens,
    segments,
    routes,
    attn_gain,
    ffn_gain,
    w_query,
    key_weight,
    value_weight,
    w_out,
    w_router,
    w_gate,
    w_up,
    w_down,
    cotangent,
):
    lower_dtype = jnp.bfloat16
    wide_type = jnp.float32
    sequence_length, model_width = tokens.shape
    top_count = routes.shape[1]
    axis_count = lax.axis_size("expert")
    owners = max(1, axis_count // EXPERTS)
    holds = max(1, EXPERTS // axis_count)
    groups = EXPERTS // holds
    capacity = max(2, 3 * sequence_length * top_count // (2 * EXPERTS))
    hidden_dev = w_gate.shape[1] // holds
    query_group_width = QUERY_HEADS // KEY_VALUE_HEADS
    score_scale = HEAD_DIM ** (-0.5)
    pair_count = sequence_length * top_count
    query_full, key_full, value_full, out_full, router_full = (
        lax.all_gather(w_query, "wshard", axis=0, tiled=True),
        lax.all_gather(key_weight, "wshard", axis=0, tiled=True),
        lax.all_gather(value_weight, "wshard", axis=0, tiled=True),
        lax.all_gather(w_out, "wshard", axis=0, tiled=True),
        lax.all_gather(w_router, "wshard", axis=0, tiled=True),
    )
    stream = tokens.astype(wide_type)
    first_norm, first_normed, first_inverse = norm_forward(stream, attn_gain)
    first_low = first_norm.astype(lower_dtype)
    cosine_lookup, sine_lookup = rotary_tables(sequence_length, HEAD_DIM)
    query_pre = jnp.dot(first_low, query_full, preferred_element_type=wide_type).reshape(
        sequence_length, QUERY_HEADS, HEAD_DIM
    )
    key_unrotated = jnp.dot(first_low, key_full, preferred_element_type=wide_type).reshape(
        sequence_length, KEY_VALUE_HEADS, HEAD_DIM
    )
    query_rotated = (
        apply_rotation(query_pre, cosine_lookup, sine_lookup)
        .astype(lower_dtype)
        .reshape(sequence_length, KEY_VALUE_HEADS, query_group_width, HEAD_DIM)
    )
    key_rotated = apply_rotation(key_unrotated, cosine_lookup, sine_lookup).astype(lower_dtype)
    value_lowered = (
        jnp.dot(first_low, value_full, preferred_element_type=wide_type)
        .astype(lower_dtype)
        .reshape(sequence_length, KEY_VALUE_HEADS, HEAD_DIM)
    )
    positions = jnp.arange(sequence_length)
    offset = positions[:, None] - positions[None, :]
    segment_row = segments[0]
    allowed = (segment_row[:, None] == segment_row[None, :]) & (offset >= 0)
    raw_scores = jnp.einsum(
        "qagd,kad->agqk", query_rotated, key_rotated, preferred_element_type=wide_type
    )
    scores = jnp.where(allowed, raw_scores * score_scale, NEG)
    score_top = jnp.max(scores, axis=-1, keepdims=True)
    expo_terms = jnp.exp(scores - score_top)
    expo_total = jnp.sum(expo_terms, axis=-1, keepdims=True)
    log_total = score_top + jnp.log(expo_total)
    probs_low = (expo_terms / expo_total).astype(lower_dtype)
    attn_low = (
        jnp.einsum("agqk,kad->qagd", probs_low, value_lowered, preferred_element_type=wide_type)
        .astype(lower_dtype)
        .reshape(sequence_length, QUERY_HEADS * HEAD_DIM)
    )
    resid = stream + jnp.dot(attn_low, out_full, preferred_element_type=wide_type)
    second_norm, second_normed, second_inverse = norm_forward(resid, ffn_gain)
    second_low = second_norm.astype(lower_dtype)
    logits = jnp.dot(second_low, router_full, preferred_element_type=wide_type)
    choose = (routes[:, :, None] == jnp.arange(EXPERTS)[None, None, :]).astype(wide_type)
    selected = jnp.sum(choose * logits[:, None, :], axis=-1)
    gate_probs = jax.nn.softmax(selected, axis=-1)
    flat_routes = routes.reshape(pair_count)
    one_hot = (flat_routes[:, None] == jnp.arange(EXPERTS)[None, :]).astype(jnp.int32)
    slot_rank = jnp.sum((jnp.cumsum(one_hot, axis=0) - 1) * one_hot, axis=1)
    slot_index = (flat_routes // holds * capacity + slot_rank) * holds + flat_routes % holds
    slot_pair = (
        jnp.full((EXPERTS * capacity,), pair_count, jnp.int32)
        .at[slot_index]
        .set(jnp.arange(pair_count, dtype=jnp.int32))
    )
    second_ext = jnp.concatenate([second_low, jnp.zeros((1, model_width), lower_dtype)], axis=0)
    send_rows = jnp.repeat(
        second_ext[slot_pair // top_count].reshape(groups, capacity, holds, model_width),
        owners,
        axis=0,
    )
    gate_local = w_gate.reshape(model_width, holds, hidden_dev)
    up_local = w_up.reshape(model_width, holds, hidden_dev)
    down_local = w_down.reshape(holds, hidden_dev, model_width)

    def owner_total(values):
        summed = jnp.sum(
            values.astype(wide_type).reshape(groups, owners, capacity, holds, model_width), axis=1
        )
        return summed.reshape(EXPERTS * capacity, model_width)

    received = lax.all_to_all(send_rows, "expert", split_axis=0, concat_axis=0, tiled=True)
    gate_pre = jnp.einsum("scld,dlf->sclf", received, gate_local, preferred_element_type=wide_type)
    up_pre = jnp.einsum("scld,dlf->sclf", received, up_local, preferred_element_type=wide_type)
    hidden = (jax.nn.silu(gate_pre) * up_pre).astype(lower_dtype)
    partial_value = jnp.einsum(
        "sclf,lfd->scld", hidden, down_local, preferred_element_type=wide_type
    ).astype(lower_dtype)
    returned = lax.all_to_all(partial_value, "expert", split_axis=0, concat_axis=0, tiled=True)
    expert_wide = owner_total(returned)[slot_index].reshape(sequence_length, top_count, model_width)
    mixed = (resid + jnp.sum(gate_probs[:, :, None] * expert_wide, axis=1)).astype(lower_dtype)
    upstream = cotangent.astype(wide_type)
    query_back, key_back, value_back, out_back, router_back = (
        lax.all_gather(w_query, "wshard", axis=0, tiled=True),
        lax.all_gather(key_weight, "wshard", axis=0, tiled=True),
        lax.all_gather(value_weight, "wshard", axis=0, tiled=True),
        lax.all_gather(w_out, "wshard", axis=0, tiled=True),
        lax.all_gather(w_router, "wshard", axis=0, tiled=True),
    )
    gate_grad = jnp.sum(expert_wide * upstream[:, None, :], axis=-1)
    sel_grad = gate_probs * (gate_grad - jnp.sum(gate_probs * gate_grad, axis=-1, keepdims=True))
    logit_grad = jnp.sum(choose * sel_grad[:, :, None], axis=1).astype(lower_dtype)
    pair_grad = (
        (gate_probs[:, :, None] * upstream[:, None, :])
        .astype(lower_dtype)
        .reshape(pair_count, model_width)
    )
    pair_ext = jnp.concatenate([pair_grad, jnp.zeros((1, model_width), lower_dtype)], axis=0)
    grad_send = jnp.repeat(
        pair_ext[slot_pair].reshape(groups, capacity, holds, model_width), owners, axis=0
    )
    grad_recv, rows_recv = (
        lax.all_to_all(grad_send, "expert", split_axis=0, concat_axis=0, tiled=True),
        lax.all_to_all(send_rows, "expert", split_axis=0, concat_axis=0, tiled=True),
    )
    gate_pre = jnp.einsum("scld,dlf->sclf", rows_recv, gate_local, preferred_element_type=wide_type)
    up_pre = jnp.einsum("scld,dlf->sclf", rows_recv, up_local, preferred_element_type=wide_type)
    sigmoid_gate = jax.nn.sigmoid(gate_pre)
    silu_gate = gate_pre * sigmoid_gate
    hidden = (silu_gate * up_pre).astype(lower_dtype)
    hidden_grad = jnp.einsum(
        "scld,lfd->sclf", grad_recv, down_local, preferred_element_type=wide_type
    )
    gate_pre_grad = (
        hidden_grad * up_pre * sigmoid_gate * (1.0 + gate_pre * (1.0 - sigmoid_gate))
    ).astype(lower_dtype)
    up_pre_grad = (hidden_grad * silu_gate).astype(lower_dtype)
    row_grad = (
        jnp.einsum("sclf,dlf->scld", gate_pre_grad, gate_local, preferred_element_type=wide_type)
        + jnp.einsum("sclf,dlf->scld", up_pre_grad, up_local, preferred_element_type=wide_type)
    ).astype(lower_dtype)
    returned_grad = lax.all_to_all(row_grad, "expert", split_axis=0, concat_axis=0, tiled=True)
    gate_wgrad = jnp.einsum(
        "scld,sclf->dlf", rows_recv, gate_pre_grad, preferred_element_type=wide_type
    ).reshape(model_width, holds * hidden_dev)
    up_wgrad = jnp.einsum(
        "scld,sclf->dlf", rows_recv, up_pre_grad, preferred_element_type=wide_type
    ).reshape(model_width, holds * hidden_dev)
    down_wgrad = jnp.einsum(
        "sclf,scld->lfd", hidden, grad_recv, preferred_element_type=wide_type
    ).reshape(holds * hidden_dev, model_width)
    gate_shard, up_shard, down_shard = (
        lax.psum_scatter(
            gate_wgrad.astype(jnp.bfloat16), "wshard", scatter_dimension=0, tiled=True
        ).astype(jnp.float32),
        lax.psum_scatter(
            up_wgrad.astype(jnp.bfloat16), "wshard", scatter_dimension=0, tiled=True
        ).astype(jnp.float32),
        lax.psum_scatter(
            down_wgrad.astype(jnp.bfloat16), "wshard", scatter_dimension=1, tiled=True
        ).astype(jnp.float32),
    )
    token_grad = owner_total(returned_grad)[slot_index].reshape(
        sequence_length, top_count, model_width
    )
    second_grad = jnp.sum(token_grad, axis=1) + jnp.dot(
        logit_grad, router_back.T, preferred_element_type=wide_type
    )
    router_wgrad = jnp.einsum("td,te->de", second_low, logit_grad, preferred_element_type=wide_type)
    resid_part, ffn_gain_grad = norm_backward(second_grad, ffn_gain, second_normed, second_inverse)
    resid_grad = upstream + resid_part
    resid_low = resid_grad.astype(lower_dtype)
    out_wgrad = jnp.einsum("tc,td->cd", attn_low, resid_low, preferred_element_type=wide_type)
    attn_grad = (
        jnp.dot(resid_low, out_back.T, preferred_element_type=wide_type)
        .astype(lower_dtype)
        .reshape(sequence_length, KEY_VALUE_HEADS, query_group_width, HEAD_DIM)
    )
    raw_again = jnp.einsum(
        "qagd,kad->agqk", query_rotated, key_rotated, preferred_element_type=wide_type
    )
    scores_again = jnp.where(allowed, raw_again * score_scale, NEG)
    probs_again = jnp.exp(scores_again - log_total)
    prob_grad = jnp.einsum(
        "qagd,kad->agqk", attn_grad, value_lowered, preferred_element_type=wide_type
    )
    row_delta = jnp.sum(probs_again * prob_grad, axis=-1, keepdims=True)
    score_grad = (probs_again * (prob_grad - row_delta) * score_scale).astype(lower_dtype)
    value_grad = (
        jnp.einsum("agqk,qagd->kad", probs_low, attn_grad, preferred_element_type=wide_type)
        .astype(lower_dtype)
        .reshape(sequence_length, KEY_VALUE_HEADS * HEAD_DIM)
    )
    query_rot_grad = jnp.einsum(
        "agqk,kad->qagd", score_grad, key_rotated, preferred_element_type=wide_type
    ).reshape(sequence_length, QUERY_HEADS, HEAD_DIM)
    key_rotated_gradient = jnp.einsum(
        "agqk,qagd->kad", score_grad, query_rotated, preferred_element_type=wide_type
    )
    query_grad = (
        reverse_rotation(query_rot_grad, cosine_lookup, sine_lookup)
        .astype(lower_dtype)
        .reshape(sequence_length, QUERY_HEADS * HEAD_DIM)
    )
    key_grad = (
        reverse_rotation(key_rotated_gradient, cosine_lookup, sine_lookup)
        .astype(lower_dtype)
        .reshape(sequence_length, KEY_VALUE_HEADS * HEAD_DIM)
    )
    query_wgrad = jnp.einsum("td,tc->dc", first_low, query_grad, preferred_element_type=wide_type)
    key_wgrad = jnp.einsum("td,tc->dc", first_low, key_grad, preferred_element_type=wide_type)
    value_wgrad = jnp.einsum("td,tc->dc", first_low, value_grad, preferred_element_type=wide_type)
    first_grad = (
        jnp.dot(query_grad, query_back.T, preferred_element_type=wide_type)
        + jnp.dot(key_grad, key_back.T, preferred_element_type=wide_type)
        + jnp.dot(value_grad, value_back.T, preferred_element_type=wide_type)
    )
    stream_part, attn_gain_grad = norm_backward(first_grad, attn_gain, first_normed, first_inverse)
    input_grad = resid_grad + stream_part
    query_part, key_part, value_part, out_part, router_part, attn_gain_part, ffn_gain_part = (
        lax.psum_scatter(
            query_wgrad.astype(jnp.bfloat16), "wshard", scatter_dimension=0, tiled=True
        ).astype(jnp.float32),
        lax.psum_scatter(
            key_wgrad.astype(jnp.bfloat16), "wshard", scatter_dimension=0, tiled=True
        ).astype(jnp.float32),
        lax.psum_scatter(
            value_wgrad.astype(jnp.bfloat16), "wshard", scatter_dimension=0, tiled=True
        ).astype(jnp.float32),
        lax.psum_scatter(
            out_wgrad.astype(jnp.bfloat16), "wshard", scatter_dimension=0, tiled=True
        ).astype(jnp.float32),
        lax.psum_scatter(
            router_wgrad.astype(jnp.bfloat16), "wshard", scatter_dimension=0, tiled=True
        ).astype(jnp.float32),
        lax.psum_scatter(
            attn_gain_grad.astype(jnp.bfloat16), "wshard", scatter_dimension=0, tiled=True
        ).astype(jnp.float32),
        lax.psum_scatter(
            ffn_gain_grad.astype(jnp.bfloat16), "wshard", scatter_dimension=0, tiled=True
        ).astype(jnp.float32),
    )
    query_sum, key_sum, value_sum, out_sum, router_sum, attn_gain_sum, ffn_gain_sum = lax.psum(
        (query_part, key_part, value_part, out_part, router_part, attn_gain_part, ffn_gain_part),
        "expert",
    )
    return (
        mixed,
        input_grad,
        attn_gain_sum,
        ffn_gain_sum,
        query_sum,
        key_sum,
        value_sum,
        out_sum,
        router_sum,
        gate_shard,
        up_shard,
        down_shard,
    )


BLOCK_OFFSETS = (-1, 1, -2, 2, -3, 3, 0, 4)


def ring_order(count):
    return [0] + list(range(1, count, 2)) + list(range(count - 2, 0, -2))


def shifted(value, step, count):
    order = ring_order(count)
    return lax.ppermute(value, "expert", [(order[i], order[(i + step) % count]) for i in range(count)])


def ahead(value, count):
    return shifted(value, 1, count)


def behind(value, count):
    return shifted(value, -1, count)


def swap_core(value):
    size = lax.axis_size("wshard")
    return lax.ppermute(value, "wshard", [(i, i ^ 1) for i in range(size)])


def swap_x(value):
    size = lax.axis_size("wshard")
    return lax.ppermute(value, "wshard", [(i, i ^ 2) for i in range(size)])


def work(flops, bytes_accessed, transcendentals):
    scale = 8
    return pl.CostEstimate(
        flops=flops // scale, bytes_accessed=bytes_accessed // scale, transcendentals=transcendentals // scale
    )


def add_low(*terms):
    return sum(term.astype(WIDE) for term in terms).astype(LOW)


def after(value, *others):
    return lax.optimization_barrier((value, *others))[0]


def places(rank_row, slots):
    rows = lax.broadcasted_iota(jnp.int32, (slots, rank_row.shape[-1]), 0)
    return rank_row == rows


def expert_ranks(routes, holds):
    tokens = routes.shape[1]
    names = [jnp.sum((routes == l).astype(WIDE), axis=0, keepdims=True) for l in range(holds)]
    names = jnp.concatenate(names + [jnp.zeros((16 - holds, tokens), WIDE)], axis=0)
    rows = lax.broadcasted_iota(jnp.int32, (tokens, tokens), 0)
    columns = lax.broadcasted_iota(jnp.int32, (tokens, tokens), 1)
    before = dot(names.astype(LOW), (rows <= columns).astype(WIDE).astype(LOW))
    return jnp.where(names > 0.0, before - 1.0, -1.0)[:holds].astype(jnp.int32)


def pack_routing(gates, routes):
    high = gates.astype(LOW).astype(WIDE)
    rows = [high, gates - high, routes.astype(WIDE)]
    spare = 16 - 3 * gates.shape[0]
    return jnp.concatenate(rows + [jnp.zeros((spare, gates.shape[1]), WIDE)], axis=0).astype(LOW)


def unpack_routing(packed):
    top_count = TOP
    packed = packed.astype(WIDE)
    return packed[:top_count] + packed[top_count : 2 * top_count], packed[2 * top_count : 3 * top_count]


def dot_t(a, b):
    return lax.dot_general(a, b, (((0,), (0,)), ((), ())), preferred_element_type=WIDE)


def dot_bt(a, b):
    return lax.dot_general(a, b, (((1,), (1,)), ((), ())), preferred_element_type=WIDE)


def dot(a, b):
    return jnp.dot(a, b, preferred_element_type=WIDE)


def expert_kernel(count, slots, aliased, *refs):
    token_ref = refs[0]
    h_refs, dz_refs = refs[1 : 1 + count], refs[1 + count : 1 + 2 * count]
    wg_ref, wu_ref, wd_ref = refs[1 + 2 * count : 4 + 2 * count]
    rest = refs[4 + 2 * count + (7 if aliased else 0) :]
    d_refs = rest[:count]
    gain_ref, rank_ref, rows_out, dz_out, gg_out, ug_out, hid_out = rest[count : count + 7]
    place_scr, back_scr, gate_scr, wg_scr, wu_scr, wd_scr, sems = rest[count + 7 :]
    e = pl.program_id(0)
    holds, tokens = rank_ref.shape[1:]
    hidden_width = wd_scr.shape[1]

    def weights(expert, slot):
        band = pl.ds(pl.multiple_of(expert * hidden_width, hidden_width), hidden_width)
        return [
            pltpu.make_async_copy(source, target.at[slot], sems.at[slot, i])
            for i, (source, target) in enumerate(
                ((wg_ref.at[:, band], wg_scr), (wu_ref.at[:, band], wu_scr), (wd_ref.at[band, :], wd_scr))
            )
        ]

    slot = lax.rem(e, 2)

    @pl.when(e == 0)
    def _():
        for copy in weights(0, 0):
            copy.start()

    @pl.when(e + 1 < holds)
    def _():
        for copy in weights(e + 1, 1 - slot):
            copy.start()

    here = pl.ds(pl.multiple_of(e * slots, slots), slots)
    @pl.when(e == 0)
    def _():
        for b, (h_ref, dz_ref) in enumerate(zip(h_refs, dz_refs)):
            gates, routes = unpack_routing(h_ref[tokens : tokens + 16, :tokens])
            routes = routes - (token_ref[1] * holds).astype(WIDE)
            ranks = expert_ranks(routes, holds)
            rank_ref[b] = ranks
            for l in range(holds):
                band = slice(l * slots, (l + 1) * slots)
                spot = places(ranks[l : l + 1], slots).astype(WIDE)
                named = jnp.where(routes == l, gates, 0.0)
                gate_scr[b, band, :] = jnp.broadcast_to(
                    jnp.sum(spot * jnp.sum(named, axis=0, keepdims=True), axis=1, keepdims=True), (slots, 128)
                )
                place_scr[b, band, :] = spot.astype(LOW)
            for source, target in ((h_ref, rows_out), (dz_ref, dz_out)):
                taken = dot(place_scr[b], source[:tokens]).astype(LOW)
                for l in range(holds):
                    target[l, b * slots : (b + 1) * slots, :] = taken[l * slots : (l + 1) * slots]

    gate = jnp.concatenate([gate_scr[b, here, :] for b in range(count)], axis=0)[:, :1]
    rows = rows_out[e]
    for copy in weights(e, slot):
        copy.wait()
    gate_pre = dot(rows, wg_scr[slot])
    up_pre = dot(rows, wu_scr[slot])
    sig = jax.nn.sigmoid(gate_pre)
    silu = gate_pre * sig
    hidden = (silu * up_pre).astype(LOW).astype(WIDE)
    back = dot_bt(dz_out[e], wd_scr[slot])
    gains = jnp.sum(back * hidden, axis=1, keepdims=True)
    back = back * gate
    gate_grad = (back * (up_pre * sig * (1.0 + gate_pre * (1.0 - sig)))).astype(LOW)
    up_grad = (back * silu).astype(LOW)
    gg_out[0] = gate_grad
    ug_out[0] = up_grad
    hid_out[0] = (hidden * gate).astype(LOW)
    row_grad = (dot_bt(gate_grad, wg_scr[slot]) + dot_bt(up_grad, wu_scr[slot])).astype(LOW)
    for b in range(count):
        band = slice(b * slots, (b + 1) * slots)
        back_scr[b, here, :] = row_grad[band]
        spot = place_scr[b, here, :].astype(WIDE)
        gain_ref[b, pl.ds(e, 1), :] = jnp.sum(spot * gains[band], axis=0, keepdims=True)

    @pl.when(e == pl.num_programs(0) - 1)
    def _():
        for b in range(count):
            d_refs[b][...] = dot_t(place_scr[b], back_scr[b]).astype(LOW)


def expert_call(token, first, blocks, dz_blocks, w_gate, w_up, w_down, kept, holds, slots, total):
    count = len(blocks)
    tokens, width = dz_blocks[0].shape
    hidden = w_gate.shape[1] // holds
    whole = lambda *shape: pl.BlockSpec(shape, lambda e: (0,) * len(shape))
    once = lambda *shape: pl.BlockSpec(shape, lambda e: (0,) * len(shape), pipeline_mode=pl.Buffered(buffer_count=1))
    aliased = kept is not None
    in_specs = (
        [pl.BlockSpec(memory_space=pltpu.SMEM)]
        + [once(*b.shape) for b in (*blocks, *dz_blocks)]
        + [pl.BlockSpec(memory_space=pl.ANY)] * 3
    )
    aliases = {len(in_specs) + i: count + i for i in range(7)} if aliased else {}
    out = pl.pallas_call(
        functools.partial(expert_kernel, count, slots, aliased),
        grid=(holds,),
        in_specs=in_specs + ([pl.BlockSpec(memory_space=pl.ANY)] * 7 if aliased else []),
        out_specs=[whole(tokens, width)] * count
        + [pl.BlockSpec((count, holds, tokens), lambda e: (first // count, 0, 0))] * 2
        + [pl.BlockSpec((holds, count * slots, width), lambda e: (0, first // count, 0))] * 2
        + [pl.BlockSpec((1, count * slots, hidden), lambda e: (e, first // count, 0))] * 3,
        out_shape=[shaped(tokens, width)] * count
        + [shaped(total, holds, tokens, dtype=WIDE), shaped(total, holds, tokens, dtype=jnp.int32)]
        + [shaped(holds, total * slots, width)] * 2
        + [shaped(holds, total * slots, hidden)] * 3,
        scratch_shapes=[
            pltpu.VMEM((count, holds * slots, tokens), LOW),
            pltpu.VMEM((count, holds * slots, width), LOW),
            pltpu.VMEM((count, holds * slots, 128), WIDE),
            pltpu.VMEM((2, width, hidden), LOW),
            pltpu.VMEM((2, width, hidden), LOW),
            pltpu.VMEM((2, hidden, width), LOW),
            pltpu.SemaphoreType.DMA((2, 3)),
        ],
        input_output_aliases=aliases,
        compiler_params=pltpu.CompilerParams(vmem_limit_bytes=60 * MIB),
        cost_estimate=work(
            flops=2 * holds * count * slots * width * (5 * hidden + 3 * tokens),
            bytes_accessed=3 * holds * width * hidden * 2
            + count * tokens * width * 6
            + holds * count * slots * (2 * width + 3 * hidden) * 2,
            transcendentals=holds * count * slots * hidden,
        ),
    )(token, *blocks, *dz_blocks, w_gate, w_up, w_down, *(kept if aliased else ()))
    return out[:count], tuple(out[count:])


def value_kernel(slots, _, rank_ref, hid_ref, wd_ref, *refs):
    total, holds, tokens = rank_ref.shape
    y_refs, (value_scr, place_scr) = refs[:total], refs[total:]
    e = pl.program_id(0)
    here = pl.ds(pl.multiple_of(e * slots, slots), slots)
    value = dot(hid_ref[0], wd_ref[...]).astype(LOW)
    for b in range(total):
        value_scr[b, here, :] = value[b * slots : (b + 1) * slots]

    @pl.when(e == pl.num_programs(0) - 1)
    def _():
        for b in range(total):
            for l in range(holds):
                spot = places(rank_ref[b, l : l + 1, :], slots)
                place_scr[l * slots : (l + 1) * slots, :] = spot.astype(WIDE).astype(LOW)
            y_refs[b][...] = dot_t(place_scr[...], value_scr[b]).astype(LOW)


def value_call(token, rank, hidden_rows, w_down, slots):
    total, holds, tokens = rank.shape
    width = w_down.shape[1]
    hidden = hidden_rows.shape[2]
    whole = lambda *shape: pl.BlockSpec(shape, lambda e: (0,) * len(shape))
    out = pl.pallas_call(
        functools.partial(value_kernel, slots),
        grid=(holds,),
        in_specs=[
            pl.BlockSpec(memory_space=pltpu.SMEM),
            whole(*rank.shape),
            pl.BlockSpec((1, total * slots, hidden), lambda e: (e, 0, 0)),
            pl.BlockSpec((hidden, width), lambda e: (e, 0)),
        ],
        out_specs=[whole(tokens, width)] * total,
        out_shape=[shaped(tokens, width)] * total,
        scratch_shapes=[pltpu.VMEM((total, holds * slots, width), LOW), pltpu.VMEM((holds * slots, tokens), LOW)],
        compiler_params=pltpu.CompilerParams(vmem_limit_bytes=60 * MIB),
        cost_estimate=work(
            flops=2 * total * holds * slots * width * (hidden + tokens),
            bytes_accessed=2 * (holds * hidden * (width + total * slots) + total * tokens * width),
            transcendentals=0,
        ),
    )(token, rank, hidden_rows, w_down)
    return out


def wgrad_kernel(apart, place_ref, rows_ref, dz_ref, gg_ref, ug_ref, hid_ref, *outs):
    step = pl.program_id(0)
    shard = outs[0].shape[1]
    columns = pl.ds(pl.multiple_of(jnp.bitwise_xor(place_ref[0], step) * shard, 128), shard)
    rows, grads = rows_ref[0, :, columns], dz_ref[0, :, columns]
    parts = [dot_t(rows, gg_ref[0]), dot_t(rows, ug_ref[0]), dot_t(grads, hid_ref[0])]
    parts = [part.astype(LOW) for part in parts]
    for s in range(4):

        @pl.when(step == s)
        def _():
            for i, part in enumerate(parts):
                if s == 3 and apart:
                    outs[3 + i][...] = part
                elif s % 2 and not apart:
                    outs[2][3 - 3 * (s // 2) + i] = part
                else:
                    outs[s if apart else s // 2][i] = part


def wgrad_call(expert, place, kept, apart=False):
    _, count, width = kept[0].shape
    hidden = kept[2].shape[2]
    shard = width // 4
    row_spec = lambda d: pl.BlockSpec((1, count, d), lambda s: (expert, 0, 0), pipeline_mode=pl.Buffered(buffer_count=1))
    shapes = [(3, shard, hidden)] * 3 + [(shard, hidden)] * 3 if apart else [(3, shard, hidden)] * 2 + [(6, shard, hidden)]
    out = pl.pallas_call(
        functools.partial(wgrad_kernel, apart),
        grid=(4,),
        in_specs=[pl.BlockSpec(memory_space=pltpu.SMEM), row_spec(width), row_spec(width)] + [row_spec(hidden)] * 3,
        out_specs=[pl.BlockSpec(shape, lambda s, zeros=(0,) * len(shape): zeros) for shape in shapes],
        out_shape=[shaped(*shape) for shape in shapes],
        compiler_params=pltpu.CompilerParams(vmem_limit_bytes=60 * MIB),
        cost_estimate=work(
            flops=2 * count * width * 3 * hidden,
            bytes_accessed=2 * (count * (2 * width + 3 * hidden) + 3 * width * hidden),
            transcendentals=0,
        ),
    )(place, *kept)
    return (out[0], out[2], out[3:], out[1]) if apart else out


def sums_call(gates, *sums):
    every = [term[0] if isinstance(term, tuple) else term for terms in sums for term in terms]

    def part_of(term, ready=()):
        array, part = term if isinstance(term, tuple) else (term, None)
        array = after(array, *ready) if ready else array
        return array if part is None else array[: len(part)] if isinstance(part, range) else array[part]

    totals = [add_low(part_of(terms[0], (*gates, *every)), *map(part_of, terms[1:])) for terms in sums]
    return totals


def finish_kernel(sizes, turned, *refs):
    outs = refs[-len(sizes) :]
    at = 0
    for counts, turn, out in zip(sizes, turned, outs):
        for i, size in enumerate(counts):
            total = sum(ref[...].astype(WIDE) for ref in refs[at : at + size])
            at += size
            if turn:
                height = out.shape[0] // len(counts)
                out[i * height : (i + 1) * height, :] = jnp.transpose(total)
            else:
                out[...] = total


def finish_call(holds, pieces, kept):
    shard, hidden = pieces[0][2][0][0][0].shape[-2:]
    steps = shard // 128
    wide, tall = shaped(shard, holds * hidden, dtype=WIDE), shaped(holds * hidden, shard, dtype=WIDE)
    flat = [term for _, _, experts in pieces for terms in experts for term in terms]
    out_specs, out_shapes = [], []
    for which, expert, experts in pieces:
        number = len(experts)
        if which < 2:
            out_specs.append(pl.BlockSpec((128, hidden), lambda s, expert=expert: (s, expert)))
        else:
            block = (number * hidden, 128)
            out_specs.append(pl.BlockSpec(block, lambda s, at=expert // number: (at, s)))
        out_shapes.append(wide if which < 2 else tall)
    kept_in = [kept[which] for which, _, _ in pieces] if kept else []
    out = pl.pallas_call(
        functools.partial(
            finish_kernel, [[len(terms) for terms in experts] for _, _, experts in pieces], [p[0] == 2 for p in pieces]
        ),
        grid=(steps,),
        in_specs=[
            pl.BlockSpec((128, hidden), lambda s: (s, 0))
            if at is None
            else pl.BlockSpec((None, 128, hidden), lambda s, at=at: (at, s, 0))
            for _, at in flat
        ]
        + [pl.BlockSpec(memory_space=pl.ANY)] * len(kept_in),
        out_specs=out_specs,
        out_shape=out_shapes,
        input_output_aliases={len(flat) + i: i for i in range(len(kept_in))},
        compiler_params=pltpu.CompilerParams(vmem_limit_bytes=20 * MIB),
        cost_estimate=work(flops=0, bytes_accessed=30 * shard * hidden, transcendentals=0),
    )(*[array for array, _ in flat], *kept_in)
    result = list(kept) if kept else [None] * 3
    for (which, _, _), value in zip(pieces, out):
        result[which] = value
    return result


def piece_columns(mine, s, shard):
    return pl.ds(pl.multiple_of(jnp.bitwise_xor(mine, s) * shard, 128), shard)


def turn(values, cos, sin):
    return values * cos + pltpu.roll(values, HEAD_DIM // 2, 1) * sin


def turn_back(values, cos, sin):
    return values * cos - pltpu.roll(values, HEAD_DIM // 2, 1) * sin


def inverse_rms(values):
    return lax.rsqrt(jnp.mean(values * values, axis=-1, keepdims=True) + EPS)


def head_slice(h):
    return slice(h * HEAD_DIM, (h + 1) * HEAD_DIM)


def stacked_heads(ref, band, group, heads):
    return jnp.concatenate([ref[band, head_slice(group * heads + h)] for h in range(heads)], axis=0)


def probabilities(queries, keys, allowed):
    scores = jnp.where(allowed, dot_bt(queries, keys) * HEAD_DIM ** (-0.5), NEG)
    expo = jnp.exp(scores - jnp.max(scores, axis=-1, keepdims=True))
    return expo * (1.0 / jnp.sum(expo, axis=-1, keepdims=True))


def allowed_pairs(seg_col_ref, seg_row_ref, band, reach, heads):
    size = band.stop - band.start
    rows = band.start + lax.broadcasted_iota(jnp.int32, (size, reach), 0)
    cols = lax.broadcasted_iota(jnp.int32, (size, reach), 1)
    ok = (seg_col_ref[band, :] == seg_row_ref[:, :reach]) & (cols <= rows)
    return jnp.concatenate([ok] * heads, axis=0)


def attention_kernel(
    mine_ref, tokens_ref, gain_ref, p0, p1, p2, p3, s0, s1, s2, s3, seg_row_ref, seg_col_ref, cos_ref, sin_ref,
    h_ref, q_ref, k_ref, v_ref, out_ref,
):
    mine = mine_ref[0]
    stream = tokens_ref[...].astype(WIDE)
    h_ref[...] = (stream * inverse_rms(stream) * gain_ref[...]).astype(LOW)
    shard = p0.shape[0]
    width = q_ref.shape[1]
    cos, sin = cos_ref[...], sin_ref[...]

    def projected(pieces, columns):
        return sum(dot(h_ref[:, piece_columns(mine, s, shard)], piece[:, columns]) for s, piece in enumerate(pieces))

    heads = QUERY_HEADS // KEY_VALUE_HEADS
    key_width = KEY_VALUE_HEADS * HEAD_DIM
    shared = (s0, s1, s2, s3)
    keys = projected(shared, slice(0, key_width))
    for g in range(KEY_VALUE_HEADS):
        k_ref[:, head_slice(g)] = turn(keys[:, head_slice(g)], cos, sin).astype(LOW)
    v_ref[...] = projected(shared, slice(key_width, 2 * key_width)).astype(LOW)
    group_width = heads * HEAD_DIM
    for g in range(KEY_VALUE_HEADS):
        queries = projected((p0, p1, p2, p3), slice(g * group_width, (g + 1) * group_width))
        for h in range(heads):
            q_ref[:, head_slice(g * heads + h)] = turn(queries[:, head_slice(h)], cos, sin).astype(LOW)
    length = q_ref.shape[0]
    tile = 128
    for start in range(0, length, tile):
        band, reach = slice(start, start + tile), start + tile
        allowed = allowed_pairs(seg_col_ref, seg_row_ref, band, reach, heads)
        for g in range(KEY_VALUE_HEADS):
            probs = probabilities(stacked_heads(q_ref, band, g, heads), k_ref[:reach, head_slice(g)], allowed)
            mixed = dot(probs.astype(LOW), v_ref[:reach, head_slice(g)]).astype(LOW)
            for h in range(heads):
                out_ref[band, head_slice(g * heads + h)] = mixed[h * tile : (h + 1) * tile]


def vmem_call(kernel, out_shape, flops, transcendentals, token, *args):
    moved = sum(a.size * a.dtype.itemsize for a in args) + sum(
        o.size * o.dtype.itemsize for o in jax.tree.leaves(out_shape)
    )
    return pl.pallas_call(
        kernel,
        in_specs=[pl.BlockSpec(memory_space=pltpu.SMEM)] + [pl.BlockSpec(memory_space=pltpu.VMEM)] * len(args),
        out_specs=[pl.BlockSpec(memory_space=pltpu.VMEM)] * len(out_shape),
        out_shape=out_shape,
        compiler_params=pltpu.CompilerParams(vmem_limit_bytes=32 * MIB),
        cost_estimate=work(flops=flops, bytes_accessed=moved, transcendentals=transcendentals),
    )(token, *args)


def shaped(*shape, dtype=LOW):
    return jax.ShapeDtypeStruct(shape, dtype)


def attention_call(mine, tokens, gain, pieces, shared_pieces, seg_row, seg_col, cos, sin):
    length, width = tokens.shape
    key_width = KEY_VALUE_HEADS * HEAD_DIM
    return vmem_call(
        attention_kernel,
        [shaped(length, width), shaped(length, width), shaped(length, key_width), shaped(length, key_width), shaped(length, width)],
        2 * length * width * (width + 2 * key_width) + 3 * length * length * width,
        QUERY_HEADS * length * length,
        mine, tokens, gain, *pieces, *shared_pieces, seg_row, seg_col, cos, sin,
    )


def project_kernel(
    mine_ref, tokens_ref, attn_ref, p0, p1, p2, p3, r0, r1, r2, r3, gain_ref, routes_ref, resid_ref, h_ref
):
    mine = mine_ref[0]
    shard = p0.shape[0]
    resid = tokens_ref[...].astype(WIDE)
    for s, piece in enumerate((p0, p1, p2, p3)):
        resid = resid + dot(attn_ref[:, piece_columns(mine, s, shard)], piece[...])
    resid_ref[...] = resid
    length, width = resid.shape
    h_ref[:length] = (resid * inverse_rms(resid) * gain_ref[...]).astype(LOW)
    logits = jnp.transpose(
        sum(
            dot(h_ref[:length, piece_columns(mine, s, shard)], piece[...])
            for s, piece in enumerate((r0, r1, r2, r3))
        )
    )
    experts = lax.broadcasted_iota(jnp.int32, logits.shape, 0)
    picked = [
        jnp.sum(jnp.where(experts == routes_ref[k : k + 1, :], logits, 0.0), axis=0, keepdims=True)
        for k in range(routes_ref.shape[0])
    ]
    top = functools.reduce(jnp.maximum, picked)
    expo = [jnp.exp(p - top) for p in picked]
    total = sum(expo)
    gates = jnp.concatenate([x / total for x in expo], axis=0)
    h_ref[length:] = jnp.zeros((16, width), LOW)
    h_ref[length:, :length] = pack_routing(gates, routes_ref[...])


def project_call(mine, tokens, attn, pieces, shared_pieces, gain, routes_t):
    length, width = tokens.shape
    whole = lambda shape: pl.BlockSpec(shape, lambda i: (0,) * len(shape), pipeline_mode=ONCE)
    shapes = [shaped(length, width, dtype=WIDE), shaped(length + 16, width)]
    return pl.pallas_call(
        project_kernel,
        grid=(1,),
        in_specs=[pl.BlockSpec(memory_space=pltpu.SMEM)]
        + [whole(a.shape) for a in (tokens, attn, *pieces)]
        + router_columns(shared_pieces)
        + [whole(gain.shape), whole(routes_t.shape)],
        out_specs=[whole(s.shape) for s in shapes],
        out_shape=shapes,
        compiler_params=pltpu.CompilerParams(vmem_limit_bytes=30 * MIB),
        cost_estimate=work(
            flops=2 * length * width * (width + EXPERTS), bytes_accessed=length * width * 20, transcendentals=length * 8
        ),
    )(mine, tokens, attn, *pieces, *shared_pieces, gain, routes_t)


def as_column(row):
    return jnp.transpose(jnp.broadcast_to(row, (8, row.shape[1])))[:, :1]


def norm_back(grad, gain, normed, inverse):
    scaled = grad * gain
    return inverse * (scaled - normed * jnp.mean(scaled * normed, axis=-1, keepdims=True))


def shard_parts(targets):
    at, parts = 0, []
    for target in targets:
        parts.append((target, slice(at, at + target.shape[0])))
        at += target.shape[0]
    return parts


def resid_back_kernel(
    mine_ref, resid_ref, gain_ref, dz_ref, t0, t1, t2, gains_ref, h_ref, attn_ref,
    p0, p1, p2, p3, r0, r1, r2, r3, grad_ref, attn_grad_ref, small_ref, o0, o1, o2, o3, o4, o5, second_scr, low_scr,
):
    mine = mine_ref[0]
    shard, width = p0.shape
    length = resid_ref.shape[0]
    routers = (r0, r1, r2, r3)
    gains = gains_ref[...]
    experts = lax.broadcasted_iota(jnp.int32, gains.shape, 0)
    gate_rows, routes = unpack_routing(h_ref[length:, :length])
    gates = jnp.zeros(gains.shape, WIDE)
    for k in range(TOP):
        gates = gates + jnp.where(experts.astype(WIDE) == routes[k : k + 1], gate_rows[k : k + 1], 0.0)
    logit_grad = gates * (gains - jnp.sum(gates * gains, axis=0, keepdims=True))
    logit_grad = jnp.concatenate([logit_grad, jnp.zeros((128 - EXPERTS, length), WIDE)], axis=0)
    logit_grad = jnp.transpose(logit_grad).astype(LOW)
    second_scr[...] = t0[...].astype(WIDE) + t1[...].astype(WIDE) + t2[...].astype(WIDE)
    for s, piece in enumerate(routers):
        columns = piece_columns(mine, s, shard)
        second_scr[:, columns] = second_scr[:, columns] + dot_bt(logit_grad, piece[...])
    resid = resid_ref[...]
    inverse = inverse_rms(resid)
    normed = resid * inverse
    second = second_scr[...]
    gain_grad = jnp.sum(second * normed, axis=0, keepdims=True)
    grad = dz_ref[...].astype(WIDE) + norm_back(second, gain_ref[...], normed, inverse)
    grad_ref[...] = grad
    low_scr[...] = grad.astype(LOW)
    second_scr[:1, :] = gain_grad
    low = low_scr[...]
    for s, piece in enumerate((p0, p1, p2, p3)):
        columns = piece_columns(mine, s, shard)
        attn_grad_ref[:, columns] = dot_bt(low, piece[...]).astype(LOW)
        out_part = dot_t(attn_ref[:, columns], low).astype(LOW)
        router_part = dot_t(h_ref[:length, columns], logit_grad)
        lanes = lax.broadcasted_iota(jnp.int32, router_part.shape, 1)
        small_ref[s] = jnp.where(lanes == EXPERTS, as_column(second_scr[:1, columns]), router_part).astype(LOW)
        for target, rows in shard_parts(((o0,), (o1,), (o2, o3), (o4, o5))[s]):
            target[...] = out_part[rows]


def router_columns(pieces):
    return [
        pl.BlockSpec((p.shape[0], 128), lambda i, at=p.shape[1] // 128 - 1: (0, at), pipeline_mode=ONCE) for p in pieces
    ]


def resid_back_call(mine, resid, gain, dz, terms, gains, h, attn, pieces, shared_pieces):
    length, width = resid.shape
    shard = pieces[0].shape[0]
    whole = lambda shape: pl.BlockSpec(shape, lambda i: (0,) * len(shape), pipeline_mode=ONCE)
    arrays = (resid, gain, dz, *terms, gains, h, attn, *pieces)
    shapes = [shaped(length, width, dtype=WIDE), shaped(length, width), shaped(4, shard, 128)]
    shapes += [shaped(shard, width)] * 2 + [shaped(shard // 2, width)] * 4
    return pl.pallas_call(
        resid_back_kernel,
        grid=(1,),
        in_specs=[pl.BlockSpec(memory_space=pltpu.SMEM)]
        + [whole(a.shape) for a in arrays]
        + router_columns(shared_pieces),
        out_specs=[whole(s.shape) for s in shapes],
        out_shape=shapes,
        scratch_shapes=[pltpu.VMEM((length, width), WIDE), pltpu.VMEM((length, width), LOW)],
        compiler_params=pltpu.CompilerParams(vmem_limit_bytes=34 * MIB),
        cost_estimate=work(
            flops=4 * length * width * (width + EXPERTS), bytes_accessed=length * width * 40, transcendentals=0
        ),
    )(mine, *arrays, *shared_pieces)


def attention_back_kernel(
    mine_ref, q_ref, k_ref, v_ref, do_ref, h_ref, tokens_ref, gain_ref, grad_ref, small_ref, p0, p1, p2, p3, s0, s1, s2, s3,
    seg_row_ref, seg_col_ref, cos_ref, sin_ref, input_ref, o0, o1, o2, o3, o4, o5, qkv_scr, dk_scr, dv_scr, dh_scr,
):
    mine = mine_ref[0]
    length, width = q_ref.shape
    shard = p0.shape[0]
    qkv_width = width + 2 * KEY_VALUE_HEADS * HEAD_DIM
    heads = QUERY_HEADS // KEY_VALUE_HEADS
    key_width = KEY_VALUE_HEADS * HEAD_DIM
    tile = 128
    dk_scr[...] = jnp.zeros_like(dk_scr)
    dv_scr[...] = jnp.zeros_like(dv_scr)
    for start in range(0, length, tile):
        band, reach = slice(start, start + tile), start + tile
        allowed = allowed_pairs(seg_col_ref, seg_row_ref, band, reach, heads)
        cos, sin = cos_ref[band, :], sin_ref[band, :]
        for g in range(KEY_VALUE_HEADS):
            queries = stacked_heads(q_ref, band, g, heads)
            grads = stacked_heads(do_ref, band, g, heads)
            keys = k_ref[:reach, head_slice(g)]
            probs = probabilities(queries, keys, allowed)
            prob_grad = dot_bt(grads, v_ref[:reach, head_slice(g)])
            delta = jnp.sum(probs * prob_grad, axis=-1, keepdims=True)
            score_grad = (probs * (prob_grad - delta) * HEAD_DIM ** (-0.5)).astype(LOW)
            dv_scr[:reach, head_slice(g)] += dot_t(probs.astype(LOW), grads)
            dk_scr[:reach, head_slice(g)] += dot_t(score_grad, queries)
            dq = dot(score_grad, keys)
            for h in range(heads):
                qkv_scr[band, head_slice(g * heads + h)] = turn_back(dq[h * tile : (h + 1) * tile], cos, sin).astype(LOW)
    for g in range(KEY_VALUE_HEADS):
        at = width + g * HEAD_DIM
        qkv_scr[:, at : at + HEAD_DIM] = turn_back(dk_scr[:, head_slice(g)], cos_ref[...], sin_ref[...]).astype(LOW)
    qkv_scr[:, width + key_width :] = dv_scr[...].astype(LOW)
    qkv = qkv_scr[...]
    for s, (piece, shared) in enumerate(zip((p0, p1, p2, p3), (s0, s1, s2, s3))):
        dh_scr[:, piece_columns(mine, s, shard)] = dot_bt(qkv[:, :width], piece[...]) + dot_bt(qkv[:, width:], shared[:, : 2 * key_width])
    stream = tokens_ref[...].astype(WIDE)
    inverse = inverse_rms(stream)
    normed = stream * inverse
    first = dh_scr[...]
    gain_grad = jnp.sum(first * normed, axis=0, keepdims=True)
    input_ref[...] = grad_ref[...] + norm_back(first, gain_ref[...], normed, inverse)
    dh_scr[:1, :] = gain_grad
    for s in range(4):
        columns = piece_columns(mine, s, shard)
        part = dot_t(h_ref[:, columns], qkv).astype(LOW)
        small = small_ref[s].astype(WIDE)
        lanes = lax.broadcasted_iota(jnp.int32, small.shape, 1)
        small = jnp.where(lanes == EXPERTS + 1, as_column(dh_scr[:1, columns]), small).astype(LOW)
        for target, rows in shard_parts(((o0,), (o1,), (o2, o3), (o4, o5))[s]):
            target[:, :qkv_width] = part[rows]
            target[:, qkv_width:] = small[rows]


def attention_back_call(
    mine, q, k, v, do, h, tokens, gain, grad, small, pieces, shared_pieces, seg_row, seg_col, cos, sin
):
    length, width = q.shape
    shard = pieces[0].shape[0]
    qkv_width = width + 2 * KEY_VALUE_HEADS * HEAD_DIM
    key_width = KEY_VALUE_HEADS * HEAD_DIM
    return pl.pallas_call(
        attention_back_kernel,
        in_specs=[pl.BlockSpec(memory_space=pltpu.SMEM)] + [pl.BlockSpec(memory_space=pltpu.VMEM)] * 21,
        out_specs=[pl.BlockSpec(memory_space=pltpu.VMEM)] * 7,
        out_shape=[shaped(length, width, dtype=WIDE)]
        + [shaped(shard, qkv_width + 128)] * 2
        + [shaped(shard * 2 // 3, qkv_width + 128), shaped(shard // 3, qkv_width + 128)] * 2,
        scratch_shapes=[
            pltpu.VMEM((length, qkv_width), LOW),
            pltpu.VMEM((length, key_width), WIDE),
            pltpu.VMEM((length, key_width), WIDE),
            pltpu.VMEM((length, width), WIDE),
        ],
        compiler_params=pltpu.CompilerParams(vmem_limit_bytes=46 * MIB),
        cost_estimate=work(
            flops=4 * length * width * qkv_width + 7 * length * length * width,
            bytes_accessed=length * width * 40,
            transcendentals=QUERY_HEADS * length * length,
        ),
    )(mine, q, k, v, do, h, tokens, gain, grad, small, *pieces, *shared_pieces, seg_row, seg_col, cos, sin)


def spread_kernel(count, token_ref, *refs):
    parts, outs, scratch = refs[2 : -count - 1], refs[-count - 1 : -1], refs[-1]
    for part, rows in shard_parts(parts):
        scratch[rows] = part[...]
    chunk = outs[0].shape[0]
    for j, out in enumerate(outs):
        rows = pl.ds(pl.multiple_of(lax.rem(token_ref[2] + j, count) * chunk, 16), chunk)
        out[...] = sum(term[rows, :].astype(WIDE) for term in (*refs[:2], scratch)).astype(LOW)


def spread_call(token, count, *terms):
    rows, width = terms[0].shape
    whole = lambda shape: pl.BlockSpec(shape, lambda i: (0, 0), pipeline_mode=ONCE)
    return pl.pallas_call(
        functools.partial(spread_kernel, count),
        grid=(1,),
        in_specs=[pl.BlockSpec(memory_space=pltpu.SMEM)] + [whole(t.shape) for t in terms],
        out_specs=[whole((rows // count, width))] * count,
        out_shape=[shaped(rows // count, width)] * count,
        scratch_shapes=[pltpu.VMEM((rows, width), LOW)],
        compiler_params=pltpu.CompilerParams(vmem_limit_bytes=16 * MIB),
        cost_estimate=work(flops=0, bytes_accessed=8 * rows * width, transcendentals=0),
    )(token, *terms)


def assemble_kernel(count, widths, token_ref, *refs):
    chunks, outs = refs[:count], refs[count:]
    chunk = chunks[0].shape[0]
    for j, ref in enumerate(chunks):
        rows = pl.ds(pl.multiple_of(lax.rem(token_ref[2] + j, count) * chunk, 16), chunk)
        values = ref[...].astype(WIDE)
        at = 0
        for width, out in zip(widths, outs):
            out[rows, :] = values[:, at : at + width]
            at += width
        if len(outs) > len(widths):
            outs[-1][rows, :] = values[:, at : at + 128]
    if len(outs) > len(widths):
        router_ref, ffn_ref, attn_ref, scratch = outs[len(widths) :]
        small = jnp.transpose(scratch[...])
        router_ref[...] = small[:EXPERTS]
        ffn_ref[...] = small[EXPERTS]
        attn_ref[...] = small[EXPERTS + 1]


def assemble_call(token, chunks, widths):
    count, (rows, width) = len(chunks), chunks[0].shape
    whole = lambda shape: pl.BlockSpec(shape, lambda i: (0,) * len(shape), pipeline_mode=ONCE)
    small = width > sum(widths)
    shapes = [(count * rows, w) for w in widths]
    shapes += [(EXPERTS, count * rows), (count * rows,), (count * rows,)] if small else []
    return pl.pallas_call(
        functools.partial(assemble_kernel, count, widths),
        grid=(1,),
        in_specs=[pl.BlockSpec(memory_space=pltpu.SMEM)] + [whole((rows, width))] * count,
        out_specs=[whole(shape) for shape in shapes],
        out_shape=[shaped(*shape, dtype=WIDE) for shape in shapes],
        scratch_shapes=[pltpu.VMEM((count * rows, 128), WIDE)] if small else [],
        compiler_params=pltpu.CompilerParams(vmem_limit_bytes=16 * MIB),
        cost_estimate=work(flops=0, bytes_accessed=6 * count * rows * width, transcendentals=0),
    )(token, *chunks)


def per_device_ring(
    tokens,
    segments,
    routes,
    attn_gain,
    ffn_gain,
    w_query,
    key_weight,
    value_weight,
    w_out,
    w_router,
    w_gate,
    w_up,
    w_down,
    cotangent,
):
    length, model_width = tokens.shape
    top_count = routes.shape[1]
    count = lax.axis_size("expert")
    holds = EXPERTS // count
    capacity = max(2, 3 * length * top_count // (2 * EXPERTS))
    slots = -(-capacity // 16) * 16
    shard = model_width // 4
    key_width = KEY_VALUE_HEADS * HEAD_DIM
    half = length // 2
    mine = lax.axis_index("wshard").astype(jnp.int32)
    order = jnp.array(ring_order(count), jnp.int32)
    spot_of = jnp.array([ring_order(count).index(i) for i in range(count)], jnp.int32)
    here = lax.axis_index("expert").astype(jnp.int32)
    spot = spot_of[here]
    token = jnp.stack([mine, here, spot])
    routes_t = routes.T

    cosine, sine = rotary_tables(length, HEAD_DIM)
    cos = jnp.concatenate([cosine, cosine], axis=1)
    sin = jnp.concatenate([-sine, sine], axis=1)
    seg_col = segments.reshape(length, 1)
    gain_one, gain_two = attn_gain[None], ffn_gain[None]

    def pieces_of(own, across, *ready):
        return (own, swap_core(own), across, swap_core(after(across, *ready)))

    dz = {0: cotangent}
    dz[-1], dz[1] = ahead(dz[0], count), behind(dz[0], count)
    query_across = swap_x(w_query)
    query_pieces = pieces_of(w_query, query_across)
    spare = jnp.zeros((shard, 128 - EXPERTS), LOW)
    shared = jnp.concatenate([key_weight, value_weight, w_router, spare], axis=1)
    shared, token, seg_col, cos, sin, routes_t, gain_one, gain_two = lax.optimization_barrier(
        (shared, token, seg_col, cos, sin, routes_t, gain_one, gain_two)
    )
    shared_across = swap_x(after(shared, query_across, dz[-1], dz[1]))
    dz[-2], dz[2] = ahead(dz[-1], count), behind(dz[1], count)
    shared_pieces = pieces_of(shared, shared_across)
    out_across = swap_x(after(w_out, shared_across))

    first_low, query, key, value, attn = attention_call(
        after(token, dz[-2], dz[2]), tokens, gain_one, query_pieces, shared_pieces, segments, seg_col, cos, sin
    )
    out_pieces = pieces_of(w_out, out_across, attn)
    dz[-3], dz[3] = ahead(dz[-2], count), behind(dz[2], count)
    resid, second = project_call(after(token, dz[-3], dz[3]), tokens, attn, out_pieces, shared_pieces, gain_two, routes_t)

    def experts(ready, first, offsets, kept):
        return expert_call(
            after(token, *ready), first, [h[j] for j in offsets], [dz[j] for j in offsets], w_gate, w_up, w_down, kept,
            holds, slots, count,
        )

    h = {0: second}
    h[-1], h[1] = ahead(h[0], count), behind(h[0], count)
    (d_own,), kept = experts((), 6, (0,), None)
    h[-2], h[2] = ahead(after(h[-1], d_own), count), behind(after(h[1], d_own), count)
    (d_l1, d_r1), kept = experts((), 0, (-1, 1), kept)
    h[-3], h[3] = ahead(after(h[-2], d_l1), count), behind(after(h[2], d_l1), count)
    (d_l2, d_r2), kept = experts((), 2, (-2, 2), kept)
    h[4], dz[4] = ahead(after(h[-3], d_l2), count), behind(after(dz[3], d_l2), count)
    (d_l3, d_r3), kept = experts((), 4, (-3, 3), kept)
    (d_far,), (gains, rank, *kept) = experts((), 7, (4,), kept)

    block_of = jnp.array([BLOCK_OFFSETS.index(j if j <= count // 2 else j - count) for j in range(count)], jnp.int32)
    gain_send = gains[block_of[(spot_of - spot) % count]]

    def weight_grads(expert, *ready):
        return wgrad_call(expert, after(token, *ready), kept)

    def over_cores(grads, *ready):
        return swap_core(after(grads[2], *ready))

    both, last = range(2), 2

    def sum_of(grads, got, part):
        return (grads[1], part), (got, part)

    up_sent, down_sent = ahead(d_far, count), behind(d_l3, count)
    grads = [wgrad_call(0, token, kept, True)]
    got = [[swap_core(v) for v in grads[0][2]]]
    grads.append(weight_grads(1, grads[0][0]))
    up, down = sums_call((grads[1][0], *got[0],), (d_r3, up_sent), (d_l2, down_sent))

    up_sent, down_sent = ahead(up, count), behind(down, count)
    got.append(over_cores(grads[1], up))
    halves = [sums_call((up,), *[((grads[0][1], i), got[0][i]) for i in range(3)])]
    across = [[(swap_x(v), None) for v in halves[0][:2]]]
    gain_dense = lax.all_to_all(after(gain_send, up), "expert", split_axis=0, concat_axis=0, tiled=True)
    gain_dense = gain_dense.reshape(EXPERTS, length)
    grads.append(weight_grads(2, *halves[0]))
    up, down = sums_call((gain_dense, grads[2][0], across[0][0][0], across[0][1][0],), (d_r2, up_sent), (d_l1, down_sent))

    up_sent, down_sent = ahead(up, count), behind(down, count)
    got.append(over_cores(grads[2], up))
    halves.append(sums_call((up,), sum_of(grads[1], got[1], both)))
    across_b = swap_x(halves[1][0])
    y = dict(zip(BLOCK_OFFSETS, value_call(after(token, *halves[1]), rank, kept[4], w_down, slots)))
    late = swap_core(after(grads[0][3], up))
    halves[1] += sums_call((y[0],), sum_of(grads[1], got[1], last))
    halves.append(sums_call((y[0],), sum_of(grads[2], got[2], both), sum_of(grads[2], got[2], last)))
    (up,) = sums_call((*halves[2], across_b, down_sent, late, halves[1][1]), (d_r1, up_sent))

    up_sent, y_down = ahead(up, count), behind(after(y[4], up), count)
    across[0].append((swap_x(after(halves[0][2], up)), None))
    across.append([(across_b, 0), (across_b, 1), (swap_x(after(halves[1][1], up)), None)])
    grads.append(weight_grads(3, up))
    (down,) = sums_call(
        (up_sent, across[0][2][0], across[1][2][0], grads[3][0]), (y[-3], y_down)
    )

    y_up, y_down, across_d = ahead(after(y[3], down), count), behind(down, count), swap_x(after(halves[2][0], down))
    grad, attn_grad, small, *out_parts = resid_back_call(
        after(token, down), resid, gain_two, cotangent, (d_own, up_sent, down_sent), gain_dense, second,
        attn, out_pieces, shared_pieces,
    )
    def terms_of(expert, i, *ready):
        other = (late, i) if expert == 0 else (got[expert], 3 + i)
        return [(after(grads[expert][0], *ready) if ready else grads[expert][0], i), other, across[expert][i]]

    def finish(ready, expert, kept_out, parts=range(3)):
        return finish_call(holds, [(i, expert, [terms_of(expert, i, *ready)]) for i in parts], kept_out)

    out_first = [swap_core(v) for v in out_parts[4:]]
    finished = finish((grad,), 0, None)
    *out_half, up, down = sums_call(
        (finished[0], across_d), *zip(out_parts[2:4], out_first), (y[2], y_up), (y[-2], y_down)
    )

    y_up, y_down, out_across = ahead(up, count), behind(down, count), [swap_x(v) for v in out_half]
    out_got = swap_core(after(out_parts[1], up))
    input_grad, *qkv_parts = attention_back_call(
        after(token, up), query, key, value, attn_grad, first_low, tokens, gain_one, grad, small, query_pieces,
        shared_pieces, segments, seg_col, cos, sin,
    )
    up, down = sums_call((input_grad, *out_across, out_got), (y[1], y_up), (y[-1], y_down))

    y_up, y_down = ahead(up, count), behind(down, count)
    qkv_first = [swap_core(after(v, up)) for v in qkv_parts[4:]]
    qkv_half = sums_call((up,), *zip(qkv_parts[2:4], qkv_first))
    qkv_across = [swap_x(qkv_half[0])]
    out_parts = spread_call(after(token, *qkv_half), count, out_parts[0], out_got, *out_across)
    finished = finish(qkv_half, 1, finished)
    qkv_got = swap_core(after(qkv_parts[1], qkv_across[0]))
    got.append(over_cores(grads[3], qkv_half[0]))
    (half_e,) = sums_call((finished[0],), sum_of(grads[3], got[3], range(3)))
    across.append([(across_d, 0), (across_d, 1)])
    finished = finish((half_e,), 2, finished, both)
    y_own = after(y[0], qkv_across[0], out_parts[0], finished[0])
    mixed = (resid + sum(t.astype(WIDE) for t in (y_own, y_up, y_down))).astype(LOW)
    qkv_across.append(swap_x(after(qkv_half[1], qkv_across[0])))

    def sum_step(parts, up, down, step):
        up = add_low(parts[step], ahead(up, count))
        down = behind(down, count)
        return up, add_low(parts[count + 1 - step], down) if step > 1 else down

    def copy_step(up, down):
        return up + [ahead(up[-1], count)], down + [behind(down[-1], count)]

    out_up, out_down = after(out_parts[4], mixed), after(out_parts[5], mixed)
    for step in (3, 2, 1):
        out_up, out_down = sum_step(out_parts, out_up, out_down, step)
        if step == 2:
            out_up = after(out_up, qkv_across[1])
    out_own = add_low(out_parts[0], ahead(out_up, count), out_down)
    across_e = [swap_x(after(halves[2][1], qkv_across[1])), swap_x(after(half_e, qkv_across[1]))]
    qkv_parts = spread_call(after(token, out_own), count, qkv_parts[0], qkv_got, *qkv_across)
    across[2].append((across_e[0], None))
    across.append([(across_e[1], i) for i in range(3)])
    out_ups, out_downs = [after(out_own, qkv_parts[0])], [after(out_own, qkv_parts[0])]
    qkv_up, qkv_down = qkv_parts[4], qkv_parts[5]
    for step in (3, 2, 1):
        out_ups, out_downs = copy_step(out_ups, out_downs)
        qkv_up, qkv_down = sum_step(qkv_parts, qkv_up, qkv_down, step)
        qkv_up = after(qkv_up, out_ups[-1], out_downs[-1])
    out_ups.append(ahead(out_ups[-1], count))
    qkv_own = add_low(qkv_parts[0], ahead(qkv_up, count), qkv_down)
    qkv_ups, qkv_downs = [qkv_own], [qkv_own]
    for step in (3, 2, 1):
        qkv_ups, qkv_downs = copy_step(qkv_ups, qkv_downs)
        if step == 3:
            qkv_ups[-1] = after(qkv_ups[-1], out_ups[-1])
    (out_sum,) = assemble_call(after(token, qkv_ups[2]), out_downs + out_ups[:0:-1], (model_width,))
    qkv_ups.append(ahead(after(qkv_ups[-1], out_sum, across_e[1]), count))
    last_rows = [terms_of(2, 2, qkv_ups[3]), terms_of(3, 2)]
    finished = finish_call(
        holds, [(0, 3, [terms_of(3, 0, qkv_ups[3])]), (1, 3, [terms_of(3, 1)]), (2, 2, last_rows)], finished
    )
    query_sum, key_sum, value_sum, router_sum, ffn_gain_sum, attn_gain_sum = assemble_call(
        after(token, finished[0]), qkv_downs + qkv_ups[:0:-1], (model_width, key_width, key_width)
    )
    gate_shard, up_shard, down_shard = finished
    return (
        mixed,
        input_grad,
        attn_gain_sum,
        ffn_gain_sum,
        query_sum,
        key_sum,
        value_sum,
        out_sum,
        router_sum.T,
        gate_shard,
        up_shard,
        down_shard,
    )


def solution(mesh):
    ring = mesh.shape["expert"] == len(BLOCK_OFFSETS) and mesh.shape["wshard"] == 4
    body = per_device_ring if ring else per_device_exchange
    in_specs = (
        P(("expert", "wshard"), None),
        P(("expert", "wshard"), None),
        P(("expert", "wshard"), None),
        P(),
        P(),
        P("wshard", None),
        P("wshard", None),
        P("wshard", None),
        P("wshard", None),
        P("wshard", None),
        P(None, "expert"),
        P(None, "expert"),
        P("expert", None),
        P(("expert", "wshard"), None),
    )
    out_specs = (
        P(("expert", "wshard"), None),
        P(("expert", "wshard"), None),
        P("wshard"),
        P("wshard"),
        P("wshard", None),
        P("wshard", None),
        P("wshard", None),
        P("wshard", None),
        P("wshard", None),
        P("wshard", "expert"),
        P("wshard", "expert"),
        P("expert", "wshard"),
    )
    return jax.shard_map(
        body, mesh=mesh, in_specs=in_specs, out_specs=out_specs, check_vma=False
    )
```

```python
import functools

import jax
import jax.numpy as jnp
from jax import lax
from jax.experimental import pallas as pl
from jax.experimental.pallas import tpu as pltpu
from jax.sharding import PartitionSpec as P

QUERY_HEADS = 12
KEY_VALUE_HEADS = 2
HEAD_DIM = 128
EXPERTS = 32
TOP = 4


EPS = 1e-06
ROPE_BASE = 10000.0
NEG = -1e30
LOW = jnp.bfloat16
WIDE = jnp.float32
MIB = 1024 * 1024
ONCE = pl.Buffered(buffer_count=1)
def norm_forward(values, gain):
    inverse = lax.rsqrt(jnp.mean(values * values, axis=-1) + EPS)
    normed = values * inverse[:, None]
    return (normed * gain, normed, inverse)


def norm_backward(grad, gain, normed, inverse):
    gain_grad = jnp.sum(grad * normed, axis=0)
    scaled = grad * gain
    centred = scaled - normed * jnp.mean(scaled * normed, axis=-1, keepdims=True)
    return (inverse[:, None] * centred, gain_grad)


def rotary_tables(seq_length, head_size):
    half_size = head_size // 2
    frequency = ROPE_BASE ** (-(jnp.arange(half_size, dtype=jnp.float32) * 2.0 / head_size))
    angles = jnp.arange(seq_length, dtype=jnp.float32)[:, None] * frequency[None, :]
    return (jnp.cos(angles), jnp.sin(angles))


def apply_rotation(values, cosine_lookup, sine_lookup):
    half_size = values.shape[-1] // 2
    first_half = values[..., :half_size]
    second_half = values[..., half_size:]
    cos_part = cosine_lookup[:, None, :]
    sin_part = sine_lookup[:, None, :]
    return jnp.concatenate(
        [
            first_half * cos_part - second_half * sin_part,
            second_half * cos_part + first_half * sin_part,
        ],
        axis=-1,
    )


def reverse_rotation(values, cosine_lookup, sine_lookup):
    half_size = values.shape[-1] // 2
    first_half = values[..., :half_size]
    second_half = values[..., half_size:]
    cos_part = cosine_lookup[:, None, :]
    sin_part = sine_lookup[:, None, :]
    return jnp.concatenate(
        [
            first_half * cos_part + second_half * sin_part,
            second_half * cos_part - first_half * sin_part,
        ],
        axis=-1,
    )


def per_device_exchange(
    tokens,
    segments,
    routes,
    attn_gain,
    ffn_gain,
    w_query,
    key_weight,
    value_weight,
    w_out,
    w_router,
    w_gate,
    w_up,
    w_down,
    cotangent,
):
    lower_dtype = jnp.bfloat16
    wide_type = jnp.float32
    sequence_length, model_width = tokens.shape
    top_count = routes.shape[1]
    axis_count = lax.axis_size("expert")
    owners = max(1, axis_count // EXPERTS)
    holds = max(1, EXPERTS // axis_count)
    groups = EXPERTS // holds
    capacity = max(2, 3 * sequence_length * top_count // (2 * EXPERTS))
    hidden_dev = w_gate.shape[1] // holds
    query_group_width = QUERY_HEADS // KEY_VALUE_HEADS
    score_scale = HEAD_DIM ** (-0.5)
    pair_count = sequence_length * top_count
    query_full, key_full, value_full, out_full, router_full = (
        lax.all_gather(w_query, "wshard", axis=0, tiled=True),
        lax.all_gather(key_weight, "wshard", axis=0, tiled=True),
        lax.all_gather(value_weight, "wshard", axis=0, tiled=True),
        lax.all_gather(w_out, "wshard", axis=0, tiled=True),
        lax.all_gather(w_router, "wshard", axis=0, tiled=True),
    )
    stream = tokens.astype(wide_type)
    first_norm, first_normed, first_inverse = norm_forward(stream, attn_gain)
    first_low = first_norm.astype(lower_dtype)
    cosine_lookup, sine_lookup = rotary_tables(sequence_length, HEAD_DIM)
    query_pre = jnp.dot(first_low, query_full, preferred_element_type=wide_type).reshape(
        sequence_length, QUERY_HEADS, HEAD_DIM
    )
    key_unrotated = jnp.dot(first_low, key_full, preferred_element_type=wide_type).reshape(
        sequence_length, KEY_VALUE_HEADS, HEAD_DIM
    )
    query_rotated = (
        apply_rotation(query_pre, cosine_lookup, sine_lookup)
        .astype(lower_dtype)
        .reshape(sequence_length, KEY_VALUE_HEADS, query_group_width, HEAD_DIM)
    )
    key_rotated = apply_rotation(key_unrotated, cosine_lookup, sine_lookup).astype(lower_dtype)
    value_lowered = (
        jnp.dot(first_low, value_full, preferred_element_type=wide_type)
        .astype(lower_dtype)
        .reshape(sequence_length, KEY_VALUE_HEADS, HEAD_DIM)
    )
    positions = jnp.arange(sequence_length)
    offset = positions[:, None] - positions[None, :]
    segment_row = segments[0]
    allowed = (segment_row[:, None] == segment_row[None, :]) & (offset >= 0)
    raw_scores = jnp.einsum(
        "qagd,kad->agqk", query_rotated, key_rotated, preferred_element_type=wide_type
    )
    scores = jnp.where(allowed, raw_scores * score_scale, NEG)
    score_top = jnp.max(scores, axis=-1, keepdims=True)
    expo_terms = jnp.exp(scores - score_top)
    expo_total = jnp.sum(expo_terms, axis=-1, keepdims=True)
    log_total = score_top + jnp.log(expo_total)
    probs_low = (expo_terms / expo_total).astype(lower_dtype)
    attn_low = (
        jnp.einsum("agqk,kad->qagd", probs_low, value_lowered, preferred_element_type=wide_type)
        .astype(lower_dtype)
        .reshape(sequence_length, QUERY_HEADS * HEAD_DIM)
    )
    resid = stream + jnp.dot(attn_low, out_full, preferred_element_type=wide_type)
    second_norm, second_normed, second_inverse = norm_forward(resid, ffn_gain)
    second_low = second_norm.astype(lower_dtype)
    logits = jnp.dot(second_low, router_full, preferred_element_type=wide_type)
    choose = (routes[:, :, None] == jnp.arange(EXPERTS)[None, None, :]).astype(wide_type)
    selected = jnp.sum(choose * logits[:, None, :], axis=-1)
    gate_probs = jax.nn.softmax(selected, axis=-1)
    flat_routes = routes.reshape(pair_count)
    one_hot = (flat_routes[:, None] == jnp.arange(EXPERTS)[None, :]).astype(jnp.int32)
    slot_rank = jnp.sum((jnp.cumsum(one_hot, axis=0) - 1) * one_hot, axis=1)
    slot_index = (flat_routes // holds * capacity + slot_rank) * holds + flat_routes % holds
    slot_pair = (
        jnp.full((EXPERTS * capacity,), pair_count, jnp.int32)
        .at[slot_index]
        .set(jnp.arange(pair_count, dtype=jnp.int32))
    )
    second_ext = jnp.concatenate([second_low, jnp.zeros((1, model_width), lower_dtype)], axis=0)
    send_rows = jnp.repeat(
        second_ext[slot_pair // top_count].reshape(groups, capacity, holds, model_width),
        owners,
        axis=0,
    )
    gate_local = w_gate.reshape(model_width, holds, hidden_dev)
    up_local = w_up.reshape(model_width, holds, hidden_dev)
    down_local = w_down.reshape(holds, hidden_dev, model_width)

    def owner_total(values):
        summed = jnp.sum(
            values.astype(wide_type).reshape(groups, owners, capacity, holds, model_width), axis=1
        )
        return summed.reshape(EXPERTS * capacity, model_width)

    received = lax.all_to_all(send_rows, "expert", split_axis=0, concat_axis=0, tiled=True)
    gate_pre = jnp.einsum("scld,dlf->sclf", received, gate_local, preferred_element_type=wide_type)
    up_pre = jnp.einsum("scld,dlf->sclf", received, up_local, preferred_element_type=wide_type)
    hidden = (jax.nn.silu(gate_pre) * up_pre).astype(lower_dtype)
    partial_value = jnp.einsum(
        "sclf,lfd->scld", hidden, down_local, preferred_element_type=wide_type
    ).astype(lower_dtype)
    returned = lax.all_to_all(partial_value, "expert", split_axis=0, concat_axis=0, tiled=True)
    expert_wide = owner_total(returned)[slot_index].reshape(sequence_length, top_count, model_width)
    mixed = (resid + jnp.sum(gate_probs[:, :, None] * expert_wide, axis=1)).astype(lower_dtype)
    upstream = cotangent.astype(wide_type)
    query_back, key_back, value_back, out_back, router_back = (
        lax.all_gather(w_query, "wshard", axis=0, tiled=True),
        lax.all_gather(key_weight, "wshard", axis=0, tiled=True),
        lax.all_gather(value_weight, "wshard", axis=0, tiled=True),
        lax.all_gather(w_out, "wshard", axis=0, tiled=True),
        lax.all_gather(w_router, "wshard", axis=0, tiled=True),
    )
    gate_grad = jnp.sum(expert_wide * upstream[:, None, :], axis=-1)
    sel_grad = gate_probs * (gate_grad - jnp.sum(gate_probs * gate_grad, axis=-1, keepdims=True))
    logit_grad = jnp.sum(choose * sel_grad[:, :, None], axis=1).astype(lower_dtype)
    pair_grad = (
        (gate_probs[:, :, None] * upstream[:, None, :])
        .astype(lower_dtype)
        .reshape(pair_count, model_width)
    )
    pair_ext = jnp.concatenate([pair_grad, jnp.zeros((1, model_width), lower_dtype)], axis=0)
    grad_send = jnp.repeat(
        pair_ext[slot_pair].reshape(groups, capacity, holds, model_width), owners, axis=0
    )
    grad_recv, rows_recv = (
        lax.all_to_all(grad_send, "expert", split_axis=0, concat_axis=0, tiled=True),
        lax.all_to_all(send_rows, "expert", split_axis=0, concat_axis=0, tiled=True),
    )
    gate_pre = jnp.einsum("scld,dlf->sclf", rows_recv, gate_local, preferred_element_type=wide_type)
    up_pre = jnp.einsum("scld,dlf->sclf", rows_recv, up_local, preferred_element_type=wide_type)
    sigmoid_gate = jax.nn.sigmoid(gate_pre)
    silu_gate = gate_pre * sigmoid_gate
    hidden = (silu_gate * up_pre).astype(lower_dtype)
    hidden_grad = jnp.einsum(
        "scld,lfd->sclf", grad_recv, down_local, preferred_element_type=wide_type
    )
    gate_pre_grad = (
        hidden_grad * up_pre * sigmoid_gate * (1.0 + gate_pre * (1.0 - sigmoid_gate))
    ).astype(lower_dtype)
    up_pre_grad = (hidden_grad * silu_gate).astype(lower_dtype)
    row_grad = (
        jnp.einsum("sclf,dlf->scld", gate_pre_grad, gate_local, preferred_element_type=wide_type)
        + jnp.einsum("sclf,dlf->scld", up_pre_grad, up_local, preferred_element_type=wide_type)
    ).astype(lower_dtype)
    returned_grad = lax.all_to_all(row_grad, "expert", split_axis=0, concat_axis=0, tiled=True)
    gate_wgrad = jnp.einsum(
        "scld,sclf->dlf", rows_recv, gate_pre_grad, preferred_element_type=wide_type
    ).reshape(model_width, holds * hidden_dev)
    up_wgrad = jnp.einsum(
        "scld,sclf->dlf", rows_recv, up_pre_grad, preferred_element_type=wide_type
    ).reshape(model_width, holds * hidden_dev)
    down_wgrad = jnp.einsum(
        "sclf,scld->lfd", hidden, grad_recv, preferred_element_type=wide_type
    ).reshape(holds * hidden_dev, model_width)
    gate_shard, up_shard, down_shard = (
        lax.psum_scatter(
            gate_wgrad.astype(jnp.bfloat16), "wshard", scatter_dimension=0, tiled=True
        ).astype(jnp.float32),
        lax.psum_scatter(
            up_wgrad.astype(jnp.bfloat16), "wshard", scatter_dimension=0, tiled=True
        ).astype(jnp.float32),
        lax.psum_scatter(
            down_wgrad.astype(jnp.bfloat16), "wshard", scatter_dimension=1, tiled=True
        ).astype(jnp.float32),
    )
    token_grad = owner_total(returned_grad)[slot_index].reshape(
        sequence_length, top_count, model_width
    )
    second_grad = jnp.sum(token_grad, axis=1) + jnp.dot(
        logit_grad, router_back.T, preferred_element_type=wide_type
    )
    router_wgrad = jnp.einsum("td,te->de", second_low, logit_grad, preferred_element_type=wide_type)
    resid_part, ffn_gain_grad = norm_backward(second_grad, ffn_gain, second_normed, second_inverse)
    resid_grad = upstream + resid_part
    resid_low = resid_grad.astype(lower_dtype)
    out_wgrad = jnp.einsum("tc,td->cd", attn_low, resid_low, preferred_element_type=wide_type)
    attn_grad = (
        jnp.dot(resid_low, out_back.T, preferred_element_type=wide_type)
        .astype(lower_dtype)
        .reshape(sequence_length, KEY_VALUE_HEADS, query_group_width, HEAD_DIM)
    )
    raw_again = jnp.einsum(
        "qagd,kad->agqk", query_rotated, key_rotated, preferred_element_type=wide_type
    )
    scores_again = jnp.where(allowed, raw_again * score_scale, NEG)
    probs_again = jnp.exp(scores_again - log_total)
    prob_grad = jnp.einsum(
        "qagd,kad->agqk", attn_grad, value_lowered, preferred_element_type=wide_type
    )
    row_delta = jnp.sum(probs_again * prob_grad, axis=-1, keepdims=True)
    score_grad = (probs_again * (prob_grad - row_delta) * score_scale).astype(lower_dtype)
    value_grad = (
        jnp.einsum("agqk,qagd->kad", probs_low, attn_grad, preferred_element_type=wide_type)
        .astype(lower_dtype)
        .reshape(sequence_length, KEY_VALUE_HEADS * HEAD_DIM)
    )
    query_rot_grad = jnp.einsum(
        "agqk,kad->qagd", score_grad, key_rotated, preferred_element_type=wide_type
    ).reshape(sequence_length, QUERY_HEADS, HEAD_DIM)
    key_rotated_gradient = jnp.einsum(
        "agqk,qagd->kad", score_grad, query_rotated, preferred_element_type=wide_type
    )
    query_grad = (
        reverse_rotation(query_rot_grad, cosine_lookup, sine_lookup)
        .astype(lower_dtype)
        .reshape(sequence_length, QUERY_HEADS * HEAD_DIM)
    )
    key_grad = (
        reverse_rotation(key_rotated_gradient, cosine_lookup, sine_lookup)
        .astype(lower_dtype)
        .reshape(sequence_length, KEY_VALUE_HEADS * HEAD_DIM)
    )
    query_wgrad = jnp.einsum("td,tc->dc", first_low, query_grad, preferred_element_type=wide_type)
    key_wgrad = jnp.einsum("td,tc->dc", first_low, key_grad, preferred_element_type=wide_type)
    value_wgrad = jnp.einsum("td,tc->dc", first_low, value_grad, preferred_element_type=wide_type)
    first_grad = (
        jnp.dot(query_grad, query_back.T, preferred_element_type=wide_type)
        + jnp.dot(key_grad, key_back.T, preferred_element_type=wide_type)
        + jnp.dot(value_grad, value_back.T, preferred_element_type=wide_type)
    )
    stream_part, attn_gain_grad = norm_backward(first_grad, attn_gain, first_normed, first_inverse)
    input_grad = resid_grad + stream_part
    query_part, key_part, value_part, out_part, router_part, attn_gain_part, ffn_gain_part = (
        lax.psum_scatter(
            query_wgrad.astype(jnp.bfloat16), "wshard", scatter_dimension=0, tiled=True
        ).astype(jnp.float32),
        lax.psum_scatter(
            key_wgrad.astype(jnp.bfloat16), "wshard", scatter_dimension=0, tiled=True
        ).astype(jnp.float32),
        lax.psum_scatter(
            value_wgrad.astype(jnp.bfloat16), "wshard", scatter_dimension=0, tiled=True
        ).astype(jnp.float32),
        lax.psum_scatter(
            out_wgrad.astype(jnp.bfloat16), "wshard", scatter_dimension=0, tiled=True
        ).astype(jnp.float32),
        lax.psum_scatter(
            router_wgrad.astype(jnp.bfloat16), "wshard", scatter_dimension=0, tiled=True
        ).astype(jnp.float32),
        lax.psum_scatter(
            attn_gain_grad.astype(jnp.bfloat16), "wshard", scatter_dimension=0, tiled=True
        ).astype(jnp.float32),
        lax.psum_scatter(
            ffn_gain_grad.astype(jnp.bfloat16), "wshard", scatter_dimension=0, tiled=True
        ).astype(jnp.float32),
    )
    query_sum, key_sum, value_sum, out_sum, router_sum, attn_gain_sum, ffn_gain_sum = lax.psum(
        (query_part, key_part, value_part, out_part, router_part, attn_gain_part, ffn_gain_part),
        "expert",
    )
    return (
        mixed,
        input_grad,
        attn_gain_sum,
        ffn_gain_sum,
        query_sum,
        key_sum,
        value_sum,
        out_sum,
        router_sum,
        gate_shard,
        up_shard,
        down_shard,
    )


BLOCK_OFFSETS = (-1, 1, -2, 2, -3, 3, 0, 4)


def ring_order(count):
    return [0] + list(range(1, count, 2)) + list(range(count - 2, 0, -2))


def shifted(value, step, count):
    order = ring_order(count)
    return lax.ppermute(value, "expert", [(order[i], order[(i + step) % count]) for i in range(count)])


def ahead(value, count):
    return shifted(value, 1, count)


def behind(value, count):
    return shifted(value, -1, count)


def swap_core(value):
    size = lax.axis_size("wshard")
    return lax.ppermute(value, "wshard", [(i, i ^ 1) for i in range(size)])


def swap_x(value):
    size = lax.axis_size("wshard")
    return lax.ppermute(value, "wshard", [(i, i ^ 2) for i in range(size)])


def work(flops, bytes_accessed, transcendentals):
    scale = 8
    return pl.CostEstimate(
        flops=flops // scale, bytes_accessed=bytes_accessed // scale, transcendentals=transcendentals // scale
    )


def add_low(*terms):
    return sum(term.astype(WIDE) for term in terms).astype(LOW)


def after(value, *others):
    return lax.optimization_barrier((value, *others))[0]


def places(rank_row, slots):
    rows = lax.broadcasted_iota(jnp.int32, (slots, rank_row.shape[-1]), 0)
    return rank_row == rows


def expert_ranks(routes, holds):
    tokens = routes.shape[1]
    names = [jnp.sum((routes == l).astype(WIDE), axis=0, keepdims=True) for l in range(holds)]
    names = jnp.concatenate(names + [jnp.zeros((16 - holds, tokens), WIDE)], axis=0)
    rows = lax.broadcasted_iota(jnp.int32, (tokens, tokens), 0)
    columns = lax.broadcasted_iota(jnp.int32, (tokens, tokens), 1)
    before = dot(names.astype(LOW), (rows <= columns).astype(WIDE).astype(LOW))
    return jnp.where(names > 0.0, before - 1.0, -1.0)[:holds].astype(jnp.int32)


def pack_routing(gates, routes):
    high = gates.astype(LOW).astype(WIDE)
    rows = [high, gates - high, routes.astype(WIDE)]
    spare = 16 - 3 * gates.shape[0]
    return jnp.concatenate(rows + [jnp.zeros((spare, gates.shape[1]), WIDE)], axis=0).astype(LOW)


def unpack_routing(packed):
    top_count = TOP
    packed = packed.astype(WIDE)
    return packed[:top_count] + packed[top_count : 2 * top_count], packed[2 * top_count : 3 * top_count]


def dot_t(a, b):
    return lax.dot_general(a, b, (((0,), (0,)), ((), ())), preferred_element_type=WIDE)


def dot_bt(a, b):
    return lax.dot_general(a, b, (((1,), (1,)), ((), ())), preferred_element_type=WIDE)


def dot(a, b):
    return jnp.dot(a, b, preferred_element_type=WIDE)


def expert_kernel(count, slots, aliased, *refs):
    token_ref = refs[0]
    h_refs, dz_refs = refs[1 : 1 + count], refs[1 + count : 1 + 2 * count]
    wg_ref, wu_ref, wd_ref = refs[1 + 2 * count : 4 + 2 * count]
    rest = refs[4 + 2 * count + (7 if aliased else 0) :]
    d_refs = rest[:count]
    gain_ref, rank_ref, rows_out, dz_out, gg_out, ug_out, hid_out = rest[count : count + 7]
    place_scr, back_scr, gate_scr, wg_scr, wu_scr, wd_scr, sems = rest[count + 7 :]
    e = pl.program_id(0)
    holds, tokens = rank_ref.shape[1:]
    hidden_width = wd_scr.shape[1]

    def weights(expert, slot):
        band = pl.ds(pl.multiple_of(expert * hidden_width, hidden_width), hidden_width)
        return [
            pltpu.make_async_copy(source, target.at[slot], sems.at[slot, i])
            for i, (source, target) in enumerate(
                ((wg_ref.at[:, band], wg_scr), (wu_ref.at[:, band], wu_scr), (wd_ref.at[band, :], wd_scr))
            )
        ]

    slot = lax.rem(e, 2)

    @pl.when(e == 0)
    def _():
        for copy in weights(0, 0):
            copy.start()

    @pl.when(e + 1 < holds)
    def _():
        for copy in weights(e + 1, 1 - slot):
            copy.start()

    here = pl.ds(pl.multiple_of(e * slots, slots), slots)
    @pl.when(e == 0)
    def _():
        for b, (h_ref, dz_ref) in enumerate(zip(h_refs, dz_refs)):
            gates, routes = unpack_routing(h_ref[tokens : tokens + 16, :tokens])
            routes = routes - (token_ref[1] * holds).astype(WIDE)
            ranks = expert_ranks(routes, holds)
            rank_ref[b] = ranks
            for l in range(holds):
                band = slice(l * slots, (l + 1) * slots)
                spot = places(ranks[l : l + 1], slots).astype(WIDE)
                named = jnp.where(routes == l, gates, 0.0)
                gate_scr[b, band, :] = jnp.broadcast_to(
                    jnp.sum(spot * jnp.sum(named, axis=0, keepdims=True), axis=1, keepdims=True), (slots, 128)
                )
                place_scr[b, band, :] = spot.astype(LOW)
            for source, target in ((h_ref, rows_out), (dz_ref, dz_out)):
                taken = dot(place_scr[b], source[:tokens]).astype(LOW)
                for l in range(holds):
                    target[l, b * slots : (b + 1) * slots, :] = taken[l * slots : (l + 1) * slots]

    gate = jnp.concatenate([gate_scr[b, here, :] for b in range(count)], axis=0)[:, :1]
    rows = rows_out[e]
    for copy in weights(e, slot):
        copy.wait()
    gate_pre = dot(rows, wg_scr[slot])
    up_pre = dot(rows, wu_scr[slot])
    sig = jax.nn.sigmoid(gate_pre)
    silu = gate_pre * sig
    hidden = (silu * up_pre).astype(LOW).astype(WIDE)
    back = dot_bt(dz_out[e], wd_scr[slot])
    gains = jnp.sum(back * hidden, axis=1, keepdims=True)
    back = back * gate
    gate_grad = (back * (up_pre * sig * (1.0 + gate_pre * (1.0 - sig)))).astype(LOW)
    up_grad = (back * silu).astype(LOW)
    gg_out[0] = gate_grad
    ug_out[0] = up_grad
    hid_out[0] = (hidden * gate).astype(LOW)
    row_grad = (dot_bt(gate_grad, wg_scr[slot]) + dot_bt(up_grad, wu_scr[slot])).astype(LOW)
    for b in range(count):
        band = slice(b * slots, (b + 1) * slots)
        back_scr[b, here, :] = row_grad[band]
        spot = place_scr[b, here, :].astype(WIDE)
        gain_ref[b, pl.ds(e, 1), :] = jnp.sum(spot * gains[band], axis=0, keepdims=True)

    @pl.when(e == pl.num_programs(0) - 1)
    def _():
        for b in range(count):
            d_refs[b][...] = dot_t(place_scr[b], back_scr[b]).astype(LOW)


def expert_call(token, first, blocks, dz_blocks, w_gate, w_up, w_down, kept, holds, slots, total):
    count = len(blocks)
    tokens, width = dz_blocks[0].shape
    hidden = w_gate.shape[1] // holds
    whole = lambda *shape: pl.BlockSpec(shape, lambda e: (0,) * len(shape))
    once = lambda *shape: pl.BlockSpec(shape, lambda e: (0,) * len(shape), pipeline_mode=pl.Buffered(buffer_count=1))
    aliased = kept is not None
    in_specs = (
        [pl.BlockSpec(memory_space=pltpu.SMEM)]
        + [once(*b.shape) for b in (*blocks, *dz_blocks)]
        + [pl.BlockSpec(memory_space=pl.ANY)] * 3
    )
    aliases = {len(in_specs) + i: count + i for i in range(7)} if aliased else {}
    out = pl.pallas_call(
        functools.partial(expert_kernel, count, slots, aliased),
        grid=(holds,),
        in_specs=in_specs + ([pl.BlockSpec(memory_space=pl.ANY)] * 7 if aliased else []),
        out_specs=[whole(tokens, width)] * count
        + [pl.BlockSpec((count, holds, tokens), lambda e: (first // count, 0, 0))] * 2
        + [pl.BlockSpec((holds, count * slots, width), lambda e: (0, first // count, 0))] * 2
        + [pl.BlockSpec((1, count * slots, hidden), lambda e: (e, first // count, 0))] * 3,
        out_shape=[shaped(tokens, width)] * count
        + [shaped(total, holds, tokens, dtype=WIDE), shaped(total, holds, tokens, dtype=jnp.int32)]
        + [shaped(holds, total * slots, width)] * 2
        + [shaped(holds, total * slots, hidden)] * 3,
        scratch_shapes=[
            pltpu.VMEM((count, holds * slots, tokens), LOW),
            pltpu.VMEM((count, holds * slots, width), LOW),
            pltpu.VMEM((count, holds * slots, 128), WIDE),
            pltpu.VMEM((2, width, hidden), LOW),
            pltpu.VMEM((2, width, hidden), LOW),
            pltpu.VMEM((2, hidden, width), LOW),
            pltpu.SemaphoreType.DMA((2, 3)),
        ],
        input_output_aliases=aliases,
        compiler_params=pltpu.CompilerParams(vmem_limit_bytes=60 * MIB),
        cost_estimate=work(
            flops=2 * holds * count * slots * width * (5 * hidden + 3 * tokens),
            bytes_accessed=3 * holds * width * hidden * 2
            + count * tokens * width * 6
            + holds * count * slots * (2 * width + 3 * hidden) * 2,
            transcendentals=holds * count * slots * hidden,
        ),
    )(token, *blocks, *dz_blocks, w_gate, w_up, w_down, *(kept if aliased else ()))
    return out[:count], tuple(out[count:])


def value_kernel(slots, _, rank_ref, hid_ref, wd_ref, *refs):
    total, holds, tokens = rank_ref.shape
    y_refs, (value_scr, place_scr) = refs[:total], refs[total:]
    e = pl.program_id(0)
    here = pl.ds(pl.multiple_of(e * slots, slots), slots)
    value = dot(hid_ref[0], wd_ref[...]).astype(LOW)
    for b in range(total):
        value_scr[b, here, :] = value[b * slots : (b + 1) * slots]

    @pl.when(e == pl.num_programs(0) - 1)
    def _():
        for b in range(total):
            for l in range(holds):
                spot = places(rank_ref[b, l : l + 1, :], slots)
                place_scr[l * slots : (l + 1) * slots, :] = spot.astype(WIDE).astype(LOW)
            y_refs[b][...] = dot_t(place_scr[...], value_scr[b]).astype(LOW)


def value_call(token, rank, hidden_rows, w_down, slots):
    total, holds, tokens = rank.shape
    width = w_down.shape[1]
    hidden = hidden_rows.shape[2]
    whole = lambda *shape: pl.BlockSpec(shape, lambda e: (0,) * len(shape))
    out = pl.pallas_call(
        functools.partial(value_kernel, slots),
        grid=(holds,),
        in_specs=[
            pl.BlockSpec(memory_space=pltpu.SMEM),
            whole(*rank.shape),
            pl.BlockSpec((1, total * slots, hidden), lambda e: (e, 0, 0)),
            pl.BlockSpec((hidden, width), lambda e: (e, 0)),
        ],
        out_specs=[whole(tokens, width)] * total,
        out_shape=[shaped(tokens, width)] * total,
        scratch_shapes=[pltpu.VMEM((total, holds * slots, width), LOW), pltpu.VMEM((holds * slots, tokens), LOW)],
        compiler_params=pltpu.CompilerParams(vmem_limit_bytes=60 * MIB),
        cost_estimate=work(
            flops=2 * total * holds * slots * width * (hidden + tokens),
            bytes_accessed=2 * (holds * hidden * (width + total * slots) + total * tokens * width),
            transcendentals=0,
        ),
    )(token, rank, hidden_rows, w_down)
    return out


def wgrad_kernel(apart, place_ref, rows_ref, dz_ref, gg_ref, ug_ref, hid_ref, *outs):
    step = pl.program_id(0)
    shard = outs[0].shape[1]
    columns = pl.ds(pl.multiple_of(jnp.bitwise_xor(place_ref[0], step) * shard, 128), shard)
    rows, grads = rows_ref[0, :, columns], dz_ref[0, :, columns]
    parts = [dot_t(rows, gg_ref[0]), dot_t(rows, ug_ref[0]), dot_t(grads, hid_ref[0])]
    parts = [part.astype(LOW) for part in parts]
    for s in range(4):

        @pl.when(step == s)
        def _():
            for i, part in enumerate(parts):
                if s == 3 and apart:
                    outs[3 + i][...] = part
                elif s % 2 and not apart:
                    outs[2][3 - 3 * (s // 2) + i] = part
                else:
                    outs[s if apart else s // 2][i] = part


def wgrad_call(expert, place, kept, apart=False):
    _, count, width = kept[0].shape
    hidden = kept[2].shape[2]
    shard = width // 4
    row_spec = lambda d: pl.BlockSpec((1, count, d), lambda s: (expert, 0, 0), pipeline_mode=pl.Buffered(buffer_count=1))
    shapes = [(3, shard, hidden)] * 3 + [(shard, hidden)] * 3 if apart else [(3, shard, hidden)] * 2 + [(6, shard, hidden)]
    out = pl.pallas_call(
        functools.partial(wgrad_kernel, apart),
        grid=(4,),
        in_specs=[pl.BlockSpec(memory_space=pltpu.SMEM), row_spec(width), row_spec(width)] + [row_spec(hidden)] * 3,
        out_specs=[pl.BlockSpec(shape, lambda s, zeros=(0,) * len(shape): zeros) for shape in shapes],
        out_shape=[shaped(*shape) for shape in shapes],
        compiler_params=pltpu.CompilerParams(vmem_limit_bytes=60 * MIB),
        cost_estimate=work(
            flops=2 * count * width * 3 * hidden,
            bytes_accessed=2 * (count * (2 * width + 3 * hidden) + 3 * width * hidden),
            transcendentals=0,
        ),
    )(place, *kept)
    return (out[0], out[2], out[3:], out[1]) if apart else out


def sums_call(gates, *sums):
    every = [term[0] if isinstance(term, tuple) else term for terms in sums for term in terms]

    def part_of(term, ready=()):
        array, part = term if isinstance(term, tuple) else (term, None)
        array = after(array, *ready) if ready else array
        return array if part is None else array[: len(part)] if isinstance(part, range) else array[part]

    totals = [add_low(part_of(terms[0], (*gates, *every)), *map(part_of, terms[1:])) for terms in sums]
    return totals


def finish_kernel(sizes, turned, *refs):
    outs = refs[-len(sizes) :]
    at = 0
    for counts, turn, out in zip(sizes, turned, outs):
        for i, size in enumerate(counts):
            total = sum(ref[...].astype(WIDE) for ref in refs[at : at + size])
            at += size
            if turn:
                height = out.shape[0] // len(counts)
                out[i * height : (i + 1) * height, :] = jnp.transpose(total)
            else:
                out[...] = total


def finish_call(holds, pieces, kept):
    shard, hidden = pieces[0][2][0][0][0].shape[-2:]
    steps = shard // 128
    wide, tall = shaped(shard, holds * hidden, dtype=WIDE), shaped(holds * hidden, shard, dtype=WIDE)
    flat = [term for _, _, experts in pieces for terms in experts for term in terms]
    out_specs, out_shapes = [], []
    for which, expert, experts in pieces:
        number = len(experts)
        if which < 2:
            out_specs.append(pl.BlockSpec((128, hidden), lambda s, expert=expert: (s, expert)))
        else:
            block = (number * hidden, 128)
            out_specs.append(pl.BlockSpec(block, lambda s, at=expert // number: (at, s)))
        out_shapes.append(wide if which < 2 else tall)
    kept_in = [kept[which] for which, _, _ in pieces] if kept else []
    out = pl.pallas_call(
        functools.partial(
            finish_kernel, [[len(terms) for terms in experts] for _, _, experts in pieces], [p[0] == 2 for p in pieces]
        ),
        grid=(steps,),
        in_specs=[
            pl.BlockSpec((128, hidden), lambda s: (s, 0))
            if at is None
            else pl.BlockSpec((None, 128, hidden), lambda s, at=at: (at, s, 0))
            for _, at in flat
        ]
        + [pl.BlockSpec(memory_space=pl.ANY)] * len(kept_in),
        out_specs=out_specs,
        out_shape=out_shapes,
        input_output_aliases={len(flat) + i: i for i in range(len(kept_in))},
        compiler_params=pltpu.CompilerParams(vmem_limit_bytes=20 * MIB),
        cost_estimate=work(flops=0, bytes_accessed=30 * shard * hidden, transcendentals=0),
    )(*[array for array, _ in flat], *kept_in)
    result = list(kept) if kept else [None] * 3
    for (which, _, _), value in zip(pieces, out):
        result[which] = value
    return result


def piece_columns(mine, s, shard):
    return pl.ds(pl.multiple_of(jnp.bitwise_xor(mine, s) * shard, 128), shard)


def turn(values, cos, sin):
    return values * cos + pltpu.roll(values, HEAD_DIM // 2, 1) * sin


def turn_back(values, cos, sin):
    return values * cos - pltpu.roll(values, HEAD_DIM // 2, 1) * sin


def inverse_rms(values):
    return lax.rsqrt(jnp.mean(values * values, axis=-1, keepdims=True) + EPS)


def head_slice(h):
    return slice(h * HEAD_DIM, (h + 1) * HEAD_DIM)


def stacked_heads(ref, band, group, heads):
    return jnp.concatenate([ref[band, head_slice(group * heads + h)] for h in range(heads)], axis=0)


def probabilities(queries, keys, allowed):
    scores = jnp.where(allowed, dot_bt(queries, keys) * HEAD_DIM ** (-0.5), NEG)
    expo = jnp.exp(scores - jnp.max(scores, axis=-1, keepdims=True))
    return expo * (1.0 / jnp.sum(expo, axis=-1, keepdims=True))


def allowed_pairs(seg_col_ref, seg_row_ref, band, reach, heads):
    size = band.stop - band.start
    rows = band.start + lax.broadcasted_iota(jnp.int32, (size, reach), 0)
    cols = lax.broadcasted_iota(jnp.int32, (size, reach), 1)
    ok = (seg_col_ref[band, :] == seg_row_ref[:, :reach]) & (cols <= rows)
    return jnp.concatenate([ok] * heads, axis=0)


def attention_kernel(
    mine_ref, tokens_ref, gain_ref, p0, p1, p2, p3, s0, s1, s2, s3, seg_row_ref, seg_col_ref, cos_ref, sin_ref,
    h_ref, q_ref, k_ref, v_ref, out_ref,
):
    mine = mine_ref[0]
    stream = tokens_ref[...].astype(WIDE)
    h_ref[...] = (stream * inverse_rms(stream) * gain_ref[...]).astype(LOW)
    shard = p0.shape[0]
    width = q_ref.shape[1]
    cos, sin = cos_ref[...], sin_ref[...]

    def projected(pieces, columns):
        return sum(dot(h_ref[:, piece_columns(mine, s, shard)], piece[:, columns]) for s, piece in enumerate(pieces))

    heads = QUERY_HEADS // KEY_VALUE_HEADS
    key_width = KEY_VALUE_HEADS * HEAD_DIM
    shared = (s0, s1, s2, s3)
    keys = projected(shared, slice(0, key_width))
    for g in range(KEY_VALUE_HEADS):
        k_ref[:, head_slice(g)] = turn(keys[:, head_slice(g)], cos, sin).astype(LOW)
    v_ref[...] = projected(shared, slice(key_width, 2 * key_width)).astype(LOW)
    group_width = heads * HEAD_DIM
    for g in range(KEY_VALUE_HEADS):
        queries = projected((p0, p1, p2, p3), slice(g * group_width, (g + 1) * group_width))
        for h in range(heads):
            q_ref[:, head_slice(g * heads + h)] = turn(queries[:, head_slice(h)], cos, sin).astype(LOW)
    length = q_ref.shape[0]
    tile = 128
    for start in range(0, length, tile):
        band, reach = slice(start, start + tile), start + tile
        allowed = allowed_pairs(seg_col_ref, seg_row_ref, band, reach, heads)
        for g in range(KEY_VALUE_HEADS):
            probs = probabilities(stacked_heads(q_ref, band, g, heads), k_ref[:reach, head_slice(g)], allowed)
            mixed = dot(probs.astype(LOW), v_ref[:reach, head_slice(g)]).astype(LOW)
            for h in range(heads):
                out_ref[band, head_slice(g * heads + h)] = mixed[h * tile : (h + 1) * tile]


def vmem_call(kernel, out_shape, flops, transcendentals, token, *args):
    moved = sum(a.size * a.dtype.itemsize for a in args) + sum(
        o.size * o.dtype.itemsize for o in jax.tree.leaves(out_shape)
    )
    return pl.pallas_call(
        kernel,
        in_specs=[pl.BlockSpec(memory_space=pltpu.SMEM)] + [pl.BlockSpec(memory_space=pltpu.VMEM)] * len(args),
        out_specs=[pl.BlockSpec(memory_space=pltpu.VMEM)] * len(out_shape),
        out_shape=out_shape,
        compiler_params=pltpu.CompilerParams(vmem_limit_bytes=32 * MIB),
        cost_estimate=work(flops=flops, bytes_accessed=moved, transcendentals=transcendentals),
    )(token, *args)


def shaped(*shape, dtype=LOW):
    return jax.ShapeDtypeStruct(shape, dtype)


def attention_call(mine, tokens, gain, pieces, shared_pieces, seg_row, seg_col, cos, sin):
    length, width = tokens.shape
    key_width = KEY_VALUE_HEADS * HEAD_DIM
    return vmem_call(
        attention_kernel,
        [shaped(length, width), shaped(length, width), shaped(length, key_width), shaped(length, key_width), shaped(length, width)],
        2 * length * width * (width + 2 * key_width) + 3 * length * length * width,
        QUERY_HEADS * length * length,
        mine, tokens, gain, *pieces, *shared_pieces, seg_row, seg_col, cos, sin,
    )


def project_kernel(
    mine_ref, tokens_ref, attn_ref, p0, p1, p2, p3, r0, r1, r2, r3, gain_ref, routes_ref, resid_ref, h_ref
):
    mine = mine_ref[0]
    shard = p0.shape[0]
    resid = tokens_ref[...].astype(WIDE)
    for s, piece in enumerate((p0, p1, p2, p3)):
        resid = resid + dot(attn_ref[:, piece_columns(mine, s, shard)], piece[...])
    resid_ref[...] = resid
    length, width = resid.shape
    h_ref[:length] = (resid * inverse_rms(resid) * gain_ref[...]).astype(LOW)
    logits = jnp.transpose(
        sum(
            dot(h_ref[:length, piece_columns(mine, s, shard)], piece[...])
            for s, piece in enumerate((r0, r1, r2, r3))
        )
    )
    experts = lax.broadcasted_iota(jnp.int32, logits.shape, 0)
    picked = [
        jnp.sum(jnp.where(experts == routes_ref[k : k + 1, :], logits, 0.0), axis=0, keepdims=True)
        for k in range(routes_ref.shape[0])
    ]
    top = functools.reduce(jnp.maximum, picked)
    expo = [jnp.exp(p - top) for p in picked]
    total = sum(expo)
    gates = jnp.concatenate([x / total for x in expo], axis=0)
    h_ref[length:] = jnp.zeros((16, width), LOW)
    h_ref[length:, :length] = pack_routing(gates, routes_ref[...])


def project_call(mine, tokens, attn, pieces, shared_pieces, gain, routes_t):
    length, width = tokens.shape
    whole = lambda shape: pl.BlockSpec(shape, lambda i: (0,) * len(shape), pipeline_mode=ONCE)
    shapes = [shaped(length, width, dtype=WIDE), shaped(length + 16, width)]
    return pl.pallas_call(
        project_kernel,
        grid=(1,),
        in_specs=[pl.BlockSpec(memory_space=pltpu.SMEM)]
        + [whole(a.shape) for a in (tokens, attn, *pieces)]
        + router_columns(shared_pieces)
        + [whole(gain.shape), whole(routes_t.shape)],
        out_specs=[whole(s.shape) for s in shapes],
        out_shape=shapes,
        compiler_params=pltpu.CompilerParams(vmem_limit_bytes=30 * MIB),
        cost_estimate=work(
            flops=2 * length * width * (width + EXPERTS), bytes_accessed=length * width * 20, transcendentals=length * 8
        ),
    )(mine, tokens, attn, *pieces, *shared_pieces, gain, routes_t)


def as_column(row):
    return jnp.transpose(jnp.broadcast_to(row, (8, row.shape[1])))[:, :1]


def norm_back(grad, gain, normed, inverse):
    scaled = grad * gain
    return inverse * (scaled - normed * jnp.mean(scaled * normed, axis=-1, keepdims=True))


def shard_parts(targets):
    at, parts = 0, []
    for target in targets:
        parts.append((target, slice(at, at + target.shape[0])))
        at += target.shape[0]
    return parts


def resid_back_kernel(
    mine_ref, resid_ref, gain_ref, dz_ref, t0, t1, t2, gains_ref, h_ref, attn_ref,
    p0, p1, p2, p3, r0, r1, r2, r3, grad_ref, attn_grad_ref, small_ref, o0, o1, o2, o3, o4, o5, second_scr, low_scr,
):
    mine = mine_ref[0]
    shard, width = p0.shape
    length = resid_ref.shape[0]
    routers = (r0, r1, r2, r3)
    gains = gains_ref[...]
    experts = lax.broadcasted_iota(jnp.int32, gains.shape, 0)
    gate_rows, routes = unpack_routing(h_ref[length:, :length])
    gates = jnp.zeros(gains.shape, WIDE)
    for k in range(TOP):
        gates = gates + jnp.where(experts.astype(WIDE) == routes[k : k + 1], gate_rows[k : k + 1], 0.0)
    logit_grad = gates * (gains - jnp.sum(gates * gains, axis=0, keepdims=True))
    logit_grad = jnp.concatenate([logit_grad, jnp.zeros((128 - EXPERTS, length), WIDE)], axis=0)
    logit_grad = jnp.transpose(logit_grad).astype(LOW)
    second_scr[...] = t0[...].astype(WIDE) + t1[...].astype(WIDE) + t2[...].astype(WIDE)
    for s, piece in enumerate(routers):
        columns = piece_columns(mine, s, shard)
        second_scr[:, columns] = second_scr[:, columns] + dot_bt(logit_grad, piece[...])
    resid = resid_ref[...]
    inverse = inverse_rms(resid)
    normed = resid * inverse
    second = second_scr[...]
    gain_grad = jnp.sum(second * normed, axis=0, keepdims=True)
    grad = dz_ref[...].astype(WIDE) + norm_back(second, gain_ref[...], normed, inverse)
    grad_ref[...] = grad
    low_scr[...] = grad.astype(LOW)
    second_scr[:1, :] = gain_grad
    low = low_scr[...]
    for s, piece in enumerate((p0, p1, p2, p3)):
        columns = piece_columns(mine, s, shard)
        attn_grad_ref[:, columns] = dot_bt(low, piece[...]).astype(LOW)
        out_part = dot_t(attn_ref[:, columns], low).astype(LOW)
        router_part = dot_t(h_ref[:length, columns], logit_grad)
        lanes = lax.broadcasted_iota(jnp.int32, router_part.shape, 1)
        small_ref[s] = jnp.where(lanes == EXPERTS, as_column(second_scr[:1, columns]), router_part).astype(LOW)
        for target, rows in shard_parts(((o0,), (o1,), (o2, o3), (o4, o5))[s]):
            target[...] = out_part[rows]


def router_columns(pieces):
    return [
        pl.BlockSpec((p.shape[0], 128), lambda i, at=p.shape[1] // 128 - 1: (0, at), pipeline_mode=ONCE) for p in pieces
    ]


def resid_back_call(mine, resid, gain, dz, terms, gains, h, attn, pieces, shared_pieces):
    length, width = resid.shape
    shard = pieces[0].shape[0]
    whole = lambda shape: pl.BlockSpec(shape, lambda i: (0,) * len(shape), pipeline_mode=ONCE)
    arrays = (resid, gain, dz, *terms, gains, h, attn, *pieces)
    shapes = [shaped(length, width, dtype=WIDE), shaped(length, width), shaped(4, shard, 128)]
    shapes += [shaped(shard, width)] * 2 + [shaped(shard // 2, width)] * 4
    return pl.pallas_call(
        resid_back_kernel,
        grid=(1,),
        in_specs=[pl.BlockSpec(memory_space=pltpu.SMEM)]
        + [whole(a.shape) for a in arrays]
        + router_columns(shared_pieces),
        out_specs=[whole(s.shape) for s in shapes],
        out_shape=shapes,
        scratch_shapes=[pltpu.VMEM((length, width), WIDE), pltpu.VMEM((length, width), LOW)],
        compiler_params=pltpu.CompilerParams(vmem_limit_bytes=34 * MIB),
        cost_estimate=work(
            flops=4 * length * width * (width + EXPERTS), bytes_accessed=length * width * 40, transcendentals=0
        ),
    )(mine, *arrays, *shared_pieces)


def attention_back_kernel(
    mine_ref, q_ref, k_ref, v_ref, do_ref, h_ref, tokens_ref, gain_ref, grad_ref, small_ref, p0, p1, p2, p3, s0, s1, s2, s3,
    seg_row_ref, seg_col_ref, cos_ref, sin_ref, input_ref, o0, o1, o2, o3, o4, o5, qkv_scr, dk_scr, dv_scr, dh_scr,
):
    mine = mine_ref[0]
    length, width = q_ref.shape
    shard = p0.shape[0]
    qkv_width = width + 2 * KEY_VALUE_HEADS * HEAD_DIM
    heads = QUERY_HEADS // KEY_VALUE_HEADS
    key_width = KEY_VALUE_HEADS * HEAD_DIM
    tile = 128
    dk_scr[...] = jnp.zeros_like(dk_scr)
    dv_scr[...] = jnp.zeros_like(dv_scr)
    for start in range(0, length, tile):
        band, reach = slice(start, start + tile), start + tile
        allowed = allowed_pairs(seg_col_ref, seg_row_ref, band, reach, heads)
        cos, sin = cos_ref[band, :], sin_ref[band, :]
        for g in range(KEY_VALUE_HEADS):
            queries = stacked_heads(q_ref, band, g, heads)
            grads = stacked_heads(do_ref, band, g, heads)
            keys = k_ref[:reach, head_slice(g)]
            probs = probabilities(queries, keys, allowed)
            prob_grad = dot_bt(grads, v_ref[:reach, head_slice(g)])
            delta = jnp.sum(probs * prob_grad, axis=-1, keepdims=True)
            score_grad = (probs * (prob_grad - delta) * HEAD_DIM ** (-0.5)).astype(LOW)
            dv_scr[:reach, head_slice(g)] += dot_t(probs.astype(LOW), grads)
            dk_scr[:reach, head_slice(g)] += dot_t(score_grad, queries)
            dq = dot(score_grad, keys)
            for h in range(heads):
                qkv_scr[band, head_slice(g * heads + h)] = turn_back(dq[h * tile : (h + 1) * tile], cos, sin).astype(LOW)
    for g in range(KEY_VALUE_HEADS):
        at = width + g * HEAD_DIM
        qkv_scr[:, at : at + HEAD_DIM] = turn_back(dk_scr[:, head_slice(g)], cos_ref[...], sin_ref[...]).astype(LOW)
    qkv_scr[:, width + key_width :] = dv_scr[...].astype(LOW)
    qkv = qkv_scr[...]
    for s, (piece, shared) in enumerate(zip((p0, p1, p2, p3), (s0, s1, s2, s3))):
        dh_scr[:, piece_columns(mine, s, shard)] = dot_bt(qkv[:, :width], piece[...]) + dot_bt(qkv[:, width:], shared[:, : 2 * key_width])
    stream = tokens_ref[...].astype(WIDE)
    inverse = inverse_rms(stream)
    normed = stream * inverse
    first = dh_scr[...]
    gain_grad = jnp.sum(first * normed, axis=0, keepdims=True)
    input_ref[...] = grad_ref[...] + norm_back(first, gain_ref[...], normed, inverse)
    dh_scr[:1, :] = gain_grad
    for s in range(4):
        columns = piece_columns(mine, s, shard)
        part = dot_t(h_ref[:, columns], qkv).astype(LOW)
        small = small_ref[s].astype(WIDE)
        lanes = lax.broadcasted_iota(jnp.int32, small.shape, 1)
        small = jnp.where(lanes == EXPERTS + 1, as_column(dh_scr[:1, columns]), small).astype(LOW)
        for target, rows in shard_parts(((o0,), (o1,), (o2, o3), (o4, o5))[s]):
            target[:, :qkv_width] = part[rows]
            target[:, qkv_width:] = small[rows]


def attention_back_call(
    mine, q, k, v, do, h, tokens, gain, grad, small, pieces, shared_pieces, seg_row, seg_col, cos, sin
):
    length, width = q.shape
    shard = pieces[0].shape[0]
    qkv_width = width + 2 * KEY_VALUE_HEADS * HEAD_DIM
    key_width = KEY_VALUE_HEADS * HEAD_DIM
    return pl.pallas_call(
        attention_back_kernel,
        in_specs=[pl.BlockSpec(memory_space=pltpu.SMEM)] + [pl.BlockSpec(memory_space=pltpu.VMEM)] * 21,
        out_specs=[pl.BlockSpec(memory_space=pltpu.VMEM)] * 7,
        out_shape=[shaped(length, width, dtype=WIDE)]
        + [shaped(shard, qkv_width + 128)] * 2
        + [shaped(shard // 2, qkv_width + 128)] * 4,
        scratch_shapes=[
            pltpu.VMEM((length, qkv_width), LOW),
            pltpu.VMEM((length, key_width), WIDE),
            pltpu.VMEM((length, key_width), WIDE),
            pltpu.VMEM((length, width), WIDE),
        ],
        compiler_params=pltpu.CompilerParams(vmem_limit_bytes=46 * MIB),
        cost_estimate=work(
            flops=4 * length * width * qkv_width + 7 * length * length * width,
            bytes_accessed=length * width * 40,
            transcendentals=QUERY_HEADS * length * length,
        ),
    )(mine, q, k, v, do, h, tokens, gain, grad, small, *pieces, *shared_pieces, seg_row, seg_col, cos, sin)


def spread_kernel(count, token_ref, *refs):
    parts, outs, scratch = refs[2 : -count - 1], refs[-count - 1 : -1], refs[-1]
    for part, rows in shard_parts(parts):
        scratch[rows] = part[...]
    chunk = outs[0].shape[0]
    for j, out in enumerate(outs):
        rows = pl.ds(pl.multiple_of(lax.rem(token_ref[2] + j, count) * chunk, 16), chunk)
        out[...] = sum(term[rows, :].astype(WIDE) for term in (*refs[:2], scratch)).astype(LOW)


def spread_call(token, count, *terms):
    rows, width = terms[0].shape
    whole = lambda shape: pl.BlockSpec(shape, lambda i: (0, 0), pipeline_mode=ONCE)
    return pl.pallas_call(
        functools.partial(spread_kernel, count),
        grid=(1,),
        in_specs=[pl.BlockSpec(memory_space=pltpu.SMEM)] + [whole(t.shape) for t in terms],
        out_specs=[whole((rows // count, width))] * count,
        out_shape=[shaped(rows // count, width)] * count,
        scratch_shapes=[pltpu.VMEM((rows, width), LOW)],
        compiler_params=pltpu.CompilerParams(vmem_limit_bytes=16 * MIB),
        cost_estimate=work(flops=0, bytes_accessed=8 * rows * width, transcendentals=0),
    )(token, *terms)


def assemble_kernel(count, widths, token_ref, *refs):
    chunks, outs = refs[:count], refs[count:]
    chunk = chunks[0].shape[0]
    for j, ref in enumerate(chunks):
        rows = pl.ds(pl.multiple_of(lax.rem(token_ref[2] + j, count) * chunk, 16), chunk)
        values = ref[...].astype(WIDE)
        at = 0
        for width, out in zip(widths, outs):
            out[rows, :] = values[:, at : at + width]
            at += width
        if len(outs) > len(widths):
            outs[-1][rows, :] = values[:, at : at + 128]
    if len(outs) > len(widths):
        router_ref, ffn_ref, attn_ref, scratch = outs[len(widths) :]
        small = jnp.transpose(scratch[...])
        router_ref[...] = small[:EXPERTS]
        ffn_ref[...] = small[EXPERTS]
        attn_ref[...] = small[EXPERTS + 1]


def assemble_call(token, chunks, widths):
    count, (rows, width) = len(chunks), chunks[0].shape
    whole = lambda shape: pl.BlockSpec(shape, lambda i: (0,) * len(shape), pipeline_mode=ONCE)
    small = width > sum(widths)
    shapes = [(count * rows, w) for w in widths]
    shapes += [(EXPERTS, count * rows), (count * rows,), (count * rows,)] if small else []
    return pl.pallas_call(
        functools.partial(assemble_kernel, count, widths),
        grid=(1,),
        in_specs=[pl.BlockSpec(memory_space=pltpu.SMEM)] + [whole((rows, width))] * count,
        out_specs=[whole(shape) for shape in shapes],
        out_shape=[shaped(*shape, dtype=WIDE) for shape in shapes],
        scratch_shapes=[pltpu.VMEM((count * rows, 128), WIDE)] if small else [],
        compiler_params=pltpu.CompilerParams(vmem_limit_bytes=16 * MIB),
        cost_estimate=work(flops=0, bytes_accessed=6 * count * rows * width, transcendentals=0),
    )(token, *chunks)


def per_device_ring(
    tokens,
    segments,
    routes,
    attn_gain,
    ffn_gain,
    w_query,
    key_weight,
    value_weight,
    w_out,
    w_router,
    w_gate,
    w_up,
    w_down,
    cotangent,
):
    length, model_width = tokens.shape
    top_count = routes.shape[1]
    count = lax.axis_size("expert")
    holds = EXPERTS // count
    capacity = max(2, 3 * length * top_count // (2 * EXPERTS))
    slots = -(-capacity // 16) * 16
    shard = model_width // 4
    key_width = KEY_VALUE_HEADS * HEAD_DIM
    half = length // 2
    mine = lax.axis_index("wshard").astype(jnp.int32)
    order = jnp.array(ring_order(count), jnp.int32)
    spot_of = jnp.array([ring_order(count).index(i) for i in range(count)], jnp.int32)
    here = lax.axis_index("expert").astype(jnp.int32)
    spot = spot_of[here]
    token = jnp.stack([mine, here, spot])
    routes_t = routes.T

    cosine, sine = rotary_tables(length, HEAD_DIM)
    cos = jnp.concatenate([cosine, cosine], axis=1)
    sin = jnp.concatenate([-sine, sine], axis=1)
    seg_col = segments.reshape(length, 1)
    gain_one, gain_two = attn_gain[None], ffn_gain[None]

    def pieces_of(own, across, *ready):
        return (own, swap_core(own), across, swap_core(after(across, *ready)))

    dz = {0: cotangent}
    dz[-1], dz[1] = ahead(dz[0], count), behind(dz[0], count)
    query_across = swap_x(w_query)
    query_pieces = pieces_of(w_query, query_across)
    spare = jnp.zeros((shard, 128 - EXPERTS), LOW)
    shared = jnp.concatenate([key_weight, value_weight, w_router, spare], axis=1)
    shared, token, seg_col, cos, sin, routes_t, gain_one, gain_two = lax.optimization_barrier(
        (shared, token, seg_col, cos, sin, routes_t, gain_one, gain_two)
    )
    shared_across = swap_x(after(shared, query_across, dz[-1], dz[1]))
    dz[-2], dz[2] = ahead(dz[-1], count), behind(dz[1], count)
    shared_pieces = pieces_of(shared, shared_across)
    out_across = swap_x(after(w_out, shared_across))

    first_low, query, key, value, attn = attention_call(
        after(token, dz[-2], dz[2]), tokens, gain_one, query_pieces, shared_pieces, segments, seg_col, cos, sin
    )
    out_pieces = pieces_of(w_out, out_across, attn)
    dz[-3], dz[3] = ahead(dz[-2], count), behind(dz[2], count)
    resid, second = project_call(after(token, dz[-3], dz[3]), tokens, attn, out_pieces, shared_pieces, gain_two, routes_t)

    def experts(ready, first, offsets, kept):
        return expert_call(
            after(token, *ready), first, [h[j] for j in offsets], [dz[j] for j in offsets], w_gate, w_up, w_down, kept,
            holds, slots, count,
        )

    h = {0: second}
    h[-1], h[1] = ahead(h[0], count), behind(h[0], count)
    (d_own,), kept = experts((), 6, (0,), None)
    h[-2], h[2] = ahead(after(h[-1], d_own), count), behind(after(h[1], d_own), count)
    (d_l1, d_r1), kept = experts((), 0, (-1, 1), kept)
    h[-3], h[3] = ahead(after(h[-2], d_l1), count), behind(after(h[2], d_l1), count)
    (d_l2, d_r2), kept = experts((), 2, (-2, 2), kept)
    h[4], dz[4] = ahead(after(h[-3], d_l2), count), behind(after(dz[3], d_l2), count)
    (d_l3, d_r3), kept = experts((), 4, (-3, 3), kept)
    (d_far,), (gains, rank, *kept) = experts((), 7, (4,), kept)

    block_of = jnp.array([BLOCK_OFFSETS.index(j if j <= count // 2 else j - count) for j in range(count)], jnp.int32)
    gain_send = gains[block_of[(spot_of - spot) % count]]

    def weight_grads(expert, *ready):
        return wgrad_call(expert, after(token, *ready), kept)

    def over_cores(grads, *ready):
        return swap_core(after(grads[2], *ready))

    both, last = range(2), 2

    def sum_of(grads, got, part):
        return (grads[1], part), (got, part)

    up_sent, down_sent = ahead(d_far, count), behind(d_l3, count)
    grads = [wgrad_call(0, token, kept, True)]
    got = [[swap_core(v) for v in grads[0][2]]]
    grads.append(weight_grads(1, grads[0][0]))
    up, down = sums_call((grads[1][0], *got[0],), (d_r3, up_sent), (d_l2, down_sent))

    up_sent, down_sent = ahead(up, count), behind(down, count)
    got.append(over_cores(grads[1], up))
    halves = [sums_call((up,), *[((grads[0][1], i), got[0][i]) for i in range(3)])]
    across = [[(swap_x(v), None) for v in halves[0][:2]]]
    gain_dense = lax.all_to_all(after(gain_send, up), "expert", split_axis=0, concat_axis=0, tiled=True)
    gain_dense = gain_dense.reshape(EXPERTS, length)
    grads.append(weight_grads(2, *halves[0]))
    up, down = sums_call((gain_dense, grads[2][0], across[0][0][0], across[0][1][0],), (d_r2, up_sent), (d_l1, down_sent))

    up_sent, down_sent = ahead(up, count), behind(down, count)
    got.append(over_cores(grads[2], up))
    halves.append(sums_call((up,), sum_of(grads[1], got[1], both)))
    across_b = swap_x(halves[1][0])
    y = dict(zip(BLOCK_OFFSETS, value_call(after(token, *halves[1]), rank, kept[4], w_down, slots)))
    late = swap_core(after(grads[0][3], up))
    halves[1] += sums_call((y[0],), sum_of(grads[1], got[1], last))
    halves.append(sums_call((y[0],), sum_of(grads[2], got[2], both), sum_of(grads[2], got[2], last)))
    (up,) = sums_call((*halves[2], across_b, down_sent, late, halves[1][1]), (d_r1, up_sent))

    up_sent, y_down = ahead(up, count), behind(after(y[4], up), count)
    across[0].append((swap_x(after(halves[0][2], up)), None))
    across.append([(across_b, 0), (across_b, 1), (swap_x(after(halves[1][1], up)), None)])
    grads.append(weight_grads(3, up))
    (down,) = sums_call(
        (up_sent, across[0][2][0], across[1][2][0], grads[3][0]), (y[-3], y_down)
    )

    y_up, y_down, across_d = ahead(after(y[3], down), count), behind(down, count), swap_x(after(halves[2][0], down))
    grad, attn_grad, small, *out_parts = resid_back_call(
        after(token, down), resid, gain_two, cotangent, (d_own, up_sent, down_sent), gain_dense, second,
        attn, out_pieces, shared_pieces,
    )
    def terms_of(expert, i, *ready):
        other = (late, i) if expert == 0 else (got[expert], 3 + i)
        return [(after(grads[expert][0], *ready) if ready else grads[expert][0], i), other, across[expert][i]]

    def finish(ready, expert, kept_out, parts=range(3)):
        return finish_call(holds, [(i, expert, [terms_of(expert, i, *ready)]) for i in parts], kept_out)

    out_first = [swap_core(v) for v in out_parts[4:]]
    finished = finish((grad,), 0, None)
    *out_half, up, down = sums_call(
        (finished[0], across_d), *zip(out_parts[2:4], out_first), (y[2], y_up), (y[-2], y_down)
    )

    y_up, y_down, out_across = ahead(up, count), behind(down, count), [swap_x(v) for v in out_half]
    out_got = swap_core(after(out_parts[1], up))
    input_grad, *qkv_parts = attention_back_call(
        after(token, up), query, key, value, attn_grad, first_low, tokens, gain_one, grad, small, query_pieces,
        shared_pieces, segments, seg_col, cos, sin,
    )
    up, down = sums_call((input_grad, *out_across, out_got), (y[1], y_up), (y[-1], y_down))

    y_up, y_down = ahead(up, count), behind(down, count)
    qkv_first = [swap_core(after(v, up)) for v in qkv_parts[4:]]
    qkv_half = sums_call((up,), *zip(qkv_parts[2:4], qkv_first))
    qkv_across = [swap_x(qkv_half[0])]
    out_parts = spread_call(after(token, *qkv_half), count, out_parts[0], out_got, *out_across)
    finished = finish(qkv_half, 1, finished)
    qkv_got = swap_core(after(qkv_parts[1], qkv_across[0]))
    got.append(over_cores(grads[3], qkv_half[0]))
    (half_e,) = sums_call((finished[0],), sum_of(grads[3], got[3], range(3)))
    across.append([(across_d, 0), (across_d, 1)])
    finished = finish((half_e,), 2, finished, both)
    def sum_step(parts, up, down, step):
        up = add_low(parts[step], ahead(up, count))
        down = behind(down, count)
        return up, add_low(parts[count + 1 - step], down) if step > 1 else down

    def copy_step(up, down):
        return up + [ahead(up[-1], count)], down + [behind(down[-1], count)]

    qkv_across.append(swap_x(after(qkv_half[1], qkv_across[0])))
    out_up, out_down = after(out_parts[4], finished[0], finished[0]), after(out_parts[5], finished[0], finished[0])
    for step in (3, 2, 1):
        out_up, out_down = sum_step(out_parts, out_up, out_down, step)
        if step == 3:
            y_own = after(y[0], qkv_across[0], out_up, out_down)
            mixed = (resid + sum(t.astype(WIDE) for t in (y_own, y_up, y_down))).astype(LOW)
            out_up, out_down = after(out_up, mixed), after(out_down, mixed)
        if step == 2:
            out_up = after(out_up, qkv_across[1])
    out_own = add_low(out_parts[0], ahead(out_up, count), out_down)
    across_e = [swap_x(after(halves[2][1], qkv_across[1])), swap_x(after(half_e, qkv_across[1]))]
    qkv_parts = spread_call(after(token, out_own), count, qkv_parts[0], qkv_got, *qkv_across)
    across[2].append((across_e[0], None))
    across.append([(across_e[1], i) for i in range(3)])
    out_ups, out_downs = [after(out_own, qkv_parts[0])], [after(out_own, qkv_parts[0])]
    qkv_up, qkv_down = qkv_parts[4], qkv_parts[5]
    for step in (3, 2, 1):
        out_ups, out_downs = copy_step(out_ups, out_downs)
        qkv_up, qkv_down = sum_step(qkv_parts, qkv_up, qkv_down, step)
        qkv_up = after(qkv_up, out_ups[-1], out_downs[-1])
    out_ups.append(ahead(out_ups[-1], count))
    qkv_own = add_low(qkv_parts[0], ahead(qkv_up, count), qkv_down)
    qkv_ups, qkv_downs = [qkv_own], [qkv_own]
    for step in (3, 2, 1):
        qkv_ups, qkv_downs = copy_step(qkv_ups, qkv_downs)
        if step == 3:
            qkv_ups[-1] = after(qkv_ups[-1], out_ups[-1])
    (out_sum,) = assemble_call(after(token, qkv_ups[2]), out_downs + out_ups[:0:-1], (model_width,))
    qkv_ups.append(ahead(after(qkv_ups[-1], out_sum, across_e[1]), count))
    last_rows = [terms_of(2, 2, qkv_ups[3]), terms_of(3, 2)]
    finished = finish_call(
        holds, [(0, 3, [terms_of(3, 0, qkv_ups[3])]), (1, 3, [terms_of(3, 1)]), (2, 2, last_rows)], finished
    )
    query_sum, key_sum, value_sum, router_sum, ffn_gain_sum, attn_gain_sum = assemble_call(
        after(token, finished[0]), qkv_downs + qkv_ups[:0:-1], (model_width, key_width, key_width)
    )
    gate_shard, up_shard, down_shard = finished
    return (
        mixed,
        input_grad,
        attn_gain_sum,
        ffn_gain_sum,
        query_sum,
        key_sum,
        value_sum,
        out_sum,
        router_sum.T,
        gate_shard,
        up_shard,
        down_shard,
    )


def solution(mesh):
    ring = mesh.shape["expert"] == len(BLOCK_OFFSETS) and mesh.shape["wshard"] == 4
    body = per_device_ring if ring else per_device_exchange
    in_specs = (
        P(("expert", "wshard"), None),
        P(("expert", "wshard"), None),
        P(("expert", "wshard"), None),
        P(),
        P(),
        P("wshard", None),
        P("wshard", None),
        P("wshard", None),
        P("wshard", None),
        P("wshard", None),
        P(None, "expert"),
        P(None, "expert"),
        P("expert", None),
        P(("expert", "wshard"), None),
    )
    out_specs = (
        P(("expert", "wshard"), None),
        P(("expert", "wshard"), None),
        P("wshard"),
        P("wshard"),
        P("wshard", None),
        P("wshard", None),
        P("wshard", None),
        P("wshard", None),
        P("wshard", None),
        P("wshard", "expert"),
        P("wshard", "expert"),
        P("expert", "wshard"),
    )
    return jax.shard_map(
        body, mesh=mesh, in_specs=in_specs, out_specs=out_specs, check_vma=False
    )
```

```python
import functools

import jax
import jax.numpy as jnp
from jax import lax
from jax.experimental import pallas as pl
from jax.experimental.pallas import tpu as pltpu
from jax.sharding import PartitionSpec as P

QUERY_HEADS = 12
KEY_VALUE_HEADS = 2
HEAD_DIM = 128
EXPERTS = 32
TOP = 4


EPS = 1e-06
ROPE_BASE = 10000.0
NEG = -1e30
LOW = jnp.bfloat16
WIDE = jnp.float32
MIB = 1024 * 1024
ONCE = pl.Buffered(buffer_count=1)
def norm_forward(values, gain):
    inverse = lax.rsqrt(jnp.mean(values * values, axis=-1) + EPS)
    normed = values * inverse[:, None]
    return (normed * gain, normed, inverse)


def norm_backward(grad, gain, normed, inverse):
    gain_grad = jnp.sum(grad * normed, axis=0)
    scaled = grad * gain
    centred = scaled - normed * jnp.mean(scaled * normed, axis=-1, keepdims=True)
    return (inverse[:, None] * centred, gain_grad)


def rotary_tables(seq_length, head_size):
    half_size = head_size // 2
    frequency = ROPE_BASE ** (-(jnp.arange(half_size, dtype=jnp.float32) * 2.0 / head_size))
    angles = jnp.arange(seq_length, dtype=jnp.float32)[:, None] * frequency[None, :]
    return (jnp.cos(angles), jnp.sin(angles))


def apply_rotation(values, cosine_lookup, sine_lookup):
    half_size = values.shape[-1] // 2
    first_half = values[..., :half_size]
    second_half = values[..., half_size:]
    cos_part = cosine_lookup[:, None, :]
    sin_part = sine_lookup[:, None, :]
    return jnp.concatenate(
        [
            first_half * cos_part - second_half * sin_part,
            second_half * cos_part + first_half * sin_part,
        ],
        axis=-1,
    )


def reverse_rotation(values, cosine_lookup, sine_lookup):
    half_size = values.shape[-1] // 2
    first_half = values[..., :half_size]
    second_half = values[..., half_size:]
    cos_part = cosine_lookup[:, None, :]
    sin_part = sine_lookup[:, None, :]
    return jnp.concatenate(
        [
            first_half * cos_part + second_half * sin_part,
            second_half * cos_part - first_half * sin_part,
        ],
        axis=-1,
    )


def per_device_exchange(
    tokens,
    segments,
    routes,
    attn_gain,
    ffn_gain,
    w_query,
    key_weight,
    value_weight,
    w_out,
    w_router,
    w_gate,
    w_up,
    w_down,
    cotangent,
):
    lower_dtype = jnp.bfloat16
    wide_type = jnp.float32
    sequence_length, model_width = tokens.shape
    top_count = routes.shape[1]
    axis_count = lax.axis_size("expert")
    owners = max(1, axis_count // EXPERTS)
    holds = max(1, EXPERTS // axis_count)
    groups = EXPERTS // holds
    capacity = max(2, 3 * sequence_length * top_count // (2 * EXPERTS))
    hidden_dev = w_gate.shape[1] // holds
    query_group_width = QUERY_HEADS // KEY_VALUE_HEADS
    score_scale = HEAD_DIM ** (-0.5)
    pair_count = sequence_length * top_count
    query_full, key_full, value_full, out_full, router_full = (
        lax.all_gather(w_query, "wshard", axis=0, tiled=True),
        lax.all_gather(key_weight, "wshard", axis=0, tiled=True),
        lax.all_gather(value_weight, "wshard", axis=0, tiled=True),
        lax.all_gather(w_out, "wshard", axis=0, tiled=True),
        lax.all_gather(w_router, "wshard", axis=0, tiled=True),
    )
    stream = tokens.astype(wide_type)
    first_norm, first_normed, first_inverse = norm_forward(stream, attn_gain)
    first_low = first_norm.astype(lower_dtype)
    cosine_lookup, sine_lookup = rotary_tables(sequence_length, HEAD_DIM)
    query_pre = jnp.dot(first_low, query_full, preferred_element_type=wide_type).reshape(
        sequence_length, QUERY_HEADS, HEAD_DIM
    )
    key_unrotated = jnp.dot(first_low, key_full, preferred_element_type=wide_type).reshape(
        sequence_length, KEY_VALUE_HEADS, HEAD_DIM
    )
    query_rotated = (
        apply_rotation(query_pre, cosine_lookup, sine_lookup)
        .astype(lower_dtype)
        .reshape(sequence_length, KEY_VALUE_HEADS, query_group_width, HEAD_DIM)
    )
    key_rotated = apply_rotation(key_unrotated, cosine_lookup, sine_lookup).astype(lower_dtype)
    value_lowered = (
        jnp.dot(first_low, value_full, preferred_element_type=wide_type)
        .astype(lower_dtype)
        .reshape(sequence_length, KEY_VALUE_HEADS, HEAD_DIM)
    )
    positions = jnp.arange(sequence_length)
    offset = positions[:, None] - positions[None, :]
    segment_row = segments[0]
    allowed = (segment_row[:, None] == segment_row[None, :]) & (offset >= 0)
    raw_scores = jnp.einsum(
        "qagd,kad->agqk", query_rotated, key_rotated, preferred_element_type=wide_type
    )
    scores = jnp.where(allowed, raw_scores * score_scale, NEG)
    score_top = jnp.max(scores, axis=-1, keepdims=True)
    expo_terms = jnp.exp(scores - score_top)
    expo_total = jnp.sum(expo_terms, axis=-1, keepdims=True)
    log_total = score_top + jnp.log(expo_total)
    probs_low = (expo_terms / expo_total).astype(lower_dtype)
    attn_low = (
        jnp.einsum("agqk,kad->qagd", probs_low, value_lowered, preferred_element_type=wide_type)
        .astype(lower_dtype)
        .reshape(sequence_length, QUERY_HEADS * HEAD_DIM)
    )
    resid = stream + jnp.dot(attn_low, out_full, preferred_element_type=wide_type)
    second_norm, second_normed, second_inverse = norm_forward(resid, ffn_gain)
    second_low = second_norm.astype(lower_dtype)
    logits = jnp.dot(second_low, router_full, preferred_element_type=wide_type)
    choose = (routes[:, :, None] == jnp.arange(EXPERTS)[None, None, :]).astype(wide_type)
    selected = jnp.sum(choose * logits[:, None, :], axis=-1)
    gate_probs = jax.nn.softmax(selected, axis=-1)
    flat_routes = routes.reshape(pair_count)
    one_hot = (flat_routes[:, None] == jnp.arange(EXPERTS)[None, :]).astype(jnp.int32)
    slot_rank = jnp.sum((jnp.cumsum(one_hot, axis=0) - 1) * one_hot, axis=1)
    slot_index = (flat_routes // holds * capacity + slot_rank) * holds + flat_routes % holds
    slot_pair = (
        jnp.full((EXPERTS * capacity,), pair_count, jnp.int32)
        .at[slot_index]
        .set(jnp.arange(pair_count, dtype=jnp.int32))
    )
    second_ext = jnp.concatenate([second_low, jnp.zeros((1, model_width), lower_dtype)], axis=0)
    send_rows = jnp.repeat(
        second_ext[slot_pair // top_count].reshape(groups, capacity, holds, model_width),
        owners,
        axis=0,
    )
    gate_local = w_gate.reshape(model_width, holds, hidden_dev)
    up_local = w_up.reshape(model_width, holds, hidden_dev)
    down_local = w_down.reshape(holds, hidden_dev, model_width)

    def owner_total(values):
        summed = jnp.sum(
            values.astype(wide_type).reshape(groups, owners, capacity, holds, model_width), axis=1
        )
        return summed.reshape(EXPERTS * capacity, model_width)

    received = lax.all_to_all(send_rows, "expert", split_axis=0, concat_axis=0, tiled=True)
    gate_pre = jnp.einsum("scld,dlf->sclf", received, gate_local, preferred_element_type=wide_type)
    up_pre = jnp.einsum("scld,dlf->sclf", received, up_local, preferred_element_type=wide_type)
    hidden = (jax.nn.silu(gate_pre) * up_pre).astype(lower_dtype)
    partial_value = jnp.einsum(
        "sclf,lfd->scld", hidden, down_local, preferred_element_type=wide_type
    ).astype(lower_dtype)
    returned = lax.all_to_all(partial_value, "expert", split_axis=0, concat_axis=0, tiled=True)
    expert_wide = owner_total(returned)[slot_index].reshape(sequence_length, top_count, model_width)
    mixed = (resid + jnp.sum(gate_probs[:, :, None] * expert_wide, axis=1)).astype(lower_dtype)
    upstream = cotangent.astype(wide_type)
    query_back, key_back, value_back, out_back, router_back = (
        lax.all_gather(w_query, "wshard", axis=0, tiled=True),
        lax.all_gather(key_weight, "wshard", axis=0, tiled=True),
        lax.all_gather(value_weight, "wshard", axis=0, tiled=True),
        lax.all_gather(w_out, "wshard", axis=0, tiled=True),
        lax.all_gather(w_router, "wshard", axis=0, tiled=True),
    )
    gate_grad = jnp.sum(expert_wide * upstream[:, None, :], axis=-1)
    sel_grad = gate_probs * (gate_grad - jnp.sum(gate_probs * gate_grad, axis=-1, keepdims=True))
    logit_grad = jnp.sum(choose * sel_grad[:, :, None], axis=1).astype(lower_dtype)
    pair_grad = (
        (gate_probs[:, :, None] * upstream[:, None, :])
        .astype(lower_dtype)
        .reshape(pair_count, model_width)
    )
    pair_ext = jnp.concatenate([pair_grad, jnp.zeros((1, model_width), lower_dtype)], axis=0)
    grad_send = jnp.repeat(
        pair_ext[slot_pair].reshape(groups, capacity, holds, model_width), owners, axis=0
    )
    grad_recv, rows_recv = (
        lax.all_to_all(grad_send, "expert", split_axis=0, concat_axis=0, tiled=True),
        lax.all_to_all(send_rows, "expert", split_axis=0, concat_axis=0, tiled=True),
    )
    gate_pre = jnp.einsum("scld,dlf->sclf", rows_recv, gate_local, preferred_element_type=wide_type)
    up_pre = jnp.einsum("scld,dlf->sclf", rows_recv, up_local, preferred_element_type=wide_type)
    sigmoid_gate = jax.nn.sigmoid(gate_pre)
    silu_gate = gate_pre * sigmoid_gate
    hidden = (silu_gate * up_pre).astype(lower_dtype)
    hidden_grad = jnp.einsum(
        "scld,lfd->sclf", grad_recv, down_local, preferred_element_type=wide_type
    )
    gate_pre_grad = (
        hidden_grad * up_pre * sigmoid_gate * (1.0 + gate_pre * (1.0 - sigmoid_gate))
    ).astype(lower_dtype)
    up_pre_grad = (hidden_grad * silu_gate).astype(lower_dtype)
    row_grad = (
        jnp.einsum("sclf,dlf->scld", gate_pre_grad, gate_local, preferred_element_type=wide_type)
        + jnp.einsum("sclf,dlf->scld", up_pre_grad, up_local, preferred_element_type=wide_type)
    ).astype(lower_dtype)
    returned_grad = lax.all_to_all(row_grad, "expert", split_axis=0, concat_axis=0, tiled=True)
    gate_wgrad = jnp.einsum(
        "scld,sclf->dlf", rows_recv, gate_pre_grad, preferred_element_type=wide_type
    ).reshape(model_width, holds * hidden_dev)
    up_wgrad = jnp.einsum(
        "scld,sclf->dlf", rows_recv, up_pre_grad, preferred_element_type=wide_type
    ).reshape(model_width, holds * hidden_dev)
    down_wgrad = jnp.einsum(
        "sclf,scld->lfd", hidden, grad_recv, preferred_element_type=wide_type
    ).reshape(holds * hidden_dev, model_width)
    gate_shard, up_shard, down_shard = (
        lax.psum_scatter(
            gate_wgrad.astype(jnp.bfloat16), "wshard", scatter_dimension=0, tiled=True
        ).astype(jnp.float32),
        lax.psum_scatter(
            up_wgrad.astype(jnp.bfloat16), "wshard", scatter_dimension=0, tiled=True
        ).astype(jnp.float32),
        lax.psum_scatter(
            down_wgrad.astype(jnp.bfloat16), "wshard", scatter_dimension=1, tiled=True
        ).astype(jnp.float32),
    )
    token_grad = owner_total(returned_grad)[slot_index].reshape(
        sequence_length, top_count, model_width
    )
    second_grad = jnp.sum(token_grad, axis=1) + jnp.dot(
        logit_grad, router_back.T, preferred_element_type=wide_type
    )
    router_wgrad = jnp.einsum("td,te->de", second_low, logit_grad, preferred_element_type=wide_type)
    resid_part, ffn_gain_grad = norm_backward(second_grad, ffn_gain, second_normed, second_inverse)
    resid_grad = upstream + resid_part
    resid_low = resid_grad.astype(lower_dtype)
    out_wgrad = jnp.einsum("tc,td->cd", attn_low, resid_low, preferred_element_type=wide_type)
    attn_grad = (
        jnp.dot(resid_low, out_back.T, preferred_element_type=wide_type)
        .astype(lower_dtype)
        .reshape(sequence_length, KEY_VALUE_HEADS, query_group_width, HEAD_DIM)
    )
    raw_again = jnp.einsum(
        "qagd,kad->agqk", query_rotated, key_rotated, preferred_element_type=wide_type
    )
    scores_again = jnp.where(allowed, raw_again * score_scale, NEG)
    probs_again = jnp.exp(scores_again - log_total)
    prob_grad = jnp.einsum(
        "qagd,kad->agqk", attn_grad, value_lowered, preferred_element_type=wide_type
    )
    row_delta = jnp.sum(probs_again * prob_grad, axis=-1, keepdims=True)
    score_grad = (probs_again * (prob_grad - row_delta) * score_scale).astype(lower_dtype)
    value_grad = (
        jnp.einsum("agqk,qagd->kad", probs_low, attn_grad, preferred_element_type=wide_type)
        .astype(lower_dtype)
        .reshape(sequence_length, KEY_VALUE_HEADS * HEAD_DIM)
    )
    query_rot_grad = jnp.einsum(
        "agqk,kad->qagd", score_grad, key_rotated, preferred_element_type=wide_type
    ).reshape(sequence_length, QUERY_HEADS, HEAD_DIM)
    key_rotated_gradient = jnp.einsum(
        "agqk,qagd->kad", score_grad, query_rotated, preferred_element_type=wide_type
    )
    query_grad = (
        reverse_rotation(query_rot_grad, cosine_lookup, sine_lookup)
        .astype(lower_dtype)
        .reshape(sequence_length, QUERY_HEADS * HEAD_DIM)
    )
    key_grad = (
        reverse_rotation(key_rotated_gradient, cosine_lookup, sine_lookup)
        .astype(lower_dtype)
        .reshape(sequence_length, KEY_VALUE_HEADS * HEAD_DIM)
    )
    query_wgrad = jnp.einsum("td,tc->dc", first_low, query_grad, preferred_element_type=wide_type)
    key_wgrad = jnp.einsum("td,tc->dc", first_low, key_grad, preferred_element_type=wide_type)
    value_wgrad = jnp.einsum("td,tc->dc", first_low, value_grad, preferred_element_type=wide_type)
    first_grad = (
        jnp.dot(query_grad, query_back.T, preferred_element_type=wide_type)
        + jnp.dot(key_grad, key_back.T, preferred_element_type=wide_type)
        + jnp.dot(value_grad, value_back.T, preferred_element_type=wide_type)
    )
    stream_part, attn_gain_grad = norm_backward(first_grad, attn_gain, first_normed, first_inverse)
    input_grad = resid_grad + stream_part
    query_part, key_part, value_part, out_part, router_part, attn_gain_part, ffn_gain_part = (
        lax.psum_scatter(
            query_wgrad.astype(jnp.bfloat16), "wshard", scatter_dimension=0, tiled=True
        ).astype(jnp.float32),
        lax.psum_scatter(
            key_wgrad.astype(jnp.bfloat16), "wshard", scatter_dimension=0, tiled=True
        ).astype(jnp.float32),
        lax.psum_scatter(
            value_wgrad.astype(jnp.bfloat16), "wshard", scatter_dimension=0, tiled=True
        ).astype(jnp.float32),
        lax.psum_scatter(
            out_wgrad.astype(jnp.bfloat16), "wshard", scatter_dimension=0, tiled=True
        ).astype(jnp.float32),
        lax.psum_scatter(
            router_wgrad.astype(jnp.bfloat16), "wshard", scatter_dimension=0, tiled=True
        ).astype(jnp.float32),
        lax.psum_scatter(
            attn_gain_grad.astype(jnp.bfloat16), "wshard", scatter_dimension=0, tiled=True
        ).astype(jnp.float32),
        lax.psum_scatter(
            ffn_gain_grad.astype(jnp.bfloat16), "wshard", scatter_dimension=0, tiled=True
        ).astype(jnp.float32),
    )
    query_sum, key_sum, value_sum, out_sum, router_sum, attn_gain_sum, ffn_gain_sum = lax.psum(
        (query_part, key_part, value_part, out_part, router_part, attn_gain_part, ffn_gain_part),
        "expert",
    )
    return (
        mixed,
        input_grad,
        attn_gain_sum,
        ffn_gain_sum,
        query_sum,
        key_sum,
        value_sum,
        out_sum,
        router_sum,
        gate_shard,
        up_shard,
        down_shard,
    )


BLOCK_OFFSETS = (-1, 1, -2, 2, -3, 3, 0, 4)


def ring_order(count):
    return [0] + list(range(1, count, 2)) + list(range(count - 2, 0, -2))


def shifted(value, step, count):
    order = ring_order(count)
    return lax.ppermute(value, "expert", [(order[i], order[(i + step) % count]) for i in range(count)])


def ahead(value, count):
    return shifted(value, 1, count)


def behind(value, count):
    return shifted(value, -1, count)


def swap_core(value):
    size = lax.axis_size("wshard")
    return lax.ppermute(value, "wshard", [(i, i ^ 1) for i in range(size)])


def swap_x(value):
    size = lax.axis_size("wshard")
    return lax.ppermute(value, "wshard", [(i, i ^ 2) for i in range(size)])


def work(flops, bytes_accessed, transcendentals):
    scale = 8
    return pl.CostEstimate(
        flops=flops // scale, bytes_accessed=bytes_accessed // scale, transcendentals=transcendentals // scale
    )


def add_low(*terms):
    return sum(term.astype(WIDE) for term in terms).astype(LOW)


def after(value, *others):
    return lax.optimization_barrier((value, *others))[0]


def places(rank_row, slots):
    rows = lax.broadcasted_iota(jnp.int32, (slots, rank_row.shape[-1]), 0)
    return rank_row == rows


def expert_ranks(routes, holds):
    tokens = routes.shape[1]
    names = [jnp.sum((routes == l).astype(WIDE), axis=0, keepdims=True) for l in range(holds)]
    names = jnp.concatenate(names + [jnp.zeros((16 - holds, tokens), WIDE)], axis=0)
    rows = lax.broadcasted_iota(jnp.int32, (tokens, tokens), 0)
    columns = lax.broadcasted_iota(jnp.int32, (tokens, tokens), 1)
    before = dot(names.astype(LOW), (rows <= columns).astype(WIDE).astype(LOW))
    return jnp.where(names > 0.0, before - 1.0, -1.0)[:holds].astype(jnp.int32)


def pack_routing(gates, routes):
    high = gates.astype(LOW).astype(WIDE)
    rows = [high, gates - high, routes.astype(WIDE)]
    spare = 16 - 3 * gates.shape[0]
    return jnp.concatenate(rows + [jnp.zeros((spare, gates.shape[1]), WIDE)], axis=0).astype(LOW)


def unpack_routing(packed):
    top_count = TOP
    packed = packed.astype(WIDE)
    return packed[:top_count] + packed[top_count : 2 * top_count], packed[2 * top_count : 3 * top_count]


def dot_t(a, b):
    return lax.dot_general(a, b, (((0,), (0,)), ((), ())), preferred_element_type=WIDE)


def dot_bt(a, b):
    return lax.dot_general(a, b, (((1,), (1,)), ((), ())), preferred_element_type=WIDE)


def dot(a, b):
    return jnp.dot(a, b, preferred_element_type=WIDE)


def expert_kernel(count, slots, aliased, *refs):
    token_ref = refs[0]
    h_refs, dz_refs = refs[1 : 1 + count], refs[1 + count : 1 + 2 * count]
    wg_ref, wu_ref, wd_ref = refs[1 + 2 * count : 4 + 2 * count]
    rest = refs[4 + 2 * count + (7 if aliased else 0) :]
    d_refs = rest[:count]
    gain_ref, rank_ref, rows_out, dz_out, gg_out, ug_out, hid_out = rest[count : count + 7]
    place_scr, back_scr, gate_scr, wg_scr, wu_scr, wd_scr, sems = rest[count + 7 :]
    e = pl.program_id(0)
    holds, tokens = rank_ref.shape[1:]
    hidden_width = wd_scr.shape[1]

    def weights(expert, slot):
        band = pl.ds(pl.multiple_of(expert * hidden_width, hidden_width), hidden_width)
        return [
            pltpu.make_async_copy(source, target.at[slot], sems.at[slot, i])
            for i, (source, target) in enumerate(
                ((wg_ref.at[:, band], wg_scr), (wu_ref.at[:, band], wu_scr), (wd_ref.at[band, :], wd_scr))
            )
        ]

    slot = lax.rem(e, 2)

    @pl.when(e == 0)
    def _():
        for copy in weights(0, 0):
            copy.start()

    @pl.when(e + 1 < holds)
    def _():
        for copy in weights(e + 1, 1 - slot):
            copy.start()

    here = pl.ds(pl.multiple_of(e * slots, slots), slots)
    @pl.when(e == 0)
    def _():
        for b, (h_ref, dz_ref) in enumerate(zip(h_refs, dz_refs)):
            gates, routes = unpack_routing(h_ref[tokens : tokens + 16, :tokens])
            routes = routes - (token_ref[1] * holds).astype(WIDE)
            ranks = expert_ranks(routes, holds)
            rank_ref[b] = ranks
            for l in range(holds):
                band = slice(l * slots, (l + 1) * slots)
                spot = places(ranks[l : l + 1], slots).astype(WIDE)
                named = jnp.where(routes == l, gates, 0.0)
                gate_scr[b, band, :] = jnp.broadcast_to(
                    jnp.sum(spot * jnp.sum(named, axis=0, keepdims=True), axis=1, keepdims=True), (slots, 128)
                )
                place_scr[b, band, :] = spot.astype(LOW)
            for source, target in ((h_ref, rows_out), (dz_ref, dz_out)):
                taken = dot(place_scr[b], source[:tokens]).astype(LOW)
                for l in range(holds):
                    target[l, b * slots : (b + 1) * slots, :] = taken[l * slots : (l + 1) * slots]

    gate = jnp.concatenate([gate_scr[b, here, :] for b in range(count)], axis=0)[:, :1]
    rows = rows_out[e]
    for copy in weights(e, slot):
        copy.wait()
    gate_pre = dot(rows, wg_scr[slot])
    up_pre = dot(rows, wu_scr[slot])
    sig = jax.nn.sigmoid(gate_pre)
    silu = gate_pre * sig
    hidden = (silu * up_pre).astype(LOW).astype(WIDE)
    back = dot_bt(dz_out[e], wd_scr[slot])
    gains = jnp.sum(back * hidden, axis=1, keepdims=True)
    back = back * gate
    gate_grad = (back * (up_pre * sig * (1.0 + gate_pre * (1.0 - sig)))).astype(LOW)
    up_grad = (back * silu).astype(LOW)
    gg_out[0] = gate_grad
    ug_out[0] = up_grad
    hid_out[0] = (hidden * gate).astype(LOW)
    row_grad = (dot_bt(gate_grad, wg_scr[slot]) + dot_bt(up_grad, wu_scr[slot])).astype(LOW)
    for b in range(count):
        band = slice(b * slots, (b + 1) * slots)
        back_scr[b, here, :] = row_grad[band]
        spot = place_scr[b, here, :].astype(WIDE)
        gain_ref[b, pl.ds(e, 1), :] = jnp.sum(spot * gains[band], axis=0, keepdims=True)

    @pl.when(e == pl.num_programs(0) - 1)
    def _():
        for b in range(count):
            d_refs[b][...] = dot_t(place_scr[b], back_scr[b]).astype(LOW)


def expert_call(token, first, blocks, dz_blocks, w_gate, w_up, w_down, kept, holds, slots, total):
    count = len(blocks)
    tokens, width = dz_blocks[0].shape
    hidden = w_gate.shape[1] // holds
    whole = lambda *shape: pl.BlockSpec(shape, lambda e: (0,) * len(shape))
    once = lambda *shape: pl.BlockSpec(shape, lambda e: (0,) * len(shape), pipeline_mode=pl.Buffered(buffer_count=1))
    aliased = kept is not None
    in_specs = (
        [pl.BlockSpec(memory_space=pltpu.SMEM)]
        + [once(*b.shape) for b in (*blocks, *dz_blocks)]
        + [pl.BlockSpec(memory_space=pl.ANY)] * 3
    )
    aliases = {len(in_specs) + i: count + i for i in range(7)} if aliased else {}
    out = pl.pallas_call(
        functools.partial(expert_kernel, count, slots, aliased),
        grid=(holds,),
        in_specs=in_specs + ([pl.BlockSpec(memory_space=pl.ANY)] * 7 if aliased else []),
        out_specs=[whole(tokens, width)] * count
        + [pl.BlockSpec((count, holds, tokens), lambda e: (first // count, 0, 0))] * 2
        + [pl.BlockSpec((holds, count * slots, width), lambda e: (0, first // count, 0))] * 2
        + [pl.BlockSpec((1, count * slots, hidden), lambda e: (e, first // count, 0))] * 3,
        out_shape=[shaped(tokens, width)] * count
        + [shaped(total, holds, tokens, dtype=WIDE), shaped(total, holds, tokens, dtype=jnp.int32)]
        + [shaped(holds, total * slots, width)] * 2
        + [shaped(holds, total * slots, hidden)] * 3,
        scratch_shapes=[
            pltpu.VMEM((count, holds * slots, tokens), LOW),
            pltpu.VMEM((count, holds * slots, width), LOW),
            pltpu.VMEM((count, holds * slots, 128), WIDE),
            pltpu.VMEM((2, width, hidden), LOW),
            pltpu.VMEM((2, width, hidden), LOW),
            pltpu.VMEM((2, hidden, width), LOW),
            pltpu.SemaphoreType.DMA((2, 3)),
        ],
        input_output_aliases=aliases,
        compiler_params=pltpu.CompilerParams(vmem_limit_bytes=60 * MIB),
        cost_estimate=work(
            flops=2 * holds * count * slots * width * (5 * hidden + 3 * tokens),
            bytes_accessed=3 * holds * width * hidden * 2
            + count * tokens * width * 6
            + holds * count * slots * (2 * width + 3 * hidden) * 2,
            transcendentals=holds * count * slots * hidden,
        ),
    )(token, *blocks, *dz_blocks, w_gate, w_up, w_down, *(kept if aliased else ()))
    return out[:count], tuple(out[count:])


def value_kernel(slots, _, rank_ref, hid_ref, wd_ref, *refs):
    total, holds, tokens = rank_ref.shape
    y_refs, (value_scr, place_scr) = refs[:total], refs[total:]
    e = pl.program_id(0)
    here = pl.ds(pl.multiple_of(e * slots, slots), slots)
    value = dot(hid_ref[0], wd_ref[...]).astype(LOW)
    for b in range(total):
        value_scr[b, here, :] = value[b * slots : (b + 1) * slots]

    @pl.when(e == pl.num_programs(0) - 1)
    def _():
        for b in range(total):
            for l in range(holds):
                spot = places(rank_ref[b, l : l + 1, :], slots)
                place_scr[l * slots : (l + 1) * slots, :] = spot.astype(WIDE).astype(LOW)
            y_refs[b][...] = dot_t(place_scr[...], value_scr[b]).astype(LOW)


def value_call(token, rank, hidden_rows, w_down, slots):
    total, holds, tokens = rank.shape
    width = w_down.shape[1]
    hidden = hidden_rows.shape[2]
    whole = lambda *shape: pl.BlockSpec(shape, lambda e: (0,) * len(shape))
    out = pl.pallas_call(
        functools.partial(value_kernel, slots),
        grid=(holds,),
        in_specs=[
            pl.BlockSpec(memory_space=pltpu.SMEM),
            whole(*rank.shape),
            pl.BlockSpec((1, total * slots, hidden), lambda e: (e, 0, 0)),
            pl.BlockSpec((hidden, width), lambda e: (e, 0)),
        ],
        out_specs=[whole(tokens, width)] * total,
        out_shape=[shaped(tokens, width)] * total,
        scratch_shapes=[pltpu.VMEM((total, holds * slots, width), LOW), pltpu.VMEM((holds * slots, tokens), LOW)],
        compiler_params=pltpu.CompilerParams(vmem_limit_bytes=60 * MIB),
        cost_estimate=work(
            flops=2 * total * holds * slots * width * (hidden + tokens),
            bytes_accessed=2 * (holds * hidden * (width + total * slots) + total * tokens * width),
            transcendentals=0,
        ),
    )(token, rank, hidden_rows, w_down)
    return out


def wgrad_kernel(apart, place_ref, rows_ref, dz_ref, gg_ref, ug_ref, hid_ref, *outs):
    step = pl.program_id(0)
    shard = outs[0].shape[1]
    columns = pl.ds(pl.multiple_of(jnp.bitwise_xor(place_ref[0], step) * shard, 128), shard)
    rows, grads = rows_ref[0, :, columns], dz_ref[0, :, columns]
    parts = [dot_t(rows, gg_ref[0]), dot_t(rows, ug_ref[0]), dot_t(grads, hid_ref[0])]
    parts = [part.astype(LOW) for part in parts]
    for s in range(4):

        @pl.when(step == s)
        def _():
            for i, part in enumerate(parts):
                if s == 3 and apart:
                    outs[3 + i][...] = part
                elif s % 2 and not apart:
                    outs[2][3 - 3 * (s // 2) + i] = part
                else:
                    outs[s if apart else s // 2][i] = part


def wgrad_call(expert, place, kept, apart=False):
    _, count, width = kept[0].shape
    hidden = kept[2].shape[2]
    shard = width // 4
    row_spec = lambda d: pl.BlockSpec((1, count, d), lambda s: (expert, 0, 0), pipeline_mode=pl.Buffered(buffer_count=1))
    shapes = [(3, shard, hidden)] * 3 + [(shard, hidden)] * 3 if apart else [(3, shard, hidden)] * 2 + [(6, shard, hidden)]
    out = pl.pallas_call(
        functools.partial(wgrad_kernel, apart),
        grid=(4,),
        in_specs=[pl.BlockSpec(memory_space=pltpu.SMEM), row_spec(width), row_spec(width)] + [row_spec(hidden)] * 3,
        out_specs=[pl.BlockSpec(shape, lambda s, zeros=(0,) * len(shape): zeros) for shape in shapes],
        out_shape=[shaped(*shape) for shape in shapes],
        compiler_params=pltpu.CompilerParams(vmem_limit_bytes=60 * MIB),
        cost_estimate=work(
            flops=2 * count * width * 3 * hidden,
            bytes_accessed=2 * (count * (2 * width + 3 * hidden) + 3 * width * hidden),
            transcendentals=0,
        ),
    )(place, *kept)
    return (out[0], out[2], out[3:], out[1]) if apart else out


def sums_call(gates, *sums):
    every = [term[0] if isinstance(term, tuple) else term for terms in sums for term in terms]

    def part_of(term, ready=()):
        array, part = term if isinstance(term, tuple) else (term, None)
        array = after(array, *ready) if ready else array
        return array if part is None else array[: len(part)] if isinstance(part, range) else array[part]

    totals = [add_low(part_of(terms[0], (*gates, *every)), *map(part_of, terms[1:])) for terms in sums]
    return totals


def finish_kernel(sizes, turned, *refs):
    outs = refs[-len(sizes) :]
    at = 0
    for counts, turn, out in zip(sizes, turned, outs):
        for i, size in enumerate(counts):
            total = sum(ref[...].astype(WIDE) for ref in refs[at : at + size])
            at += size
            if turn:
                height = out.shape[0] // len(counts)
                out[i * height : (i + 1) * height, :] = jnp.transpose(total)
            else:
                out[...] = total


def finish_call(holds, pieces, kept):
    shard, hidden = pieces[0][2][0][0][0].shape[-2:]
    steps = shard // 128
    wide, tall = shaped(shard, holds * hidden, dtype=WIDE), shaped(holds * hidden, shard, dtype=WIDE)
    flat = [term for _, _, experts in pieces for terms in experts for term in terms]
    out_specs, out_shapes = [], []
    for which, expert, experts in pieces:
        number = len(experts)
        if which < 2:
            out_specs.append(pl.BlockSpec((128, hidden), lambda s, expert=expert: (s, expert)))
        else:
            block = (number * hidden, 128)
            out_specs.append(pl.BlockSpec(block, lambda s, at=expert // number: (at, s)))
        out_shapes.append(wide if which < 2 else tall)
    kept_in = [kept[which] for which, _, _ in pieces] if kept else []
    out = pl.pallas_call(
        functools.partial(
            finish_kernel, [[len(terms) for terms in experts] for _, _, experts in pieces], [p[0] == 2 for p in pieces]
        ),
        grid=(steps,),
        in_specs=[
            pl.BlockSpec((128, hidden), lambda s: (s, 0))
            if at is None
            else pl.BlockSpec((None, 128, hidden), lambda s, at=at: (at, s, 0))
            for _, at in flat
        ]
        + [pl.BlockSpec(memory_space=pl.ANY)] * len(kept_in),
        out_specs=out_specs,
        out_shape=out_shapes,
        input_output_aliases={len(flat) + i: i for i in range(len(kept_in))},
        compiler_params=pltpu.CompilerParams(vmem_limit_bytes=20 * MIB),
        cost_estimate=work(flops=0, bytes_accessed=30 * shard * hidden, transcendentals=0),
    )(*[array for array, _ in flat], *kept_in)
    result = list(kept) if kept else [None] * 3
    for (which, _, _), value in zip(pieces, out):
        result[which] = value
    return result


def piece_columns(mine, s, shard):
    return pl.ds(pl.multiple_of(jnp.bitwise_xor(mine, s) * shard, 128), shard)


def turn(values, cos, sin):
    return values * cos + pltpu.roll(values, HEAD_DIM // 2, 1) * sin


def turn_back(values, cos, sin):
    return values * cos - pltpu.roll(values, HEAD_DIM // 2, 1) * sin


def inverse_rms(values):
    return lax.rsqrt(jnp.mean(values * values, axis=-1, keepdims=True) + EPS)


def head_slice(h):
    return slice(h * HEAD_DIM, (h + 1) * HEAD_DIM)


def stacked_heads(ref, band, group, heads):
    return jnp.concatenate([ref[band, head_slice(group * heads + h)] for h in range(heads)], axis=0)


def probabilities(queries, keys, allowed):
    scores = jnp.where(allowed, dot_bt(queries, keys) * HEAD_DIM ** (-0.5), NEG)
    expo = jnp.exp(scores - jnp.max(scores, axis=-1, keepdims=True))
    return expo * (1.0 / jnp.sum(expo, axis=-1, keepdims=True))


def allowed_pairs(seg_col_ref, seg_row_ref, band, reach, heads):
    size = band.stop - band.start
    rows = band.start + lax.broadcasted_iota(jnp.int32, (size, reach), 0)
    cols = lax.broadcasted_iota(jnp.int32, (size, reach), 1)
    ok = (seg_col_ref[band, :] == seg_row_ref[:, :reach]) & (cols <= rows)
    return jnp.concatenate([ok] * heads, axis=0)


def attention_kernel(
    mine_ref, tokens_ref, gain_ref, p0, p1, p2, p3, s0, s1, s2, s3, seg_row_ref, seg_col_ref, cos_ref, sin_ref,
    h_ref, q_ref, k_ref, v_ref, out_ref,
):
    mine = mine_ref[0]
    stream = tokens_ref[...].astype(WIDE)
    h_ref[...] = (stream * inverse_rms(stream) * gain_ref[...]).astype(LOW)
    shard = p0.shape[0]
    width = q_ref.shape[1]
    cos, sin = cos_ref[...], sin_ref[...]

    def projected(pieces, columns):
        return sum(dot(h_ref[:, piece_columns(mine, s, shard)], piece[:, columns]) for s, piece in enumerate(pieces))

    heads = QUERY_HEADS // KEY_VALUE_HEADS
    key_width = KEY_VALUE_HEADS * HEAD_DIM
    shared = (s0, s1, s2, s3)
    keys = projected(shared, slice(0, key_width))
    for g in range(KEY_VALUE_HEADS):
        k_ref[:, head_slice(g)] = turn(keys[:, head_slice(g)], cos, sin).astype(LOW)
    v_ref[...] = projected(shared, slice(key_width, 2 * key_width)).astype(LOW)
    group_width = heads * HEAD_DIM
    for g in range(KEY_VALUE_HEADS):
        queries = projected((p0, p1, p2, p3), slice(g * group_width, (g + 1) * group_width))
        for h in range(heads):
            q_ref[:, head_slice(g * heads + h)] = turn(queries[:, head_slice(h)], cos, sin).astype(LOW)
    length = q_ref.shape[0]
    tile = 128
    for start in range(0, length, tile):
        band, reach = slice(start, start + tile), start + tile
        allowed = allowed_pairs(seg_col_ref, seg_row_ref, band, reach, heads)
        for g in range(KEY_VALUE_HEADS):
            probs = probabilities(stacked_heads(q_ref, band, g, heads), k_ref[:reach, head_slice(g)], allowed)
            mixed = dot(probs.astype(LOW), v_ref[:reach, head_slice(g)]).astype(LOW)
            for h in range(heads):
                out_ref[band, head_slice(g * heads + h)] = mixed[h * tile : (h + 1) * tile]


def vmem_call(kernel, out_shape, flops, transcendentals, token, *args):
    moved = sum(a.size * a.dtype.itemsize for a in args) + sum(
        o.size * o.dtype.itemsize for o in jax.tree.leaves(out_shape)
    )
    return pl.pallas_call(
        kernel,
        in_specs=[pl.BlockSpec(memory_space=pltpu.SMEM)] + [pl.BlockSpec(memory_space=pltpu.VMEM)] * len(args),
        out_specs=[pl.BlockSpec(memory_space=pltpu.VMEM)] * len(out_shape),
        out_shape=out_shape,
        compiler_params=pltpu.CompilerParams(vmem_limit_bytes=60 * MIB),
        cost_estimate=work(flops=flops, bytes_accessed=moved, transcendentals=transcendentals),
    )(token, *args)


def shaped(*shape, dtype=LOW):
    return jax.ShapeDtypeStruct(shape, dtype)


def attention_call(mine, tokens, gain, pieces, shared_pieces, seg_row, seg_col, cos, sin):
    length, width = tokens.shape
    key_width = KEY_VALUE_HEADS * HEAD_DIM
    return vmem_call(
        attention_kernel,
        [shaped(length, width), shaped(length, width), shaped(length, key_width), shaped(length, key_width), shaped(length, width)],
        2 * length * width * (width + 2 * key_width) + 3 * length * length * width,
        QUERY_HEADS * length * length,
        mine, tokens, gain, *pieces, *shared_pieces, seg_row, seg_col, cos, sin,
    )


def project_kernel(
    mine_ref, tokens_ref, attn_ref, p0, p1, p2, p3, r0, r1, r2, r3, gain_ref, routes_ref, resid_ref, h_ref
):
    mine = mine_ref[0]
    shard = p0.shape[0]
    resid = tokens_ref[...].astype(WIDE)
    for s, piece in enumerate((p0, p1, p2, p3)):
        resid = resid + dot(attn_ref[:, piece_columns(mine, s, shard)], piece[...])
    resid_ref[...] = resid
    length, width = resid.shape
    h_ref[:length] = (resid * inverse_rms(resid) * gain_ref[...]).astype(LOW)
    logits = jnp.transpose(
        sum(
            dot(h_ref[:length, piece_columns(mine, s, shard)], piece[...])
            for s, piece in enumerate((r0, r1, r2, r3))
        )
    )
    experts = lax.broadcasted_iota(jnp.int32, logits.shape, 0)
    picked = [
        jnp.sum(jnp.where(experts == routes_ref[k : k + 1, :], logits, 0.0), axis=0, keepdims=True)
        for k in range(routes_ref.shape[0])
    ]
    top = functools.reduce(jnp.maximum, picked)
    expo = [jnp.exp(p - top) for p in picked]
    total = sum(expo)
    gates = jnp.concatenate([x / total for x in expo], axis=0)
    h_ref[length:] = jnp.zeros((16, width), LOW)
    h_ref[length:, :length] = pack_routing(gates, routes_ref[...])


def project_call(mine, tokens, attn, pieces, shared_pieces, gain, routes_t):
    length, width = tokens.shape
    whole = lambda shape: pl.BlockSpec(shape, lambda i: (0,) * len(shape), pipeline_mode=ONCE)
    shapes = [shaped(length, width, dtype=WIDE), shaped(length + 16, width)]
    return pl.pallas_call(
        project_kernel,
        grid=(1,),
        in_specs=[pl.BlockSpec(memory_space=pltpu.SMEM)]
        + [whole(a.shape) for a in (tokens, attn, *pieces)]
        + router_columns(shared_pieces)
        + [whole(gain.shape), whole(routes_t.shape)],
        out_specs=[whole(s.shape) for s in shapes],
        out_shape=shapes,
        compiler_params=pltpu.CompilerParams(vmem_limit_bytes=60 * MIB),
        cost_estimate=work(
            flops=2 * length * width * (width + EXPERTS), bytes_accessed=length * width * 20, transcendentals=length * 8
        ),
    )(mine, tokens, attn, *pieces, *shared_pieces, gain, routes_t)


def as_column(row):
    return jnp.transpose(jnp.broadcast_to(row, (8, row.shape[1])))[:, :1]


def norm_back(grad, gain, normed, inverse):
    scaled = grad * gain
    return inverse * (scaled - normed * jnp.mean(scaled * normed, axis=-1, keepdims=True))


def shard_parts(targets):
    at, parts = 0, []
    for target in targets:
        parts.append((target, slice(at, at + target.shape[0])))
        at += target.shape[0]
    return parts


def resid_back_kernel(
    mine_ref, resid_ref, gain_ref, dz_ref, t0, t1, t2, gains_ref, h_ref, attn_ref,
    p0, p1, p2, p3, r0, r1, r2, r3, grad_ref, attn_grad_ref, small_ref, o0, o1, o2, o3, o4, o5, second_scr, low_scr,
):
    mine = mine_ref[0]
    shard, width = p0.shape
    length = resid_ref.shape[0]
    routers = (r0, r1, r2, r3)
    gains = gains_ref[...]
    experts = lax.broadcasted_iota(jnp.int32, gains.shape, 0)
    gate_rows, routes = unpack_routing(h_ref[length:, :length])
    gates = jnp.zeros(gains.shape, WIDE)
    for k in range(TOP):
        gates = gates + jnp.where(experts.astype(WIDE) == routes[k : k + 1], gate_rows[k : k + 1], 0.0)
    logit_grad = gates * (gains - jnp.sum(gates * gains, axis=0, keepdims=True))
    logit_grad = jnp.concatenate([logit_grad, jnp.zeros((128 - EXPERTS, length), WIDE)], axis=0)
    logit_grad = jnp.transpose(logit_grad).astype(LOW)
    second_scr[...] = t0[...].astype(WIDE) + t1[...].astype(WIDE) + t2[...].astype(WIDE)
    for s, piece in enumerate(routers):
        columns = piece_columns(mine, s, shard)
        second_scr[:, columns] = second_scr[:, columns] + dot_bt(logit_grad, piece[...])
    resid = resid_ref[...]
    inverse = inverse_rms(resid)
    normed = resid * inverse
    second = second_scr[...]
    gain_grad = jnp.sum(second * normed, axis=0, keepdims=True)
    grad = dz_ref[...].astype(WIDE) + norm_back(second, gain_ref[...], normed, inverse)
    grad_ref[...] = grad
    low_scr[...] = grad.astype(LOW)
    second_scr[:1, :] = gain_grad
    low = low_scr[...]
    for s, piece in enumerate((p0, p1, p2, p3)):
        columns = piece_columns(mine, s, shard)
        attn_grad_ref[:, columns] = dot_bt(low, piece[...]).astype(LOW)
        out_part = dot_t(attn_ref[:, columns], low).astype(LOW)
        router_part = dot_t(h_ref[:length, columns], logit_grad)
        lanes = lax.broadcasted_iota(jnp.int32, router_part.shape, 1)
        small_ref[s] = jnp.where(lanes == EXPERTS, as_column(second_scr[:1, columns]), router_part).astype(LOW)
        for target, rows in shard_parts(((o0,), (o1,), (o2, o3), (o4, o5))[s]):
            target[...] = out_part[rows]


def router_columns(pieces):
    return [
        pl.BlockSpec((p.shape[0], 128), lambda i, at=p.shape[1] // 128 - 1: (0, at), pipeline_mode=ONCE) for p in pieces
    ]


def resid_back_call(mine, resid, gain, dz, terms, gains, h, attn, pieces, shared_pieces):
    length, width = resid.shape
    shard = pieces[0].shape[0]
    whole = lambda shape: pl.BlockSpec(shape, lambda i: (0,) * len(shape), pipeline_mode=ONCE)
    arrays = (resid, gain, dz, *terms, gains, h, attn, *pieces)
    shapes = [shaped(length, width, dtype=WIDE), shaped(length, width), shaped(4, shard, 128)]
    shapes += [shaped(shard, width)] * 2 + [shaped(shard // 2, width)] * 4
    return pl.pallas_call(
        resid_back_kernel,
        grid=(1,),
        in_specs=[pl.BlockSpec(memory_space=pltpu.SMEM)]
        + [whole(a.shape) for a in arrays]
        + router_columns(shared_pieces),
        out_specs=[whole(s.shape) for s in shapes],
        out_shape=shapes,
        scratch_shapes=[pltpu.VMEM((length, width), WIDE), pltpu.VMEM((length, width), LOW)],
        compiler_params=pltpu.CompilerParams(vmem_limit_bytes=60 * MIB),
        cost_estimate=work(
            flops=4 * length * width * (width + EXPERTS), bytes_accessed=length * width * 40, transcendentals=0
        ),
    )(mine, *arrays, *shared_pieces)


def attention_back_kernel(
    mine_ref, q_ref, k_ref, v_ref, do_ref, h_ref, tokens_ref, gain_ref, grad_ref, small_ref, p0, p1, p2, p3, s0, s1, s2, s3,
    seg_row_ref, seg_col_ref, cos_ref, sin_ref, input_ref, o0, o1, o2, o3, o4, o5, qkv_scr, dk_scr, dv_scr, dh_scr,
):
    mine = mine_ref[0]
    length, width = q_ref.shape
    shard = p0.shape[0]
    qkv_width = width + 2 * KEY_VALUE_HEADS * HEAD_DIM
    heads = QUERY_HEADS // KEY_VALUE_HEADS
    key_width = KEY_VALUE_HEADS * HEAD_DIM
    tile = 128
    dk_scr[...] = jnp.zeros_like(dk_scr)
    dv_scr[...] = jnp.zeros_like(dv_scr)
    for start in range(0, length, tile):
        band, reach = slice(start, start + tile), start + tile
        allowed = allowed_pairs(seg_col_ref, seg_row_ref, band, reach, heads)
        cos, sin = cos_ref[band, :], sin_ref[band, :]
        for g in range(KEY_VALUE_HEADS):
            queries = stacked_heads(q_ref, band, g, heads)
            grads = stacked_heads(do_ref, band, g, heads)
            keys = k_ref[:reach, head_slice(g)]
            probs = probabilities(queries, keys, allowed)
            prob_grad = dot_bt(grads, v_ref[:reach, head_slice(g)])
            delta = jnp.sum(probs * prob_grad, axis=-1, keepdims=True)
            score_grad = (probs * (prob_grad - delta) * HEAD_DIM ** (-0.5)).astype(LOW)
            dv_scr[:reach, head_slice(g)] += dot_t(probs.astype(LOW), grads)
            dk_scr[:reach, head_slice(g)] += dot_t(score_grad, queries)
            dq = dot(score_grad, keys)
            for h in range(heads):
                qkv_scr[band, head_slice(g * heads + h)] = turn_back(dq[h * tile : (h + 1) * tile], cos, sin).astype(LOW)
    for g in range(KEY_VALUE_HEADS):
        at = width + g * HEAD_DIM
        qkv_scr[:, at : at + HEAD_DIM] = turn_back(dk_scr[:, head_slice(g)], cos_ref[...], sin_ref[...]).astype(LOW)
    qkv_scr[:, width + key_width :] = dv_scr[...].astype(LOW)
    qkv = qkv_scr[...]
    for s, (piece, shared) in enumerate(zip((p0, p1, p2, p3), (s0, s1, s2, s3))):
        dh_scr[:, piece_columns(mine, s, shard)] = dot_bt(qkv[:, :width], piece[...]) + dot_bt(qkv[:, width:], shared[:, : 2 * key_width])
    stream = tokens_ref[...].astype(WIDE)
    inverse = inverse_rms(stream)
    normed = stream * inverse
    first = dh_scr[...]
    gain_grad = jnp.sum(first * normed, axis=0, keepdims=True)
    input_ref[...] = grad_ref[...] + norm_back(first, gain_ref[...], normed, inverse)
    dh_scr[:1, :] = gain_grad
    for s in range(4):
        columns = piece_columns(mine, s, shard)
        part = dot_t(h_ref[:, columns], qkv).astype(LOW)
        small = small_ref[s].astype(WIDE)
        lanes = lax.broadcasted_iota(jnp.int32, small.shape, 1)
        small = jnp.where(lanes == EXPERTS + 1, as_column(dh_scr[:1, columns]), small).astype(LOW)
        for target, rows in shard_parts(((o0,), (o1,), (o2, o3), (o4, o5))[s]):
            target[:, :qkv_width] = part[rows]
            target[:, qkv_width:] = small[rows]


def attention_back_call(
    mine, q, k, v, do, h, tokens, gain, grad, small, pieces, shared_pieces, seg_row, seg_col, cos, sin
):
    length, width = q.shape
    shard = pieces[0].shape[0]
    qkv_width = width + 2 * KEY_VALUE_HEADS * HEAD_DIM
    key_width = KEY_VALUE_HEADS * HEAD_DIM
    return pl.pallas_call(
        attention_back_kernel,
        in_specs=[pl.BlockSpec(memory_space=pltpu.SMEM)] + [pl.BlockSpec(memory_space=pltpu.VMEM)] * 21,
        out_specs=[pl.BlockSpec(memory_space=pltpu.VMEM)] * 7,
        out_shape=[shaped(length, width, dtype=WIDE)]
        + [shaped(shard, qkv_width + 128)] * 2
        + [shaped(shard // 2, qkv_width + 128)] * 4,
        scratch_shapes=[
            pltpu.VMEM((length, qkv_width), LOW),
            pltpu.VMEM((length, key_width), WIDE),
            pltpu.VMEM((length, key_width), WIDE),
            pltpu.VMEM((length, width), WIDE),
        ],
        compiler_params=pltpu.CompilerParams(vmem_limit_bytes=46 * MIB),
        cost_estimate=work(
            flops=4 * length * width * qkv_width + 7 * length * length * width,
            bytes_accessed=length * width * 40,
            transcendentals=QUERY_HEADS * length * length,
        ),
    )(mine, q, k, v, do, h, tokens, gain, grad, small, *pieces, *shared_pieces, seg_row, seg_col, cos, sin)


def spread_kernel(count, token_ref, *refs):
    parts, outs, scratch = refs[2 : -count - 1], refs[-count - 1 : -1], refs[-1]
    for part, rows in shard_parts(parts):
        scratch[rows] = part[...]
    chunk = outs[0].shape[0]
    for j, out in enumerate(outs):
        rows = pl.ds(pl.multiple_of(lax.rem(token_ref[2] + j, count) * chunk, 16), chunk)
        out[...] = sum(term[rows, :].astype(WIDE) for term in (*refs[:2], scratch)).astype(LOW)


def spread_call(token, count, *terms):
    rows, width = terms[0].shape
    whole = lambda shape: pl.BlockSpec(shape, lambda i: (0, 0), pipeline_mode=ONCE)
    return pl.pallas_call(
        functools.partial(spread_kernel, count),
        grid=(1,),
        in_specs=[pl.BlockSpec(memory_space=pltpu.SMEM)] + [whole(t.shape) for t in terms],
        out_specs=[whole((rows // count, width))] * count,
        out_shape=[shaped(rows // count, width)] * count,
        scratch_shapes=[pltpu.VMEM((rows, width), LOW)],
        compiler_params=pltpu.CompilerParams(vmem_limit_bytes=16 * MIB),
        cost_estimate=work(flops=0, bytes_accessed=8 * rows * width, transcendentals=0),
    )(token, *terms)


def assemble_kernel(count, widths, token_ref, *refs):
    chunks, outs = refs[:count], refs[count:]
    chunk = chunks[0].shape[0]
    for j, ref in enumerate(chunks):
        rows = pl.ds(pl.multiple_of(lax.rem(token_ref[2] + j, count) * chunk, 16), chunk)
        values = ref[...].astype(WIDE)
        at = 0
        for width, out in zip(widths, outs):
            out[rows, :] = values[:, at : at + width]
            at += width
        if len(outs) > len(widths):
            outs[-1][rows, :] = values[:, at : at + 128]
    if len(outs) > len(widths):
        router_ref, ffn_ref, attn_ref, scratch = outs[len(widths) :]
        small = jnp.transpose(scratch[...])
        router_ref[...] = small[:EXPERTS]
        ffn_ref[...] = small[EXPERTS]
        attn_ref[...] = small[EXPERTS + 1]


def assemble_call(token, chunks, widths):
    count, (rows, width) = len(chunks), chunks[0].shape
    whole = lambda shape: pl.BlockSpec(shape, lambda i: (0,) * len(shape), pipeline_mode=ONCE)
    small = width > sum(widths)
    shapes = [(count * rows, w) for w in widths]
    shapes += [(EXPERTS, count * rows), (count * rows,), (count * rows,)] if small else []
    return pl.pallas_call(
        functools.partial(assemble_kernel, count, widths),
        grid=(1,),
        in_specs=[pl.BlockSpec(memory_space=pltpu.SMEM)] + [whole((rows, width))] * count,
        out_specs=[whole(shape) for shape in shapes],
        out_shape=[shaped(*shape, dtype=WIDE) for shape in shapes],
        scratch_shapes=[pltpu.VMEM((count * rows, 128), WIDE)] if small else [],
        compiler_params=pltpu.CompilerParams(vmem_limit_bytes=16 * MIB),
        cost_estimate=work(flops=0, bytes_accessed=6 * count * rows * width, transcendentals=0),
    )(token, *chunks)


def per_device_ring(
    tokens,
    segments,
    routes,
    attn_gain,
    ffn_gain,
    w_query,
    key_weight,
    value_weight,
    w_out,
    w_router,
    w_gate,
    w_up,
    w_down,
    cotangent,
):
    length, model_width = tokens.shape
    top_count = routes.shape[1]
    count = lax.axis_size("expert")
    holds = EXPERTS // count
    capacity = max(2, 3 * length * top_count // (2 * EXPERTS))
    slots = -(-capacity // 16) * 16
    shard = model_width // 4
    key_width = KEY_VALUE_HEADS * HEAD_DIM
    half = length // 2
    mine = lax.axis_index("wshard").astype(jnp.int32)
    order = jnp.array(ring_order(count), jnp.int32)
    spot_of = jnp.array([ring_order(count).index(i) for i in range(count)], jnp.int32)
    here = lax.axis_index("expert").astype(jnp.int32)
    spot = spot_of[here]
    token = jnp.stack([mine, here, spot])
    routes_t = routes.T

    cosine, sine = rotary_tables(length, HEAD_DIM)
    cos = jnp.concatenate([cosine, cosine], axis=1)
    sin = jnp.concatenate([-sine, sine], axis=1)
    seg_col = segments.reshape(length, 1)
    gain_one, gain_two = attn_gain[None], ffn_gain[None]

    def pieces_of(own, across, *ready):
        return (own, swap_core(own), across, swap_core(after(across, *ready)))

    dz = {0: cotangent}
    dz[-1], dz[1] = ahead(dz[0], count), behind(dz[0], count)
    query_across = swap_x(w_query)
    query_pieces = pieces_of(w_query, query_across)
    spare = jnp.zeros((shard, 128 - EXPERTS), LOW)
    shared = jnp.concatenate([key_weight, value_weight, w_router, spare], axis=1)
    shared, token, seg_col, cos, sin, routes_t, gain_one, gain_two = lax.optimization_barrier(
        (shared, token, seg_col, cos, sin, routes_t, gain_one, gain_two)
    )
    shared_across = swap_x(after(shared, query_across, dz[-1], dz[1]))
    dz[-2], dz[2] = ahead(dz[-1], count), behind(dz[1], count)
    shared_pieces = pieces_of(shared, shared_across)
    out_across = swap_x(after(w_out, shared_across))

    first_low, query, key, value, attn = attention_call(
        after(token, dz[-2], dz[2]), tokens, gain_one, query_pieces, shared_pieces, segments, seg_col, cos, sin
    )
    out_pieces = pieces_of(w_out, out_across, attn)
    dz[-3], dz[3] = ahead(dz[-2], count), behind(dz[2], count)
    resid, second = project_call(after(token, dz[-3], dz[3]), tokens, attn, out_pieces, shared_pieces, gain_two, routes_t)

    def experts(ready, first, offsets, kept):
        return expert_call(
            after(token, *ready), first, [h[j] for j in offsets], [dz[j] for j in offsets], w_gate, w_up, w_down, kept,
            holds, slots, count,
        )

    h = {0: second}
    h[-1], h[1] = ahead(h[0], count), behind(h[0], count)
    (d_own,), kept = experts((), 6, (0,), None)
    h[-2], h[2] = ahead(after(h[-1], d_own), count), behind(after(h[1], d_own), count)
    (d_l1, d_r1), kept = experts((), 0, (-1, 1), kept)
    h[-3], h[3] = ahead(after(h[-2], d_l1), count), behind(after(h[2], d_l1), count)
    (d_l2, d_r2), kept = experts((), 2, (-2, 2), kept)
    h[4], dz[4] = ahead(after(h[-3], d_l2), count), behind(after(dz[3], d_l2), count)
    (d_l3, d_r3), kept = experts((), 4, (-3, 3), kept)
    (d_far,), (gains, rank, *kept) = experts((), 7, (4,), kept)

    block_of = jnp.array([BLOCK_OFFSETS.index(j if j <= count // 2 else j - count) for j in range(count)], jnp.int32)
    gain_send = gains[block_of[(spot_of - spot) % count]]

    def weight_grads(expert, *ready):
        return wgrad_call(expert, after(token, *ready), kept)

    def over_cores(grads, *ready):
        return swap_core(after(grads[2], *ready))

    both, last = range(2), 2

    def sum_of(grads, got, part):
        return (grads[1], part), (got, part)

    up_sent, down_sent = ahead(d_far, count), behind(d_l3, count)
    grads = [wgrad_call(0, token, kept, True)]
    got = [[swap_core(v) for v in grads[0][2]]]
    grads.append(weight_grads(1, grads[0][0]))
    up, down = sums_call((grads[1][0], *got[0],), (d_r3, up_sent), (d_l2, down_sent))

    up_sent, down_sent = ahead(up, count), behind(down, count)
    got.append(over_cores(grads[1], up))
    halves = [sums_call((up,), *[((grads[0][1], i), got[0][i]) for i in range(3)])]
    across = [[(swap_x(v), None) for v in halves[0][:2]]]
    gain_dense = lax.all_to_all(after(gain_send, up), "expert", split_axis=0, concat_axis=0, tiled=True)
    gain_dense = gain_dense.reshape(EXPERTS, length)
    grads.append(weight_grads(2, *halves[0]))
    up, down = sums_call((gain_dense, grads[2][0], across[0][0][0], across[0][1][0],), (d_r2, up_sent), (d_l1, down_sent))

    up_sent, down_sent = ahead(up, count), behind(down, count)
    got.append(over_cores(grads[2], up))
    halves.append(sums_call((up,), sum_of(grads[1], got[1], both)))
    across_b = swap_x(halves[1][0])
    y = dict(zip(BLOCK_OFFSETS, value_call(after(token, *halves[1]), rank, kept[4], w_down, slots)))
    late = swap_core(after(grads[0][3], up))
    halves[1] += sums_call((y[0],), sum_of(grads[1], got[1], last))
    halves.append(sums_call((y[0],), sum_of(grads[2], got[2], both), sum_of(grads[2], got[2], last)))
    (up,) = sums_call((*halves[2], across_b, down_sent, late, halves[1][1]), (d_r1, up_sent))

    up_sent, y_down = ahead(up, count), behind(after(y[4], up), count)
    across[0].append((swap_x(after(halves[0][2], up)), None))
    across.append([(across_b, 0), (across_b, 1), (swap_x(after(halves[1][1], up)), None)])
    grads.append(weight_grads(3, up))
    (down,) = sums_call(
        (up_sent, across[0][2][0], across[1][2][0], grads[3][0]), (y[-3], y_down)
    )

    y_up, y_down, across_d = ahead(after(y[3], down), count), behind(down, count), swap_x(after(halves[2][0], down))
    grad, attn_grad, small, *out_parts = resid_back_call(
        after(token, down), resid, gain_two, cotangent, (d_own, up_sent, down_sent), gain_dense, second,
        attn, out_pieces, shared_pieces,
    )
    def terms_of(expert, i, *ready):
        other = (late, i) if expert == 0 else (got[expert], 3 + i)
        return [(after(grads[expert][0], *ready) if ready else grads[expert][0], i), other, across[expert][i]]

    def finish(ready, expert, kept_out, parts=range(3)):
        return finish_call(holds, [(i, expert, [terms_of(expert, i, *ready)]) for i in parts], kept_out)

    out_first = [swap_core(v) for v in out_parts[4:]]
    finished = finish((grad,), 0, None)
    *out_half, up, down = sums_call(
        (finished[0], across_d), *zip(out_parts[2:4], out_first), (y[2], y_up), (y[-2], y_down)
    )

    y_up, y_down, out_across = ahead(up, count), behind(down, count), [swap_x(v) for v in out_half]
    out_got = swap_core(after(out_parts[1], up))
    input_grad, *qkv_parts = attention_back_call(
        after(token, up), query, key, value, attn_grad, first_low, tokens, gain_one, grad, small, query_pieces,
        shared_pieces, segments, seg_col, cos, sin,
    )
    up, down = sums_call((input_grad, *out_across, out_got), (y[1], y_up), (y[-1], y_down))

    y_up, y_down = ahead(up, count), behind(down, count)
    qkv_first = [swap_core(after(v, up)) for v in qkv_parts[4:]]
    qkv_half = sums_call((up,), *zip(qkv_parts[2:4], qkv_first))
    qkv_across = [swap_x(qkv_half[0])]
    out_parts = spread_call(after(token, *qkv_half), count, out_parts[0], out_got, *out_across)
    finished = finish(qkv_half, 1, finished)
    qkv_got = swap_core(after(qkv_parts[1], qkv_across[0]))
    got.append(over_cores(grads[3], qkv_half[0]))
    (half_e,) = sums_call((finished[0],), sum_of(grads[3], got[3], range(3)))
    across.append([(across_d, 0), (across_d, 1)])
    finished = finish((half_e,), 2, finished, both)
    def sum_step(parts, up, down, step):
        up = add_low(parts[step], ahead(up, count))
        down = behind(down, count)
        return up, add_low(parts[count + 1 - step], down) if step > 1 else down

    def copy_step(up, down):
        return up + [ahead(up[-1], count)], down + [behind(down[-1], count)]

    qkv_across.append(swap_x(after(qkv_half[1], qkv_across[0])))
    out_up, out_down = after(out_parts[4], finished[0], finished[0]), after(out_parts[5], finished[0], finished[0])
    for step in (3, 2, 1):
        out_up, out_down = sum_step(out_parts, out_up, out_down, step)
        if step == 3:
            y_own = after(y[0], qkv_across[0], out_up, out_down)
            mixed = (resid + sum(t.astype(WIDE) for t in (y_own, y_up, y_down))).astype(LOW)
            out_up, out_down = after(out_up, mixed), after(out_down, mixed)
        if step == 2:
            out_up = after(out_up, qkv_across[1])
    out_own = add_low(out_parts[0], ahead(out_up, count), out_down)
    across_e = [swap_x(after(halves[2][1], qkv_across[1])), swap_x(after(half_e, qkv_across[1]))]
    qkv_parts = spread_call(after(token, out_own), count, qkv_parts[0], qkv_got, *qkv_across)
    across[2].append((across_e[0], None))
    across.append([(across_e[1], i) for i in range(3)])
    out_ups, out_downs = [after(out_own, qkv_parts[0])], [after(out_own, qkv_parts[0])]
    qkv_up, qkv_down = qkv_parts[4], qkv_parts[5]
    for step in (3, 2, 1):
        out_ups, out_downs = copy_step(out_ups, out_downs)
        qkv_up, qkv_down = sum_step(qkv_parts, qkv_up, qkv_down, step)
        qkv_up = after(qkv_up, out_ups[-1], out_downs[-1])
    out_ups.append(ahead(out_ups[-1], count))
    qkv_own = add_low(qkv_parts[0], ahead(qkv_up, count), qkv_down)
    qkv_ups, qkv_downs = [qkv_own], [qkv_own]
    for step in (3, 2, 1):
        qkv_ups, qkv_downs = copy_step(qkv_ups, qkv_downs)
        if step == 3:
            qkv_ups[-1] = after(qkv_ups[-1], out_ups[-1])
    (out_sum,) = assemble_call(after(token, qkv_ups[2]), out_downs + out_ups[:0:-1], (model_width,))
    qkv_ups.append(ahead(after(qkv_ups[-1], out_sum, across_e[1]), count))
    last_rows = [terms_of(2, 2, qkv_ups[3]), terms_of(3, 2)]
    finished = finish_call(
        holds, [(0, 3, [terms_of(3, 0, qkv_ups[3])]), (1, 3, [terms_of(3, 1)]), (2, 2, last_rows)], finished
    )
    query_sum, key_sum, value_sum, router_sum, ffn_gain_sum, attn_gain_sum = assemble_call(
        after(token, finished[0]), qkv_downs + qkv_ups[:0:-1], (model_width, key_width, key_width)
    )
    gate_shard, up_shard, down_shard = finished
    return (
        mixed,
        input_grad,
        attn_gain_sum,
        ffn_gain_sum,
        query_sum,
        key_sum,
        value_sum,
        out_sum,
        router_sum.T,
        gate_shard,
        up_shard,
        down_shard,
    )


def solution(mesh):
    ring = mesh.shape["expert"] == len(BLOCK_OFFSETS) and mesh.shape["wshard"] == 4
    body = per_device_ring if ring else per_device_exchange
    in_specs = (
        P(("expert", "wshard"), None),
        P(("expert", "wshard"), None),
        P(("expert", "wshard"), None),
        P(),
        P(),
        P("wshard", None),
        P("wshard", None),
        P("wshard", None),
        P("wshard", None),
        P("wshard", None),
        P(None, "expert"),
        P(None, "expert"),
        P("expert", None),
        P(("expert", "wshard"), None),
    )
    out_specs = (
        P(("expert", "wshard"), None),
        P(("expert", "wshard"), None),
        P("wshard"),
        P("wshard"),
        P("wshard", None),
        P("wshard", None),
        P("wshard", None),
        P("wshard", None),
        P("wshard", None),
        P("wshard", "expert"),
        P("wshard", "expert"),
        P("expert", "wshard"),
    )
    return jax.shard_map(
        body, mesh=mesh, in_specs=in_specs, out_specs=out_specs, check_vma=False
    )
```
